32 devices in a mesh: seq: 8 (over z, core), dp: 4 (over y, x).
Axes of the slice: x: 2, y: 2, z: 4, core: 2. Of those that a mesh axis runs over, the one named last changes fastest.
Arguments:
- block_input: bfloat16 [32, 1024, 768], P('dp', 'seq'), may hold values from -6 to 6
- doc_bounds: int32 [32, 2], P('dp'), may hold values from 1 to 1024, as said below
- first_gain: bfloat16 [768], P('dp'), may hold values from 0.5 to 1.5
- first_shift: bfloat16 [768], P('dp'), may hold values from -1 to 1
- qkv_weight: bfloat16 [768, 2304], P('dp'), may hold values from -0.21875 to 0.21875
- qv_bias: bfloat16 [1536], P('dp'), may hold values from -1 to 1
- score_weight: bfloat16 [768, 12], P('dp'), may hold values from -0.3125 to 0.3125
- out_weight: bfloat16 [768, 768], P('dp'), may hold values from -0.625 to 0.625
- out_bias: bfloat16 [768], P('dp'), may hold values from -1 to 1
- second_gain: bfloat16 [768], P('dp'), may hold values from 0.5 to 1.5
- second_shift: bfloat16 [768], P('dp'), may hold values from -1 to 1
- fc_weight: bfloat16 [768, 3072], P('dp'), may hold values from -0.21875 to 0.21875
- fc_bias: bfloat16 [3072], P('dp'), may hold values from -1 to 1
- down_weight: bfloat16 [3072, 768], P('dp'), may hold values from -0.21875 to 0.21875
- down_bias: bfloat16 [768], P('dp'), may hold values from -1 to 1
- cotangent: bfloat16 [32, 1024, 768], P('dp', 'seq'), may hold values from -6 to 6
Outputs:
- block_output: bfloat16 [32, 1024, 768], P('dp', 'seq')
- input_grad: float32 [32, 1024, 768], P('dp', 'seq')
- first_gain_grad: float32 [768], P('dp')
- first_shift_grad: float32 [768], P('dp')
- qkv_weight_grad: float32 [768, 2304], P('dp')
- qv_bias_grad: float32 [1536], P('dp')
- score_weight_grad: float32 [768, 12], P('dp')
- out_weight_grad: float32 [768, 768], P('dp')
- out_bias_grad: float32 [768], P('dp')
- second_gain_grad: float32 [768], P('dp')
- second_shift_grad: float32 [768], P('dp')
- fc_weight_grad: float32 [768, 3072], P('dp')
- fc_bias_grad: float32 [3072], P('dp')
- down_weight_grad: float32 [3072, 768], P('dp')
- down_bias_grad: float32 [768], P('dp')
The draws below stay inside these ranges and needn't reach their ends.
Inputs may be any that keep to these rules, and one draw needn't show every extreme that they name: `doc_bounds`: the first entry of a row is the start of its second document, below 128; the second entry is the start of its third document, above 896, or 1024 where the row holds two documents.
All inputs are finite; a program needn't handle non-finite values.
Results may differ from the reference program's by a relative error of at most 0.018.
Values may be sent and summed in bfloat16 or wider, within the bound.
No kernel may reach another device: no remote copies, remote signals or barrier semaphores. Data moves between devices by JAX's collectives and lax.ppermute only.
A program may use at most 192 MiB of HBM per device.

```python
import math
from functools import partial
import jax
import jax.numpy as jnp
from jax import lax

D = 768
H = 12
FF = 3072
KTOP = 64
WINDOW = 64
BLOCK = 128
LENGTH = 1024
SEQS = 32
N_SEQ = 8


def draw_doc_bounds(key, part):
    key = jax.random.fold_in(key, 11)
    key_first, key_second, key_pick, key_least = jax.random.split(key, 4)
    first = jax.random.randint(key_first, (SEQS, 1), 1, BLOCK)
    second = jax.random.randint(key_second, (SEQS, 1), LENGTH - BLOCK + 1, LENGTH + 1)
    row_index = jnp.arange(SEQS)[:, None]
    second = jnp.where(row_index == jax.random.randint(key_pick, (), 0, SEQS), LENGTH, second)
    first = jnp.where(row_index == jax.random.randint(key_least, (), 0, SEQS), 1, first)
    return jnp.concatenate([first, second], axis=1).astype(jnp.int32)


def strengthened(drawn, stream_key, source, target, blocks, factor):
    owner, partner = [(jnp.arange(drawn.shape[axis_at]) // (drawn.shape[axis_at] // blocks)).reshape([-1 if axis == axis_at else 1 for axis in range(drawn.ndim)]) for axis_at in (source, target)]
    chosen = jax.random.permutation(stream_key, blocks)[partner]
    strong = (owner == chosen) | (owner == (partner + blocks // 2) % blocks)
    return jnp.where(strong, factor * drawn, drawn)


def levels(key, shape, cuts, smallest, high):
    def one(dim, blocks):
        steps = jax.random.uniform(jax.random.fold_in(jax.random.fold_in(key, 6), dim), (blocks,), jnp.float32, smallest / len(cuts), high / len(cuts))
        return jnp.repeat(jnp.exp(steps), shape[dim] // blocks).reshape((-1,) + (1,) * (len(shape) - dim - 1))

    level = one(*cuts[0])
    for cut in cuts[1:]:
        level = level * one(*cut)
    return level


def normal_values(stream_key, dims, spread, limit, cuts=(), kind=jnp.bfloat16):
    values = spread * jax.random.normal(stream_key, dims, jnp.float32)
    if cuts:
        values = values * levels(stream_key, dims, cuts, -0.22, 0.18)
    return jnp.clip(values, -limit, limit).astype(kind)


def heavy_noise(own_key, dims, scale, bound, pieces, heavy, held_as=jnp.bfloat16):
    entries = scale * jax.random.normal(own_key, dims, jnp.float32)
    if pieces:
        entries = entries * levels(own_key, dims, pieces, -0.22, 0.18)
    return jnp.clip(strengthened(entries, jax.random.fold_in(own_key, 3), *heavy), -bound, bound).astype(held_as)


def setup_inputs(seed: int = 0) -> dict:
    key_list = jax.random.split(jax.random.key(seed), 17)
    block_input = heavy_noise(key_list[0], (SEQS, LENGTH, D), 1.0, 6.0, ((0, 4), (1, 8)), (0, 2, 4, 2.0))
    doc_bounds = draw_doc_bounds(jax.random.fold_in(key_list[16], 71), 0)
    first_gain = jnp.clip(1.0 + 0.1 * jax.random.normal(key_list[2], (D,), jnp.float32), 0.5, 1.5).astype(jnp.bfloat16)
    first_shift = normal_values(key_list[3], (D,), 0.2, 1.0, ((0, 4),))
    qkv_weight = normal_values(key_list[4], (D, 3 * D), D ** -0.5, 0.21875, ((0, 4),))
    qv_bias = normal_values(key_list[5], (2 * D,), 0.2, 1.0, ((0, 4),))
    score_weight = normal_values(key_list[6], (D, H), (D // 2) ** -0.5, 0.3125, ((0, 4),))
    out_weight = normal_values(key_list[7], (D, D), (D // 8) ** -0.5, 0.625, ((0, 4),))
    out_bias = normal_values(key_list[8], (D,), 0.2, 1.0, ((0, 4),))
    second_gain = jnp.clip(1.0 + 0.1 * jax.random.normal(key_list[9], (D,), jnp.float32), 0.5, 1.5).astype(jnp.bfloat16)
    second_shift = normal_values(key_list[10], (D,), 0.2, 1.0, ((0, 4),))
    fc_weight = normal_values(key_list[11], (D, FF), D ** -0.5, 0.21875, ((0, 4),))
    fc_bias = normal_values(key_list[12], (FF,), 0.2, 1.0, ((0, 4),))
    down_weight = normal_values(key_list[13], (FF, D), (FF // 4) ** -0.5, 0.21875, ((0, 4),))
    down_bias = normal_values(key_list[14], (D,), 0.2, 1.0, ((0, 4),))
    cotangent = normal_values(key_list[15], (SEQS, LENGTH, D), 1.0, 6.0, ((0, 4), (1, 8)))
    return {"block_input": block_input, "doc_bounds": doc_bounds, "first_gain": first_gain, "first_shift": first_shift, "qkv_weight": qkv_weight, "qv_bias": qv_bias, "score_weight": score_weight, "out_weight": out_weight, "out_bias": out_bias, "second_gain": second_gain, "second_shift": second_shift, "fc_weight": fc_weight, "fc_bias": fc_bias, "down_weight": down_weight, "down_bias": down_bias, "cotangent": cotangent}


@jax.custom_vjp
def low(v):
    return lax.optimization_barrier(v.astype(jnp.bfloat16)).astype(jnp.float32)

@jax.custom_vjp
def low_back(v):
    return v

def low_keep(v):
    return (low(v), None)

def low_pass(kept, grad):
    return (grad,)

def back_keep(v):
    return (v, None)

def back_low(kept, grad):
    return (low(grad),)
low.defvjp(low_keep, low_pass)
low_back.defvjp(back_keep, back_low)
EPSILON = 1e-05
HIGH = lax.Precision.HIGHEST
NEGATIVE = -1e+30

def layer_norm(values, norm_gain, norm_shift):
    average = lax.optimization_barrier(jnp.mean(values, axis=-1, keepdims=True))
    centred = values - average
    variance = lax.optimization_barrier(jnp.mean(centred * centred, axis=-1, keepdims=True))
    return centred * lax.rsqrt(variance + EPSILON) * norm_gain + norm_shift

def segment_at(places, bounds):
    return (places[None, :] >= bounds[:, 0:1]).astype(jnp.int32) + (places[None, :] >= bounds[:, 1:2]).astype(jnp.int32)

def with_halo(blockwise):
    tail_part = blockwise[:, :-1, BLOCK - WINDOW:]
    padded = jnp.concatenate([jnp.zeros_like(blockwise[:, :1, :WINDOW]), tail_part], axis=1)
    return jnp.concatenate([padded, blockwise], axis=2)

def forward(params, inputs, bounds):
    g_first, s_first, w_qkv, b_qv, w_score, w_out, b_out, g_second, s_second, w_fc, b_fc, w_down, b_down = params
    groups = inputs.shape[0]
    width = inputs.shape[2]
    heads = w_score.shape[1]
    head_dim = width // heads
    normed = low(layer_norm(inputs, g_first, s_first))
    full_bias = jnp.concatenate([b_qv[:width], jnp.zeros((width,), jnp.float32), b_qv[width:]])
    projected = low(low_back(jnp.einsum('gld,de->gle', normed, w_qkv, precision=HIGH) + full_bias))
    shaped = projected.reshape(groups, N_SEQ, BLOCK, 3, heads, head_dim)
    queries = shaped[:, :, :, 0]
    keys_all = with_halo(shaped[:, :, :, 1])
    values_all = with_halo(shaped[:, :, :, 2])
    importance = jnp.einsum('gld,dh->glh', normed, w_score, precision=HIGH)
    position = jnp.arange(LENGTH, dtype=jnp.int32)
    segment = segment_at(position, bounds)
    peak = lax.optimization_barrier(jnp.max(importance, axis=1, keepdims=True))
    scaled = jnp.exp(importance - peak)
    mass = jnp.zeros_like(scaled)
    for doc_index in range(3):
        member = (segment == doc_index).astype(jnp.float32)[:, :, None]
        mass = mass + member * jnp.cumsum(scaled * member, axis=1)
    threshold = (peak + jnp.log(mass) - math.log(KTOP)).reshape(groups, N_SEQ, BLOCK, heads)
    imp_blocks = importance.reshape(groups, N_SEQ, BLOCK, heads)
    query_pos = position.reshape(N_SEQ, BLOCK)
    key_pos = query_pos[:, :1] - WINDOW + jnp.arange(WINDOW + BLOCK, dtype=jnp.int32)[None, :]
    query_seg = segment.reshape(groups, N_SEQ, BLOCK)
    key_seg = segment_at(key_pos.reshape(-1), bounds).reshape(groups, N_SEQ, WINDOW + BLOCK)
    distance = query_pos[:, :, None] - key_pos[:, None, :]
    in_block = jnp.arange(WINDOW + BLOCK)[None, None, :] >= WINDOW
    allowed = (distance >= 0) & (key_pos[:, None, :] >= 0) & ((distance < WINDOW) | in_block)
    allowed = allowed[None] & (query_seg[..., None] == key_seg[:, :, None, :])
    raw = low_back(jnp.einsum('gnihd,gnjhd->gnhij', queries, keys_all, precision=HIGH))
    difference = jnp.transpose(threshold, (0, 1, 3, 2))[..., None] - jnp.transpose(imp_blocks, (0, 1, 3, 2))[..., None, :]
    inner_window = distance[:, :, WINDOW:] < WINDOW
    gated = jnp.where(inner_window[None, :, None], 0.0, -jax.nn.softplus(difference))
    bias_all = jnp.concatenate([jnp.zeros(gated.shape[:-1] + (WINDOW,), jnp.float32), gated], axis=-1)
    logits = jnp.where(allowed[:, :, None], raw / math.sqrt(head_dim) + bias_all, NEGATIVE)
    probs = low(jax.nn.softmax(logits, axis=-1))
    attended = jnp.einsum('gnhij,gnjhd->gnihd', probs, values_all, precision=HIGH).reshape(groups, LENGTH, width)
    attended = low(low_back(attended))
    middle = inputs + low_back(jnp.einsum('gld,de->gle', attended, w_out, precision=HIGH) + b_out)
    second = low(layer_norm(middle, g_second, s_second))
    pre_act = low_back(jnp.einsum('gld,df->glf', second, w_fc, precision=HIGH) + b_fc)
    hidden = low(jax.nn.gelu(pre_act, approximate=True))
    return middle + jnp.einsum('glf,fd->gld', hidden, w_down, precision=HIGH) + b_down

def reference(block_input, doc_bounds, first_gain, first_shift, qkv_weight, qv_bias, score_weight, out_weight, out_bias, second_gain, second_shift, fc_weight, fc_bias, down_weight, down_bias, cotangent):
    params = tuple((weight.astype(jnp.float32) for weight in (first_gain, first_shift, qkv_weight, qv_bias, score_weight, out_weight, out_bias, second_gain, second_shift, fc_weight, fc_bias, down_weight, down_bias)))
    group = math.gcd(SEQS, max(1, 4096 // LENGTH))
    group_count = SEQS // group
    inputs = block_input.astype(jnp.float32).reshape(group_count, group, LENGTH, D)
    bounds = doc_bounds.reshape(group_count, group, 2)
    incoming = cotangent.astype(jnp.float32).reshape(group_count, group, LENGTH, D)

    def group_step(running, scan_item):
        piece_in, piece_bounds, piece_cot = scan_item
        result, pullback = jax.vjp(partial(forward, bounds=piece_bounds), params, piece_in)
        grad_params, grad_in = pullback(piece_cot)
        return (jax.tree.map(jnp.add, running, grad_params), (result.astype(jnp.bfloat16), grad_in))
    initial = jax.tree.map(jnp.zeros_like, params)
    totals, (results, input_grads) = lax.scan(group_step, initial, (inputs, bounds, incoming))
    return (results.reshape(SEQS, LENGTH, D), input_grads.reshape(SEQS, LENGTH, D), totals[0], totals[1], totals[2], totals[3], totals[4], totals[5], totals[6], totals[7], totals[8], totals[9], totals[10], totals[11], totals[12])
```

```python
import math

import jax
import jax.numpy as jnp
from jax import lax
from jax.experimental import pallas as pl
from jax.experimental.pallas import tpu as pltpu
from jax.sharding import PartitionSpec as P

KTOP = 64
WINDOW = 64
HEAD = 64
LANES = 128
EPSILON = 1e-05
NEGATIVE = -1e30
SCALE = 1.0 / math.sqrt(HEAD)
GELU_A = math.sqrt(2.0 / math.pi)
GELU_B = 0.044715
BF = jnp.bfloat16
F32 = jnp.float32
NN = ((1,), (0,))
NT = ((1,), (1,))
TN = ((0,), (0,))
CHUNKS = 2
BLOCKS = 2
VMEM_LIMIT = 56 * 2**20


def mm(left, right, dims=NN):
    return lax.dot_general(left, right, (dims, ((), ())), preferred_element_type=F32)


def mm_split(mask, value, dims=NN):
    high = value.astype(BF)
    low = (value - high.astype(F32)).astype(BF)
    return mm(mask, high, dims) + mm(mask, low, dims)


def whole_spec(shape):
    return pl.BlockSpec(shape, lambda *_: (0,) * len(shape))


def call(kernel, name, grid, in_specs, out_specs, out_shape, scratch=(), prefetch=0, flops=0, moved=0):
    return pl.pallas_call(
        kernel,
        grid_spec=pltpu.PrefetchScalarGridSpec(
            num_scalar_prefetch=prefetch,
            grid=grid,
            in_specs=in_specs,
            out_specs=out_specs,
            scratch_shapes=list(scratch),
        ),
        out_shape=out_shape,
        compiler_params=pltpu.CompilerParams(vmem_limit_bytes=VMEM_LIMIT),
        cost_estimate=pl.CostEstimate(flops=int(flops), bytes_accessed=int(moved), transcendentals=0),
        name=name,
    )


def iota(shape, axis):
    return lax.broadcasted_iota(jnp.int32, shape, axis)


def segment(places, first, second):
    return (places >= first).astype(jnp.int32) + (places >= second).astype(jnp.int32)


def normalise(values):
    average = jnp.mean(values, axis=-1, keepdims=True)
    centred = values - average
    variance = jnp.mean(centred * centred, axis=-1, keepdims=True)
    scale = lax.rsqrt(variance + EPSILON)
    return centred * scale, scale


def norm_back(d_norm, unit, scale, gain):
    weighted = d_norm * gain
    return scale * (
        weighted
        - jnp.mean(weighted, axis=-1, keepdims=True)
        - unit * jnp.mean(weighted * unit, axis=-1, keepdims=True)
    )


def prep_kernel(info, bounds, x_ref, tail_ref, gain_ref, shift_ref, score_ref, normed_ref, tail_out_ref, imp_ref, mass_ref, stat_ref):
    s = pl.program_id(0)
    blocks = x_ref.shape[0]
    gain = gain_ref[...]
    shift = shift_ref[...]
    normed = (normalise(x_ref[...].astype(F32))[0] * gain + shift).astype(BF)
    normed_ref[...] = normed
    tail_out_ref[...] = (normalise(tail_ref[...].astype(F32))[0] * gain + shift).astype(BF)
    importance = mm(normed, score_ref[...])
    imp_ref[...] = importance
    start = info[0]
    first, second = bounds[2 * s], bounds[2 * s + 1]
    rows = iota((blocks, blocks), 0)
    cols = iota((blocks, blocks), 1)
    lower = (cols <= rows) & (segment(start + rows, first, second) == segment(start + cols, first, second))
    peak = jnp.max(importance, axis=0, keepdims=True)
    mass = mm_split(lower.astype(BF), jnp.exp(importance - peak))
    mass_ref[...] = mass
    stat_ref[0, 0:1, :] = peak
    stat_ref[0, 1:2, :] = mass[blocks - 1 :, :]


def qkv_kernel(normed_ref, tail_ref, weight_ref, bias_ref, out_ref, tail_out_ref):
    j = pl.program_id(0)
    weight = weight_ref[0]
    bias = bias_ref[0]
    factor = jnp.where(j == 0, SCALE, 1.0)
    out_ref[0] = ((mm(normed_ref[...], weight) + bias).astype(BF).astype(F32) * factor).astype(BF)

    @pl.when(j > 0)
    def _():
        tail_out_ref[0] = (mm(tail_ref[...], weight) + bias).astype(BF)


def lane_masks():
    first = (iota((1, LANES), 1) < HEAD)
    return first.astype(BF), (~first).astype(BF)


def grouped(part, keep_first, keep_second):
    return jnp.concatenate([part * keep_first, part * keep_second], axis=0)


def tile_masks(start, half, first, second):
    shape = (WINDOW, LANES)
    row = iota(shape, 0)
    col = iota(shape, 1) & (HEAD - 1)
    base = start + WINDOW * half
    mine = segment(base + row, first, second)
    far = segment(base - WINDOW + col, first, second) == mine
    near = (col <= row) & (segment(base + col, first, second) == mine)
    if half == 0:
        far = far & (col > row) & (base - WINDOW + col >= 0)
    return far, near, col <= row


def spread(columns, pair, rows):
    left = columns[:, 2 * pair : 2 * pair + 1]
    right = columns[:, 2 * pair + 1 : 2 * pair + 2]
    lane = iota((rows, LANES), 1)
    return jnp.where(lane < HEAD, left, right)


def attention_kernel(info, bounds, qkv_ref, halo_ref, imp_ref, mass_ref, peak_ref, before_ref, att_ref, probs_ref, sig_ref, inv_ref):
    s = pl.program_id(0)
    blocks = imp_ref.shape[0]
    start = info[0]
    first, second = bounds[2 * s], bounds[2 * s + 1]
    pairs = att_ref.shape[1] // LANES
    peak = peak_ref[0, 0:1, :]
    carry_peak = before_ref[0, 0:1, :]
    carry_total = before_ref[0, 1:2, :]
    top = before_ref[0, 2:3, :]
    joined = jnp.maximum(peak, carry_peak)
    place = start + iota((blocks, LANES), 0)
    continues = segment(place, first, second) == segment(jnp.full((1, LANES), start - 1, jnp.int32), first, second)
    mass = mass_ref[...] * jnp.exp(peak - joined) + jnp.where(
        continues, carry_total * jnp.exp(carry_peak - joined), 0.0
    )
    threshold = joined + jnp.log(mass) - math.log(KTOP)
    late = threshold[WINDOW:]
    inv_ref[...] = 1.0 / (mass[WINDOW:] * jnp.exp(joined - top))
    imp_rows = imp_ref[...].T
    keep_first, keep_second = lane_masks()
    ones = jnp.ones((WINDOW, LANES), BF)
    one_group = grouped(ones, keep_first, keep_second)
    masks = [tile_masks(start, half, first, second) for half in (0, 1)]
    lane = iota((WINDOW, LANES), 1) < HEAD
    for pair in range(pairs):
        ls = slice(pair * LANES, (pair + 1) * LANES)
        keys = [grouped(part, keep_first, keep_second) for part in (halo_ref[0, :, ls], qkv_ref[1, :WINDOW, ls], qkv_ref[1, WINDOW:, ls])]
        values = [
            jnp.concatenate([grouped(part, keep_first, keep_second), one_group], axis=1)
            for part in (halo_ref[1, :, ls], qkv_ref[2, :WINDOW, ls], qkv_ref[2, WINDOW:, ls])
        ]
        for half in (0, 1):
            rs = slice(half * WINDOW, (half + 1) * WINDOW)
            far_ok, near_ok, gated = masks[half]
            logits = mm(qkv_ref[0, rs, ls], jnp.concatenate(keys[half : half + 2], axis=0), NT)
            far, near = logits[:, :LANES], logits[:, LANES:]
            if half == 1:
                row = jnp.concatenate(
                    [imp_rows[2 * pair : 2 * pair + 1, :WINDOW], imp_rows[2 * pair + 1 : 2 * pair + 2, :WINDOW]], axis=1
                )
                gap = spread(late, pair, WINDOW) - row
                small = jnp.exp(-jnp.abs(gap))
                soft = jnp.maximum(gap, 0.0) + jnp.log(1.0 + small)
                sig_ref[:, ls] = (jnp.where(gap >= 0, 1.0, small) / (1.0 + small)).astype(BF)
                far = jnp.where(gated, far - soft, far)
            far = jnp.where(far_ok, far, NEGATIVE)
            near = jnp.where(near_ok, near, NEGATIVE)
            best = jnp.maximum(far, near)
            best_first = jnp.max(jnp.where(lane, best, NEGATIVE), axis=1, keepdims=True)
            best_second = jnp.max(jnp.where(lane, NEGATIVE, best), axis=1, keepdims=True)
            best = jnp.where(lane, best_first, best_second)
            far = jnp.exp(far - best)
            near = jnp.exp(near - best)
            weights = jnp.concatenate([far.astype(BF), near.astype(BF)], axis=1)
            mixed = mm(weights, jnp.concatenate(values[half : half + 2], axis=0))
            inverse = 1.0 / mixed[:, LANES:]
            att_ref[rs, ls] = (mixed[:, :LANES] * inverse).astype(BF)
            probs_ref[rs, 2 * pair * LANES : (2 * pair + 1) * LANES] = (far * inverse).astype(BF)
            probs_ref[rs, (2 * pair + 1) * LANES : (2 * pair + 2) * LANES] = (near * inverse).astype(BF)


def project_kernel(att_ref, x_ref, weight_ref, bias_ref, gain_ref, shift_ref, middle_ref, second_ref):
    middle = x_ref[...].astype(F32) + mm(att_ref[...], weight_ref[...]) + bias_ref[...]
    middle_ref[...] = middle
    second_ref[...] = (normalise(middle)[0] * gain_ref[...] + shift_ref[...]).astype(BF)


def feed_kernel(*refs, heads_in):
    if heads_in:
        order, sec_ref, dy_ref, fc_ref, down_ref, bias_ref, out_in, dsec_in, out_ref, dsec_ref, keep_ref, send_ref, db_ref = refs
    else:
        order, sec_ref, dy_ref, fc_ref, down_ref, bias_ref, out_ref, dsec_ref, keep_ref, send_ref, db_ref = refs
    j = pl.program_id(0)
    shards = keep_ref.shape[0]
    core = order[0]
    fc = fc_ref[0]
    down = down_ref[0]
    pre = mm(sec_ref[...], fc) + bias_ref[0]
    d_hidden = mm(dy_ref[...], down, NT)
    square = pre * pre
    tanh = jnp.tanh(pre * (GELU_A + GELU_A * GELU_B * square))
    half = 0.5 + 0.5 * tanh
    hidden = (pre * half).astype(BF)
    slope = half + pre * (0.5 * GELU_A + 1.5 * GELU_A * GELU_B * square) * (1.0 - tanh * tanh)
    d_pre = d_hidden * slope
    d_low = d_pre.astype(BF)
    db_ref[0] = jnp.sum(d_pre, axis=0, keepdims=True)
    out = mm(hidden, down)
    d_second = mm(d_low, fc, NT)

    @pl.when(j == 0)
    def _():
        if heads_in:
            out_ref[...] = out_in[...] + out
            dsec_ref[...] = dsec_in[...] + d_second
        else:
            out_ref[...] = out
            dsec_ref[...] = d_second

    @pl.when(j > 0)
    def _():
        out_ref[...] += out
        dsec_ref[...] += d_second

    d_fc = mm(sec_ref[...], d_low, TN).astype(BF)
    d_down = mm(hidden, dy_ref[...], TN).astype(BF)
    rows = d_fc.shape[0] // shards
    per_block = shards // BLOCKS
    deep = d_down.shape[0] // per_block
    where = pl.multiple_of(j * rows, rows)

    def store(fc_to, fc_order, down_to, down_order):
        for shard in range(shards):
            fc_to[order[fc_order + shard], pl.ds(where, rows), :] = d_fc[shard * rows : (shard + 1) * rows]
        for shard in range(per_block):
            down_to[order[down_order + j * per_block + shard]] = d_down[shard * deep : (shard + 1) * deep]

    @pl.when(core == 0)
    def _():
        store(keep_ref, 1, send_ref, 1 + shards)

    @pl.when(core != 0)
    def _():
        store(send_ref, 1 + shards, keep_ref, 1)


def middle_kernel(order, dsec_ref, middle_ref, dy_ref, out_ref, att_ref, weight_ref, gain_ref, down_bias_ref, block_ref, dmid_ref, datt_ref, keep_ref, send_ref, sums_ref, total):
    i = pl.program_id(0)
    steps = pl.num_programs(0)
    shards = keep_ref.shape[0]
    core = order[0]
    middle = middle_ref[...]
    block_ref[...] = (middle + out_ref[...] + down_bias_ref[...]).astype(BF)
    unit, scale = normalise(middle)
    d_norm = dsec_ref[...]
    dy = dy_ref[...].astype(F32)
    d_middle = dy + norm_back(d_norm, unit, scale, gain_ref[...])
    dmid_ref[...] = d_middle
    branch = d_middle.astype(BF)
    datt_ref[...] = mm(branch, weight_ref[...], NT).astype(BF)
    part = mm(att_ref[...], branch, TN)
    sums = [
        jnp.sum(d_norm * unit, axis=0, keepdims=True),
        jnp.sum(d_norm, axis=0, keepdims=True),
        jnp.sum(branch.astype(F32), axis=0, keepdims=True),
        jnp.sum(dy, axis=0, keepdims=True),
    ]

    @pl.when(i == 0)
    def _():
        total[...] = part
        for k in range(4):
            sums_ref[k : k + 1] = sums[k]

    @pl.when(i > 0)
    def _():
        total[...] += part
        for k in range(4):
            sums_ref[k : k + 1] += sums[k]

    @pl.when(i == steps - 1)
    def _():
        rows = total.shape[0] // shards
        half = rows // 2

        def store(side, to, to_order):
            for shard in range(shards):
                begin = shard * rows + side * half
                to[order[to_order + shard]] = total[begin : begin + half].astype(BF)

        @pl.when(core == 0)
        def _():
            store(0, keep_ref, 1)
            store(1, send_ref, 1 + shards)

        @pl.when(core != 0)
        def _():
            store(1, keep_ref, 1)
            store(0, send_ref, 1 + shards)


def attention_back_kernel(info, bounds, qkv_ref, halo_ref, att_ref, datt_ref, probs_ref, sig_ref, inv_ref, imp_ref, before_ref, dqkv_ref, dhalo_ref, dimp_ref, total_ref, rows_scratch):
    s = pl.program_id(0)
    blocks = imp_ref.shape[0]
    start = info[0]
    first, second = bounds[2 * s], bounds[2 * s + 1]
    pairs = att_ref.shape[1] // LANES
    keep_first, keep_second = lane_masks()
    ones = jnp.ones((WINDOW, LANES), BF)
    one_group = grouped(ones, keep_first, keep_second)
    lane = iota((WINDOW, LANES), 1) < HEAD
    gated = (iota((WINDOW, LANES), 1) & (HEAD - 1)) <= iota((WINDOW, LANES), 0)
    head_lane = iota((LANES, LANES), 1)
    head_row = iota((LANES, LANES), 0)
    d_threshold = jnp.zeros((WINDOW, LANES), F32)
    rows_scratch[...] = jnp.zeros_like(rows_scratch)
    for pair in range(pairs):
        ls = slice(pair * LANES, (pair + 1) * LANES)
        keys = [grouped(part, keep_first, keep_second) for part in (halo_ref[0, :, ls], qkv_ref[1, :WINDOW, ls], qkv_ref[1, WINDOW:, ls])]
        values = [
            jnp.concatenate([grouped(part, keep_first, keep_second), one_group], axis=1)
            for part in (halo_ref[1, :, ls], qkv_ref[2, :WINDOW, ls], qkv_ref[2, WINDOW:, ls])
        ]
        far_keys, near_keys, far_values, near_values = [], [], [], []
        for half in (0, 1):
            rs = slice(half * WINDOW, (half + 1) * WINDOW)
            d_out = datt_ref[rs, ls]
            product = (-(d_out.astype(F32) * att_ref[rs, ls].astype(F32))).astype(BF)
            left = jnp.concatenate([d_out, product], axis=1)
            centred = mm(left, jnp.concatenate(values[half : half + 2], axis=0), NT)
            probs = probs_ref[rs, 2 * pair * LANES : (2 * pair + 2) * LANES]
            d_logits = probs.astype(F32) * centred
            low = d_logits.astype(BF)
            dqkv_ref[0, rs, ls] = (mm(low, jnp.concatenate(keys[half : half + 2], axis=0)) * SCALE).astype(BF)
            d_keys = mm(low, qkv_ref[0, rs, ls], TN)
            d_values = mm(probs, d_out, TN)
            far_keys.append(jnp.where(lane, d_keys[:WINDOW], d_keys[WINDOW : 2 * WINDOW]))
            near_keys.append(jnp.where(lane, d_keys[2 * WINDOW : 3 * WINDOW], d_keys[3 * WINDOW :]))
            far_values.append(jnp.where(lane, d_values[:WINDOW], d_values[WINDOW : 2 * WINDOW]))
            near_values.append(jnp.where(lane, d_values[2 * WINDOW : 3 * WINDOW], d_values[3 * WINDOW :]))
            if half == 1:
                gate = jnp.where(gated, d_logits[:, :LANES] * sig_ref[:, ls].astype(F32), 0.0)
                rows_scratch[pair : pair + 1, :] = jnp.sum(gate, axis=0, keepdims=True)
                chosen = (head_lane == 2 * pair + (head_row >= HEAD).astype(jnp.int32)).astype(BF)
                d_threshold = d_threshold - mm(gate.astype(BF), chosen)
        dhalo_ref[0, :, ls] = far_keys[0].astype(BF)
        dhalo_ref[1, :, ls] = far_values[0].astype(BF)
        dqkv_ref[1, :WINDOW, ls] = (near_keys[0] + far_keys[1]).astype(BF)
        dqkv_ref[1, WINDOW:, ls] = near_keys[1].astype(BF)
        dqkv_ref[2, :WINDOW, ls] = (near_values[0] + far_values[1]).astype(BF)
        dqkv_ref[2, WINDOW:, ls] = near_values[1].astype(BF)
    weighted = d_threshold * inv_ref[...]
    row = iota((blocks, WINDOW), 0)
    col = iota((blocks, WINDOW), 1) + WINDOW
    after = (col >= row) & (segment(start + row, first, second) == segment(start + col, first, second))
    later = mm_split(after.astype(BF), weighted)
    total_ref[0, 0:1, :] = later[0:1]
    turned = rows_scratch[...].T
    pick_first = (head_lane == 2 * head_row).astype(BF)
    pick_second = (head_lane == 2 * head_row + 1).astype(BF)

    def pick(values, chosen):
        high = values.astype(BF)
        return mm(high, chosen) + mm((values - high.astype(F32)).astype(BF), chosen)

    direct = pick(turned[:HEAD], pick_first) + pick(turned[HEAD:], pick_second)
    local = jnp.exp(imp_ref[...] - before_ref[0, 2:3, :]) * later
    dimp_ref[:WINDOW] = local[:WINDOW] + direct
    dimp_ref[WINDOW:] = local[WINDOW:]


def tail_back_kernel(dhalo_ref, weight_ref, x_ref, gain_ref, out_ref, sums_ref):
    d_norm = mm(dhalo_ref[0], weight_ref[1], NT) + mm(dhalo_ref[1], weight_ref[2], NT)
    unit, scale = normalise(x_ref[...].astype(F32))
    out_ref[...] = norm_back(d_norm, unit, scale, gain_ref[...]).astype(BF)
    sums_ref[0:1] = jnp.sum(d_norm * unit, axis=0, keepdims=True)
    sums_ref[1:2] = jnp.sum(d_norm, axis=0, keepdims=True)


def qkv_grad_kernel(order, normed_ref, tail_ref, dqkv_ref, dhalo_ref, keep_ref, send_ref, sums_ref):
    j = pl.program_id(0)
    shards = keep_ref.shape[0]
    core = order[0]
    local = dqkv_ref[0]
    halo = jnp.where(j > 0, dhalo_ref[0], jnp.zeros_like(dhalo_ref[0]))
    total = (mm(normed_ref[...], local, TN) + mm(tail_ref[...], halo, TN)).astype(BF)
    sums_ref[0] = jnp.sum(local.astype(F32), axis=0, keepdims=True) + jnp.sum(halo.astype(F32), axis=0, keepdims=True)
    rows = total.shape[0] // shards
    half = rows // 2

    def store(side, to, to_order):
        for shard in range(shards):
            begin = shard * rows + side * half
            to[order[to_order + shard], pl.ds(pl.multiple_of(j * half, half), half), :] = total[begin : begin + half]

    @pl.when(core == 0)
    def _():
        store(0, keep_ref, 1)
        store(1, send_ref, 1 + shards)

    @pl.when(core != 0)
    def _():
        store(1, keep_ref, 1)
        store(0, send_ref, 1 + shards)


def input_grad_kernel(info, bounds, dqkv_ref, weight_ref, score_ref, normed_ref, x_ref, gain_ref, dmid_ref, back_ref, dimp_ref, imp_ref, before_ref, after_ref, out_ref, sums_ref, score_out_ref):
    i = pl.program_id(0)
    seqs = back_ref.shape[0]
    blocks = x_ref.shape[0] // seqs
    start = info[0]
    d_imps = []
    for s in range(seqs):
        first, second = bounds[2 * (i * seqs + s)], bounds[2 * (i * seqs + s) + 1]
        place = start + iota((blocks, LANES), 0)
        onward = segment(place, first, second) == segment(jnp.full((1, LANES), start + blocks, jnp.int32), first, second)
        rs = slice(s * blocks, (s + 1) * blocks)
        extra = jnp.exp(imp_ref[rs] - before_ref[s, 2:3, :]) * after_ref[s, 0:1, :]
        d_imps.append(dimp_ref[rs] + jnp.where(onward, extra, 0.0))
    d_imp = jnp.concatenate(d_imps, axis=0).astype(BF)
    d_norm = mm(d_imp, score_ref[...], NT)
    for j in range(3):
        d_norm = d_norm + mm(dqkv_ref[j], weight_ref[j], NT)
    unit, scale = normalise(x_ref[...].astype(F32))
    d_value = norm_back(d_norm, unit, scale, gain_ref[...]) + dmid_ref[...]
    for s in range(seqs):
        rs = slice(s * blocks, s * blocks + WINDOW)
        out_ref[rs] = d_value[rs]
        rs = slice(s * blocks + WINDOW, (s + 1) * blocks)
        out_ref[rs] = d_value[rs] + back_ref[s].astype(F32)
    sums = [jnp.sum(d_norm * unit, axis=0, keepdims=True), jnp.sum(d_norm, axis=0, keepdims=True)]
    score = mm(normed_ref[...], d_imp, TN)

    @pl.when(i == 0)
    def _():
        score_out_ref[...] = score
        for k in range(2):
            sums_ref[k : k + 1] = sums[k]

    @pl.when(i > 0)
    def _():
        score_out_ref[...] += score
        for k in range(2):
            sums_ref[k : k + 1] += sums[k]


class Net:
    def __init__(self):
        self.n_seq = lax.axis_size("seq")
        self.n_dp = lax.axis_size("dp")
        self.seq = lax.axis_index("seq")
        self.dp = lax.axis_index("dp")
        self.core = self.seq % 2
        self.bits = self.n_dp.bit_length() - 1
        half = self.bits // 2
        straight = list(range(self.bits))
        self.orders = (straight, straight[half:] + straight[:half])

    def send(self, value, target):
        pairs = []
        for s in range(self.n_seq):
            for d in range(self.n_dp):
                goal = target(s, d)
                if goal is not None and 0 <= goal[0] < self.n_seq:
                    pairs.append((s * self.n_dp + d, goal[0] * self.n_dp + goal[1]))
        return lax.ppermute(value, ("seq", "dp"), pairs)

    def across(self, value, step):
        return self.send(value, lambda s, d: (s, d ^ (1 << self.orders[s % 2][step])))

    def chip(self, value):
        return self.send(value, lambda s, d: (s ^ 1, d))

    def along(self, value, bit):
        return self.send(value, lambda s, d: (s ^ (1 << bit), d))

    def shifted(self, value, by):
        return self.send(value, lambda s, d: (s + by, d))

    def table(self, order, first_high):
        far = jnp.arange(self.n_dp, dtype=jnp.int32) ^ self.dp
        index = jnp.zeros_like(far)
        for step, bit in enumerate(order):
            place = self.bits - 1 - step if first_high else step
            index = index | (((far >> bit) & 1) << place)
        return index

    def tables(self, first_high):
        even, odd = (self.table(order, first_high) for order in self.orders)
        mine = jnp.where(self.core == 0, even, odd)
        other = jnp.where(self.core == 0, odd, even)
        return mine, other

    def gather(self, own):
        held = own[None]
        for step in range(self.bits):
            held = jnp.concatenate([held, self.across(held, step)], axis=0)
        return held

    def reduce(self, current):
        size = self.n_dp
        for step in range(self.bits):
            size //= 2
            got = self.across(current[size:], step)
            current = add(current[:size], got)
        current = current[0]
        z_bits = (self.n_seq // 2).bit_length() - 1
        half = current.shape[0] // 2
        upper = (self.seq // 2) % 2
        low, high = current[:half], current[half:]
        kept = jnp.where(upper == 1, high, low)
        given = jnp.where(upper == 1, low, high)
        kept = add(kept, self.along(given, 1))
        for bit in range(1, z_bits):
            kept = add(kept, self.along(kept, bit + 1))
        got = self.along(kept, 1)
        low = jnp.where(upper == 1, got, kept)
        high = jnp.where(upper == 1, kept, got)
        return jnp.concatenate([low, high], axis=0)

    def sum_all(self, value):
        value = value + self.chip(value)
        for step in range(self.bits):
            value = value + self.across(value, step)
        for bit in range(1, self.n_seq.bit_length() - 1):
            value = value + self.along(value, bit)
        return value


def add(left, right):
    return (left.astype(F32) + right.astype(F32)).astype(BF)


def combine(peak_a, total_a, peak_b, total_b):
    joined = jnp.maximum(peak_a, peak_b)
    return joined, total_a * jnp.exp(peak_a - joined) + total_b * jnp.exp(peak_b - joined)


def body(block_input, doc_bounds, first_gain, first_shift, qkv_weight, qv_bias, score_weight, out_weight, out_bias, second_gain, second_shift, fc_weight, fc_bias, down_weight, down_bias, cotangent):
    net = Net()
    seqs, blocks, width = block_input.shape
    tokens = seqs * blocks
    heads = score_weight.shape[1]
    shards = net.n_dp
    rows = width // shards
    hidden = fc_weight.shape[1]
    tail = seqs * WINDOW
    start = (net.seq * blocks).astype(jnp.int32)
    info = jnp.reshape(start, (1,))
    bounds = doc_bounds.reshape(-1)
    x_flat = block_input.reshape(tokens, width)
    dy = cotangent.reshape(tokens, width)
    core = net.core.astype(jnp.int32)

    small_parts = [first_gain, first_shift, second_gain, second_shift, out_bias, down_bias, qv_bias, fc_bias, score_weight.reshape(-1)]
    sizes = [part.shape[0] for part in small_parts]
    packed = jnp.concatenate(small_parts)
    got_small = net.gather(packed.reshape(-1, LANES) if packed.shape[0] % LANES == 0 else packed.reshape(1, -1))
    mine_gather, other_gather = net.tables(False)
    mine_reduce, other_reduce = net.tables(True)
    order = jnp.concatenate([jnp.reshape(core, (1,)), mine_reduce, other_reduce]).astype(jnp.int32)

    def pick(buffer, index):
        return lax.dynamic_index_in_dim(buffer, index, 0, keepdims=False)

    small_all = jnp.stack([pick(got_small, mine_gather[d]).reshape(-1) for d in range(shards)])
    pieces = []
    begin = 0
    for size in sizes:
        pieces.append(small_all[:, begin : begin + size].reshape(-1))
        begin += size
    g_first, s_first, g_second, s_second, b_out, b_down, b_qv, b_fc, w_score = pieces
    g_first, s_first, g_second, s_second, b_out, b_down = (
        part.astype(F32).reshape(1, width) for part in (g_first, s_first, g_second, s_second, b_out, b_down)
    )
    w_score = jnp.pad(w_score.reshape(width, heads), ((0, 0), (0, LANES - heads)))
    b_qkv = jnp.stack([b_qv[:width], jnp.zeros((width,), b_qv.dtype), b_qv[width:]]).astype(F32).reshape(3, 1, width)

    x_tail = net.shifted(block_input[:, blocks - WINDOW :], 1).reshape(tail, width)

    def halves(value, axis):
        size = value.shape[axis] // 2
        first = lax.slice_in_dim(value, 0, size, axis=axis)
        second = lax.slice_in_dim(value, size, 2 * size, axis=axis)
        return first, second

    def gathered(first, second):
        own = jnp.where(core == 0, first, second)
        mine = net.gather(own)
        other = net.chip(mine)
        mine = jnp.stack([pick(mine, mine_gather[d]) for d in range(shards)])
        other = jnp.stack([pick(other, other_gather[d]) for d in range(shards)])
        return jnp.where(core == 0, mine, other), jnp.where(core == 0, other, mine)

    qkv_blocks = jnp.transpose(qkv_weight.reshape(rows, 3, width), (1, 0, 2))
    half_rows = rows // 2
    first, second = halves(qkv_blocks, 1)
    first, second = gathered(first.reshape(3 * half_rows, width), second.reshape(3 * half_rows, width))

    def joined_blocks(first, second, count):
        both = jnp.stack([part.reshape(shards, count, half_rows, width) for part in (first, second)], axis=2)
        return jnp.transpose(both, (1, 0, 2, 3, 4)).reshape(count, width, width)

    w_qkv = joined_blocks(first, second, 3)

    deep = hidden // shards // CHUNKS
    fc_parts = fc_weight.reshape(rows, BLOCKS, shards // BLOCKS, CHUNKS, deep)
    down_parts = down_weight.reshape(CHUNKS, deep, width)
    bias_parts = b_fc.astype(F32).reshape(BLOCKS, shards // BLOCKS, CHUNKS, deep)
    out_first, out_second = halves(out_weight, 0)
    feeds = []
    w_out = None
    for chunk in range(CHUNKS):
        fc = jnp.transpose(fc_parts[:, :, :, chunk], (1, 0, 2, 3)).reshape(BLOCKS * rows, width)
        down = down_parts[chunk]
        if chunk == 0:
            fc = jnp.concatenate([fc, out_first], axis=0)
            down = jnp.concatenate([down, out_second], axis=0)
        fc, down = gathered(fc, down)
        if chunk == 0:
            main = BLOCKS * rows
            w_out = joined_blocks(fc[:, main:], down[:, main:], 1)[0]
            fc, down = fc[:, :main], down[:, :main]
        fc = jnp.transpose(fc.reshape(shards, BLOCKS, rows, width), (1, 0, 2, 3)).reshape(BLOCKS, width, width)
        down = down.reshape(BLOCKS, width, width)
        feeds.append((fc, down, bias_parts[:, :, chunk].reshape(BLOCKS, 1, width)))

    by_seq = lambda rows_, cols: pl.BlockSpec((rows_, cols), lambda s, *_: (s, 0))
    by_layer = lambda count, rows_, cols: pl.BlockSpec((count, rows_, cols), lambda s, *_: (0, s, 0))
    stat = pl.BlockSpec((1, 8, LANES), lambda s, *_: (s, 0, 0))
    shape = jax.ShapeDtypeStruct
    normed, normed_tail, importance, mass, stats = call(
        prep_kernel,
        "prep",
        (seqs,),
        [by_seq(blocks, width), by_seq(WINDOW, width), whole_spec((1, width)), whole_spec((1, width)), whole_spec((width, LANES))],
        [by_seq(blocks, width), by_seq(WINDOW, width), by_seq(blocks, LANES), by_seq(blocks, LANES), stat],
        [shape((tokens, width), BF), shape((tail, width), BF), shape((tokens, LANES), F32), shape((tokens, LANES), F32), shape((seqs, 8, LANES), F32)],
        prefetch=2,
        flops=2 * tokens * width * LANES,
        moved=2 * 2 * (tokens + tail) * width,
    )(info, bounds, x_flat, x_tail, g_first, s_first, w_score)

    peak_all, total_all = stats[:, 0], stats[:, 1]
    peak_before, total_before = jnp.full_like(peak_all, NEGATIVE), jnp.zeros_like(total_all)
    for bit in range(net.n_seq.bit_length() - 1):
        got = net.along(jnp.stack([peak_all, total_all]), bit)
        later = (net.seq >> bit) % 2 == 1
        peak_new, total_new = combine(peak_before, total_before, got[0], got[1])
        peak_before = jnp.where(later, peak_new, peak_before)
        total_before = jnp.where(later, total_new, total_before)
        peak_all, total_all = combine(peak_all, total_all, got[0], got[1])
    before = jnp.stack([peak_before, total_before, peak_all], axis=1)

    qkv, qkv_tail = call(
        qkv_kernel,
        "qkv",
        (3,),
        [whole_spec((tokens, width)), whole_spec((tail, width)), pl.BlockSpec((1, width, width), lambda j: (j, 0, 0)), pl.BlockSpec((1, 1, width), lambda j: (j, 0, 0))],
        [pl.BlockSpec((1, tokens, width), lambda j: (j, 0, 0)), pl.BlockSpec((1, tail, width), lambda j: (jnp.maximum(j - 1, 0), 0, 0))],
        [shape((3, tokens, width), BF), shape((2, tail, width), BF)],
        flops=2 * width * width * (3 * tokens + 2 * tail),
        moved=2 * width * (4 * tokens + 3 * tail + 3 * width),
    )(normed, normed_tail, w_qkv, b_qkv)

    three = pl.BlockSpec((1, 3, LANES), lambda s, *_: (s, 0, 0))
    attended, probs, gates, inverse = call(
        attention_kernel,
        "attention",
        (seqs,),
        [by_layer(3, blocks, width), by_layer(2, WINDOW, width), by_seq(blocks, LANES), by_seq(blocks, LANES), stat, three],
        [by_seq(blocks, width), by_seq(blocks, 2 * width), by_seq(WINDOW, width), by_seq(WINDOW, LANES)],
        [shape((tokens, width), BF), shape((tokens, 2 * width), BF), shape((tail, width), BF), shape((tail, LANES), F32)],
        prefetch=2,
        flops=8 * tokens * 2 * WINDOW * width,
        moved=2 * width * (7 * tokens + 3 * tail),
    )(info, bounds, qkv, qkv_tail, importance, mass, stats, before)

    tile = 2 * blocks
    by_tile = pl.BlockSpec((tile, width), lambda i, *_: (i, 0))
    middle, normed_second = call(
        project_kernel,
        "project",
        (tokens // tile,),
        [by_tile, by_tile, whole_spec((width, width)), whole_spec((1, width)), whole_spec((1, width)), whole_spec((1, width))],
        [by_tile, by_tile],
        [shape((tokens, width), F32), shape((tokens, width), BF)],
        flops=2 * tokens * width * width,
        moved=10 * tokens * width + 2 * width * width,
    )(attended, x_flat, w_out, b_out, g_second, s_second)

    block = pl.BlockSpec((1, width, width), lambda j, *_: (j, 0, 0))
    thin = pl.BlockSpec((1, 1, width), lambda j, *_: (j, 0, 0))
    full = whole_spec((tokens, width))
    chunk_rows = BLOCKS * rows
    bucket = whole_spec((shards, chunk_rows, width))
    sums_so_far = ()
    buckets = []
    d_fc_bias = []
    for chunk in range(CHUNKS):
        fc, down, bias = feeds[chunk]
        sums_so_far_specs = [full] * len(sums_so_far)
        out_sum, d_second, keep, give, d_bias = call(
            lambda *refs, first=(chunk == 0): feed_kernel(*refs, heads_in=not first),
            "feed",
            (BLOCKS,),
            [full, full, block, block, thin] + sums_so_far_specs,
            [full, full, bucket, bucket, thin],
            [shape((tokens, width), F32), shape((tokens, width), F32), shape((shards, chunk_rows, width), BF), shape((shards, chunk_rows, width), BF), shape((BLOCKS, 1, width), F32)],
            prefetch=1,
            flops=12 * tokens * width * width * BLOCKS,
            moved=2 * width * (2 * tokens + 8 * width) + 12 * tokens * width,
        )(order, normed_second, dy, fc, down, bias, *sums_so_far)
        sums_so_far = (out_sum, d_second)
        buckets.append((keep, give))
        d_fc_bias.append(d_bias.reshape(BLOCKS, shards // BLOCKS, 1, deep))
    out_sum, d_second = sums_so_far

    out_bucket = whole_spec((shards, half_rows, width))
    block_output, d_middle, d_attended, keep_out, give_out, sums_second = call(
        middle_kernel,
        "middle",
        (tokens // tile,),
        [by_tile, by_tile, by_tile, by_tile, by_tile, whole_spec((width, width)), whole_spec((1, width)), whole_spec((1, width))],
        [by_tile, by_tile, by_tile, out_bucket, out_bucket, whole_spec((8, width))],
        [shape((tokens, width), BF), shape((tokens, width), F32), shape((tokens, width), BF), shape((shards, half_rows, width), BF), shape((shards, half_rows, width), BF), shape((8, width), F32)],
        scratch=[pltpu.VMEM((width, width), F32)],
        prefetch=1,
        flops=4 * tokens * width * width,
        moved=22 * tokens * width,
    )(order, d_second, middle, dy, out_sum, attended, w_out, g_second, b_down)

    dqkv, d_halo, d_imp, totals = call(
        attention_back_kernel,
        "attention_back",
        (seqs,),
        [by_layer(3, blocks, width), by_layer(2, WINDOW, width), by_seq(blocks, width), by_seq(blocks, width), by_seq(blocks, 2 * width), by_seq(WINDOW, width), by_seq(WINDOW, LANES), by_seq(blocks, LANES), three],
        [by_layer(3, blocks, width), by_layer(2, WINDOW, width), by_seq(blocks, LANES), pl.BlockSpec((1, 1, LANES), lambda s, *_: (s, 0, 0))],
        [shape((3, tokens, width), BF), shape((2, tail, width), BF), shape((tokens, LANES), F32), shape((seqs, 1, LANES), F32)],
        scratch=[pltpu.VMEM((LANES, LANES), F32)],
        prefetch=2,
        flops=16 * tokens * 2 * WINDOW * width,
        moved=2 * width * (10 * tokens + 5 * tail),
    )(info, bounds, qkv, qkv_tail, attended, d_attended, probs, gates, inverse, importance, before)

    total_all = totals
    total_after = jnp.zeros_like(totals)
    for bit in range(net.n_seq.bit_length() - 1):
        got = net.along(total_all, bit)
        earlier = (net.seq >> bit) % 2 == 0
        total_after = jnp.where(earlier, total_after + got, total_after)
        total_all = total_all + got

    d_tail, sums_tail = call(
        tail_back_kernel,
        "tail_back",
        (1,),
        [whole_spec((2, tail, width)), whole_spec((3, width, width)), whole_spec((tail, width)), whole_spec((1, width))],
        [whole_spec((tail, width)), whole_spec((8, width))],
        [shape((tail, width), BF), shape((8, width), F32)],
        flops=4 * tail * width * width,
        moved=2 * width * (4 * tail + 3 * width),
    )(d_halo, w_qkv, x_tail, g_first)
    back = net.shifted(d_tail, -1).reshape(seqs, WINDOW, width)

    qkv_bucket = whole_spec((shards, 3 * half_rows, width))
    keep_qkv, give_qkv, sums_qkv = call(
        qkv_grad_kernel,
        "qkv_grad",
        (3,),
        [full, whole_spec((tail, width)), pl.BlockSpec((1, tokens, width), lambda j, *_: (j, 0, 0)), pl.BlockSpec((1, tail, width), lambda j, *_: (jnp.maximum(j - 1, 0), 0, 0))],
        [qkv_bucket, qkv_bucket, thin],
        [shape((shards, 3 * half_rows, width), BF), shape((shards, 3 * half_rows, width), BF), shape((3, 1, width), F32)],
        prefetch=1,
        flops=2 * width * width * (3 * tokens + 2 * tail),
        moved=2 * width * (4 * tokens + 3 * tail + 3 * width),
    )(order, normed, normed_tail, dqkv, d_halo)

    per_tile = tile // blocks
    input_grad, sums_first, d_score = call(
        input_grad_kernel,
        "input_grad",
        (tokens // tile,),
        [
            pl.BlockSpec((3, tile, width), lambda i, *_: (0, i, 0)),
            whole_spec((3, width, width)),
            whole_spec((width, LANES)),
            by_tile,
            by_tile,
            whole_spec((1, width)),
            by_tile,
            pl.BlockSpec((per_tile, WINDOW, width), lambda i, *_: (i, 0, 0)),
            pl.BlockSpec((tile, LANES), lambda i, *_: (i, 0)),
            pl.BlockSpec((tile, LANES), lambda i, *_: (i, 0)),
            pl.BlockSpec((per_tile, 3, LANES), lambda i, *_: (i, 0, 0)),
            pl.BlockSpec((per_tile, 1, LANES), lambda i, *_: (i, 0, 0)),
        ],
        [by_tile, whole_spec((8, width)), whole_spec((width, LANES))],
        [shape((tokens, width), F32), shape((8, width), F32), shape((width, LANES), F32)],
        prefetch=2,
        flops=6 * tokens * width * width,
        moved=20 * tokens * width + 6 * width * width,
    )(info, bounds, dqkv, w_qkv, w_score, normed, x_flat, g_first, d_middle, back, d_imp, importance, before, total_after)

    def chip_sum(keep, give):
        return add(keep, net.chip(give))

    def split_cores(mine):
        other = net.chip(mine)
        return jnp.where(core == 0, mine, other), jnp.where(core == 0, other, mine)

    d_fc, d_down = [], []
    fc, down = split_cores(net.reduce(chip_sum(*buckets[0])))
    d_fc.append(fc)
    d_down.append(down)
    late = jnp.concatenate([chip_sum(*buckets[1]), chip_sum(keep_out, give_out)], axis=1)
    fc, down = split_cores(net.reduce(late))
    d_fc.append(fc[:chunk_rows])
    d_down.append(down[:chunk_rows])
    d_out = jnp.concatenate([fc[chunk_rows:], down[chunk_rows:]], axis=0).astype(F32)
    first, second = split_cores(net.reduce(chip_sum(keep_qkv, give_qkv)))
    d_qkv = jnp.stack([part.reshape(3, half_rows, width) for part in (first, second)], axis=1)
    d_qkv = jnp.transpose(d_qkv.reshape(3, rows, width), (1, 0, 2)).reshape(rows, 3 * width).astype(F32)
    d_fc = jnp.stack([part.reshape(BLOCKS, rows, shards // BLOCKS, deep) for part in d_fc], axis=3)
    d_fc = jnp.transpose(d_fc, (1, 0, 2, 3, 4)).reshape(rows, hidden).astype(F32)
    d_down = jnp.stack(d_down).reshape(hidden // shards, width).astype(F32)

    d_fc_bias = jnp.concatenate(d_fc_bias, axis=2).reshape(-1)
    small_grads = [
        sums_first[0] + sums_tail[0],
        sums_first[1] + sums_tail[1],
        sums_second[0],
        sums_second[1],
        sums_second[2],
        sums_second[3],
        jnp.concatenate([sums_qkv[0, 0], sums_qkv[2, 0]]),
        d_fc_bias,
        d_score[:, :heads].reshape(-1),
    ]
    packed = jnp.concatenate([part.reshape(shards, -1) for part in small_grads], axis=1)
    packed = net.sum_all(packed)
    packed = lax.dynamic_index_in_dim(packed, net.dp, 0, keepdims=False)
    outs = []
    begin = 0
    for size in sizes:
        outs.append(packed[begin : begin + size])
        begin += size
    dg_first, ds_first, dg_second, ds_second, db_out, db_down, db_qv, db_fc, d_score = outs
    return (
        block_output.reshape(seqs, blocks, width),
        input_grad.reshape(seqs, blocks, width),
        dg_first,
        ds_first,
        d_qkv,
        db_qv,
        d_score.reshape(rows, heads),
        d_out,
        db_out,
        dg_second,
        ds_second,
        d_fc,
        db_fc,
        d_down,
        db_down,
    )


def solution(mesh):
    split = P("dp", "seq", None)
    rows = P("dp", None)
    flat = P("dp")
    in_specs = (split, rows, flat, flat, rows, flat, rows, rows, flat, flat, flat, rows, flat, rows, flat, split)
    out_specs = (split, split, flat, flat, rows, flat, rows, rows, flat, flat, flat, rows, flat, rows, flat)
    return jax.shard_map(body, mesh=mesh, in_specs=in_specs, out_specs=out_specs, check_vma=False)
```

```python
import math

import jax
import jax.numpy as jnp
from jax import lax
from jax.experimental import pallas as pl
from jax.experimental.pallas import tpu as pltpu
from jax.sharding import PartitionSpec as P

KTOP = 64
WINDOW = 64
HEAD = 64
LANES = 128
EPSILON = 1e-05
NEGATIVE = -1e30
SCALE = 1.0 / math.sqrt(HEAD)
GELU_A = math.sqrt(2.0 / math.pi)
GELU_B = 0.044715
BF = jnp.bfloat16
F32 = jnp.float32
NN = ((1,), (0,))
NT = ((1,), (1,))
TN = ((0,), (0,))
CHUNKS = 2
BLOCKS = 2
MIB = 2**20
GAIN1, SHIFT1, GAIN2, SHIFT2, BIAS_OUT, BIAS_DOWN, BIAS_QKV, BIAS_FC = 0, 1, 2, 3, 4, 5, 6, 9
VECTORS = 6
QV_ROWS = 2
FC_ROWS = 4


def mm(left, right, dims=NN):
    return lax.dot_general(left, right, (dims, ((), ())), preferred_element_type=F32)


def mm_split(mask, value, dims=NN):
    high = value.astype(BF)
    low = (value - high.astype(F32)).astype(BF)
    return mm(mask, high, dims) + mm(mask, low, dims)


def whole_spec(shape):
    return pl.BlockSpec(shape, lambda *_: (0,) * len(shape))


ANY = pl.BlockSpec(memory_space=pl.ANY)


def call(kernel, name, grid, in_specs, out_specs, out_shape, scratch=(), prefetch=0, micros=1.0, limit=16, alias=None, far=(), far_in=()):
    many = isinstance(out_shape, (list, tuple))
    outs = [pltpu.HBM(one.shape, one.dtype) if k in far else one for k, one in enumerate(out_shape if many else [out_shape])]
    inner = pl.pallas_call(
        kernel,
        grid_spec=pltpu.PrefetchScalarGridSpec(
            num_scalar_prefetch=prefetch,
            grid=grid,
            in_specs=in_specs,
            out_specs=out_specs,
            scratch_shapes=list(scratch),
        ),
        out_shape=outs if many else outs[0],
        input_output_aliases=alias or {},
        compiler_params=pltpu.CompilerParams(vmem_limit_bytes=limit * MIB),
        cost_estimate=pl.CostEstimate(flops=int(micros * 1.1e9), bytes_accessed=1024, transcendentals=0),
        name=name,
    )

    def run(*operands):
        return inner(*[pltpu.with_memory_space_constraint(one, pltpu.HBM) if k - prefetch in far_in else one for k, one in enumerate(operands)])

    return run


def shape(dims, kind):
    return jax.ShapeDtypeStruct(dims, kind)


def iota(dims, axis):
    return lax.broadcasted_iota(jnp.int32, dims, axis)


def segment(places, first, second):
    return (places >= first).astype(jnp.int32) + (places >= second).astype(jnp.int32)


def normalise(values):
    average = jnp.mean(values, axis=-1, keepdims=True)
    centred = values - average
    variance = jnp.mean(centred * centred, axis=-1, keepdims=True)
    scale = lax.rsqrt(variance + EPSILON)
    return centred * scale, scale


def norm_back(d_norm, unit, scale, gain):
    weighted = d_norm * gain
    return scale * (
        weighted
        - jnp.mean(weighted, axis=-1, keepdims=True)
        - unit * jnp.mean(weighted * unit, axis=-1, keepdims=True)
    )


def bit_orders(count):
    bits = count.bit_length() - 1
    straight = list(range(bits))
    half = bits // 2
    return straight, straight[half:] + straight[:half]


def crossed(count, core, index, first_high):
    order = bit_orders(count)[core]
    mask = 0
    for step, bit in enumerate(order):
        place = len(order) - 1 - step if first_high else step
        mask |= ((index >> place) & 1) << bit
    return mask


def rank(count, core, far, first_high):
    order = bit_orders(count)[core]
    index = 0
    for step, bit in enumerate(order):
        place = len(order) - 1 - step if first_high else step
        index |= ((far >> bit) & 1) << place
    return index


def by_core(core, even, odd):
    return jnp.where(core == 0, even, odd)


def copy_all(copies, sems):
    started = [pltpu.make_async_copy(source, target, sems.at[k]) for k, (source, target) in enumerate(copies)]
    for copy in started:
        copy.start()
    for copy in started:
        copy.wait()


def params_kernel(info, *refs):
    pieces, (table_ref, score_ref, held) = refs[:-3], refs[-3:]
    shards = len(pieces)
    core, me = info[1], info[2]
    for k, piece in enumerate(pieces):
        held[k] = piece[...].astype(F32)

    def at(shard):
        far = shard ^ me
        index = jnp.int32(0)
        for k in range(shards):
            mask = by_core(core, crossed(shards, 0, k, False), crossed(shards, 1, k, False))
            index = jnp.where(mask == far, k, index)
        return held[index]

    parts = [at(shard) for shard in range(shards)]

    def line(shard_range, rows):
        return jnp.concatenate([parts[s][r : r + 1] for s in shard_range for r in rows], axis=1)

    table_ref[...] = jnp.zeros_like(table_ref)
    for r in range(VECTORS):
        table_ref[r : r + 1] = line(range(shards), [r])
    qv = list(range(VECTORS, VECTORS + QV_ROWS))
    table_ref[BIAS_QKV : BIAS_QKV + 1] = line(range(shards // 2), qv)
    table_ref[BIAS_QKV + 2 : BIAS_QKV + 3] = line(range(shards // 2, shards), qv)
    base = VECTORS + QV_ROWS
    per_block = shards // BLOCKS
    per_chunk = FC_ROWS // CHUNKS
    for chunk in range(CHUNKS):
        for block in range(BLOCKS):
            rows = [base + chunk * per_chunk + k for k in range(per_chunk)]
            row = BIAS_FC + chunk * BLOCKS + block
            table_ref[row : row + 1] = line(range(block * per_block, (block + 1) * per_block), rows)
    base += FC_ROWS
    heads = parts[0].shape[0] - base
    score_ref[...] = jnp.zeros_like(score_ref)
    for head in range(heads):
        score_ref[head : head + 1] = line(range(shards), [base + head]).astype(BF)


def prep_kernel(info, bounds, x_ref, tail_ref, table_ref, score_ref, normed_ref, tail_out_ref, imp_ref, mass_ref, stat_ref):
    seqs = stat_ref.shape[0]
    blocks = x_ref.shape[0] // seqs
    gain = table_ref[GAIN1 : GAIN1 + 1]
    shift = table_ref[SHIFT1 : SHIFT1 + 1]
    start = info[0]
    rows = iota((blocks, blocks), 0)
    cols = iota((blocks, blocks), 1)
    for k in range(seqs):
        rs = slice(k * blocks, (k + 1) * blocks)
        ts = slice(k * WINDOW, (k + 1) * WINDOW)
        normed = (normalise(x_ref[rs].astype(F32))[0] * gain + shift).astype(BF)
        normed_ref[rs] = normed
        tail_out_ref[ts] = (normalise(tail_ref[ts].astype(F32))[0] * gain + shift).astype(BF)
        importance = mm(normed, score_ref[...], NT)
        imp_ref[rs] = importance
        s = pl.program_id(0) * seqs + k
        first, second = bounds[s, 0], bounds[s, 1]
        lower = (cols <= rows) & (segment(start + rows, first, second) == segment(start + cols, first, second))
        peak = jnp.max(importance, axis=0, keepdims=True)
        mass = mm_split(lower.astype(BF), jnp.exp(importance - peak))
        mass_ref[rs] = mass
        stat_ref[k, 0:1, :] = peak
        stat_ref[k, 1:2, :] = mass[blocks - 1 :, :]
        stat_ref[k, 2:3, :] = jnp.full_like(peak, NEGATIVE)
        stat_ref[k, 3:4, :] = jnp.zeros_like(peak)
        stat_ref[k, 4:5, :] = peak


def scan_kernel(info, mine_ref, got_ref, out_ref, *, bit):
    peak_got, total_got = got_ref[:, 0:1], got_ref[:, 1:2]
    later = ((info[3] >> bit) & 1) == 1

    def joined(peak, total):
        top = jnp.maximum(peak, peak_got)
        return top, total * jnp.exp(peak - top) + total_got * jnp.exp(peak_got - top)

    out_ref[...] = mine_ref[...]
    peak, total = joined(mine_ref[:, 0:1], mine_ref[:, 1:2])
    out_ref[:, 0:1] = peak
    out_ref[:, 1:2] = total

    @pl.when(later)
    def _():
        peak, total = joined(mine_ref[:, 2:3], mine_ref[:, 3:4])
        out_ref[:, 2:3] = peak
        out_ref[:, 3:4] = total


def qkv_build_kernel(info, *refs):
    own, pieces, out, sems = refs[0], refs[1:-2], refs[-2], refs[-1]
    shards = len(pieces) // 2 + 1
    rows, width = own.shape
    half = width // 2
    me = info[2]

    def build(core):
        copies = [(own, out.at[pl.ds(pl.multiple_of(me * rows, 16), rows)])]
        for k in range(1, shards):
            for side, group in ((core, 0), (1 - core, shards - 1)):
                at = pl.multiple_of((me ^ crossed(shards, side, k, False)) * rows, 16)
                target = out.at[pl.ds(at, rows), side * half : (side + 1) * half]
                copies.append((pieces[group + k - 1], target))
        copy_all(copies, sems)

    @pl.when(info[1] == 0)
    def _():
        build(0)

    @pl.when(info[1] != 0)
    def _():
        build(1)


def feed_build_kernel(info, *refs, with_out):
    if with_out:
        own_fc, own_down, own_out = refs[:3]
        pieces, (fc_ref, down_ref, out_ref, sems) = refs[3:-4], refs[-4:]
    else:
        own_fc, own_down = refs[:2]
        pieces, (fc_ref, down_ref, sems) = refs[2:-3], refs[-3:]
    shards = len(pieces) // 2 + 1
    rows, wide = own_fc.shape
    deep, width = own_down.shape
    split = width // 2
    me = info[2]

    def build(core):
        at_rows = lambda shard: pl.multiple_of(shard * rows, 16)
        copies = [
            (own_fc, fc_ref.at[pl.ds(at_rows(me), rows)]),
            (own_down, down_ref.at[pl.ds(pl.multiple_of(me * deep, 16), deep)]),
        ]
        if with_out:
            copies.append((own_out, out_ref.at[pl.ds(at_rows(me), rows)]))
        for k in range(1, shards):
            for side, group in ((core, 0), (1 - core, shards - 1)):
                piece = pieces[group + k - 1]
                shard = me ^ crossed(shards, side, k, False)
                if side == 0:
                    copies.append((piece.at[:, :wide], fc_ref.at[pl.ds(at_rows(shard), rows)]))
                else:
                    for part in range(deep // rows):
                        at = pl.multiple_of(shard * deep + part * rows, 16)
                        copies.append((piece.at[:, part * width : (part + 1) * width], down_ref.at[pl.ds(at, rows)]))
                if with_out:
                    copies.append((piece.at[:, wide:], out_ref.at[pl.ds(at_rows(shard), rows), side * split : (side + 1) * split]))
        copy_all(copies, sems)

    @pl.when(info[1] == 0)
    def _():
        build(0)

    @pl.when(info[1] != 0)
    def _():
        build(1)


def qkv_kernel(normed_ref, tail_ref, weight_ref, table_ref, out_ref, tail_out_ref):
    j = pl.program_id(0)
    weight = weight_ref[...]
    bias = table_ref[pl.ds(BIAS_QKV + j, 1)]
    factor = jnp.where(j == 0, SCALE, 1.0)
    out_ref[...] = ((mm(normed_ref[...], weight) + bias).astype(BF).astype(F32) * factor).astype(BF)

    @pl.when(j > 0)
    def _():
        tail_out_ref[...] = (mm(tail_ref[...], weight) + bias).astype(BF)


def lane_masks():
    first = iota((1, LANES), 1) < HEAD
    return first.astype(BF), (~first).astype(BF)


def grouped(part, keep_first, keep_second):
    return jnp.concatenate([part * keep_first, part * keep_second], axis=0)


def tile_masks(start, half, first, second):
    dims = (WINDOW, LANES)
    row = iota(dims, 0)
    col = iota(dims, 1) & (HEAD - 1)
    base = start + WINDOW * half
    mine = segment(base + row, first, second)
    far = segment(base - WINDOW + col, first, second) == mine
    near = (col <= row) & (segment(base + col, first, second) == mine)
    if half == 0:
        far = far & (col > row) & (base - WINDOW + col >= 0)
    return far, near, col <= row


def spread(columns, pair, rows):
    left = columns[:, 2 * pair : 2 * pair + 1]
    right = columns[:, 2 * pair + 1 : 2 * pair + 2]
    return jnp.where(iota((rows, LANES), 1) < HEAD, left, right)


def key_groups(qkv_ref, halo_ref, width, pair, keep_first, keep_second, one_group):
    at = slice(pair * LANES, (pair + 1) * LANES)
    ks = slice(width + pair * LANES, width + (pair + 1) * LANES)
    vs = slice(2 * width + pair * LANES, 2 * width + (pair + 1) * LANES)
    keys = [grouped(part, keep_first, keep_second) for part in (halo_ref[:, at], qkv_ref[:WINDOW, ks], qkv_ref[WINDOW:, ks])]
    values = [
        jnp.concatenate([grouped(part, keep_first, keep_second), one_group], axis=1)
        for part in (halo_ref[:, ks], qkv_ref[:WINDOW, vs], qkv_ref[WINDOW:, vs])
    ]
    return keys, values


def attention_kernel(info, bounds, qkv_ref, halo_ref, imp_ref, mass_ref, before_ref, att_ref, probs_ref, sig_ref, inv_ref):
    s = pl.program_id(0)
    blocks, width = att_ref.shape
    start = info[0]
    first, second = bounds[s, 0], bounds[s, 1]
    pairs = width // LANES
    peak = before_ref[0, 4:5, :]
    carry_peak = before_ref[0, 2:3, :]
    carry_total = before_ref[0, 3:4, :]
    top = before_ref[0, 0:1, :]
    joined = jnp.maximum(peak, carry_peak)
    place = start + iota((blocks, LANES), 0)
    continues = segment(place, first, second) == segment(jnp.full((1, LANES), start - 1, jnp.int32), first, second)
    mass = mass_ref[...] * jnp.exp(peak - joined) + jnp.where(
        continues, carry_total * jnp.exp(carry_peak - joined), 0.0
    )
    threshold = joined + jnp.log(mass) - math.log(KTOP)
    late = threshold[WINDOW:]
    inv_ref[...] = 1.0 / (mass[WINDOW:] * jnp.exp(joined - top))
    imp_rows = imp_ref[...].T
    keep_first, keep_second = lane_masks()
    one_group = grouped(jnp.ones((WINDOW, LANES), BF), keep_first, keep_second)
    masks = [tile_masks(start, half, first, second) for half in (0, 1)]
    lane = iota((WINDOW, LANES), 1) < HEAD
    for pair in range(pairs):
        ls = slice(pair * LANES, (pair + 1) * LANES)
        keys, values = key_groups(qkv_ref, halo_ref, width, pair, keep_first, keep_second, one_group)
        for half in (0, 1):
            rs = slice(half * WINDOW, (half + 1) * WINDOW)
            far_ok, near_ok, gated = masks[half]
            logits = mm(qkv_ref[rs, ls], jnp.concatenate(keys[half : half + 2], axis=0), NT)
            far, near = logits[:, :LANES], logits[:, LANES:]
            if half == 1:
                row = jnp.concatenate(
                    [imp_rows[2 * pair : 2 * pair + 1, :WINDOW], imp_rows[2 * pair + 1 : 2 * pair + 2, :WINDOW]], axis=1
                )
                gap = spread(late, pair, WINDOW) - row
                small = jnp.exp(-jnp.abs(gap))
                soft = jnp.maximum(gap, 0.0) + jnp.log(1.0 + small)
                sig_ref[:, ls] = (jnp.where(gap >= 0, 1.0, small) / (1.0 + small)).astype(BF)
                far = jnp.where(gated, far - soft, far)
            far = jnp.where(far_ok, far, NEGATIVE)
            near = jnp.where(near_ok, near, NEGATIVE)
            best = jnp.maximum(far, near)
            best_first = jnp.max(jnp.where(lane, best, NEGATIVE), axis=1, keepdims=True)
            best_second = jnp.max(jnp.where(lane, NEGATIVE, best), axis=1, keepdims=True)
            best = jnp.where(lane, best_first, best_second)
            far = jnp.exp(far - best)
            near = jnp.exp(near - best)
            weights = jnp.concatenate([far.astype(BF), near.astype(BF)], axis=1)
            mixed = mm(weights, jnp.concatenate(values[half : half + 2], axis=0))
            inverse = 1.0 / mixed[:, LANES:]
            att_ref[rs, ls] = (mixed[:, :LANES] * inverse).astype(BF)
            probs_ref[rs, 2 * pair * LANES : (2 * pair + 1) * LANES] = (far * inverse).astype(BF)
            probs_ref[rs, (2 * pair + 1) * LANES : (2 * pair + 2) * LANES] = (near * inverse).astype(BF)


def project_kernel(att_ref, x_ref, weight_ref, table_ref, middle_ref, second_ref):
    middle = x_ref[...].astype(F32) + mm(att_ref[...], weight_ref[...]) + table_ref[BIAS_OUT : BIAS_OUT + 1]
    middle_ref[...] = middle
    second_ref[...] = (normalise(middle)[0] * table_ref[GAIN2 : GAIN2 + 1] + table_ref[SHIFT2 : SHIFT2 + 1]).astype(BF)


def feed_kernel(info, sec_ref, dy_ref, fc_ref, down_ref, table_ref, hid_ref, dpre_ref, db_ref, keep_ref, give_ref, *, chunk, block):
    fc = fc_ref[...]
    down = down_ref[...]
    row = BIAS_FC + chunk * BLOCKS + block
    pre = mm(sec_ref[...], fc) + table_ref[row : row + 1]
    d_hidden = mm(dy_ref[...], down, NT)
    square = pre * pre
    tanh = jnp.tanh(pre * (GELU_A + GELU_A * GELU_B * square))
    half = 0.5 + 0.5 * tanh
    hidden = (pre * half).astype(BF)
    slope = half + pre * (0.5 * GELU_A + 1.5 * GELU_A * GELU_B * square) * (1.0 - tanh * tanh)
    d_pre = d_hidden * slope
    d_low = d_pre.astype(BF)
    hid_ref[...] = hidden
    dpre_ref[...] = d_low
    db_ref[...] = jnp.broadcast_to(jnp.sum(d_pre, axis=0, keepdims=True), db_ref.shape)
    d_down = mm(hidden, dy_ref[...], TN).astype(BF)
    d_fc = mm(sec_ref[...], d_low, TN).astype(BF)

    @pl.when(info[1] == 0)
    def _():
        keep_ref[...] = d_fc
        give_ref[...] = d_down

    @pl.when(info[1] != 0)
    def _():
        keep_ref[...] = d_down
        give_ref[...] = d_fc


def feed_add_kernel(info, *refs):
    keeps, gots, (keep_ref, give_ref, held) = refs[:BLOCKS], refs[BLOCKS : 2 * BLOCKS], refs[2 * BLOCKS :]
    shards, rows, wide = held.shape
    width = keeps[0].shape[0]
    me = info[2]
    per_block = shards // BLOCKS
    deep = width // per_block

    def put(core):
        for block in range(BLOCKS):
            total = add(keeps[block][...], gots[block][...])
            if core == 0:
                for shard in range(shards):
                    held[ranked(shards, 0, me ^ shard), :, block * width : (block + 1) * width] = total[shard * rows : (shard + 1) * rows]
            else:
                for k in range(per_block):
                    place = ranked(shards, 1, me ^ (block * per_block + k))
                    for part in range(deep // rows):
                        begin = k * deep + part * rows
                        held[place, :, part * width : (part + 1) * width] = total[begin : begin + rows]

    @pl.when(info[1] == 0)
    def _():
        put(0)

    @pl.when(info[1] != 0)
    def _():
        put(1)

    half = shards // 2
    keep_ref[...] = held[:half]
    give_ref[...] = held[half:]


def ranked(shards, core, far):
    order = bit_orders(shards)[core]
    index = jnp.int32(0)
    for step, bit in enumerate(order):
        index = index | (((far >> bit) & 1) << (len(order) - 1 - step))
    return index


def middle_kernel(info, *refs):
    count = CHUNKS * BLOCKS
    dpre_refs = refs[:count]
    fc_refs = refs[count : count + CHUNKS]
    middle_ref, dy_ref, att_ref, weight_ref, table_ref, dmid_ref, datt_ref, keep_ref, give_ref, sums_ref, total = refs[count + CHUNKS :]
    i = pl.program_id(0)
    steps = pl.num_programs(0)
    shards, rows, split = keep_ref.shape
    width = middle_ref.shape[1]
    core, me = info[1], info[2]
    d_norm = None
    for k in range(count):
        part = mm(dpre_refs[k][...], fc_refs[k // BLOCKS][:, (k % BLOCKS) * width : (k % BLOCKS + 1) * width], NT)
        d_norm = part if d_norm is None else d_norm + part
    unit, scale = normalise(middle_ref[...])
    dy = dy_ref[...].astype(F32)
    d_middle = dy + norm_back(d_norm, unit, scale, table_ref[GAIN2 : GAIN2 + 1])
    dmid_ref[...] = d_middle
    branch = d_middle.astype(BF)
    datt_ref[...] = mm(branch, weight_ref[...], NT).astype(BF)
    part = mm(att_ref[...], branch, TN)
    sums = [
        jnp.sum(d_norm * unit, axis=0, keepdims=True),
        jnp.sum(d_norm, axis=0, keepdims=True),
        jnp.sum(branch.astype(F32), axis=0, keepdims=True),
        jnp.sum(dy, axis=0, keepdims=True),
    ]

    @pl.when(i == 0)
    def _():
        total[...] = part
        for k in range(4):
            sums_ref[k : k + 1] = sums[k]

    @pl.when(i > 0)
    def _():
        total[...] += part
        for k in range(4):
            sums_ref[k : k + 1] += sums[k]

    @pl.when(i == steps - 1)
    def _():
        store_halves(info, total, keep_ref, give_ref, shards, rows, split)


def store_halves(info, total, keep_ref, give_ref, shards, rows, split):
    me = info[2]

    def store(side, to):
        for shard in range(shards):
            value = total[shard * rows : (shard + 1) * rows, side * split : (side + 1) * split]
            to[ranked(shards, side, me ^ shard)] = value.astype(BF)

    @pl.when(info[1] == 0)
    def _():
        store(0, keep_ref)
        store(1, give_ref)

    @pl.when(info[1] != 0)
    def _():
        store(1, keep_ref)
        store(0, give_ref)


def attention_back_kernel(info, bounds, qkv_ref, halo_ref, att_ref, datt_ref, probs_ref, sig_ref, inv_ref, imp_ref, before_ref, dqkv_ref, dhalo_ref, dimp_ref, total_ref, rows_scratch, *, first_pair, pairs):
    s = pl.program_id(0)
    blocks, width = att_ref.shape
    start = info[0]
    first, second = bounds[s, 0], bounds[s, 1]
    keep_first, keep_second = lane_masks()
    one_group = grouped(jnp.ones((WINDOW, LANES), BF), keep_first, keep_second)
    lane = iota((WINDOW, LANES), 1) < HEAD
    gated = (iota((WINDOW, LANES), 1) & (HEAD - 1)) <= iota((WINDOW, LANES), 0)
    head_lane = iota((LANES, LANES), 1)
    head_row = iota((LANES, LANES), 0)
    d_threshold = jnp.zeros((WINDOW, LANES), F32)
    rows_scratch[...] = jnp.zeros_like(rows_scratch)
    wide = pairs * LANES
    for k in range(pairs):
        pair = first_pair + k
        ls = slice(pair * LANES, (pair + 1) * LANES)
        keys, values = key_groups(qkv_ref, halo_ref, width, pair, keep_first, keep_second, one_group)
        far_keys, near_keys, far_values, near_values = [], [], [], []
        for half in (0, 1):
            rs = slice(half * WINDOW, (half + 1) * WINDOW)
            d_out = datt_ref[rs, ls]
            product = (-(d_out.astype(F32) * att_ref[rs, ls].astype(F32))).astype(BF)
            left = jnp.concatenate([d_out, product], axis=1)
            centred = mm(left, jnp.concatenate(values[half : half + 2], axis=0), NT)
            probs = probs_ref[rs, 2 * pair * LANES : (2 * pair + 2) * LANES]
            d_logits = probs.astype(F32) * centred
            low = d_logits.astype(BF)
            dqkv_ref[rs, k * LANES : (k + 1) * LANES] = (mm(low, jnp.concatenate(keys[half : half + 2], axis=0)) * SCALE).astype(BF)
            d_keys = mm(low, qkv_ref[rs, ls], TN)
            d_values = mm(probs, d_out, TN)
            far_keys.append(jnp.where(lane, d_keys[:WINDOW], d_keys[WINDOW : 2 * WINDOW]))
            near_keys.append(jnp.where(lane, d_keys[2 * WINDOW : 3 * WINDOW], d_keys[3 * WINDOW :]))
            far_values.append(jnp.where(lane, d_values[:WINDOW], d_values[WINDOW : 2 * WINDOW]))
            near_values.append(jnp.where(lane, d_values[2 * WINDOW : 3 * WINDOW], d_values[3 * WINDOW :]))
            if half == 1:
                gate = jnp.where(gated, d_logits[:, :LANES] * sig_ref[:, ls].astype(F32), 0.0)
                rows_scratch[pair : pair + 1, :] = jnp.sum(gate, axis=0, keepdims=True)
                chosen = (head_lane == 2 * pair + (head_row >= HEAD).astype(jnp.int32)).astype(BF)
                d_threshold = d_threshold - mm(gate.astype(BF), chosen)
        here = slice(k * LANES, (k + 1) * LANES)
        ks = slice(wide + k * LANES, wide + (k + 1) * LANES)
        vs = slice(2 * wide + k * LANES, 2 * wide + (k + 1) * LANES)
        dhalo_ref[:, here] = far_keys[0].astype(BF)
        dhalo_ref[:, ks] = far_values[0].astype(BF)
        dqkv_ref[:WINDOW, ks] = (near_keys[0] + far_keys[1]).astype(BF)
        dqkv_ref[WINDOW:, ks] = near_keys[1].astype(BF)
        dqkv_ref[:WINDOW, vs] = (near_values[0] + far_values[1]).astype(BF)
        dqkv_ref[WINDOW:, vs] = near_values[1].astype(BF)
    weighted = d_threshold * inv_ref[...]
    row = iota((blocks, WINDOW), 0)
    col = iota((blocks, WINDOW), 1) + WINDOW
    after = (col >= row) & (segment(start + row, first, second) == segment(start + col, first, second))
    later = mm_split(after.astype(BF), weighted)
    total_ref[0, 0:1, :] = later[0:1]
    turned = rows_scratch[...].T
    pick_first = (head_lane == 2 * head_row).astype(BF)
    pick_second = (head_lane == 2 * head_row + 1).astype(BF)

    def pick(values, chosen):
        high = values.astype(BF)
        return mm(high, chosen) + mm((values - high.astype(F32)).astype(BF), chosen)

    direct = pick(turned[:HEAD], pick_first) + pick(turned[HEAD:], pick_second)
    local = jnp.exp(imp_ref[...] - before_ref[0, 0:1, :]) * later
    dimp_ref[:WINDOW] = local[:WINDOW] + direct
    dimp_ref[WINDOW:] = local[WINDOW:]


def weight_part(weight_ref, layer, first_pair, pairs):
    width = weight_ref.shape[0]
    begin = layer * width + first_pair * LANES
    return weight_ref[:, begin : begin + pairs * LANES]


def tail_back_kernel(*refs, parts):
    dhalo_refs = refs[: len(parts)]
    weight_ref, x_ref, table_ref, out_ref, sums_ref = refs[len(parts) :]
    d_norm = None
    for (first_pair, pairs), dhalo_ref in zip(parts, dhalo_refs):
        wide = pairs * LANES
        for layer in (1, 2):
            part = mm(dhalo_ref[:, (layer - 1) * wide : layer * wide], weight_part(weight_ref, layer, first_pair, pairs), NT)
            d_norm = part if d_norm is None else d_norm + part
    unit, scale = normalise(x_ref[...].astype(F32))
    out_ref[...] = norm_back(d_norm, unit, scale, table_ref[GAIN1 : GAIN1 + 1]).astype(BF)
    sums_ref[0:1] = jnp.sum(d_norm * unit, axis=0, keepdims=True)
    sums_ref[1:2] = jnp.sum(d_norm, axis=0, keepdims=True)


def qkv_grad_kernel(info, normed_ref, tail_ref, dqkv_ref, dhalo_ref, keep_ref, give_ref, sums_ref):
    shards, rows, split = keep_ref.shape
    wide = dqkv_ref.shape[1] // 3
    me = info[2]
    for layer in range(3):
        local = dqkv_ref[:, layer * wide : (layer + 1) * wide]
        total = mm(normed_ref[...], local, TN)
        sums = jnp.sum(local.astype(F32), axis=0, keepdims=True)
        if layer > 0:
            halo = dhalo_ref[:, (layer - 1) * wide : layer * wide]
            total = total + mm(tail_ref[...], halo, TN)
            sums = sums + jnp.sum(halo.astype(F32), axis=0, keepdims=True)
        total = total.astype(BF)
        sums_ref[layer : layer + 1] = sums
        begin, end = layer * wide, (layer + 1) * wide
        pieces = []
        for side in (0, 1):
            low, high = max(begin, side * split), min(end, (side + 1) * split)
            if low < high:
                pieces.append((side, low - begin, high - begin, low - side * split))

        def store(core):
            for side, low, high, at in pieces:
                to = keep_ref if side == core else give_ref
                for shard in range(shards):
                    to[ranked(shards, side, me ^ shard), :, at : at + high - low] = total[shard * rows : (shard + 1) * rows, low:high]

        @pl.when(info[1] == 0)
        def _():
            store(0)

        @pl.when(info[1] != 0)
        def _():
            store(1)


def input_grad_kernel(info, bounds, *refs, parts):
    count = len(parts)
    dqkv_refs, dimp_refs = refs[:count], refs[count : 2 * count]
    weight_ref, score_ref, normed_ref, x_ref, table_ref, dmid_ref, back_ref, imp_ref, before_ref, after_ref, out_ref, sums_ref, score_out_ref = refs[2 * count :]
    i = pl.program_id(0)
    seqs = back_ref.shape[0]
    blocks = x_ref.shape[0] // seqs
    start = info[0]
    d_imps = []
    for s in range(seqs):
        first, second = bounds[i * seqs + s, 0], bounds[i * seqs + s, 1]
        place = start + iota((blocks, LANES), 0)
        onward = segment(place, first, second) == segment(jnp.full((1, LANES), start + blocks, jnp.int32), first, second)
        rs = slice(s * blocks, (s + 1) * blocks)
        extra = jnp.exp(imp_ref[rs] - before_ref[s, 0:1, :]) * after_ref[s, 0:1, :]
        d_imp = jnp.where(onward, extra, 0.0)
        for dimp_ref in dimp_refs:
            d_imp = d_imp + dimp_ref[rs]
        d_imps.append(d_imp)
    d_imp = jnp.concatenate(d_imps, axis=0).astype(BF)
    d_norm = mm(d_imp, score_ref[...])
    for (first_pair, pairs), dqkv_ref in zip(parts, dqkv_refs):
        wide = pairs * LANES
        for layer in range(3):
            d_norm = d_norm + mm(dqkv_ref[:, layer * wide : (layer + 1) * wide], weight_part(weight_ref, layer, first_pair, pairs), NT)
    unit, scale = normalise(x_ref[...].astype(F32))
    d_value = norm_back(d_norm, unit, scale, table_ref[GAIN1 : GAIN1 + 1]) + dmid_ref[...]
    for s in range(seqs):
        rs = slice(s * blocks, s * blocks + WINDOW)
        out_ref[rs] = d_value[rs]
        rs = slice(s * blocks + WINDOW, (s + 1) * blocks)
        out_ref[rs] = d_value[rs] + back_ref[s].astype(F32)
    sums = [jnp.sum(d_norm * unit, axis=0, keepdims=True), jnp.sum(d_norm, axis=0, keepdims=True)]
    score = mm(d_imp, normed_ref[...], TN)

    @pl.when(i == 0)
    def _():
        score_out_ref[...] = score
        for k in range(2):
            sums_ref[k : k + 1] = sums[k]

    @pl.when(i > 0)
    def _():
        score_out_ref[...] += score
        for k in range(2):
            sums_ref[k : k + 1] += sums[k]


def output_kernel(*refs):
    count = CHUNKS * BLOCKS
    hid_refs = refs[:count]
    down_refs = refs[count : count + CHUNKS]
    middle_ref, table_ref, out_ref = refs[count + CHUNKS :]
    width = middle_ref.shape[1]
    total = middle_ref[...] + table_ref[BIAS_DOWN : BIAS_DOWN + 1]
    for k in range(count):
        total = total + mm(hid_refs[k][...], down_refs[k // BLOCKS][(k % BLOCKS) * width : (k % BLOCKS + 1) * width])
    out_ref[...] = total.astype(BF)


def small_pack_kernel(info, first_ref, tail_ref, second_ref, *refs, spans):
    qkv_refs = refs[: len(spans)]
    bias_refs = refs[len(spans) : len(spans) + CHUNKS * BLOCKS]
    score_ref, out_ref, whole = refs[len(spans) + CHUNKS * BLOCKS :]
    shards, count, rows = out_ref.shape
    me = info[2]
    whole[0:2] = first_ref[0:2] + tail_ref[0:2]
    whole[2:VECTORS] = second_ref[0 : VECTORS - 2]
    for row, layer in ((VECTORS, 0), (VECTORS + 1, 2)):
        begin = 0
        for ref, span in zip(qkv_refs, spans):
            whole[row : row + 1, begin : begin + span] = ref[layer : layer + 1]
            begin += span
    base = VECTORS + 2
    for k in range(CHUNKS * BLOCKS):
        whole[base + k : base + k + 1] = bias_refs[k][0:1]
    heads = count - VECTORS - QV_ROWS - FC_ROWS
    whole[base + CHUNKS * BLOCKS : base + CHUNKS * BLOCKS + heads] = score_ref[0:heads]
    per_block = shards // BLOCKS
    per_chunk = FC_ROWS // CHUNKS
    for shard in range(shards):
        at = slice(shard * rows, (shard + 1) * rows)
        lines = [whole[0:VECTORS, at]]
        row = VECTORS + shard // (shards // 2)
        for k in range(QV_ROWS):
            begin = (shard % (shards // 2)) * QV_ROWS * rows + k * rows
            lines.append(whole[row : row + 1, begin : begin + rows])
        for chunk in range(CHUNKS):
            row = base + chunk * BLOCKS + shard // per_block
            for k in range(per_chunk):
                begin = (shard % per_block) * per_chunk * rows + k * rows
                lines.append(whole[row : row + 1, begin : begin + rows])
        lines.append(whole[base + CHUNKS * BLOCKS : base + CHUNKS * BLOCKS + heads, at])
        place = jnp.where(info[1] == 0, ranked(shards, 0, me ^ shard), ranked(shards, 1, me ^ shard))
        out_ref[place] = jnp.concatenate(lines, axis=0)


def add(left, right):
    return (left.astype(F32) + right.astype(F32)).astype(BF)


def combine(peak_a, total_a, peak_b, total_b):
    joined = jnp.maximum(peak_a, peak_b)
    return joined, total_a * jnp.exp(peak_a - joined) + total_b * jnp.exp(peak_b - joined)


def tie(*values):
    return lax.optimization_barrier(values)


class Net:
    def __init__(self):
        self.n_seq = lax.axis_size("seq")
        self.n_dp = lax.axis_size("dp")
        self.seq = lax.axis_index("seq")
        self.dp = lax.axis_index("dp")
        self.core = self.seq % 2
        self.orders = bit_orders(self.n_dp)
        self.bits = len(self.orders[0])
        self.seq_bits = self.n_seq.bit_length() - 1

    def send(self, value, target):
        pairs = []
        for s in range(self.n_seq):
            for d in range(self.n_dp):
                goal = target(s, d)
                if 0 <= goal[0] < self.n_seq:
                    pairs.append((s * self.n_dp + d, goal[0] * self.n_dp + goal[1]))
        return lax.ppermute(value, ("seq", "dp"), pairs)

    def across(self, value, step):
        return self.send(value, lambda s, d: (s, d ^ (1 << self.orders[s % 2][step])))

    def chip(self, value):
        return self.send(value, lambda s, d: (s ^ 1, d))

    def along(self, value, bit):
        return self.send(value, lambda s, d: (s ^ (1 << bit), d))

    def shifted(self, value, by):
        return self.send(value, lambda s, d: (s + by, d))

    def gather_step(self, pieces, step):
        return pieces + [self.across(piece, step) for piece in pieces]

    def sum_all(self, value):
        value = value + self.chip(value)
        for step in range(self.bits):
            value = value + self.across(value, step)
        for bit in range(1, self.seq_bits):
            value = value + self.along(value, bit)
        return value


class Reduction:
    def __init__(self, net, keep, give):
        self.net = net
        self.keep, self.give = keep, give
        z_bits = list(range(1, net.seq_bits))
        self.z_orders = (z_bits, z_bits[1:2] + z_bits[:1] + z_bits[2:])
        self.todo = ["across"] * net.bits + ["split"] + ["swap"] * (len(z_bits) - 1) + ["join"]
        self.done = 0
        self.got = None

    def along(self, value, place):
        return self.net.send(value, lambda s, d: (s ^ (1 << self.z_orders[s % 2][place]), d))

    def start(self):
        kind = self.todo[0]
        if kind == "across":
            self.got = self.net.across(self.give, self.done)
        elif kind == "split":
            half = self.keep.shape[0] // 2
            z_bit = jnp.where(self.net.core == 0, self.z_orders[0][0], self.z_orders[1][0])
            self.upper = (self.net.seq >> z_bit) % 2 == 1
            low, high = self.keep[:half], self.keep[half:]
            self.got = self.along(jnp.where(self.upper, low, high), 0)
            self.keep = jnp.where(self.upper, high, low)
        elif kind == "swap":
            self.got = self.along(self.keep, self.done - self.net.bits)
        else:
            self.got = self.along(self.keep, 0)

    def finish(self):
        kind = self.todo.pop(0)
        self.done += 1
        if kind == "join":
            low, high = jnp.where(self.upper, self.got, self.keep), jnp.where(self.upper, self.keep, self.got)
            self.keep = jnp.concatenate([low, high], axis=0)
            return
        total = add(self.keep, self.got)
        if kind == "across":
            half = total.shape[0] // 2
            if half:
                self.keep, self.give = total[:half], total[half:]
            else:
                self.keep = total[0]
        else:
            self.keep = total

    def run(self):
        while self.todo:
            self.start()
            self.finish()


def pin(value, *reds):
    held = [value]
    for red in reds:
        held += [red.keep] + ([red.give] if red.todo and red.todo[0] == "across" else [])
    held = list(tie(*held))
    value = held.pop(0)
    for red in reds:
        red.keep = held.pop(0)
        if red.todo and red.todo[0] == "across":
            red.give = held.pop(0)
    return value


def body(block_input, doc_bounds, first_gain, first_shift, qkv_weight, qv_bias, score_weight, out_weight, out_bias, second_gain, second_shift, fc_weight, fc_bias, down_weight, down_bias, cotangent):
    net = Net()
    seqs, blocks, width = block_input.shape
    tokens = seqs * blocks
    heads = score_weight.shape[1]
    shards = net.n_dp
    rows = width // shards
    hidden = fc_weight.shape[1]
    tail = seqs * WINDOW
    core = net.core
    place = jnp.arange(4, dtype=jnp.int32)
    info = jnp.where(place == 0, net.seq * blocks, jnp.where(place == 1, core, jnp.where(place == 2, net.dp, net.seq))).astype(jnp.int32)
    bounds = doc_bounds
    x_flat = block_input.reshape(tokens, width)
    dy = cotangent.reshape(tokens, width)
    wide = hidden // CHUNKS
    deep = hidden // shards // CHUNKS
    half_qkv = 3 * width // 2
    sems = lambda count: pltpu.SemaphoreType.DMA((count,))
    by_seq = lambda rows_, cols: pl.BlockSpec((rows_, cols), lambda s, *_: (s, 0))
    stat = pl.BlockSpec((1, 8, LANES), lambda s, *_: (s, 0, 0))
    table_spec = whole_spec((16, width))
    full = whole_spec((tokens, width))
    tile = 2 * blocks
    by_tile = pl.BlockSpec((tile, width), lambda i, *_: (i, 0))
    pairs = width // LANES
    parts = [(0, pairs)]

    small = jnp.concatenate([first_gain, first_shift, second_gain, second_shift, out_bias, down_bias, qv_bias, fc_bias]).reshape(-1, rows)
    small = jnp.concatenate([small, score_weight.T], axis=0)
    small_rows = small.shape[0]
    own = lax.dynamic_slice_in_dim(qkv_weight, core * half_qkv, half_qkv, 1)

    def begin_gather(own):
        return [own, net.across(own, 0)], [net.across(own, 1)] if net.bits > 1 else []

    def end_gather(pieces, ahead):
        if net.bits > 1:
            pieces = pieces + ahead + [net.across(pieces[1], 1)]
        for step in range(2, net.bits):
            pieces = net.gather_step(pieces, step)
        return pieces

    small_state = begin_gather(small)
    qkv_state = begin_gather(own)
    x_tail = net.shifted(block_input[:, blocks - WINDOW :], 1).reshape(tail, width)
    small_pieces = end_gather(*small_state)
    qkv_pieces = end_gather(*qkv_state)

    table, score = call(
        params_kernel,
        "params",
        (1,),
        [whole_spec((small_rows, rows))] * shards,
        [table_spec, whole_spec((LANES, width))],
        [shape((16, width), F32), shape((LANES, width), BF)],
        scratch=[pltpu.VMEM((shards, small_rows, rows), F32)],
        prefetch=1,
        micros=1,
    )(info, *small_pieces)

    group = seqs // 2
    normed, normed_tail, importance, mass, stats = call(
        prep_kernel,
        "prep",
        (seqs // group,),
        [by_seq(group * blocks, width), by_seq(group * WINDOW, width), table_spec, whole_spec((LANES, width))],
        [by_seq(group * blocks, width), by_seq(group * WINDOW, width), by_seq(group * blocks, LANES), by_seq(group * blocks, LANES), pl.BlockSpec((group, 8, LANES), lambda s, *_: (s, 0, 0))],
        [shape((tokens, width), BF), shape((tail, width), BF), shape((tokens, LANES), F32), shape((tokens, LANES), F32), shape((seqs, 8, LANES), F32)],
        prefetch=2,
        micros=4,
    )(info, bounds, x_flat, x_tail, table, score)

    def scan_step(state, bit):
        got = net.along(state, bit)
        spec = whole_spec((seqs, 8, LANES))
        return call(
            lambda *refs: scan_kernel(*refs, bit=bit),
            "scan",
            (1,),
            [spec, spec],
            spec,
            shape((seqs, 8, LANES), F32),
            prefetch=1,
            micros=0.5,
        )(info, state, got)

    stats, *qkv_pieces = tie(stats, *qkv_pieces)
    for bit in range(net.seq_bits - 1):
        stats = scan_step(stats, bit)
    qkv_others = [net.chip(piece) for piece in qkv_pieces[1:]]
    w_qkv = call(
        qkv_build_kernel,
        "qkv_build",
        (1,),
        [whole_spec((rows, 3 * width))] + [whole_spec((rows, half_qkv))] * (2 * shards - 2),
        ANY,
        shape((width, 3 * width), BF),
        scratch=[sems(2 * shards)],
        prefetch=1,
        micros=2,
    )(info, qkv_weight, *qkv_pieces[1:], *qkv_others)

    fc_own, down_own, feed_own = [], [], []
    for chunk in range(CHUNKS):
        fc_own.append(jnp.concatenate([fc_weight[:, d * hidden // shards + chunk * deep : d * hidden // shards + (chunk + 1) * deep] for d in range(shards)], axis=1))
        down = down_weight[chunk * deep : (chunk + 1) * deep]
        down_own.append(down)
        first, second = [fc_own[chunk]], [down[k * rows : (k + 1) * rows] for k in range(deep // rows)]
        if chunk == 0:
            first.append(out_weight[:, : width // 2])
            second.append(out_weight[:, width // 2 :])
        feed_own.append(jnp.where(core == 0, jnp.concatenate(first, axis=1), jnp.concatenate(second, axis=1)))
    first_own, _ = tie(feed_own[0], qkv_pieces[-1])
    a_state = begin_gather(first_own)

    def build_feed(chunk, pieces):
        others = [net.chip(piece) for piece in pieces[1:]]
        with_out = chunk == 0
        owns = [fc_own[chunk], down_own[chunk]] + ([out_weight] if with_out else [])
        outs = [shape((width, wide), BF), shape((wide, width), BF)] + ([shape((width, width), BF)] if with_out else [])
        count = 3 + (shards - 1) * (1 + deep // rows + 2)
        return call(
            lambda *refs: feed_build_kernel(*refs, with_out=with_out),
            "feed_build",
            (1,),
            [whole_spec(one.shape) for one in owns] + [whole_spec(pieces[0].shape)] * (2 * shards - 2),
            [ANY] * len(outs),
            outs,
            scratch=[sems(count)],
            prefetch=1,
            micros=2,
        )(info, *owns, *pieces[1:], *others)

    w_qkv, stats = tie(w_qkv, stats)
    col = lambda rows_: pl.BlockSpec((rows_, width), lambda j: (0, j))
    qkv, qkv_tail = call(
        qkv_kernel,
        "qkv",
        (3,),
        [full, whole_spec((tail, width)), col(width), table_spec],
        [col(tokens), pl.BlockSpec((tail, width), lambda j: (0, jnp.maximum(j - 1, 0)))],
        [shape((tokens, 3 * width), BF), shape((tail, 2 * width), BF)],
        micros=6.5,
        limit=24,
    )(normed, normed_tail, w_qkv, table)
    before = scan_step(stats, net.seq_bits - 1)
    qkv, *held = tie(qkv, *a_state[0], *a_state[1])
    a_pieces = end_gather(held[:2], held[2:])

    attended, probs, gates, inverse = call(
        attention_kernel,
        "attention",
        (seqs,),
        [by_seq(blocks, 3 * width), by_seq(WINDOW, 2 * width), by_seq(blocks, LANES), by_seq(blocks, LANES), stat],
        [by_seq(blocks, width), by_seq(blocks, 2 * width), by_seq(WINDOW, width), by_seq(WINDOW, LANES)],
        [shape((tokens, width), BF), shape((tokens, 2 * width), BF), shape((tail, width), BF), shape((tail, LANES), F32)],
        prefetch=2,
        micros=10.5,
        far=(1, 2, 3),
    )(info, bounds, qkv, qkv_tail, importance, mass, before)

    attended, *a_pieces = tie(attended, *a_pieces)
    second_own, _ = tie(feed_own[1], a_pieces[-1])
    b_state = begin_gather(second_own)
    fc_a, down_a, w_out = build_feed(0, a_pieces)

    middle, normed_second = call(
        project_kernel,
        "project",
        (tokens // tile,),
        [by_tile, by_tile, whole_spec((width, width)), table_spec],
        [by_tile, by_tile],
        [shape((tokens, width), F32), shape((tokens, width), BF)],
        micros=3,
        far=(0,),
        far_in=(1,),
    )(attended, x_flat, w_out, table)

    hids, dpres, d_fc_bias = [], [], []

    def feed(chunk, block, fc, down, normed_second):
        square = whole_spec((width, width))
        hid, dpre, d_bias, keep, give = call(
            lambda *refs: feed_kernel(*refs, chunk=chunk, block=block),
            "feed",
            (1,),
            [full, full, pl.BlockSpec((width, width), lambda *_: (0, block)), pl.BlockSpec((width, width), lambda *_: (block, 0)), table_spec],
            [full, full, whole_spec((8, width)), square, square],
            [shape((tokens, width), BF), shape((tokens, width), BF), shape((8, width), F32), shape((width, width), BF), shape((width, width), BF)],
            prefetch=1,
            micros=8,
            limit=36,
            far=(0, 1),
        )(info, normed_second, dy, fc, down, table)
        hids.append(hid)
        dpres.append(dpre)
        d_fc_bias.append(d_bias)
        return keep, net.chip(give)

    def feed_add(blocks_):
        half = (shards // 2, rows, wide)
        square = whole_spec((width, width))
        keep, give = call(
            feed_add_kernel,
            "feed_add",
            (1,),
            [square] * (2 * BLOCKS),
            [whole_spec(half)] * 2,
            [shape(half, BF)] * 2,
            scratch=[pltpu.VMEM((shards, rows, wide), BF)],
            prefetch=1,
            micros=2,
            limit=28,
        )(info, *[keep for keep, _ in blocks_], *[got for _, got in blocks_])
        return Reduction(net, keep, give)

    grads = [feed(0, 0, fc_a, down_a, normed_second)]
    normed_second, *held = tie(normed_second, dpres[0], *b_state[0], *b_state[1])
    b_pieces = end_gather(held[1:3], held[3:])
    grads.append(feed(0, 1, fc_a, down_a, normed_second))
    fc_b, down_b = build_feed(1, b_pieces)
    late = [feed(1, 0, fc_b, down_b, normed_second)]
    red_a = feed_add(grads)
    normed_second, _ = tie(normed_second, dpres[2])
    normed_second = pin(normed_second, red_a)
    red_a.start()
    late.append(feed(1, 1, fc_b, down_b, normed_second))

    half_out = whole_spec((shards, rows, width // 2))
    d_middle, d_attended, keep_out, give_out, sums_second = call(
        middle_kernel,
        "middle",
        (tokens // tile,),
        [by_tile] * (CHUNKS * BLOCKS) + [whole_spec((width, wide))] * CHUNKS + [by_tile, by_tile, by_tile, whole_spec((width, width)), table_spec],
        [by_tile, by_tile, half_out, half_out, whole_spec((8, width))],
        [shape((tokens, width), F32), shape((tokens, width), BF), shape((shards, rows, width // 2), BF), shape((shards, rows, width // 2), BF), shape((8, width), F32)],
        scratch=[pltpu.VMEM((width, width), F32)],
        prefetch=1,
        micros=15,
        limit=32,
        far=(0,),
        far_in=(0, 1, 2, 3, 6, 7, 8),
    )(info, *dpres, fc_a, fc_b, middle, dy, attended, w_out, table)

    red_a.finish()
    out_sum = add(keep_out, net.chip(give_out))
    red_b = feed_add(late)
    red_b.keep = jnp.concatenate([red_b.keep, out_sum[: shards // 2]], axis=2)
    red_b.give = jnp.concatenate([red_b.give, out_sum[shards // 2 :]], axis=2)
    d_attended = pin(d_attended, red_a, red_b)
    red_a.start()
    red_b.start()
    backs = []

    def attention_back(first_pair, count, d_attended):
        span = count * LANES
        return call(
            lambda *refs: attention_back_kernel(*refs, first_pair=first_pair, pairs=count),
            "attention_back",
            (seqs,),
            [by_seq(blocks, 3 * width), by_seq(WINDOW, 2 * width), by_seq(blocks, width), by_seq(blocks, width), by_seq(blocks, 2 * width), by_seq(WINDOW, width), by_seq(WINDOW, LANES), by_seq(blocks, LANES), stat],
            [by_seq(blocks, 3 * span), by_seq(WINDOW, 2 * span), by_seq(blocks, LANES), pl.BlockSpec((1, 1, LANES), lambda s, *_: (s, 0, 0))],
            [shape((tokens, 3 * span), BF), shape((tail, 2 * span), BF), shape((tokens, LANES), F32), shape((seqs, 1, LANES), F32)],
            scratch=[pltpu.VMEM((LANES, LANES), F32)],
            prefetch=2,
            micros=2.5 * count,
            far_in=(4, 5, 6),
        )(info, bounds, qkv, qkv_tail, attended, d_attended, probs, gates, inverse, importance, before)

    def qkv_grad(count, dqkv, d_halo):
        span = count * LANES
        bucket_spec = whole_spec((shards, rows, 3 * span // 2))
        return call(
            qkv_grad_kernel,
            "qkv_grad",
            (1,),
            [full, whole_spec((tail, width)), whole_spec((tokens, 3 * span)), whole_spec((tail, 2 * span))],
            [bucket_spec, bucket_spec, whole_spec((8, span))],
            [shape((shards, rows, 3 * span // 2), BF), shape((shards, rows, 3 * span // 2), BF), shape((8, span), F32)],
            prefetch=1,
            micros=5,
            limit=32,
        )(info, normed, normed_tail, dqkv, d_halo)

    half_shards = shards // 2

    def halved(total):
        return Reduction(net, total[:half_shards], total[half_shards:])

    backs.append(attention_back(*parts[0], d_attended))
    red_a.finish()
    dqkv = pin(backs[0][0], red_a)
    red_a.start()
    keep_qkv, give_qkv, sums_qkv = qkv_grad(parts[0][1], dqkv, backs[0][1])

    got_qkv = net.chip(give_qkv)
    red_b.finish()
    red_a.finish()
    d_halos = [back[1] for back in backs]
    d_halos[0], keep_qkv = tie(d_halos[0], keep_qkv)
    d_halos[0] = pin(d_halos[0], red_a, red_b)
    red_b.start()
    total_all = backs[0][3]
    total_after = jnp.zeros_like(total_all)

    def suffix_step(total_after, total_all, bit):
        got = net.along(total_all, bit)
        earlier = (net.seq >> bit) % 2 == 0
        return jnp.where(earlier, total_after + got, total_after), total_all + got

    total_after, total_all = suffix_step(total_after, total_all, 0)
    d_tail, sums_tail = call(
        lambda *refs: tail_back_kernel(*refs, parts=parts),
        "tail_back",
        (1,),
        [whole_spec(d_halo.shape) for d_halo in d_halos] + [whole_spec((width, 3 * width)), whole_spec((tail, width)), table_spec],
        [whole_spec((tail, width)), whole_spec((8, width))],
        [shape((tail, width), BF), shape((8, width), F32)],
        micros=3,
        limit=32,
    )(*d_halos, w_qkv, x_tail, table)
    red_c = halved(add(keep_qkv, got_qkv))
    d_tail, total_all, total_after = tie(d_tail, total_all, total_after)
    d_tail = pin(d_tail, red_c)
    red_c.start()
    back = net.shifted(d_tail, -1).reshape(seqs, WINDOW, width)
    total_after, total_all = suffix_step(total_after, total_all, 1)
    middle, _ = tie(middle, d_tail)
    block_output = call(
        output_kernel,
        "output",
        (tokens // tile,),
        [by_tile] * (CHUNKS * BLOCKS) + [whole_spec((wide, width))] * CHUNKS + [by_tile, table_spec],
        by_tile,
        shape((tokens, width), BF),
        micros=6.5,
        limit=32,
        far_in=(0, 1, 2, 3, 6),
    )(*hids, down_a, down_b, middle, table)
    red_b.finish()
    total_all, block_output = tie(total_all, block_output)
    total_all = pin(total_all, red_a, red_b)
    for bit in range(2, net.seq_bits):
        total_after, total_all = suffix_step(total_after, total_all, bit)
    red_c.finish()
    total_after = pin(total_after, red_c)
    red_a.start()
    red_b.start()
    red_c.start()

    per_tile = tile // blocks
    by_lane = pl.BlockSpec((tile, LANES), lambda i, *_: (i, 0))
    input_grad, sums_first, d_score = call(
        lambda *refs: input_grad_kernel(*refs, parts=parts),
        "input_grad",
        (tokens // tile,),
        [pl.BlockSpec((tile, 3 * count * LANES), lambda i, *_: (i, 0)) for _, count in parts]
        + [by_lane] * len(parts)
        + [
            whole_spec((width, 3 * width)),
            whole_spec((LANES, width)),
            by_tile,
            by_tile,
            table_spec,
            by_tile,
            pl.BlockSpec((per_tile, WINDOW, width), lambda i, *_: (i, 0, 0)),
            by_lane,
            pl.BlockSpec((per_tile, 8, LANES), lambda i, *_: (i, 0, 0)),
            pl.BlockSpec((per_tile, 1, LANES), lambda i, *_: (i, 0, 0)),
        ],
        [by_tile, whole_spec((8, width)), whole_spec((LANES, width))],
        [shape((tokens, width), F32), shape((8, width), F32), shape((LANES, width), F32)],
        prefetch=2,
        micros=9,
        limit=28,
        far_in=tuple(range(2 * len(parts))) + tuple(2 * len(parts) + k for k in (2, 3, 5, 6, 7)),
    )(info, bounds, *[back_[0] for back_ in backs], *[back_[2] for back_ in backs], w_qkv, score, normed, x_flat, table, d_middle, back, importance, before, total_after)

    spans = [count * LANES for _, count in parts]
    packed = call(
        lambda *refs: small_pack_kernel(*refs, spans=spans),
        "small_pack",
        (1,),
        [whole_spec((8, width))] * 3 + [whole_spec((8, span)) for span in spans] + [whole_spec((8, width))] * (CHUNKS * BLOCKS) + [whole_spec((LANES, width))],
        whole_spec((shards, small_rows, rows)),
        shape((shards, small_rows, rows), F32),
        scratch=[pltpu.VMEM((32, width), F32)],
        prefetch=1,
        micros=1,
    )(info, sums_first, sums_tail, sums_second, sums_qkv, *d_fc_bias, d_score)

    reds = [red_a, red_b, red_c]
    small_steps = [lambda value, k=k: value[: value.shape[0] // 2] + net.across(value[value.shape[0] // 2 :], k) for k in range(net.bits)]
    small_steps += [lambda value, k=k: value + net.along(value, k) for k in range(1, net.seq_bits)]
    small_steps += [lambda value: value + net.chip(value)]
    waiting = list(reds)
    while waiting or small_steps:
        for red in waiting:
            red.finish()
        packed = pin(packed, *waiting)
        waiting = [red for red in waiting if red.todo]
        for red in waiting:
            red.start()
        if small_steps:
            packed = small_steps.pop(0)(packed)
    packed = packed[0]

    def finish(red):
        other = net.chip(red.keep)
        return jnp.where(core == 0, red.keep, other), jnp.where(core == 0, other, red.keep)

    fc_grads, down_grads = zip(finish(red_a), finish(red_b))
    out_grads = [fc_grads[1][:, wide:], down_grads[1][:, wide:]]
    fc_grads, down_grads = [part[:, :wide] for part in fc_grads], [part[:, :wide] for part in down_grads]
    d_out = jnp.concatenate(out_grads, axis=1).astype(F32)
    d_qkv = jnp.concatenate(finish(red_c), axis=1).astype(F32)
    d_fc = jnp.concatenate([part[:, d * deep : (d + 1) * deep] for d in range(shards) for part in fc_grads], axis=1).astype(F32)
    d_down = jnp.concatenate([part[:, k * width : (k + 1) * width] for part in down_grads for k in range(deep // rows)], axis=0).astype(F32)
    base = VECTORS + QV_ROWS
    dg_first, ds_first, dg_second, ds_second, db_out, db_down = (packed[k] for k in range(VECTORS))
    db_qv = packed[VECTORS:base].reshape(-1)
    db_fc = packed[base : base + FC_ROWS].reshape(-1)
    d_score = packed[base + FC_ROWS :].T
    return (
        block_output.reshape(seqs, blocks, width),
        input_grad.reshape(seqs, blocks, width),
        dg_first,
        ds_first,
        d_qkv,
        db_qv,
        d_score,
        d_out,
        db_out,
        dg_second,
        ds_second,
        d_fc,
        db_fc,
        d_down,
        db_down,
    )


def solution(mesh):
    split = P("dp", "seq", None)
    rows = P("dp", None)
    flat = P("dp")
    in_specs = (split, rows, flat, flat, rows, flat, rows, rows, flat, flat, flat, rows, flat, rows, flat, split)
    out_specs = (split, split, flat, flat, rows, flat, rows, rows, flat, flat, flat, rows, flat, rows, flat)
    return jax.shard_map(body, mesh=mesh, in_specs=in_specs, out_specs=out_specs, check_vma=False)
```

```python
import math

import jax
import jax.numpy as jnp
from jax import lax
from jax.experimental import pallas as pl
from jax.experimental.pallas import tpu as pltpu
from jax.sharding import PartitionSpec as P

KTOP = 64
WINDOW = 64
HEAD = 64
LANES = 128
EPSILON = 1e-05
NEGATIVE = -1e30
SCALE = 1.0 / math.sqrt(HEAD)
GELU_A = math.sqrt(2.0 / math.pi)
GELU_B = 0.044715
BF = jnp.bfloat16
F32 = jnp.float32
NN = ((1,), (0,))
NT = ((1,), (1,))
TN = ((0,), (0,))
CHUNKS = 2
BLOCKS = 2
MIB = 2**20
GAIN1, SHIFT1, GAIN2, SHIFT2, BIAS_OUT, BIAS_DOWN, BIAS_QKV, BIAS_FC = 0, 1, 2, 3, 4, 5, 6, 9
VECTORS = 6
QV_ROWS = 2
FC_ROWS = 4


def mm(left, right, dims=NN):
    return lax.dot_general(left, right, (dims, ((), ())), preferred_element_type=F32)


def mm_split(mask, value, dims=NN):
    high = value.astype(BF)
    low = (value - high.astype(F32)).astype(BF)
    return mm(mask, high, dims) + mm(mask, low, dims)


def whole_spec(shape):
    return pl.BlockSpec(shape, lambda *_: (0,) * len(shape))


ANY = pl.BlockSpec(memory_space=pl.ANY)


def call(kernel, name, grid, in_specs, out_specs, out_shape, scratch=(), prefetch=0, micros=1.0, limit=16, alias=None, far=(), far_in=()):
    many = isinstance(out_shape, (list, tuple))
    outs = [pltpu.HBM(one.shape, one.dtype) if k in far else one for k, one in enumerate(out_shape if many else [out_shape])]
    inner = pl.pallas_call(
        kernel,
        grid_spec=pltpu.PrefetchScalarGridSpec(
            num_scalar_prefetch=prefetch,
            grid=grid,
            in_specs=in_specs,
            out_specs=out_specs,
            scratch_shapes=list(scratch),
        ),
        out_shape=outs if many else outs[0],
        input_output_aliases=alias or {},
        compiler_params=pltpu.CompilerParams(vmem_limit_bytes=limit * MIB),
        cost_estimate=pl.CostEstimate(flops=int(micros * 1.1e9), bytes_accessed=1024, transcendentals=0),
        name=name,
    )

    def run(*operands):
        return inner(*[pltpu.with_memory_space_constraint(one, pltpu.HBM) if k - prefetch in far_in else one for k, one in enumerate(operands)])

    return run


def shape(dims, kind):
    return jax.ShapeDtypeStruct(dims, kind)


def iota(dims, axis):
    return lax.broadcasted_iota(jnp.int32, dims, axis)


def segment(places, first, second):
    return (places >= first).astype(jnp.int32) + (places >= second).astype(jnp.int32)


def normalise(values):
    average = jnp.mean(values, axis=-1, keepdims=True)
    centred = values - average
    variance = jnp.mean(centred * centred, axis=-1, keepdims=True)
    scale = lax.rsqrt(variance + EPSILON)
    return centred * scale, scale


def norm_back(d_norm, unit, scale, gain):
    weighted = d_norm * gain
    return scale * (
        weighted
        - jnp.mean(weighted, axis=-1, keepdims=True)
        - unit * jnp.mean(weighted * unit, axis=-1, keepdims=True)
    )


def bit_orders(count):
    bits = count.bit_length() - 1
    straight = list(range(bits))
    half = bits // 2
    return straight, straight[half:] + straight[:half]


def crossed(count, core, index, first_high):
    order = bit_orders(count)[core]
    mask = 0
    for step, bit in enumerate(order):
        place = len(order) - 1 - step if first_high else step
        mask |= ((index >> place) & 1) << bit
    return mask


def rank(count, core, far, first_high):
    order = bit_orders(count)[core]
    index = 0
    for step, bit in enumerate(order):
        place = len(order) - 1 - step if first_high else step
        index |= ((far >> bit) & 1) << place
    return index


def by_core(core, even, odd):
    return jnp.where(core == 0, even, odd)


def copy_all(copies, sems):
    started = [pltpu.make_async_copy(source, target, sems.at[k]) for k, (source, target) in enumerate(copies)]
    for copy in started:
        copy.start()
    for copy in started:
        copy.wait()


def start_kernel(info, *refs, names):
    vectors = refs[:names]
    score_ref, own_ref, x_ref, small_ref, own_out, tail_ref = refs[names:]
    rows = small_ref.shape[1]
    row = 0
    for ref in vectors:
        for k in range(ref.shape[0] // rows):
            small_ref[row : row + 1] = ref[k * rows : (k + 1) * rows].reshape(1, rows)
            row += 1
    small_ref[row:] = score_ref[...].T
    own_out[...] = own_ref[...]
    for s in range(x_ref.shape[0]):
        tail_ref[s * WINDOW : (s + 1) * WINDOW] = x_ref[s]


def feed_pack_kernel(info, fc_ref, down_ref, weight_ref, *outs):
    fc_refs, own_refs = outs[:CHUNKS], outs[CHUNKS:]
    rows, hidden = fc_ref.shape
    width = down_ref.shape[1]
    wide = fc_refs[0].shape[1]
    deep = down_ref.shape[0] // CHUNKS
    shards = hidden // (deep * CHUNKS)
    for chunk in range(CHUNKS):
        for shard in range(shards):
            begin = (shard * CHUNKS + chunk) * deep
            fc_refs[chunk][:, shard * deep : (shard + 1) * deep] = fc_ref[:, begin : begin + deep]

        @pl.when(info[1] == 0)
        def _():
            own_refs[chunk][:, :wide] = fc_refs[chunk][...]
            if chunk == 0:
                own_refs[chunk][:, wide:] = weight_ref[:, : width // 2]

        @pl.when(info[1] != 0)
        def _():
            for part in range(deep // rows):
                begin = chunk * deep + part * rows
                own_refs[chunk][:, part * width : (part + 1) * width] = down_ref[begin : begin + rows]
            if chunk == 0:
                own_refs[chunk][:, wide:] = weight_ref[:, width // 2 :]


def end_kernel(packed_ref, *outs):
    row = 0
    rows = packed_ref.shape[1]
    for ref in outs[:-1]:
        for k in range(ref.shape[0] // rows):
            ref[k * rows : (k + 1) * rows] = packed_ref[row : row + 1].reshape(rows)
            row += 1
    outs[-1][...] = packed_ref[row:].T


def params_kernel(info, *refs):
    pieces, (table_ref, score_ref, held) = refs[:-3], refs[-3:]
    shards = len(pieces)
    core, me = info[1], info[2]
    for k, piece in enumerate(pieces):
        held[k] = piece[...].astype(F32)

    def at(shard):
        far = shard ^ me
        index = jnp.int32(0)
        for k in range(shards):
            mask = by_core(core, crossed(shards, 0, k, False), crossed(shards, 1, k, False))
            index = jnp.where(mask == far, k, index)
        return held[index]

    parts = [at(shard) for shard in range(shards)]

    def line(shard_range, rows):
        return jnp.concatenate([parts[s][r : r + 1] for s in shard_range for r in rows], axis=1)

    table_ref[...] = jnp.zeros_like(table_ref)
    for r in range(VECTORS):
        table_ref[r : r + 1] = line(range(shards), [r])
    qv = list(range(VECTORS, VECTORS + QV_ROWS))
    table_ref[BIAS_QKV : BIAS_QKV + 1] = line(range(shards // 2), qv)
    table_ref[BIAS_QKV + 2 : BIAS_QKV + 3] = line(range(shards // 2, shards), qv)
    base = VECTORS + QV_ROWS
    per_block = shards // BLOCKS
    per_chunk = FC_ROWS // CHUNKS
    for chunk in range(CHUNKS):
        for block in range(BLOCKS):
            rows = [base + chunk * per_chunk + k for k in range(per_chunk)]
            row = BIAS_FC + chunk * BLOCKS + block
            table_ref[row : row + 1] = line(range(block * per_block, (block + 1) * per_block), rows)
    base += FC_ROWS
    heads = parts[0].shape[0] - base
    score_ref[...] = jnp.zeros_like(score_ref)
    for head in range(heads):
        score_ref[head : head + 1] = line(range(shards), [base + head]).astype(BF)


def prep_kernel(info, bounds, x_ref, tail_ref, table_ref, score_ref, normed_ref, tail_out_ref, imp_ref, mass_ref, stat_ref):
    seqs = stat_ref.shape[0]
    blocks = x_ref.shape[0] // seqs
    gain = table_ref[GAIN1 : GAIN1 + 1]
    shift = table_ref[SHIFT1 : SHIFT1 + 1]
    start = info[0]
    rows = iota((blocks, blocks), 0)
    cols = iota((blocks, blocks), 1)
    for k in range(seqs):
        rs = slice(k * blocks, (k + 1) * blocks)
        ts = slice(k * WINDOW, (k + 1) * WINDOW)
        normed = (normalise(x_ref[rs].astype(F32))[0] * gain + shift).astype(BF)
        normed_ref[rs] = normed
        tail_out_ref[ts] = (normalise(tail_ref[ts].astype(F32))[0] * gain + shift).astype(BF)
        importance = mm(normed, score_ref[...], NT)
        imp_ref[rs] = importance
        s = pl.program_id(0) * seqs + k
        first, second = bounds[s, 0], bounds[s, 1]
        lower = (cols <= rows) & (segment(start + rows, first, second) == segment(start + cols, first, second))
        peak = jnp.max(importance, axis=0, keepdims=True)
        mass = mm_split(lower.astype(BF), jnp.exp(importance - peak))
        mass_ref[rs] = mass
        stat_ref[k, 0:1, :] = peak
        stat_ref[k, 1:2, :] = mass[blocks - 1 :, :]
        stat_ref[k, 2:3, :] = jnp.full_like(peak, NEGATIVE)
        stat_ref[k, 3:4, :] = jnp.zeros_like(peak)
        stat_ref[k, 4:5, :] = peak


def scan_kernel(info, mine_ref, *refs, masks):
    got_refs, out_ref = refs[:-1], refs[-1]

    def joined(peak, total, got):
        top = jnp.maximum(peak, got[:, 0:1])
        return top, total * jnp.exp(peak - top) + got[:, 1:2] * jnp.exp(got[:, 0:1] - top)

    out_ref[...] = mine_ref[...]
    for mask, got in zip(masks, got_refs):
        peak, total = joined(out_ref[:, 0:1], out_ref[:, 1:2], got)
        out_ref[:, 0:1] = peak
        out_ref[:, 1:2] = total

        @pl.when((info[3] ^ mask) < info[3])
        def _():
            peak, total = joined(out_ref[:, 2:3], out_ref[:, 3:4], got)
            out_ref[:, 2:3] = peak
            out_ref[:, 3:4] = total


def qkv_build_kernel(info, *refs):
    own, pieces, out, sems = refs[0], refs[1:-2], refs[-2], refs[-1]
    shards = len(pieces) // 2 + 1
    rows, width = own.shape
    half = width // 2
    me = info[2]

    def build(core):
        copies = [(own, out.at[pl.ds(pl.multiple_of(me * rows, 16), rows)])]
        for k in range(1, shards):
            for side, group in ((core, 0), (1 - core, shards - 1)):
                at = pl.multiple_of((me ^ crossed(shards, side, k, False)) * rows, 16)
                target = out.at[pl.ds(at, rows), side * half : (side + 1) * half]
                copies.append((pieces[group + k - 1], target))
        copy_all(copies, sems)

    @pl.when(info[1] == 0)
    def _():
        build(0)

    @pl.when(info[1] != 0)
    def _():
        build(1)


def feed_build_kernel(info, *refs, with_out):
    if with_out:
        own_fc, own_down, own_out = refs[:3]
        pieces, (fc_ref, down_ref, out_ref, sems) = refs[3:-4], refs[-4:]
    else:
        own_fc, own_down = refs[:2]
        pieces, (fc_ref, down_ref, sems) = refs[2:-3], refs[-3:]
    shards = len(pieces) // 2 + 1
    rows, wide = own_fc.shape
    deep, width = own_down.shape
    split = width // 2
    me = info[2]

    def build(core):
        at_rows = lambda shard: pl.multiple_of(shard * rows, 16)
        copies = [
            (own_fc, fc_ref.at[pl.ds(at_rows(me), rows)]),
            (own_down, down_ref.at[pl.ds(pl.multiple_of(me * deep, 16), deep)]),
        ]
        if with_out:
            copies.append((own_out, out_ref.at[pl.ds(at_rows(me), rows)]))
        for k in range(1, shards):
            for side, group in ((core, 0), (1 - core, shards - 1)):
                piece = pieces[group + k - 1]
                shard = me ^ crossed(shards, side, k, False)
                if side == 0:
                    copies.append((piece.at[:, :wide], fc_ref.at[pl.ds(at_rows(shard), rows)]))
                else:
                    for part in range(deep // rows):
                        at = pl.multiple_of(shard * deep + part * rows, 16)
                        copies.append((piece.at[:, part * width : (part + 1) * width], down_ref.at[pl.ds(at, rows)]))
                if with_out:
                    copies.append((piece.at[:, wide:], out_ref.at[pl.ds(at_rows(shard), rows), side * split : (side + 1) * split]))
        copy_all(copies, sems)

    @pl.when(info[1] == 0)
    def _():
        build(0)

    @pl.when(info[1] != 0)
    def _():
        build(1)


def qkv_kernel(normed_ref, tail_ref, weight_ref, table_ref, out_ref, tail_out_ref):
    j = pl.program_id(0)
    weight = weight_ref[...]
    bias = table_ref[pl.ds(BIAS_QKV + j, 1)]
    factor = jnp.where(j == 0, SCALE, 1.0)
    out_ref[...] = ((mm(normed_ref[...], weight) + bias).astype(BF).astype(F32) * factor).astype(BF)

    @pl.when(j > 0)
    def _():
        tail_out_ref[...] = (mm(tail_ref[...], weight) + bias).astype(BF)


def lane_masks():
    first = iota((1, LANES), 1) < HEAD
    return first.astype(BF), (~first).astype(BF)


def grouped(part, keep_first, keep_second):
    return jnp.concatenate([part * keep_first, part * keep_second], axis=0)


def tile_masks(start, half, first, second):
    dims = (WINDOW, LANES)
    row = iota(dims, 0)
    col = iota(dims, 1) & (HEAD - 1)
    base = start + WINDOW * half
    mine = segment(base + row, first, second)
    far = segment(base - WINDOW + col, first, second) == mine
    near = (col <= row) & (segment(base + col, first, second) == mine)
    if half == 0:
        far = far & (col > row) & (base - WINDOW + col >= 0)
    return far, near, col <= row


def spread(columns, pair, rows):
    left = columns[:, 2 * pair : 2 * pair + 1]
    right = columns[:, 2 * pair + 1 : 2 * pair + 2]
    return jnp.where(iota((rows, LANES), 1) < HEAD, left, right)


def key_groups(qkv_ref, halo_ref, width, pair, keep_first, keep_second, one_group):
    at = slice(pair * LANES, (pair + 1) * LANES)
    ks = slice(width + pair * LANES, width + (pair + 1) * LANES)
    vs = slice(2 * width + pair * LANES, 2 * width + (pair + 1) * LANES)
    keys = [grouped(part, keep_first, keep_second) for part in (halo_ref[:, at], qkv_ref[:WINDOW, ks], qkv_ref[WINDOW:, ks])]
    values = [
        jnp.concatenate([grouped(part, keep_first, keep_second), one_group], axis=1)
        for part in (halo_ref[:, ks], qkv_ref[:WINDOW, vs], qkv_ref[WINDOW:, vs])
    ]
    return keys, values


def attention_kernel(info, bounds, qkv_ref, halo_ref, imp_ref, mass_ref, before_ref, att_ref, probs_ref, sig_ref, inv_ref):
    s = pl.program_id(0)
    blocks, width = att_ref.shape
    start = info[0]
    first, second = bounds[s, 0], bounds[s, 1]
    pairs = width // LANES
    peak = before_ref[0, 4:5, :]
    carry_peak = before_ref[0, 2:3, :]
    carry_total = before_ref[0, 3:4, :]
    top = before_ref[0, 0:1, :]
    joined = jnp.maximum(peak, carry_peak)
    place = start + iota((blocks, LANES), 0)
    continues = segment(place, first, second) == segment(jnp.full((1, LANES), start - 1, jnp.int32), first, second)
    mass = mass_ref[...] * jnp.exp(peak - joined) + jnp.where(
        continues, carry_total * jnp.exp(carry_peak - joined), 0.0
    )
    threshold = joined + jnp.log(mass) - math.log(KTOP)
    late = threshold[WINDOW:]
    inv_ref[...] = 1.0 / (mass[WINDOW:] * jnp.exp(joined - top))
    imp_rows = imp_ref[...].T
    keep_first, keep_second = lane_masks()
    one_group = grouped(jnp.ones((WINDOW, LANES), BF), keep_first, keep_second)
    masks = [tile_masks(start, half, first, second) for half in (0, 1)]
    lane = iota((WINDOW, LANES), 1) < HEAD
    for pair in range(pairs):
        ls = slice(pair * LANES, (pair + 1) * LANES)
        keys, values = key_groups(qkv_ref, halo_ref, width, pair, keep_first, keep_second, one_group)
        for half in (0, 1):
            rs = slice(half * WINDOW, (half + 1) * WINDOW)
            far_ok, near_ok, gated = masks[half]
            logits = mm(qkv_ref[rs, ls], jnp.concatenate(keys[half : half + 2], axis=0), NT)
            far, near = logits[:, :LANES], logits[:, LANES:]
            if half == 1:
                row = jnp.concatenate(
                    [imp_rows[2 * pair : 2 * pair + 1, :WINDOW], imp_rows[2 * pair + 1 : 2 * pair + 2, :WINDOW]], axis=1
                )
                gap = spread(late, pair, WINDOW) - row
                small = jnp.exp(-jnp.abs(gap))
                soft = jnp.maximum(gap, 0.0) + jnp.log(1.0 + small)
                sig_ref[:, ls] = (jnp.where(gap >= 0, 1.0, small) / (1.0 + small)).astype(BF)
                far = jnp.where(gated, far - soft, far)
            far = jnp.where(far_ok, far, NEGATIVE)
            near = jnp.where(near_ok, near, NEGATIVE)
            best = jnp.maximum(far, near)
            best_first = jnp.max(jnp.where(lane, best, NEGATIVE), axis=1, keepdims=True)
            best_second = jnp.max(jnp.where(lane, NEGATIVE, best), axis=1, keepdims=True)
            best = jnp.where(lane, best_first, best_second)
            far = jnp.exp(far - best)
            near = jnp.exp(near - best)
            weights = jnp.concatenate([far.astype(BF), near.astype(BF)], axis=1)
            mixed = mm(weights, jnp.concatenate(values[half : half + 2], axis=0))
            inverse = 1.0 / mixed[:, LANES:]
            att_ref[rs, ls] = (mixed[:, :LANES] * inverse).astype(BF)
            probs_ref[rs, 2 * pair * LANES : (2 * pair + 1) * LANES] = (far * inverse).astype(BF)
            probs_ref[rs, (2 * pair + 1) * LANES : (2 * pair + 2) * LANES] = (near * inverse).astype(BF)


def project_kernel(att_ref, x_ref, weight_ref, table_ref, middle_ref, second_ref):
    middle = x_ref[...].astype(F32) + mm(att_ref[...], weight_ref[...]) + table_ref[BIAS_OUT : BIAS_OUT + 1]
    middle_ref[...] = middle
    second_ref[...] = (normalise(middle)[0] * table_ref[GAIN2 : GAIN2 + 1] + table_ref[SHIFT2 : SHIFT2 + 1]).astype(BF)


def feed_kernel(info, sec_ref, dy_ref, fc_ref, down_ref, table_ref, hid_ref, dpre_ref, db_ref, keep_ref, give_ref, *, chunk, block):
    fc = fc_ref[...]
    down = down_ref[...]
    row = BIAS_FC + chunk * BLOCKS + block
    pre = mm(sec_ref[...], fc) + table_ref[row : row + 1]
    d_hidden = mm(dy_ref[...], down, NT)
    square = pre * pre
    tanh = jnp.tanh(pre * (GELU_A + GELU_A * GELU_B * square))
    half = 0.5 + 0.5 * tanh
    hidden = (pre * half).astype(BF)
    slope = half + pre * (0.5 * GELU_A + 1.5 * GELU_A * GELU_B * square) * (1.0 - tanh * tanh)
    d_pre = d_hidden * slope
    d_low = d_pre.astype(BF)
    hid_ref[...] = hidden
    dpre_ref[...] = d_low
    db_ref[...] = jnp.broadcast_to(jnp.sum(d_pre, axis=0, keepdims=True), db_ref.shape)
    d_down = mm(hidden, dy_ref[...], TN).astype(BF)
    d_fc = mm(sec_ref[...], d_low, TN).astype(BF)

    @pl.when(info[1] == 0)
    def _():
        keep_ref[...] = d_fc
        give_ref[...] = d_down

    @pl.when(info[1] != 0)
    def _():
        keep_ref[...] = d_down
        give_ref[...] = d_fc


def feed_add_kernel(info, *refs):
    keeps, gots, (keep_ref, give_ref, held) = refs[:BLOCKS], refs[BLOCKS : 2 * BLOCKS], refs[2 * BLOCKS :]
    shards, rows, wide = held.shape
    width = keeps[0].shape[0]
    me = info[2]
    per_block = shards // BLOCKS
    deep = width // per_block

    def put(core):
        for block in range(BLOCKS):
            total = add(keeps[block][...], gots[block][...])
            if core == 0:
                for shard in range(shards):
                    held[ranked(shards, 0, me ^ shard), :, block * width : (block + 1) * width] = total[shard * rows : (shard + 1) * rows]
            else:
                for k in range(per_block):
                    place = ranked(shards, 1, me ^ (block * per_block + k))
                    for part in range(deep // rows):
                        begin = k * deep + part * rows
                        held[place, :, part * width : (part + 1) * width] = total[begin : begin + rows]

    @pl.when(info[1] == 0)
    def _():
        put(0)

    @pl.when(info[1] != 0)
    def _():
        put(1)

    half = shards // 2
    keep_ref[...] = held[:half]
    give_ref[...] = held[half:]


def ranked(shards, core, far):
    order = bit_orders(shards)[core]
    index = jnp.int32(0)
    for step, bit in enumerate(order):
        index = index | (((far >> bit) & 1) << (len(order) - 1 - step))
    return index


def middle_kernel(*refs):
    count = CHUNKS * BLOCKS
    dpre_refs = refs[:count]
    fc_refs = refs[count : count + CHUNKS]
    middle_ref, dy_ref, table_ref, dmid_ref, branch_ref, sums_ref = refs[count + CHUNKS :]
    width = middle_ref.shape[1]
    part_rows = middle_ref.shape[0] // 2
    totals = [0.0] * 4
    for part in range(2):
        rs = slice(part * part_rows, (part + 1) * part_rows)
        d_norm = None
        for k in range(count):
            piece = mm(dpre_refs[k][rs], fc_refs[k // BLOCKS][:, (k % BLOCKS) * width : (k % BLOCKS + 1) * width], NT)
            d_norm = piece if d_norm is None else d_norm + piece
        unit, scale = normalise(middle_ref[rs])
        dy = dy_ref[rs].astype(F32)
        d_middle = dy + norm_back(d_norm, unit, scale, table_ref[GAIN2 : GAIN2 + 1])
        dmid_ref[rs] = d_middle
        branch = d_middle.astype(BF)
        branch_ref[rs] = branch
        for k, value in enumerate((d_norm * unit, d_norm, branch.astype(F32), dy)):
            totals[k] = totals[k] + jnp.sum(value, axis=0, keepdims=True)

    @pl.when(pl.program_id(0) == 0)
    def _():
        for k in range(4):
            sums_ref[k : k + 1] = totals[k]

    @pl.when(pl.program_id(0) > 0)
    def _():
        for k in range(4):
            sums_ref[k : k + 1] += totals[k]


def branch_kernel(info, branch_ref, att_ref, weight_ref, datt_ref, keep_ref, give_ref):
    shards, rows, split = keep_ref.shape
    store_halves(info, mm(att_ref[...], branch_ref[...], TN), keep_ref, give_ref, shards, rows, split)
    datt_ref[...] = mm(branch_ref[...], weight_ref[...], NT).astype(BF)


def store_halves(info, total, keep_ref, give_ref, shards, rows, split):
    me = info[2]

    def store(side, to):
        for shard in range(shards):
            value = total[shard * rows : (shard + 1) * rows, side * split : (side + 1) * split]
            to[ranked(shards, side, me ^ shard)] = value.astype(BF)

    @pl.when(info[1] == 0)
    def _():
        store(0, keep_ref)
        store(1, give_ref)

    @pl.when(info[1] != 0)
    def _():
        store(1, keep_ref)
        store(0, give_ref)


def attention_back_kernel(info, bounds, qkv_ref, halo_ref, att_ref, datt_ref, probs_ref, sig_ref, inv_ref, imp_ref, before_ref, dqkv_ref, dhalo_ref, dimp_ref, total_ref, rows_scratch, *, first_seq, pairs):
    s = first_seq + pl.program_id(0)
    blocks, width = att_ref.shape
    start = info[0]
    first, second = bounds[s, 0], bounds[s, 1]
    keep_first, keep_second = lane_masks()
    one_group = grouped(jnp.ones((WINDOW, LANES), BF), keep_first, keep_second)
    lane = iota((WINDOW, LANES), 1) < HEAD
    gated = (iota((WINDOW, LANES), 1) & (HEAD - 1)) <= iota((WINDOW, LANES), 0)
    head_lane = iota((LANES, LANES), 1)
    head_row = iota((LANES, LANES), 0)
    d_threshold = jnp.zeros((WINDOW, LANES), F32)
    rows_scratch[...] = jnp.zeros_like(rows_scratch)
    wide = pairs * LANES
    for k in range(pairs):
        pair = k
        ls = slice(pair * LANES, (pair + 1) * LANES)
        keys, values = key_groups(qkv_ref, halo_ref, width, pair, keep_first, keep_second, one_group)
        far_keys, near_keys, far_values, near_values = [], [], [], []
        for half in (0, 1):
            rs = slice(half * WINDOW, (half + 1) * WINDOW)
            d_out = datt_ref[rs, ls]
            product = (-(d_out.astype(F32) * att_ref[rs, ls].astype(F32))).astype(BF)
            left = jnp.concatenate([d_out, product], axis=1)
            centred = mm(left, jnp.concatenate(values[half : half + 2], axis=0), NT)
            probs = probs_ref[rs, 2 * pair * LANES : (2 * pair + 2) * LANES]
            d_logits = probs.astype(F32) * centred
            low = d_logits.astype(BF)
            dqkv_ref[rs, k * LANES : (k + 1) * LANES] = (mm(low, jnp.concatenate(keys[half : half + 2], axis=0)) * SCALE).astype(BF)
            d_keys = mm(low, qkv_ref[rs, ls], TN)
            d_values = mm(probs, d_out, TN)
            far_keys.append(jnp.where(lane, d_keys[:WINDOW], d_keys[WINDOW : 2 * WINDOW]))
            near_keys.append(jnp.where(lane, d_keys[2 * WINDOW : 3 * WINDOW], d_keys[3 * WINDOW :]))
            far_values.append(jnp.where(lane, d_values[:WINDOW], d_values[WINDOW : 2 * WINDOW]))
            near_values.append(jnp.where(lane, d_values[2 * WINDOW : 3 * WINDOW], d_values[3 * WINDOW :]))
            if half == 1:
                gate = jnp.where(gated, d_logits[:, :LANES] * sig_ref[:, ls].astype(F32), 0.0)
                rows_scratch[pair : pair + 1, :] = jnp.sum(gate, axis=0, keepdims=True)
                chosen = (head_lane == 2 * pair + (head_row >= HEAD).astype(jnp.int32)).astype(BF)
                d_threshold = d_threshold - mm(gate.astype(BF), chosen)
        ks = slice(wide + k * LANES, wide + (k + 1) * LANES)
        vs = slice(2 * wide + k * LANES, 2 * wide + (k + 1) * LANES)
        dhalo_ref[:, ks] = far_keys[0].astype(BF)
        dhalo_ref[:, vs] = far_values[0].astype(BF)
        dqkv_ref[:WINDOW, ks] = (near_keys[0] + far_keys[1]).astype(BF)
        dqkv_ref[WINDOW:, ks] = near_keys[1].astype(BF)
        dqkv_ref[:WINDOW, vs] = (near_values[0] + far_values[1]).astype(BF)
        dqkv_ref[WINDOW:, vs] = near_values[1].astype(BF)
    dhalo_ref[:, :wide] = jnp.zeros((WINDOW, wide), BF)
    weighted = d_threshold * inv_ref[...]
    row = iota((blocks, WINDOW), 0)
    col = iota((blocks, WINDOW), 1) + WINDOW
    after = (col >= row) & (segment(start + row, first, second) == segment(start + col, first, second))
    later = mm_split(after.astype(BF), weighted)
    total_ref[0, 0:1, :] = later[0:1]
    turned = rows_scratch[...].T
    pick_first = (head_lane == 2 * head_row).astype(BF)
    pick_second = (head_lane == 2 * head_row + 1).astype(BF)

    def pick(values, chosen):
        high = values.astype(BF)
        return mm(high, chosen) + mm((values - high.astype(F32)).astype(BF), chosen)

    direct = pick(turned[:HEAD], pick_first) + pick(turned[HEAD:], pick_second)
    local = jnp.exp(imp_ref[...] - before_ref[0, 0:1, :]) * later
    dimp_ref[:WINDOW] = local[:WINDOW] + direct
    dimp_ref[WINDOW:] = local[WINDOW:]


def tail_back_kernel(*refs):
    dhalo_refs = refs[:-5]
    weight_ref, x_ref, table_ref, out_ref, sums_ref = refs[-5:]
    width = x_ref.shape[1]
    begin = 0
    totals = [0.0, 0.0]
    for dhalo_ref in dhalo_refs:
        rs = slice(begin, begin + dhalo_ref.shape[0])
        begin += dhalo_ref.shape[0]
        d_norm = mm(dhalo_ref[:, width:], weight_ref[:, width:], NT)
        unit, scale = normalise(x_ref[rs].astype(F32))
        out_ref[rs] = norm_back(d_norm, unit, scale, table_ref[GAIN1 : GAIN1 + 1]).astype(BF)
        for k, value in enumerate((d_norm * unit, d_norm)):
            totals[k] = totals[k] + jnp.sum(value, axis=0, keepdims=True)
    for k in range(2):
        sums_ref[k : k + 1] = totals[k]


def qkv_grad_kernel(info, normed_ref, tail_ref, *refs, groups, mine):
    dqkv_refs, dhalo_refs, (out_ref, sums_ref) = refs[:groups], refs[groups : 2 * groups], refs[2 * groups :]
    shards, rows, split = out_ref.shape
    me = info[2]
    owner = info[1] if mine else 1 - info[1]
    total, sums = 0.0, 0.0
    for left_ref, right_refs in ((normed_ref, dqkv_refs), (tail_ref, dhalo_refs)):
        begin = 0
        for right_ref in right_refs:
            rs = slice(begin, begin + right_ref.shape[0])
            begin += right_ref.shape[0]
            total = total + mm(left_ref[rs], right_ref[...], TN)
            sums = sums + jnp.sum(right_ref[...].astype(F32), axis=0, keepdims=True)
    sums_ref[0:1] = sums
    for shard in range(shards):
        far = me ^ shard
        place = jnp.where(owner == 0, ranked(shards, 0, far), ranked(shards, 1, far))
        out_ref[place] = total[shard * rows : (shard + 1) * rows].astype(BF)


def input_grad_kernel(info, bounds, *refs, groups):
    dqkv_refs, dimp_refs = refs[:groups], refs[groups : 2 * groups]
    weight_ref, score_ref, normed_ref, x_ref, table_ref, dmid_ref, back_ref, imp_ref, before_ref, after_ref, out_ref, sums_ref, score_out_ref = refs[2 * groups :]
    i = pl.program_id(0)
    per_group = pl.num_programs(0) // groups
    seqs = back_ref.shape[0]
    blocks = x_ref.shape[0] // seqs
    start = info[0]

    def chosen(refs):
        value = refs[0][...]
        for k in range(1, groups):
            value = jnp.where(i >= k * per_group, refs[k][...], value)
        return value

    dqkv, d_local = chosen(dqkv_refs), chosen(dimp_refs)
    d_imps = []
    for s in range(seqs):
        rs = slice(s * blocks, (s + 1) * blocks)
        first, second = bounds[i * seqs + s, 0], bounds[i * seqs + s, 1]
        place = start + iota((blocks, LANES), 0)
        onward = segment(place, first, second) == segment(jnp.full((1, LANES), start + blocks, jnp.int32), first, second)
        extra = jnp.exp(imp_ref[rs] - before_ref[s, 0:1, :]) * after_ref[s, 0:1, :]
        d_imps.append(d_local[rs] + jnp.where(onward, extra, 0.0))
    d_imp = jnp.concatenate(d_imps, axis=0).astype(BF)
    d_norm = mm(dqkv, weight_ref[...], NT) + mm(d_imp, score_ref[...])
    unit, scale = normalise(x_ref[...].astype(F32))
    d_value = norm_back(d_norm, unit, scale, table_ref[GAIN1 : GAIN1 + 1]) + dmid_ref[...]
    for s in range(seqs):
        rs = slice(s * blocks, s * blocks + WINDOW)
        out_ref[rs] = d_value[rs]
        rs = slice(s * blocks + WINDOW, (s + 1) * blocks)
        out_ref[rs] = d_value[rs] + back_ref[s].astype(F32)
    sums = [jnp.sum(value, axis=0, keepdims=True) for value in (d_norm * unit, d_norm)]
    score = mm(d_imp, normed_ref[...], TN)

    @pl.when(i == 0)
    def _():
        score_out_ref[...] = score
        for k in range(2):
            sums_ref[k : k + 1] = sums[k]

    @pl.when(i > 0)
    def _():
        score_out_ref[...] += score
        for k in range(2):
            sums_ref[k : k + 1] += sums[k]


def output_kernel(*refs):
    count = CHUNKS * BLOCKS
    hid_refs = refs[:count]
    down_refs = refs[count : count + CHUNKS]
    middle_ref, table_ref, out_ref = refs[count + CHUNKS :]
    width = middle_ref.shape[1]
    total = middle_ref[...] + table_ref[BIAS_DOWN : BIAS_DOWN + 1]
    for k in range(count):
        total = total + mm(hid_refs[k][...], down_refs[k // BLOCKS][(k % BLOCKS) * width : (k % BLOCKS + 1) * width])
    out_ref[...] = total.astype(BF)


def small_pack_kernel(info, first_ref, tail_ref, second_ref, kept_ref, given_ref, *refs):
    bias_refs = refs[: CHUNKS * BLOCKS]
    score_ref, out_ref, whole = refs[CHUNKS * BLOCKS :]
    shards, count, rows = out_ref.shape
    me = info[2]
    whole[0:2] = first_ref[0:2] + tail_ref[0:2]
    whole[2:VECTORS] = second_ref[0 : VECTORS - 2]
    width = whole.shape[1]
    even = info[1] == 0
    whole[VECTORS : VECTORS + 1] = jnp.where(even, kept_ref[0:1, :width], given_ref[0:1, :width])
    whole[VECTORS + 1 : VECTORS + 2] = jnp.where(even, given_ref[0:1, width // 2 :], kept_ref[0:1, width // 2 :])
    base = VECTORS + 2
    for k in range(CHUNKS * BLOCKS):
        whole[base + k : base + k + 1] = bias_refs[k][0:1]
    heads = count - VECTORS - QV_ROWS - FC_ROWS
    whole[base + CHUNKS * BLOCKS : base + CHUNKS * BLOCKS + heads] = score_ref[0:heads]
    per_block = shards // BLOCKS
    per_chunk = FC_ROWS // CHUNKS
    for shard in range(shards):
        at = slice(shard * rows, (shard + 1) * rows)
        lines = [whole[0:VECTORS, at]]
        row = VECTORS + shard // (shards // 2)
        for k in range(QV_ROWS):
            begin = (shard % (shards // 2)) * QV_ROWS * rows + k * rows
            lines.append(whole[row : row + 1, begin : begin + rows])
        for chunk in range(CHUNKS):
            row = base + chunk * BLOCKS + shard // per_block
            for k in range(per_chunk):
                begin = (shard % per_block) * per_chunk * rows + k * rows
                lines.append(whole[row : row + 1, begin : begin + rows])
        lines.append(whole[base + CHUNKS * BLOCKS : base + CHUNKS * BLOCKS + heads, at])
        place = jnp.where(info[1] == 0, ranked(shards, 0, me ^ shard), ranked(shards, 1, me ^ shard))
        out_ref[place] = jnp.concatenate(lines, axis=0)


def add(left, right):
    return (left.astype(F32) + right.astype(F32)).astype(BF)


def combine(peak_a, total_a, peak_b, total_b):
    joined = jnp.maximum(peak_a, peak_b)
    return joined, total_a * jnp.exp(peak_a - joined) + total_b * jnp.exp(peak_b - joined)


def tie(*values):
    return lax.optimization_barrier(values)


class Net:
    def __init__(self):
        self.n_seq = lax.axis_size("seq")
        self.n_dp = lax.axis_size("dp")
        self.seq = lax.axis_index("seq")
        self.dp = lax.axis_index("dp")
        self.core = self.seq % 2
        self.orders = bit_orders(self.n_dp)
        self.bits = len(self.orders[0])
        self.seq_bits = self.n_seq.bit_length() - 1

    def send(self, value, target):
        pairs = []
        for s in range(self.n_seq):
            for d in range(self.n_dp):
                goal = target(s, d)
                if 0 <= goal[0] < self.n_seq:
                    pairs.append((s * self.n_dp + d, goal[0] * self.n_dp + goal[1]))
        return lax.ppermute(value, ("seq", "dp"), pairs)

    def across(self, value, step):
        return self.send(value, lambda s, d: (s, d ^ (1 << self.orders[s % 2][step])))

    def chip(self, value):
        return self.send(value, lambda s, d: (s ^ 1, d))

    def along(self, value, bit):
        return self.send(value, lambda s, d: (s ^ (1 << bit), d))

    def masked(self, value, mask):
        return self.send(value, lambda s, d: (s ^ mask, d))

    def shifted(self, value, by):
        return self.send(value, lambda s, d: (s + by, d))

    def gather_step(self, pieces, step):
        return pieces + [self.across(piece, step) for piece in pieces]

    def sum_all(self, value):
        value = value + self.chip(value)
        for step in range(self.bits):
            value = value + self.across(value, step)
        for bit in range(1, self.seq_bits):
            value = value + self.along(value, bit)
        return value


class Reduction:
    def __init__(self, net, keep, give):
        self.net = net
        self.keep, self.give = keep, give
        z_bits = list(range(1, net.seq_bits))
        self.z_orders = (z_bits, z_bits[1:2] + z_bits[:1] + z_bits[2:])
        self.todo = ["across"] * net.bits + ["split"] + ["swap"] * (len(z_bits) - 1) + ["join"]
        self.done = 0
        self.got = None
        self.pending = False

    def along(self, value, place):
        return self.net.send(value, lambda s, d: (s ^ (1 << self.z_orders[s % 2][place]), d))

    def start(self):
        kind = self.todo[0]
        self.pending = True
        if kind == "across":
            self.got = self.net.across(self.give, self.done)
        elif kind == "split":
            half = self.keep.shape[0] // 2
            z_bit = jnp.where(self.net.core == 0, self.z_orders[0][0], self.z_orders[1][0])
            self.upper = (self.net.seq >> z_bit) % 2 == 1
            low, high = self.keep[:half], self.keep[half:]
            self.got = self.along(jnp.where(self.upper, low, high), 0)
            self.keep = jnp.where(self.upper, high, low)
        elif kind == "swap":
            self.got = self.along(self.keep, self.done - self.net.bits)
        else:
            self.got = self.along(self.keep, 0)

    def finish(self):
        kind = self.todo.pop(0)
        self.done += 1
        self.pending = False
        if kind == "join":
            low, high = jnp.where(self.upper, self.got, self.keep), jnp.where(self.upper, self.keep, self.got)
            self.keep = jnp.concatenate([low, high], axis=0)
            return
        total = add(self.keep, self.got)
        if kind == "across":
            half = total.shape[0] // 2
            if half:
                self.keep, self.give = total[:half], total[half:]
            else:
                self.keep = total[0]
        else:
            self.keep = total


def pin(value, *reds):
    held = [value]
    for red in reds:
        held += [red.keep] + ([red.give] if red.todo and red.todo[0] == "across" else [])
    held = list(tie(*held))
    value = held.pop(0)
    for red in reds:
        red.keep = held.pop(0)
        if red.todo and red.todo[0] == "across":
            red.give = held.pop(0)
    return value


def body(block_input, doc_bounds, first_gain, first_shift, qkv_weight, qv_bias, score_weight, out_weight, out_bias, second_gain, second_shift, fc_weight, fc_bias, down_weight, down_bias, cotangent):
    net = Net()
    seqs, blocks, width = block_input.shape
    tokens = seqs * blocks
    heads = score_weight.shape[1]
    shards = net.n_dp
    rows = width // shards
    hidden = fc_weight.shape[1]
    tail = seqs * WINDOW
    core = net.core
    place = jnp.arange(4, dtype=jnp.int32)
    info = jnp.where(place == 0, net.seq * blocks, jnp.where(place == 1, core, jnp.where(place == 2, net.dp, net.seq))).astype(jnp.int32)
    bounds = doc_bounds
    x_flat = block_input.reshape(tokens, width)
    dy = cotangent.reshape(tokens, width)
    wide = hidden // CHUNKS
    deep = hidden // shards // CHUNKS
    half_qkv = 3 * width // 2
    sems = lambda count: pltpu.SemaphoreType.DMA((count,))
    by_seq = lambda rows_, cols: pl.BlockSpec((rows_, cols), lambda s, *_: (s, 0))
    stat = pl.BlockSpec((1, 8, LANES), lambda s, *_: (s, 0, 0))
    table_spec = whole_spec((16, width))
    full = whole_spec((tokens, width))
    tile = 2 * blocks
    by_tile = pl.BlockSpec((tile, width), lambda i, *_: (i, 0))
    pairs = width // LANES
    parts = [(0, pairs)]

    vectors = [first_gain, first_shift, second_gain, second_shift, out_bias, down_bias, qv_bias, fc_bias]
    small_rows = sum(part.shape[0] for part in vectors) // rows + heads
    small, own, x_tail = call(
        lambda *refs: start_kernel(*refs, names=len(vectors)),
        "start",
        (1,),
        [pl.BlockSpec(part.shape, lambda *_: (0,)) for part in vectors]
        + [whole_spec((rows, heads)), pl.BlockSpec((rows, half_qkv), lambda _, info: (0, info[1])), pl.BlockSpec((seqs, WINDOW, width), lambda *_: (0, blocks // WINDOW - 1, 0))],
        [whole_spec((small_rows, rows)), whole_spec((rows, half_qkv)), whole_spec((tail, width))],
        [shape((small_rows, rows), BF), shape((rows, half_qkv), BF), shape((tail, width), BF)],
        prefetch=1,
        micros=2,
        far_in=tuple(range(len(vectors) + 3)),
    )(info, *vectors, score_weight, qkv_weight, block_input)

    def begin_gather(own):
        return [own, net.across(own, 0)], [net.across(own, 1)] if net.bits > 1 else []

    def end_gather(pieces, ahead):
        if net.bits > 1:
            pieces = pieces + ahead + [net.across(pieces[1], 1)]
        for step in range(2, net.bits):
            pieces = net.gather_step(pieces, step)
        return pieces

    small_state = begin_gather(small)
    qkv_state = begin_gather(own)
    x_tail = net.shifted(x_tail, 1)
    small_pieces = end_gather(*small_state)
    qkv_pieces = end_gather(*qkv_state)

    table, score = call(
        params_kernel,
        "params",
        (1,),
        [whole_spec((small_rows, rows))] * shards,
        [table_spec, whole_spec((LANES, width))],
        [shape((16, width), F32), shape((LANES, width), BF)],
        scratch=[pltpu.VMEM((shards, small_rows, rows), F32)],
        prefetch=1,
        micros=1,
    )(info, *small_pieces)

    group = seqs // 2
    normed, normed_tail, importance, mass, stats = call(
        prep_kernel,
        "prep",
        (seqs // group,),
        [by_seq(group * blocks, width), by_seq(group * WINDOW, width), table_spec, whole_spec((LANES, width))],
        [by_seq(group * blocks, width), by_seq(group * WINDOW, width), by_seq(group * blocks, LANES), by_seq(group * blocks, LANES), pl.BlockSpec((group, 8, LANES), lambda s, *_: (s, 0, 0))],
        [shape((tokens, width), BF), shape((tail, width), BF), shape((tokens, LANES), F32), shape((tokens, LANES), F32), shape((seqs, 8, LANES), F32)],
        prefetch=2,
        micros=4,
    )(info, bounds, x_flat, x_tail, table, score)

    def scan_step(state, masks):
        spec = whole_spec((seqs, 8, LANES))
        got = [net.masked(state, mask) for mask in masks]
        return call(
            lambda *refs: scan_kernel(*refs, masks=masks),
            "scan",
            (1,),
            [spec] * (1 + len(masks)),
            spec,
            shape((seqs, 8, LANES), F32),
            prefetch=1,
            micros=0.5,
        )(info, state, *got)

    chip_masks = [2 * k for k in range(1, net.n_seq // 2)]
    stats, *qkv_pieces = tie(scan_step(stats, [1]), *qkv_pieces)
    qkv_others = [net.chip(piece) for piece in qkv_pieces[1:]]
    w_qkv = call(
        qkv_build_kernel,
        "qkv_build",
        (1,),
        [whole_spec((rows, 3 * width))] + [whole_spec((rows, half_qkv))] * (2 * shards - 2),
        ANY,
        shape((width, 3 * width), BF),
        scratch=[sems(2 * shards)],
        prefetch=1,
        micros=2,
    )(info, qkv_weight, *qkv_pieces[1:], *qkv_others)

    fc_weight, _ = tie(fc_weight, small)
    packs = call(
        feed_pack_kernel,
        "feed_pack",
        (1,),
        [whole_spec((rows, hidden)), whole_spec(down_weight.shape), whole_spec((rows, width))],
        [whole_spec((rows, wide))] * CHUNKS + [whole_spec((rows, wide + width // 2)), whole_spec((rows, wide))],
        [shape((rows, wide), BF)] * CHUNKS + [shape((rows, wide + width // 2), BF), shape((rows, wide), BF)],
        prefetch=1,
        micros=2,
        limit=24,
        far_in=(0, 1, 2),
    )(info, fc_weight, down_weight, out_weight)
    fc_own, feed_own = packs[:CHUNKS], packs[CHUNKS:]
    first_own, _ = tie(feed_own[0], qkv_pieces[1])
    a_state = begin_gather(first_own)

    def build_feed(chunk, pieces):
        others = [net.chip(piece) for piece in pieces[1:]]
        with_out = chunk == 0
        owns = [fc_own[chunk], down_weight] + ([out_weight] if with_out else [])
        specs = [whole_spec((rows, wide)), pl.BlockSpec((deep, width), lambda *_: (chunk, 0))] + ([whole_spec((rows, width))] if with_out else [])
        outs = [shape((width, wide), BF), shape((wide, width), BF)] + ([shape((width, width), BF)] if with_out else [])
        count = 3 + (shards - 1) * (1 + deep // rows + 2)
        return call(
            lambda *refs: feed_build_kernel(*refs, with_out=with_out),
            "feed_build",
            (1,),
            specs + [whole_spec(pieces[0].shape)] * (2 * shards - 2),
            [ANY] * len(outs),
            outs,
            scratch=[sems(count)],
            prefetch=1,
            micros=2,
        )(info, *owns, *pieces[1:], *others)

    col = lambda rows_: pl.BlockSpec((rows_, width), lambda j: (0, j))
    qkv, qkv_tail = call(
        qkv_kernel,
        "qkv",
        (3,),
        [full, whole_spec((tail, width)), col(width), table_spec],
        [col(tokens), pl.BlockSpec((tail, width), lambda j: (0, jnp.maximum(j - 1, 0)))],
        [shape((tokens, 3 * width), BF), shape((tail, 2 * width), BF)],
        micros=6.5,
        limit=24,
    )(normed, normed_tail, w_qkv, table)
    before = scan_step(stats, chip_masks)
    qkv, *held = tie(qkv, *a_state[0], *a_state[1])
    a_pieces = end_gather(held[:2], held[2:])
    second_own, _ = tie(feed_own[1], held[1])
    b_state = begin_gather(second_own)

    attended, probs, gates, inverse = call(
        attention_kernel,
        "attention",
        (seqs,),
        [by_seq(blocks, 3 * width), by_seq(WINDOW, 2 * width), by_seq(blocks, LANES), by_seq(blocks, LANES), stat],
        [by_seq(blocks, width), by_seq(blocks, 2 * width), by_seq(WINDOW, width), by_seq(WINDOW, LANES)],
        [shape((tokens, width), BF), shape((tokens, 2 * width), BF), shape((tail, width), BF), shape((tail, LANES), F32)],
        prefetch=2,
        micros=10.5,
        far=(1, 2, 3),
    )(info, bounds, qkv, qkv_tail, importance, mass, before)

    attended, *a_pieces = tie(attended, *a_pieces)
    fc_a, down_a, w_out = build_feed(0, a_pieces)

    middle, normed_second = call(
        project_kernel,
        "project",
        (tokens // tile,),
        [by_tile, by_tile, whole_spec((width, width)), table_spec],
        [by_tile, by_tile],
        [shape((tokens, width), F32), shape((tokens, width), BF)],
        micros=3,
        far=(0,),
        far_in=(1,),
    )(attended, x_flat, w_out, table)

    hids, dpres, d_fc_bias = [], [], []

    def feed(chunk, block, fc, down, normed_second):
        square = whole_spec((width, width))
        hid, dpre, d_bias, keep, give = call(
            lambda *refs: feed_kernel(*refs, chunk=chunk, block=block),
            "feed",
            (1,),
            [full, full, pl.BlockSpec((width, width), lambda *_: (0, block)), pl.BlockSpec((width, width), lambda *_: (block, 0)), table_spec],
            [full, full, whole_spec((8, width)), square, square],
            [shape((tokens, width), BF), shape((tokens, width), BF), shape((8, width), F32), shape((width, width), BF), shape((width, width), BF)],
            prefetch=1,
            micros=8,
            limit=36,
            far=(0, 1),
        )(info, normed_second, dy, fc, down, table)
        hids.append(hid)
        dpres.append(dpre)
        d_fc_bias.append(d_bias)
        return keep, net.chip(give)

    def feed_add(blocks_):
        half = (shards // 2, rows, wide)
        square = whole_spec((width, width))
        keep, give = call(
            feed_add_kernel,
            "feed_add",
            (1,),
            [square] * (2 * BLOCKS),
            [whole_spec(half)] * 2,
            [shape(half, BF)] * 2,
            scratch=[pltpu.VMEM((shards, rows, wide), BF)],
            prefetch=1,
            micros=2,
            limit=28,
        )(info, *[keep for keep, _ in blocks_], *[got for _, got in blocks_])
        return Reduction(net, keep, give)

    grads = [feed(0, 0, fc_a, down_a, normed_second)]
    normed_second, *held = tie(normed_second, dpres[0], *b_state[0], *b_state[1])
    b_pieces = end_gather(held[1:3], held[3:])
    grads.append(feed(0, 1, fc_a, down_a, normed_second))
    fc_b, down_b = build_feed(1, b_pieces)
    late = [feed(1, 0, fc_b, down_b, normed_second)]
    red_a = feed_add(grads)
    normed_second, _ = tie(normed_second, dpres[2])
    normed_second = pin(normed_second, red_a)
    red_a.start()
    late.append(feed(1, 1, fc_b, down_b, normed_second))

    half_out = (shards, rows, width // 2)
    groups = 2
    part_tokens, part_tail, part_seqs = tokens // groups, tail // groups, seqs // groups
    by_part = pl.BlockSpec((part_tokens, width), lambda i, *_: (i, 0))
    d_middle, branch, sums_second = call(
        middle_kernel,
        "middle",
        (groups,),
        [by_part] * (CHUNKS * BLOCKS) + [whole_spec((width, wide))] * CHUNKS + [by_part, by_part, table_spec],
        [by_part, by_part, whole_spec((8, width))],
        [shape((tokens, width), F32), shape((tokens, width), BF), shape((8, width), F32)],
        micros=1,
        limit=36,
        far=(0,),
        far_in=(0, 1, 2, 3, 6, 7),
    )(*dpres, fc_a, fc_b, middle, dy, table)

    red_a.finish()
    red_b = feed_add(late)
    branch = pin(branch, red_a, red_b)
    red_a.start()
    red_b.start()
    d_attended, keep_out, give_out = call(
        branch_kernel,
        "branch",
        (1,),
        [full, full, whole_spec((width, width))],
        [full, whole_spec(half_out), whole_spec(half_out)],
        [shape((tokens, width), BF), shape(half_out, BF), shape(half_out, BF)],
        prefetch=1,
        micros=1,
        limit=24,
    )(info, branch, attended, w_out)
    got_out = net.chip(give_out)

    def attention_back(part, d_attended):
        shifted = lambda rows_, cols: pl.BlockSpec((rows_, cols), lambda s, *_: (part * part_seqs + s, 0))
        return call(
            lambda *refs: attention_back_kernel(*refs, first_seq=part * part_seqs, pairs=pairs),
            "attention_back",
            (part_seqs,),
            [shifted(blocks, 3 * width), shifted(WINDOW, 2 * width), shifted(blocks, width), shifted(blocks, width), shifted(blocks, 2 * width), shifted(WINDOW, width), shifted(WINDOW, LANES), shifted(blocks, LANES), pl.BlockSpec((1, 8, LANES), lambda s, *_: (part * part_seqs + s, 0, 0))],
            [by_seq(blocks, 3 * width), by_seq(WINDOW, 3 * width), by_seq(blocks, LANES), pl.BlockSpec((1, 1, LANES), lambda s, *_: (s, 0, 0))],
            [shape((part_tokens, 3 * width), BF), shape((part_tail, 3 * width), BF), shape((part_tokens, LANES), F32), shape((part_seqs, 1, LANES), F32)],
            scratch=[pltpu.VMEM((LANES, LANES), F32)],
            prefetch=2,
            micros=7,
            far_in=(4, 5, 6),
        )(info, bounds, qkv, qkv_tail, attended, d_attended, probs, gates, inverse, importance, before)

    def qkv_grad(mine, backs):
        side = (lambda *args: (0, args[-1][1])) if mine else (lambda *args: (0, 1 - args[-1][1]))
        result = (shards, rows, half_qkv)
        return call(
            lambda *refs: qkv_grad_kernel(*refs, groups=groups, mine=mine),
            "qkv_grad",
            (1,),
            [full, whole_spec((tail, width))] + [pl.BlockSpec((part_tokens, half_qkv), side)] * groups + [pl.BlockSpec((part_tail, half_qkv), side)] * groups,
            [whole_spec(result), whole_spec((8, half_qkv))],
            [shape(result, BF), shape((8, half_qkv), F32)],
            prefetch=1,
            micros=4,
            limit=32,
        )(info, normed, normed_tail, *[back[0] for back in backs], *[back[1] for back in backs])

    half_shards = shards // 2

    def halved(total):
        return Reduction(net, total[:half_shards], total[half_shards:])

    red_o = halved(add(keep_out, got_out))
    d_attended = pin(d_attended, red_o)
    red_o.start()
    backs = [list(attention_back(0, d_attended))]
    red_a.finish()
    red_b.finish()
    red_o.finish()
    red_b.keep = jnp.concatenate([red_b.keep, red_o.keep], axis=2)
    red_b.give = jnp.concatenate([red_b.give, red_o.give], axis=2)
    d_attended, _ = tie(d_attended, backs[0][0])
    d_attended = pin(d_attended, red_a, red_b)
    red_a.start()
    red_b.start()
    backs.append(list(attention_back(1, d_attended)))
    red_a.finish()
    red_b.finish()
    backs[1][0] = pin(backs[1][0], red_a, red_b)
    red_a.start()
    red_b.start()
    give_qkv, sums_given = qkv_grad(False, backs)
    got_qkv = net.chip(give_qkv)
    backs[1][0], give_qkv = tie(backs[1][0], give_qkv)
    keep_qkv, sums_kept = qkv_grad(True, backs)

    red_a.finish()
    red_b.finish()
    red_c = halved(add(keep_qkv, got_qkv))
    total_all = jnp.concatenate([back[3] for back in backs], axis=0)
    total_all = pin(total_all, red_a, red_b, red_c)
    red_c.start()
    total_after = jnp.zeros_like(total_all)

    def suffix_step(total_after, total_all, masks):
        got = [net.masked(total_all, mask) for mask in masks]
        for mask, value in zip(masks, got):
            total_after = jnp.where((net.seq ^ mask) > net.seq, total_after + value, total_after)
            total_all = total_all + value
        return total_after, total_all

    total_after, total_all = suffix_step(total_after, total_all, [1])
    d_halos = [back[1] for back in backs]
    d_halos[0], keep_qkv = tie(d_halos[0], keep_qkv)
    d_tail, sums_tail = call(
        tail_back_kernel,
        "tail_back",
        (1,),
        [whole_spec((part_tail, 3 * width))] * groups + [whole_spec((width, 3 * width)), whole_spec((tail, width)), table_spec],
        [whole_spec((tail, width)), whole_spec((8, width))],
        [shape((tail, width), BF), shape((8, width), F32)],
        micros=2,
        limit=32,
    )(*d_halos, w_qkv, x_tail, table)
    d_tail, total_all, total_after = tie(d_tail, total_all, total_after)
    back = net.shifted(d_tail, -1).reshape(seqs, WINDOW, width)
    total_after, _ = suffix_step(total_after, total_all, chip_masks)
    red_a.start()
    red_b.start()
    middle, _ = tie(middle, d_tail)
    block_output = call(
        output_kernel,
        "output",
        (tokens // tile,),
        [by_tile] * (CHUNKS * BLOCKS) + [whole_spec((wide, width))] * CHUNKS + [by_tile, table_spec],
        by_tile,
        shape((tokens, width), BF),
        micros=6.5,
        limit=32,
        far_in=(0, 1, 2, 3, 6),
    )(*hids, down_a, down_b, middle, table)
    total_after, back, block_output = tie(total_after, back, block_output)
    red_a.finish()
    red_b.finish()
    red_c.finish()
    total_after = pin(total_after, red_a, red_b, red_c)
    red_b.start()
    red_c.start()

    per_tile = tile // blocks
    per_group = tokens // tile // groups
    grouped_tile = lambda cols: [pl.BlockSpec((tile, cols), lambda i, *_, k=k: (jnp.clip(i - k * per_group, 0, per_group - 1), 0)) for k in range(groups)]
    by_lane = pl.BlockSpec((tile, LANES), lambda i, *_: (i, 0))
    input_grad, sums_first, d_score = call(
        lambda *refs: input_grad_kernel(*refs, groups=groups),
        "input_grad",
        (tokens // tile,),
        grouped_tile(3 * width)
        + grouped_tile(LANES)
        + [
            whole_spec((width, 3 * width)),
            whole_spec((LANES, width)),
            by_tile,
            by_tile,
            table_spec,
            by_tile,
            pl.BlockSpec((per_tile, WINDOW, width), lambda i, *_: (i, 0, 0)),
            by_lane,
            pl.BlockSpec((per_tile, 8, LANES), lambda i, *_: (i, 0, 0)),
            pl.BlockSpec((per_tile, 1, LANES), lambda i, *_: (i, 0, 0)),
        ],
        [by_tile, whole_spec((8, width)), whole_spec((LANES, width))],
        [shape((tokens, width), F32), shape((8, width), F32), shape((LANES, width), F32)],
        prefetch=2,
        micros=9,
        limit=28,
        far_in=tuple(2 * groups + k for k in (3, 5)),
    )(info, bounds, *[back_[0] for back_ in backs], *[back_[2] for back_ in backs], w_qkv, score, normed, x_flat, table, d_middle, back, importance, before, total_after)

    packed = call(
        small_pack_kernel,
        "small_pack",
        (1,),
        [whole_spec((8, width))] * 3 + [whole_spec((8, half_qkv))] * 2 + [whole_spec((8, width))] * (CHUNKS * BLOCKS) + [whole_spec((LANES, width))],
        whole_spec((shards, small_rows, rows)),
        shape((shards, small_rows, rows), F32),
        scratch=[pltpu.VMEM((32, width), F32)],
        prefetch=1,
        micros=1,
    )(info, sums_first, sums_tail, sums_second, sums_kept, sums_given, *d_fc_bias, d_score)

    reds = [red_a, red_b, red_c]
    small_steps = [lambda value, k=k: value[: value.shape[0] // 2] + net.across(value[value.shape[0] // 2 :], k) for k in range(net.bits)]
    small_steps += [lambda value, k=k: value + net.along(value, k) for k in range(1, net.seq_bits)]
    small_steps += [lambda value: value + net.chip(value)]
    while small_steps or any(red.todo for red in reds):
        active = [red for red in reds if red.pending]
        for red in active:
            red.finish()
        packed = pin(packed, *active)
        for red in reds:
            if red.todo:
                red.start()
        if small_steps:
            packed = small_steps.pop(0)(packed)
    packed = packed[0]

    def finish(red):
        other = net.chip(red.keep)
        return jnp.where(core == 0, red.keep, other), jnp.where(core == 0, other, red.keep)

    fc_grads, down_grads = zip(finish(red_a), finish(red_b))
    out_grads = [fc_grads[1][:, wide:], down_grads[1][:, wide:]]
    fc_grads, down_grads = [part[:, :wide] for part in fc_grads], [part[:, :wide] for part in down_grads]
    d_out = jnp.concatenate(out_grads, axis=1).astype(F32)
    d_qkv = jnp.concatenate(finish(red_c), axis=1).astype(F32)
    d_fc = jnp.concatenate([part[:, d * deep : (d + 1) * deep] for d in range(shards) for part in fc_grads], axis=1).astype(F32)
    d_down = jnp.concatenate([part[:, k * width : (k + 1) * width] for part in down_grads for k in range(deep // rows)], axis=0).astype(F32)
    small_outs = [shape(part.shape, F32) for part in vectors] + [shape((rows, heads), F32)]
    dg_first, ds_first, dg_second, ds_second, db_out, db_down, db_qv, db_fc, d_score = call(
        end_kernel,
        "end",
        (1,),
        [whole_spec((small_rows, rows))],
        [pl.BlockSpec(part.shape, lambda *_, n=len(part.shape): (0,) * n) for part in small_outs],
        small_outs,
        micros=1,
    )(packed)
    return (
        block_output.reshape(seqs, blocks, width),
        input_grad.reshape(seqs, blocks, width),
        dg_first,
        ds_first,
        d_qkv,
        db_qv,
        d_score,
        d_out,
        db_out,
        dg_second,
        ds_second,
        d_fc,
        db_fc,
        d_down,
        db_down,
    )


def solution(mesh):
    split = P("dp", "seq", None)
    rows = P("dp", None)
    flat = P("dp")
    in_specs = (split, rows, flat, flat, rows, flat, rows, rows, flat, flat, flat, rows, flat, rows, flat, split)
    out_specs = (split, split, flat, flat, rows, flat, rows, rows, flat, flat, flat, rows, flat, rows, flat)
    return jax.shard_map(body, mesh=mesh, in_specs=in_specs, out_specs=out_specs, check_vma=False)
```

```python
import math

import jax
import jax.numpy as jnp
from jax import lax
from jax.experimental import pallas as pl
from jax.experimental.pallas import tpu as pltpu
from jax.sharding import PartitionSpec as P

KTOP = 64
WINDOW = 64
HEAD = 64
LANES = 128
EPSILON = 1e-05
NEGATIVE = -1e30
SCALE = 1.0 / math.sqrt(HEAD)
GELU_A = math.sqrt(2.0 / math.pi)
GELU_B = 0.044715
BF = jnp.bfloat16
F32 = jnp.float32
NN = ((1,), (0,))
NT = ((1,), (1,))
TN = ((0,), (0,))
CHUNKS = 2
BLOCKS = 2
MIB = 2**20
GAIN1, SHIFT1, GAIN2, SHIFT2, BIAS_OUT, BIAS_DOWN, BIAS_QKV, BIAS_FC = 0, 1, 2, 3, 4, 5, 6, 9
VECTORS = 6
QV_ROWS = 2
FC_ROWS = 4


def mm(left, right, dims=NN):
    return lax.dot_general(left, right, (dims, ((), ())), preferred_element_type=F32)


def mm_split(mask, value, dims=NN):
    high = value.astype(BF)
    low = (value - high.astype(F32)).astype(BF)
    return mm(mask, high, dims) + mm(mask, low, dims)


def whole_spec(shape):
    return pl.BlockSpec(shape, lambda *_: (0,) * len(shape))


ANY = pl.BlockSpec(memory_space=pl.ANY)


def call(kernel, name, grid, in_specs, out_specs, out_shape, scratch=(), prefetch=0, micros=1.0, limit=16, alias=None, far=(), far_in=()):
    many = isinstance(out_shape, (list, tuple))
    if grid == (1,):
        once = lambda spec: spec if spec.block_shape is None else pl.BlockSpec(spec.block_shape, spec.index_map, pipeline_mode=pl.Buffered(1))
        in_specs = [once(spec) for spec in in_specs]
        out_specs = [once(spec) for spec in out_specs] if many else once(out_specs)
    outs = [pltpu.HBM(one.shape, one.dtype) if k in far else one for k, one in enumerate(out_shape if many else [out_shape])]
    inner = pl.pallas_call(
        kernel,
        grid_spec=pltpu.PrefetchScalarGridSpec(
            num_scalar_prefetch=prefetch,
            grid=grid,
            in_specs=in_specs,
            out_specs=out_specs,
            scratch_shapes=list(scratch),
        ),
        out_shape=outs if many else outs[0],
        input_output_aliases=alias or {},
        compiler_params=pltpu.CompilerParams(vmem_limit_bytes=limit * MIB),
        cost_estimate=pl.CostEstimate(flops=int(micros * 1.1e9), bytes_accessed=1024, transcendentals=0),
        name=name,
    )

    def run(*operands):
        return inner(*[pltpu.with_memory_space_constraint(one, pltpu.HBM) if k - prefetch in far_in else one for k, one in enumerate(operands)])

    return run


def shape(dims, kind):
    return jax.ShapeDtypeStruct(dims, kind)


def iota(dims, axis):
    return lax.broadcasted_iota(jnp.int32, dims, axis)


def segment(places, first, second):
    return (places >= first).astype(jnp.int32) + (places >= second).astype(jnp.int32)


def normalise(values):
    average = jnp.mean(values, axis=-1, keepdims=True)
    centred = values - average
    variance = jnp.mean(centred * centred, axis=-1, keepdims=True)
    scale = lax.rsqrt(variance + EPSILON)
    return centred * scale, scale


def norm_back(d_norm, unit, scale, gain):
    weighted = d_norm * gain
    return scale * (
        weighted
        - jnp.mean(weighted, axis=-1, keepdims=True)
        - unit * jnp.mean(weighted * unit, axis=-1, keepdims=True)
    )


def bit_orders(count):
    bits = count.bit_length() - 1
    straight = list(range(bits))
    half = bits // 2
    return straight, straight[half:] + straight[:half]


def crossed(count, core, index, first_high):
    order = bit_orders(count)[core]
    mask = 0
    for step, bit in enumerate(order):
        place = len(order) - 1 - step if first_high else step
        mask |= ((index >> place) & 1) << bit
    return mask


def rank(count, core, far, first_high):
    order = bit_orders(count)[core]
    index = 0
    for step, bit in enumerate(order):
        place = len(order) - 1 - step if first_high else step
        index |= ((far >> bit) & 1) << place
    return index


def by_core(core, even, odd):
    return jnp.where(core == 0, even, odd)


def copy_all(copies, sems):
    started = [pltpu.make_async_copy(source, target, sems.at[k]) for k, (source, target) in enumerate(copies)]
    for copy in started:
        copy.start()
    for copy in started:
        copy.wait()


def start_kernel(*refs):
    vectors, (score_ref, small_ref) = refs[:-2], refs[-2:]
    rows = small_ref.shape[1]
    row = 0
    for ref in vectors:
        for k in range(ref.shape[0] // rows):
            small_ref[row : row + 1] = ref[k * rows : (k + 1) * rows].reshape(1, rows)
            row += 1
    small_ref[row:] = score_ref[...]


def first_pack_kernel(info, own_ref, x_ref, own_out, tail_ref):
    own_out[...] = own_ref[...]
    for s in range(x_ref.shape[0]):
        tail_ref[s * WINDOW : (s + 1) * WINDOW] = x_ref[s]


def feed_pack_kernel(info, fc_ref, down_ref, weight_ref, *outs):
    fc_refs, own_refs = outs[:CHUNKS], outs[CHUNKS:]
    rows, hidden = fc_ref.shape
    width = down_ref.shape[1]
    wide = fc_refs[0].shape[1]
    deep = down_ref.shape[0] // CHUNKS
    shards = hidden // (deep * CHUNKS)
    for chunk in range(CHUNKS):
        for shard in range(shards):
            begin = (shard * CHUNKS + chunk) * deep
            fc_refs[chunk][:, shard * deep : (shard + 1) * deep] = fc_ref[:, begin : begin + deep]

        @pl.when(info[1] == 0)
        def _():
            own_refs[chunk][:, :wide] = fc_refs[chunk][...]
            if chunk == 0:
                own_refs[chunk][:, wide:] = weight_ref[:, : width // 2]

        @pl.when(info[1] != 0)
        def _():
            for part in range(deep // rows):
                begin = chunk * deep + part * rows
                own_refs[chunk][:, part * width : (part + 1) * width] = down_ref[begin : begin + rows]
            if chunk == 0:
                own_refs[chunk][:, wide:] = weight_ref[:, width // 2 :]


def end_kernel(packed_ref, *outs):
    row = 0
    rows = packed_ref.shape[1]
    for ref in outs[:-1]:
        for k in range(ref.shape[0] // rows):
            ref[k * rows : (k + 1) * rows] = packed_ref[row : row + 1].reshape(rows)
            row += 1
    outs[-1][...] = packed_ref[row:]


def params_kernel(info, *refs):
    pieces, (table_ref, score_ref, held) = refs[:-3], refs[-3:]
    shards = len(pieces)
    core, me = info[1], info[2]
    for k, piece in enumerate(pieces):
        held[k] = piece[...].astype(F32)

    def at(shard):
        far = shard ^ me
        index = jnp.int32(0)
        for k in range(shards):
            mask = by_core(core, crossed(shards, 0, k, False), crossed(shards, 1, k, False))
            index = jnp.where(mask == far, k, index)
        return held[index]

    parts = [at(shard) for shard in range(shards)]

    def line(shard_range, rows):
        return jnp.concatenate([parts[s][r : r + 1] for s in shard_range for r in rows], axis=1)

    table_ref[...] = jnp.zeros_like(table_ref)
    for r in range(VECTORS):
        table_ref[r : r + 1] = line(range(shards), [r])
    qv = list(range(VECTORS, VECTORS + QV_ROWS))
    table_ref[BIAS_QKV : BIAS_QKV + 1] = line(range(shards // 2), qv)
    table_ref[BIAS_QKV + 2 : BIAS_QKV + 3] = line(range(shards // 2, shards), qv)
    base = VECTORS + QV_ROWS
    per_block = shards // BLOCKS
    per_chunk = FC_ROWS // CHUNKS
    for chunk in range(CHUNKS):
        for block in range(BLOCKS):
            rows = [base + chunk * per_chunk + k for k in range(per_chunk)]
            row = BIAS_FC + chunk * BLOCKS + block
            table_ref[row : row + 1] = line(range(block * per_block, (block + 1) * per_block), rows)
    base += FC_ROWS
    heads = parts[0].shape[0] - base
    score_ref[...] = jnp.zeros_like(score_ref)
    for head in range(heads):
        score_ref[head : head + 1] = line(range(shards), [base + head]).astype(BF)


def prep_kernel(info, bounds, x_ref, table_ref, score_ref, normed_ref, imp_ref, mass_ref, stat_ref):
    seqs = stat_ref.shape[0]
    blocks = x_ref.shape[0] // seqs
    gain = table_ref[GAIN1 : GAIN1 + 1]
    shift = table_ref[SHIFT1 : SHIFT1 + 1]
    start = info[0]
    rows = iota((blocks, blocks), 0)
    cols = iota((blocks, blocks), 1)
    for k in range(seqs):
        rs = slice(k * blocks, (k + 1) * blocks)
        normed = (normalise(x_ref[rs].astype(F32))[0] * gain + shift).astype(BF)
        normed_ref[rs] = normed
        importance = mm(normed, score_ref[...], NT)
        imp_ref[rs] = importance
        s = pl.program_id(0) * seqs + k
        first, second = bounds[0, s], bounds[1, s]
        lower = (cols <= rows) & (segment(start + rows, first, second) == segment(start + cols, first, second))
        peak = jnp.max(importance, axis=0, keepdims=True)
        mass = mm_split(lower.astype(BF), jnp.exp(importance - peak))
        mass_ref[rs] = mass
        stat_ref[k, 0:1, :] = peak
        stat_ref[k, 1:2, :] = mass[blocks - 1 :, :]
        stat_ref[k, 2:3, :] = jnp.full_like(peak, NEGATIVE)
        stat_ref[k, 3:4, :] = jnp.zeros_like(peak)
        stat_ref[k, 4:5, :] = peak


def prep_tail_kernel(x_ref, table_ref, out_ref):
    gain = table_ref[GAIN1 : GAIN1 + 1]
    shift = table_ref[SHIFT1 : SHIFT1 + 1]
    out_ref[...] = (normalise(x_ref[...].astype(F32))[0] * gain + shift).astype(BF)


def scan_kernel(info, mine_ref, *refs, masks):
    got_refs, out_ref = refs[:-1], refs[-1]

    def joined(peak, total, got):
        top = jnp.maximum(peak, got[:, 0:1])
        return top, total * jnp.exp(peak - top) + got[:, 1:2] * jnp.exp(got[:, 0:1] - top)

    out_ref[...] = mine_ref[...]
    for mask, got in zip(masks, got_refs):
        peak, total = joined(out_ref[:, 0:1], out_ref[:, 1:2], got)
        out_ref[:, 0:1] = peak
        out_ref[:, 1:2] = total

        @pl.when((info[3] ^ mask) < info[3])
        def _():
            peak, total = joined(out_ref[:, 2:3], out_ref[:, 3:4], got)
            out_ref[:, 2:3] = peak
            out_ref[:, 3:4] = total


def qkv_build_kernel(info, *refs):
    own, pieces, out, sems = refs[0], refs[1:-2], refs[-2], refs[-1]
    shards = len(pieces) // 2 + 1
    rows, width = own.shape
    half = width // 2
    me = info[2]

    def build(core):
        copies = [(own, out.at[pl.ds(pl.multiple_of(me * rows, 16), rows)])]
        for k in range(1, shards):
            for side, group in ((core, 0), (1 - core, shards - 1)):
                at = pl.multiple_of((me ^ crossed(shards, side, k, False)) * rows, 16)
                target = out.at[pl.ds(at, rows), side * half : (side + 1) * half]
                copies.append((pieces[group + k - 1], target))
        copy_all(copies, sems)

    @pl.when(info[1] == 0)
    def _():
        build(0)

    @pl.when(info[1] != 0)
    def _():
        build(1)


def feed_build_kernel(info, *refs, with_out, by_pair):
    if with_out:
        own_fc, own_down, own_out = refs[:3]
        pieces, (fc_ref, down_ref, out_ref, sems) = refs[3:-4], refs[-4:]
    else:
        own_fc, own_down = refs[:2]
        pieces, (fc_ref, down_ref, sems) = refs[2:-3], refs[-3:]
    shards = len(pieces) // 2 + 1
    rows, wide = own_fc.shape
    deep, width = own_down.shape
    split = width // 2
    me = info[2]

    kinds = [info[1] ^ ((info[3] >> 1) & 1), None] if by_pair else [info[1], None]
    kinds[1] = 1 - kinds[0]

    def away(k, partner):
        return jnp.where(kinds[partner] == 0, crossed(shards, 0, k, False), crossed(shards, 1, k, False))

    def build(core):
        at_rows = lambda shard: pl.multiple_of(shard * rows, 16)
        copies = [
            (own_fc, fc_ref.at[pl.ds(at_rows(me), rows)]),
            (own_down, down_ref.at[pl.ds(pl.multiple_of(me * deep, 16), deep)]),
        ]
        if with_out:
            copies.append((own_out, out_ref.at[pl.ds(at_rows(me), rows)]))
        for k in range(1, shards):
            for partner, side in enumerate((core, 1 - core)):
                piece = pieces[partner * (shards - 1) + k - 1]
                shard = me ^ away(k, partner)
                if side == 0:
                    copies.append((piece.at[:, :wide], fc_ref.at[pl.ds(at_rows(shard), rows)]))
                else:
                    for part in range(deep // rows):
                        at = pl.multiple_of(shard * deep + part * rows, 16)
                        copies.append((piece.at[:, part * width : (part + 1) * width], down_ref.at[pl.ds(at, rows)]))
                if with_out:
                    copies.append((piece.at[:, wide:], out_ref.at[pl.ds(at_rows(shard), rows), side * split : (side + 1) * split]))
        copy_all(copies, sems)

    @pl.when(info[1] == 0)
    def _():
        build(0)

    @pl.when(info[1] != 0)
    def _():
        build(1)


def qkv_kernel(normed_ref, tail_ref, weight_ref, table_ref, out_ref, tail_out_ref):
    j = pl.program_id(0)
    weight = weight_ref[...]
    bias = table_ref[pl.ds(BIAS_QKV + j, 1)]
    factor = jnp.where(j == 0, SCALE, 1.0)
    out_ref[...] = ((mm(normed_ref[...], weight) + bias).astype(BF).astype(F32) * factor).astype(BF)

    @pl.when(j > 0)
    def _():
        tail_out_ref[...] = (mm(tail_ref[...], weight) + bias).astype(BF)


def lane_masks():
    first = iota((1, LANES), 1) < HEAD
    return first.astype(BF), (~first).astype(BF)


def grouped(part, keep_first, keep_second):
    return jnp.concatenate([part * keep_first, part * keep_second], axis=0)


def tile_masks(start, half, first, second):
    dims = (WINDOW, LANES)
    row = iota(dims, 0)
    col = iota(dims, 1) & (HEAD - 1)
    base = start + WINDOW * half
    mine = segment(base + row, first, second)
    far = segment(base - WINDOW + col, first, second) == mine
    near = (col <= row) & (segment(base + col, first, second) == mine)
    if half == 0:
        far = far & (col > row) & (base - WINDOW + col >= 0)
    return far, near, col <= row


def spread(columns, pair, rows):
    left = columns[:, 2 * pair : 2 * pair + 1]
    right = columns[:, 2 * pair + 1 : 2 * pair + 2]
    return jnp.where(iota((rows, LANES), 1) < HEAD, left, right)


def key_groups(qkv_ref, halo_ref, width, pair, keep_first, keep_second, one_group):
    at = slice(pair * LANES, (pair + 1) * LANES)
    ks = slice(width + pair * LANES, width + (pair + 1) * LANES)
    vs = slice(2 * width + pair * LANES, 2 * width + (pair + 1) * LANES)
    keys = [grouped(part, keep_first, keep_second) for part in (halo_ref[:, at], qkv_ref[:WINDOW, ks], qkv_ref[WINDOW:, ks])]
    values = [
        jnp.concatenate([grouped(part, keep_first, keep_second), one_group], axis=1)
        for part in (halo_ref[:, ks], qkv_ref[:WINDOW, vs], qkv_ref[WINDOW:, vs])
    ]
    return keys, values


def attention_kernel(info, bounds, qkv_ref, halo_ref, imp_ref, mass_ref, before_ref, att_ref, probs_ref, sig_ref, inv_ref):
    s = pl.program_id(0)
    blocks, width = att_ref.shape
    start = info[0]
    first, second = bounds[0, s], bounds[1, s]
    pairs = width // LANES
    peak = before_ref[0, 4:5, :]
    carry_peak = before_ref[0, 2:3, :]
    carry_total = before_ref[0, 3:4, :]
    top = before_ref[0, 0:1, :]
    joined = jnp.maximum(peak, carry_peak)
    place = start + iota((blocks, LANES), 0)
    continues = segment(place, first, second) == segment(jnp.full((1, LANES), start - 1, jnp.int32), first, second)
    mass = mass_ref[...] * jnp.exp(peak - joined) + jnp.where(
        continues, carry_total * jnp.exp(carry_peak - joined), 0.0
    )
    threshold = joined + jnp.log(mass) - math.log(KTOP)
    late = threshold[WINDOW:]
    inv_ref[...] = 1.0 / (mass[WINDOW:] * jnp.exp(joined - top))
    imp_rows = imp_ref[...].T
    keep_first, keep_second = lane_masks()
    one_group = grouped(jnp.ones((WINDOW, LANES), BF), keep_first, keep_second)
    masks = [tile_masks(start, half, first, second) for half in (0, 1)]
    lane = iota((WINDOW, LANES), 1) < HEAD
    for pair in range(pairs):
        ls = slice(pair * LANES, (pair + 1) * LANES)
        keys, values = key_groups(qkv_ref, halo_ref, width, pair, keep_first, keep_second, one_group)
        for half in (0, 1):
            rs = slice(half * WINDOW, (half + 1) * WINDOW)
            far_ok, near_ok, gated = masks[half]
            logits = mm(qkv_ref[rs, ls], jnp.concatenate(keys[half : half + 2], axis=0), NT)
            far, near = logits[:, :LANES], logits[:, LANES:]
            if half == 1:
                row = jnp.concatenate(
                    [imp_rows[2 * pair : 2 * pair + 1, :WINDOW], imp_rows[2 * pair + 1 : 2 * pair + 2, :WINDOW]], axis=1
                )
                gap = spread(late, pair, WINDOW) - row
                small = jnp.exp(-jnp.abs(gap))
                soft = jnp.maximum(gap, 0.0) + jnp.log(1.0 + small)
                sig_ref[:, ls] = (jnp.where(gap >= 0, 1.0, small) / (1.0 + small)).astype(BF)
                far = jnp.where(gated, far - soft, far)
            far = jnp.where(far_ok, far, NEGATIVE)
            near = jnp.where(near_ok, near, NEGATIVE)
            best = jnp.maximum(far, near)
            best_first = jnp.max(jnp.where(lane, best, NEGATIVE), axis=1, keepdims=True)
            best_second = jnp.max(jnp.where(lane, NEGATIVE, best), axis=1, keepdims=True)
            best = jnp.where(lane, best_first, best_second)
            far = jnp.exp(far - best)
            near = jnp.exp(near - best)
            weights = jnp.concatenate([far.astype(BF), near.astype(BF)], axis=1)
            mixed = mm(weights, jnp.concatenate(values[half : half + 2], axis=0))
            inverse = 1.0 / mixed[:, LANES:]
            att_ref[rs, ls] = (mixed[:, :LANES] * inverse).astype(BF)
            probs_ref[rs, 2 * pair * LANES : (2 * pair + 1) * LANES] = (far * inverse).astype(BF)
            probs_ref[rs, (2 * pair + 1) * LANES : (2 * pair + 2) * LANES] = (near * inverse).astype(BF)


def project_kernel(att_ref, x_ref, weight_ref, table_ref, middle_ref, second_ref):
    middle = x_ref[...].astype(F32) + mm(att_ref[...], weight_ref[...]) + table_ref[BIAS_OUT : BIAS_OUT + 1]
    middle_ref[...] = middle
    second_ref[...] = (normalise(middle)[0] * table_ref[GAIN2 : GAIN2 + 1] + table_ref[SHIFT2 : SHIFT2 + 1]).astype(BF)


def feed_kernel(info, sec_ref, dy_ref, fc_ref, down_ref, table_ref, hid_ref, dpre_ref, db_ref, keep_ref, give_ref, *, chunk):
    fc = fc_ref[...]
    down = down_ref[...]
    row = BIAS_FC + chunk * BLOCKS + pl.program_id(0)
    pre = mm(sec_ref[...], fc) + table_ref[pl.ds(row, 1)]
    d_hidden = mm(dy_ref[...], down, NT)
    square = pre * pre
    tanh = jnp.tanh(pre * (GELU_A + GELU_A * GELU_B * square))
    half = 0.5 + 0.5 * tanh
    hidden = (pre * half).astype(BF)
    slope = half + pre * (0.5 * GELU_A + 1.5 * GELU_A * GELU_B * square) * (1.0 - tanh * tanh)
    d_pre = d_hidden * slope
    d_low = d_pre.astype(BF)
    hid_ref[...] = hidden
    dpre_ref[...] = d_low
    db_ref[...] = jnp.broadcast_to(jnp.sum(d_pre, axis=0, keepdims=True), db_ref.shape)
    d_down = mm(hidden, dy_ref[...], TN).astype(BF)
    d_fc = mm(sec_ref[...], d_low, TN).astype(BF)

    @pl.when(info[1] == 0)
    def _():
        keep_ref[...] = d_fc
        give_ref[...] = d_down

    @pl.when(info[1] != 0)
    def _():
        keep_ref[...] = d_down
        give_ref[...] = d_fc


def feed_add_kernel(info, kept_ref, got_ref, keep_ref, give_ref, held):
    shards, rows, wide = held.shape
    width = kept_ref.shape[1]
    me = info[2]
    per_block = shards // BLOCKS
    deep = width // per_block

    def put(core):
        for block in range(BLOCKS):
            at = slice(block * width, (block + 1) * width)
            total = add(kept_ref[at], got_ref[at])
            if core == 0:
                for shard in range(shards):
                    held[ranked(shards, 0, me ^ shard), :, at] = total[shard * rows : (shard + 1) * rows]
            else:
                for k in range(per_block):
                    place = ranked(shards, 1, me ^ (block * per_block + k))
                    for part in range(deep // rows):
                        begin = k * deep + part * rows
                        held[place, :, part * width : (part + 1) * width] = total[begin : begin + rows]

    @pl.when(info[1] == 0)
    def _():
        put(0)

    @pl.when(info[1] != 0)
    def _():
        put(1)

    half = shards // 2
    keep_ref[...] = held[:half]
    give_ref[...] = held[half:]


def ranked(shards, core, far):
    order = bit_orders(shards)[core]
    index = jnp.int32(0)
    for step, bit in enumerate(order):
        index = index | (((far >> bit) & 1) << (len(order) - 1 - step))
    return index


def middle_kernel(*refs):
    dpre_refs = refs[:CHUNKS]
    fc_refs = refs[CHUNKS : 2 * CHUNKS]
    middle_ref, dy_ref, table_ref, dmid_ref, branch_ref, sums_ref = refs[2 * CHUNKS :]
    part_rows = middle_ref.shape[0] // 2
    totals = [0.0] * 4
    for part in range(2):
        rs = slice(part * part_rows, (part + 1) * part_rows)
        d_norm = None
        for dpre_ref, fc_ref in zip(dpre_refs, fc_refs):
            piece = mm(dpre_ref[rs], fc_ref[...], NT)
            d_norm = piece if d_norm is None else d_norm + piece
        unit, scale = normalise(middle_ref[rs])
        dy = dy_ref[rs].astype(F32)
        d_middle = dy + norm_back(d_norm, unit, scale, table_ref[GAIN2 : GAIN2 + 1])
        dmid_ref[rs] = d_middle
        branch = d_middle.astype(BF)
        branch_ref[rs] = branch
        for k, value in enumerate((d_norm * unit, d_norm, branch.astype(F32), dy)):
            totals[k] = totals[k] + jnp.sum(value, axis=0, keepdims=True)

    @pl.when(pl.program_id(0) == 0)
    def _():
        for k in range(4):
            sums_ref[k : k + 1] = totals[k]

    @pl.when(pl.program_id(0) > 0)
    def _():
        for k in range(4):
            sums_ref[k : k + 1] += totals[k]


def branch_kernel(info, branch_ref, att_ref, weight_ref, datt_ref, keep_ref, give_ref):
    shards, rows, split = keep_ref.shape
    store_halves(info, mm(att_ref[...], branch_ref[...], TN), keep_ref, give_ref, shards, rows, split)
    datt_ref[...] = mm(branch_ref[...], weight_ref[...], NT).astype(BF)


def store_halves(info, total, keep_ref, give_ref, shards, rows, split):
    me = info[2]

    def store(side, to):
        for shard in range(shards):
            value = total[shard * rows : (shard + 1) * rows, side * split : (side + 1) * split]
            to[ranked(shards, side, me ^ shard)] = value.astype(BF)

    @pl.when(info[1] == 0)
    def _():
        store(0, keep_ref)
        store(1, give_ref)

    @pl.when(info[1] != 0)
    def _():
        store(1, keep_ref)
        store(0, give_ref)


def attention_back_kernel(info, bounds, qkv_ref, halo_ref, att_ref, datt_ref, probs_ref, sig_ref, inv_ref, imp_ref, before_ref, dqkv_ref, dhalo_ref, dimp_ref, total_ref, rows_scratch, *, first_seq, pairs):
    s = first_seq + pl.program_id(0)
    blocks, width = att_ref.shape
    start = info[0]
    first, second = bounds[0, s], bounds[1, s]
    keep_first, keep_second = lane_masks()
    one_group = grouped(jnp.ones((WINDOW, LANES), BF), keep_first, keep_second)
    lane = iota((WINDOW, LANES), 1) < HEAD
    gated = (iota((WINDOW, LANES), 1) & (HEAD - 1)) <= iota((WINDOW, LANES), 0)
    head_lane = iota((LANES, LANES), 1)
    head_row = iota((LANES, LANES), 0)
    d_threshold = jnp.zeros((WINDOW, LANES), F32)
    rows_scratch[...] = jnp.zeros_like(rows_scratch)
    wide = pairs * LANES
    for k in range(pairs):
        pair = k
        ls = slice(pair * LANES, (pair + 1) * LANES)
        keys, values = key_groups(qkv_ref, halo_ref, width, pair, keep_first, keep_second, one_group)
        far_keys, near_keys, far_values, near_values = [], [], [], []
        for half in (0, 1):
            rs = slice(half * WINDOW, (half + 1) * WINDOW)
            d_out = datt_ref[rs, ls]
            product = (-(d_out.astype(F32) * att_ref[rs, ls].astype(F32))).astype(BF)
            left = jnp.concatenate([d_out, product], axis=1)
            centred = mm(left, jnp.concatenate(values[half : half + 2], axis=0), NT)
            probs = probs_ref[rs, 2 * pair * LANES : (2 * pair + 2) * LANES]
            d_logits = probs.astype(F32) * centred
            low = d_logits.astype(BF)
            dqkv_ref[rs, k * LANES : (k + 1) * LANES] = (mm(low, jnp.concatenate(keys[half : half + 2], axis=0)) * SCALE).astype(BF)
            d_keys = mm(low, qkv_ref[rs, ls], TN)
            d_values = mm(probs, d_out, TN)
            far_keys.append(jnp.where(lane, d_keys[:WINDOW], d_keys[WINDOW : 2 * WINDOW]))
            near_keys.append(jnp.where(lane, d_keys[2 * WINDOW : 3 * WINDOW], d_keys[3 * WINDOW :]))
            far_values.append(jnp.where(lane, d_values[:WINDOW], d_values[WINDOW : 2 * WINDOW]))
            near_values.append(jnp.where(lane, d_values[2 * WINDOW : 3 * WINDOW], d_values[3 * WINDOW :]))
            if half == 1:
                gate = jnp.where(gated, d_logits[:, :LANES] * sig_ref[:, ls].astype(F32), 0.0)
                rows_scratch[pair : pair + 1, :] = jnp.sum(gate, axis=0, keepdims=True)
                chosen = (head_lane == 2 * pair + (head_row >= HEAD).astype(jnp.int32)).astype(BF)
                d_threshold = d_threshold - mm(gate.astype(BF), chosen)
        ks = slice(wide + k * LANES, wide + (k + 1) * LANES)
        vs = slice(2 * wide + k * LANES, 2 * wide + (k + 1) * LANES)
        dhalo_ref[:, ks] = far_keys[0].astype(BF)
        dhalo_ref[:, vs] = far_values[0].astype(BF)
        dqkv_ref[:WINDOW, ks] = (near_keys[0] + far_keys[1]).astype(BF)
        dqkv_ref[WINDOW:, ks] = near_keys[1].astype(BF)
        dqkv_ref[:WINDOW, vs] = (near_values[0] + far_values[1]).astype(BF)
        dqkv_ref[WINDOW:, vs] = near_values[1].astype(BF)
    dhalo_ref[:, :wide] = jnp.zeros((WINDOW, wide), BF)
    weighted = d_threshold * inv_ref[...]
    row = iota((blocks, WINDOW), 0)
    col = iota((blocks, WINDOW), 1) + WINDOW
    after = (col >= row) & (segment(start + row, first, second) == segment(start + col, first, second))
    later = mm_split(after.astype(BF), weighted)
    total_ref[0, 0:1, :] = later[0:1]
    turned = rows_scratch[...].T
    pick_first = (head_lane == 2 * head_row).astype(BF)
    pick_second = (head_lane == 2 * head_row + 1).astype(BF)

    def pick(values, chosen):
        high = values.astype(BF)
        return mm(high, chosen) + mm((values - high.astype(F32)).astype(BF), chosen)

    direct = pick(turned[:HEAD], pick_first) + pick(turned[HEAD:], pick_second)
    local = jnp.exp(imp_ref[...] - before_ref[0, 0:1, :]) * later
    dimp_ref[:WINDOW] = local[:WINDOW] + direct
    dimp_ref[WINDOW:] = local[WINDOW:]


def tail_back_kernel(*refs):
    dhalo_refs = refs[:-5]
    weight_ref, x_ref, table_ref, out_ref, sums_ref = refs[-5:]
    width = x_ref.shape[1]
    begin = 0
    totals = [0.0, 0.0]
    for dhalo_ref in dhalo_refs:
        rs = slice(begin, begin + dhalo_ref.shape[0])
        begin += dhalo_ref.shape[0]
        d_norm = mm(dhalo_ref[:, width:], weight_ref[:, width:], NT)
        unit, scale = normalise(x_ref[rs].astype(F32))
        out_ref[rs] = norm_back(d_norm, unit, scale, table_ref[GAIN1 : GAIN1 + 1]).astype(BF)
        for k, value in enumerate((d_norm * unit, d_norm)):
            totals[k] = totals[k] + jnp.sum(value, axis=0, keepdims=True)
    for k in range(2):
        sums_ref[k : k + 1] = totals[k]


def qkv_grad_kernel(info, normed_ref, tail_ref, *refs, groups):
    dqkv_refs, dhalo_refs = refs[:groups], refs[groups : 2 * groups]
    give_ref, keep_ref, given_sums, kept_sums = refs[2 * groups :]
    shards, rows, split = keep_ref.shape
    me = info[2]
    step = pl.program_id(0)
    owner = jnp.where(step == 0, 1 - info[1], info[1])
    total, sums = 0.0, 0.0
    for left_ref, right_refs in ((normed_ref, dqkv_refs), (tail_ref, dhalo_refs)):
        begin = 0
        for right_ref in right_refs:
            rs = slice(begin, begin + right_ref.shape[0])
            begin += right_ref.shape[0]
            total = total + mm(left_ref[rs], right_ref[...], TN)
            sums = sums + jnp.sum(right_ref[...].astype(F32), axis=0, keepdims=True)

    def store(to, sums_to):
        sums_to[0:1] = sums
        for shard in range(shards):
            far = me ^ shard
            place = jnp.where(owner == 0, ranked(shards, 0, far), ranked(shards, 1, far))
            to[place] = total[shard * rows : (shard + 1) * rows].astype(BF)

    @pl.when(step == 0)
    def _():
        store(give_ref, given_sums)

    @pl.when(step != 0)
    def _():
        store(keep_ref, kept_sums)


def input_grad_kernel(info, bounds, *refs, groups):
    dqkv_refs, dimp_refs = refs[:groups], refs[groups : 2 * groups]
    weight_ref, score_ref, normed_ref, x_ref, table_ref, dmid_ref, back_ref, imp_ref, before_ref, after_ref, out_ref, sums_ref, score_out_ref = refs[2 * groups :]
    i = pl.program_id(0)
    per_group = pl.num_programs(0) // groups
    seqs = back_ref.shape[0]
    blocks = x_ref.shape[0] // seqs
    start = info[0]

    def chosen(refs):
        value = refs[0][...]
        for k in range(1, groups):
            value = jnp.where(i >= k * per_group, refs[k][...], value)
        return value

    dqkv, d_local = chosen(dqkv_refs), chosen(dimp_refs)
    d_imps = []
    for s in range(seqs):
        rs = slice(s * blocks, (s + 1) * blocks)
        first, second = bounds[0, i * seqs + s], bounds[1, i * seqs + s]
        place = start + iota((blocks, LANES), 0)
        onward = segment(place, first, second) == segment(jnp.full((1, LANES), start + blocks, jnp.int32), first, second)
        extra = jnp.exp(imp_ref[rs] - before_ref[s, 0:1, :]) * after_ref[s, 0:1, :]
        d_imps.append(d_local[rs] + jnp.where(onward, extra, 0.0))
    d_imp = jnp.concatenate(d_imps, axis=0).astype(BF)
    d_norm = mm(dqkv, weight_ref[...], NT) + mm(d_imp, score_ref[...])
    unit, scale = normalise(x_ref[...].astype(F32))
    d_value = norm_back(d_norm, unit, scale, table_ref[GAIN1 : GAIN1 + 1]) + dmid_ref[...]
    for s in range(seqs):
        rs = slice(s * blocks, s * blocks + WINDOW)
        out_ref[rs] = d_value[rs]
        rs = slice(s * blocks + WINDOW, (s + 1) * blocks)
        out_ref[rs] = d_value[rs] + back_ref[s].astype(F32)
    sums = [jnp.sum(value, axis=0, keepdims=True) for value in (d_norm * unit, d_norm)]
    score = mm(d_imp, normed_ref[...], TN)

    @pl.when(i == 0)
    def _():
        score_out_ref[...] = score
        for k in range(2):
            sums_ref[k : k + 1] = sums[k]

    @pl.when(i > 0)
    def _():
        score_out_ref[...] += score
        for k in range(2):
            sums_ref[k : k + 1] += sums[k]


def output_kernel(*refs):
    hid_refs, down_refs, (middle_ref, table_ref, out_ref) = refs[:CHUNKS], refs[CHUNKS : 2 * CHUNKS], refs[2 * CHUNKS :]
    total = middle_ref[...] + table_ref[BIAS_DOWN : BIAS_DOWN + 1]
    for hid_ref, down_ref in zip(hid_refs, down_refs):
        total = total + mm(hid_ref[...], down_ref[...])
    out_ref[...] = total.astype(BF)


def small_pack_kernel(info, first_ref, tail_ref, second_ref, kept_ref, given_ref, *refs):
    bias_refs = refs[:CHUNKS]
    score_ref, out_ref, whole = refs[CHUNKS:]
    shards, count, rows = out_ref.shape
    me = info[2]
    whole[0:2] = first_ref[0:2] + tail_ref[0:2]
    whole[2:VECTORS] = second_ref[0 : VECTORS - 2]
    width = whole.shape[1]
    even = info[1] == 0
    whole[VECTORS : VECTORS + 1] = jnp.where(even, kept_ref[0:1, :width], given_ref[0:1, :width])
    whole[VECTORS + 1 : VECTORS + 2] = jnp.where(even, given_ref[0:1, width // 2 :], kept_ref[0:1, width // 2 :])
    base = VECTORS + 2
    for k in range(CHUNKS * BLOCKS):
        whole[base + k : base + k + 1] = bias_refs[k // BLOCKS][0:1, (k % BLOCKS) * width : (k % BLOCKS + 1) * width]
    heads = count - VECTORS - QV_ROWS - FC_ROWS
    whole[base + CHUNKS * BLOCKS : base + CHUNKS * BLOCKS + heads] = score_ref[0:heads]
    per_block = shards // BLOCKS
    per_chunk = FC_ROWS // CHUNKS
    for shard in range(shards):
        at = slice(shard * rows, (shard + 1) * rows)
        lines = [whole[0:VECTORS, at]]
        row = VECTORS + shard // (shards // 2)
        for k in range(QV_ROWS):
            begin = (shard % (shards // 2)) * QV_ROWS * rows + k * rows
            lines.append(whole[row : row + 1, begin : begin + rows])
        for chunk in range(CHUNKS):
            row = base + chunk * BLOCKS + shard // per_block
            for k in range(per_chunk):
                begin = (shard % per_block) * per_chunk * rows + k * rows
                lines.append(whole[row : row + 1, begin : begin + rows])
        lines.append(whole[base + CHUNKS * BLOCKS : base + CHUNKS * BLOCKS + heads, at])
        out_ref[ranked(shards, 0, me ^ shard)] = jnp.concatenate(lines, axis=0)


def add(left, right):
    return (left.astype(F32) + right.astype(F32)).astype(BF)


def combine(peak_a, total_a, peak_b, total_b):
    joined = jnp.maximum(peak_a, peak_b)
    return joined, total_a * jnp.exp(peak_a - joined) + total_b * jnp.exp(peak_b - joined)


def tie(*values):
    return lax.optimization_barrier(values)


class Net:
    def __init__(self):
        self.n_seq = lax.axis_size("seq")
        self.n_dp = lax.axis_size("dp")
        self.seq = lax.axis_index("seq")
        self.dp = lax.axis_index("dp")
        self.core = self.seq % 2
        self.orders = bit_orders(self.n_dp)
        self.bits = len(self.orders[0])
        self.seq_bits = self.n_seq.bit_length() - 1
        self.by_pair = self.bits == 2 and self.seq_bits >= 2

    def send(self, value, target):
        pairs = []
        for s in range(self.n_seq):
            for d in range(self.n_dp):
                goal = target(s, d)
                if 0 <= goal[0] < self.n_seq:
                    pairs.append((s * self.n_dp + d, goal[0] * self.n_dp + goal[1]))
        return lax.ppermute(value, ("seq", "dp"), pairs)

    def across(self, value, step):
        return self.send(value, lambda s, d: (s, d ^ (1 << self.orders[s % 2][step])))

    def chip(self, value):
        return self.send(value, lambda s, d: (s ^ 1, d))

    def along(self, value, bit):
        return self.send(value, lambda s, d: (s ^ (1 << bit), d))

    def masked(self, value, mask):
        return self.send(value, lambda s, d: (s ^ mask, d))

    def shifted(self, value, by):
        return self.send(value, lambda s, d: (s + by, d))

    def across_pair(self, value, step):
        return self.send(value, lambda s, d: (s, d ^ (1 << self.orders[(s ^ (s >> 1)) % 2][step])))

    def gather_step(self, pieces, step):
        return pieces + [self.across(piece, step) for piece in pieces]

    def sum_all(self, value):
        value = value + self.chip(value)
        for step in range(self.bits):
            value = value + self.across(value, step)
        for bit in range(1, self.seq_bits):
            value = value + self.along(value, bit)
        return value


class Reduction:
    def __init__(self, net, keep, give):
        self.net = net
        self.keep, self.give = keep, give
        z_bits = list(range(1, net.seq_bits))
        self.z_orders = (z_bits, z_bits[1:2] + z_bits[:1] + z_bits[2:])
        self.todo = ["across"] * net.bits + ["split"] + ["swap"] * (len(z_bits) - 1) + ["join"]
        self.done = 0
        self.got = None
        self.pending = False

    def along(self, value, place):
        return self.net.send(value, lambda s, d: (s ^ (1 << self.z_orders[s % 2][place]), d))

    def start(self):
        if not self.todo:
            return
        kind = self.todo[0]
        self.pending = True
        if kind == "across":
            self.got = self.net.across(self.give, self.done)
        elif kind == "split":
            half = self.keep.shape[0] // 2
            z_bit = jnp.where(self.net.core == 0, self.z_orders[0][0], self.z_orders[1][0])
            self.upper = (self.net.seq >> z_bit) % 2 == 1
            low, high = self.keep[:half], self.keep[half:]
            self.got = self.along(jnp.where(self.upper, low, high), 0)
            self.keep = jnp.where(self.upper, high, low)
        elif kind == "swap":
            self.got = self.along(self.keep, self.done - self.net.bits)
        else:
            self.got = self.along(self.keep, 0)

    def finish(self, after=None):
        if not self.pending:
            return
        if after is not None:
            self.got, _ = tie(self.got, after)
        kind = self.todo.pop(0)
        self.done += 1
        self.pending = False
        if kind == "join":
            low, high = jnp.where(self.upper, self.got, self.keep), jnp.where(self.upper, self.keep, self.got)
            self.keep = jnp.concatenate([low, high], axis=0)
            return
        total = add(self.keep, self.got)
        if kind == "across":
            half = total.shape[0] // 2
            if half:
                self.keep, self.give = total[:half], total[half:]
            else:
                self.keep = total[0]
        else:
            self.keep = total


def pin(value, *reds):
    held = [value]
    for red in reds:
        held += [red.keep] + ([red.give] if red.todo and red.todo[0] == "across" else [])
    held = list(tie(*held))
    value = held.pop(0)
    for red in reds:
        red.keep = held.pop(0)
        if red.todo and red.todo[0] == "across":
            red.give = held.pop(0)
    return value


def body(block_input, doc_bounds, first_gain, first_shift, qkv_weight, qv_bias, score_weight, out_weight, out_bias, second_gain, second_shift, fc_weight, fc_bias, down_weight, down_bias, cotangent):
    net = Net()
    seqs, blocks, width = block_input.shape
    tokens = seqs * blocks
    heads = score_weight.shape[1]
    shards = net.n_dp
    rows = width // shards
    hidden = fc_weight.shape[1]
    tail = seqs * WINDOW
    core = net.core
    place = jnp.arange(4, dtype=jnp.int32)
    info = jnp.where(place == 0, net.seq * blocks, jnp.where(place == 1, core, jnp.where(place == 2, net.dp, net.seq))).astype(jnp.int32)
    bounds = doc_bounds.T
    x_flat = block_input.reshape(tokens, width)
    dy = cotangent.reshape(tokens, width)
    wide = hidden // CHUNKS
    deep = hidden // shards // CHUNKS
    half_qkv = 3 * width // 2
    sems = lambda count: pltpu.SemaphoreType.DMA((count,))
    by_seq = lambda rows_, cols: pl.BlockSpec((rows_, cols), lambda s, *_: (s, 0))
    stat = pl.BlockSpec((1, 8, LANES), lambda s, *_: (s, 0, 0))
    table_spec = whole_spec((16, width))
    full = whole_spec((tokens, width))
    tile = 2 * blocks
    by_tile = pl.BlockSpec((tile, width), lambda i, *_: (i, 0))
    pairs = width // LANES
    parts = [(0, pairs)]

    vectors = [first_gain, first_shift, second_gain, second_shift, out_bias, down_bias, qv_bias, fc_bias]
    small_rows = sum(part.shape[0] for part in vectors) // rows + heads
    small = call(
        start_kernel,
        "start",
        (1,),
        [pl.BlockSpec(part.shape, lambda *_: (0,)) for part in vectors] + [whole_spec((heads, rows))],
        whole_spec((small_rows, rows)),
        shape((small_rows, rows), BF),
        micros=1,
        far_in=tuple(range(len(vectors) + 1)),
    )(*vectors, score_weight.T)

    def begin_gather(own):
        return [own, net.across(own, 0)], [net.across(own, 1)] if net.bits > 1 else []

    def end_gather(pieces, ahead):
        if net.bits > 1:
            pieces = pieces + ahead + [net.across(pieces[1], 1)]
        for step in range(2, net.bits):
            pieces = net.gather_step(pieces, step)
        return pieces

    small_state = begin_gather(small)
    first_weight, _ = tie(qkv_weight, small)
    own, x_tail = call(
        first_pack_kernel,
        "first_pack",
        (1,),
        [pl.BlockSpec((rows, half_qkv), lambda _, info: (0, info[1])), pl.BlockSpec((seqs, WINDOW, width), lambda *_: (0, blocks // WINDOW - 1, 0))],
        [whole_spec((rows, half_qkv)), whole_spec((tail, width))],
        [shape((rows, half_qkv), BF), shape((tail, width), BF)],
        prefetch=1,
        micros=2,
        far_in=(0, 1),
    )(info, first_weight, block_input)
    own, x_tail, *held = tie(own, x_tail, *small_state[0], *small_state[1])
    small_pieces = end_gather(held[:2], held[2:])
    qkv_state = begin_gather(own)
    x_tail = net.shifted(x_tail, 1)
    qkv_pieces = end_gather(*qkv_state)

    fc_weight, _ = tie(fc_weight, own)
    packs = call(
        feed_pack_kernel,
        "feed_pack",
        (1,),
        [whole_spec((rows, hidden)), whole_spec(down_weight.shape), whole_spec((rows, width))],
        [whole_spec((rows, wide))] * CHUNKS + [whole_spec((rows, wide + width // 2)), whole_spec((rows, wide))],
        [shape((rows, wide), BF)] * CHUNKS + [shape((rows, wide + width // 2), BF), shape((rows, wide), BF)],
        prefetch=1,
        micros=2,
        limit=24,
        far_in=(0, 1, 2),
    )(info, fc_weight, down_weight, out_weight)
    fc_own, feed_own = packs[:CHUNKS], packs[CHUNKS:]
    small_pieces[-1], *feed_own = tie(small_pieces[-1], *feed_own)
    first_own, _ = tie(feed_own[0], qkv_pieces[1])

    def begin_feed(own):
        if not net.by_pair:
            return begin_gather(own)
        return [own, net.across_pair(own, 0)], []

    def end_feed(pieces, ahead):
        if not net.by_pair:
            return end_gather(pieces, ahead)
        return pieces + [net.masked(pieces[1], 2), net.across_pair(pieces[1], 1)]

    a_state = begin_feed(first_own)

    table, score = call(
        params_kernel,
        "params",
        (1,),
        [whole_spec((small_rows, rows))] * shards,
        [table_spec, whole_spec((LANES, width))],
        [shape((16, width), F32), shape((LANES, width), BF)],
        scratch=[pltpu.VMEM((shards, small_rows, rows), F32)],
        prefetch=1,
        micros=1,
    )(info, *small_pieces)

    group = seqs // 2
    normed, importance, mass, stats = call(
        prep_kernel,
        "prep",
        (seqs // group,),
        [by_seq(group * blocks, width), table_spec, whole_spec((LANES, width))],
        [by_seq(group * blocks, width), by_seq(group * blocks, LANES), by_seq(group * blocks, LANES), pl.BlockSpec((group, 8, LANES), lambda s, *_: (s, 0, 0))],
        [shape((tokens, width), BF), shape((tokens, LANES), F32), shape((tokens, LANES), F32), shape((seqs, 8, LANES), F32)],
        prefetch=2,
        micros=3,
    )(info, bounds, x_flat, table, score)

    def scan_step(state, masks, got):
        spec = whole_spec((seqs, 8, LANES))
        return call(
            lambda *refs: scan_kernel(*refs, masks=masks),
            "scan",
            (1,),
            [spec] * (1 + len(masks)),
            spec,
            shape((seqs, 8, LANES), F32),
            prefetch=1,
            micros=0.5,
        )(info, state, *got)

    for bit in range(net.seq_bits - 1):
        stats = scan_step(stats, [1 << bit], [net.along(stats, bit)])
        if bit == 0:
            stats, *qkv_pieces = tie(stats, *qkv_pieces)
    qkv_others = [net.chip(piece) for piece in qkv_pieces[1:]]
    w_qkv = call(
        qkv_build_kernel,
        "qkv_build",
        (1,),
        [whole_spec((rows, 3 * width))] + [whole_spec((rows, half_qkv))] * (2 * shards - 2),
        ANY,
        shape((width, 3 * width), BF),
        scratch=[sems(2 * shards)],
        prefetch=1,
        micros=2,
    )(info, qkv_weight, *qkv_pieces[1:], *qkv_others)

    def build_feed(chunk, pieces, others):
        with_out = chunk == 0
        owns = [fc_own[chunk], down_weight] + ([out_weight] if with_out else [])
        specs = [whole_spec((rows, wide)), pl.BlockSpec((deep, width), lambda *_: (chunk, 0))] + ([whole_spec((rows, width))] if with_out else [])
        outs = [shape((width, wide), BF), shape((wide, width), BF)] + ([shape((width, width), BF)] if with_out else [])
        count = 3 + (shards - 1) * (1 + deep // rows + 2)
        return call(
            lambda *refs: feed_build_kernel(*refs, with_out=with_out, by_pair=net.by_pair),
            "feed_build",
            (1,),
            specs + [whole_spec(pieces[0].shape)] * (2 * shards - 2),
            [ANY] * len(outs),
            outs,
            scratch=[sems(count)],
            prefetch=1,
            micros=2,
        )(info, *owns, *pieces[1:], *others)

    normed_tail = call(
        prep_tail_kernel,
        "prep_tail",
        (1,),
        [whole_spec((tail, width)), table_spec],
        whole_spec((tail, width)),
        shape((tail, width), BF),
        micros=1,
    )(x_tail, table)
    w_qkv, *held = tie(w_qkv, *a_state[0], *a_state[1])
    a_pieces = end_feed(held[:2], held[2:])
    second_own, _ = tie(feed_own[1], held[1])
    b_state = begin_feed(second_own)
    col = lambda rows_: pl.BlockSpec((rows_, width), lambda j: (0, j))
    qkv, qkv_tail = call(
        qkv_kernel,
        "qkv",
        (3,),
        [full, whole_spec((tail, width)), col(width), table_spec],
        [col(tokens), pl.BlockSpec((tail, width), lambda j: (0, jnp.maximum(j - 1, 0)))],
        [shape((tokens, 3 * width), BF), shape((tail, 2 * width), BF)],
        micros=6.5,
        limit=24,
    )(normed, normed_tail, w_qkv, table)
    qkv, got = tie(qkv, net.along(stats, net.seq_bits - 1))
    before = scan_step(stats, [1 << (net.seq_bits - 1)], [got])

    attended, probs, gates, inverse = call(
        attention_kernel,
        "attention",
        (seqs,),
        [by_seq(blocks, 3 * width), by_seq(WINDOW, 2 * width), by_seq(blocks, LANES), by_seq(blocks, LANES), stat],
        [by_seq(blocks, width), by_seq(blocks, 2 * width), by_seq(WINDOW, width), by_seq(WINDOW, LANES)],
        [shape((tokens, width), BF), shape((tokens, 2 * width), BF), shape((tail, width), BF), shape((tail, LANES), F32)],
        prefetch=2,
        micros=10.5,
        far=(1, 2, 3),
    )(info, bounds, qkv, qkv_tail, importance, mass, before)

    attended, *held = tie(attended, *a_pieces, *b_state[0], *b_state[1])
    a_pieces, held = held[: len(a_pieces)], held[len(a_pieces) :]
    b_pieces = end_feed(held[:2], held[2:])
    fc_a, down_a, w_out = build_feed(0, a_pieces, [net.chip(piece) for piece in a_pieces[1:]])

    middle, normed_second = call(
        project_kernel,
        "project",
        (tokens // tile,),
        [by_tile, by_tile, whole_spec((width, width)), table_spec],
        [by_tile, by_tile],
        [shape((tokens, width), F32), shape((tokens, width), BF)],
        micros=3,
    )(attended, x_flat, w_out, table)

    hids, dpres, d_fc_bias = [], [], []

    def feed(chunk, fc, down, normed_second):
        still = pl.BlockSpec((tokens, width), lambda *_: (0, 0), pipeline_mode=pl.Buffered(1))
        column = lambda rows_: pl.BlockSpec((rows_, width), lambda j, *_: (0, j))
        row = pl.BlockSpec((width, width), lambda j, *_: (j, 0))
        hid, dpre, d_bias, keep, give = call(
            lambda *refs: feed_kernel(*refs, chunk=chunk),
            "feed",
            (BLOCKS,),
            [still, still, column(width), row, table_spec],
            [column(tokens), column(tokens), column(8), row, row],
            [shape((tokens, wide), BF), shape((tokens, wide), BF), shape((8, wide), F32), shape((wide, width), BF), shape((wide, width), BF)],
            prefetch=1,
            micros=15,
            limit=34,
            far=(0, 1, 3, 4),
        )(info, normed_second, dy, fc, down, table)
        hids.append(hid)
        dpres.append(dpre)
        d_fc_bias.append(d_bias)
        return keep, give

    def feed_add(kept, got):
        half = (shards // 2, rows, wide)
        keep, give = call(
            feed_add_kernel,
            "feed_add",
            (1,),
            [whole_spec((wide, width))] * 2,
            [whole_spec(half)] * 2,
            [shape(half, BF)] * 2,
            scratch=[pltpu.VMEM((shards, rows, wide), BF)],
            prefetch=1,
            micros=2,
            limit=20,
        )(info, kept, got)
        return Reduction(net, keep, give)

    b_first = net.chip(b_pieces[1])
    normed_second, b_first = tie(normed_second, b_first)
    kept_a, give_a = feed(0, fc_a, down_a, normed_second)
    give_a, *b_pieces = tie(give_a, *b_pieces)
    got_a = net.chip(give_a)
    fc_b, down_b = build_feed(1, b_pieces, [b_first] + [net.chip(piece) for piece in b_pieces[2:]])
    red_a = feed_add(kept_a, got_a)
    fc_b = pin(fc_b, red_a)
    red_a.start()
    kept_b, give_b = feed(1, fc_b, down_b, normed_second)
    got_b = net.chip(give_b)
    red_a.finish(kept_b)
    dpres[1] = pin(dpres[1], red_a)
    red_a.start()

    half_out = (shards, rows, width // 2)
    groups = 2
    part_tokens, part_tail, part_seqs = tokens // groups, tail // groups, seqs // groups
    by_part = pl.BlockSpec((part_tokens, width), lambda i, *_: (i, 0))
    d_middle, branch, sums_second = call(
        middle_kernel,
        "middle",
        (groups,),
        [pl.BlockSpec((part_tokens, wide), lambda i, *_: (i, 0))] * CHUNKS + [whole_spec((width, wide))] * CHUNKS + [by_part, by_part, table_spec],
        [by_part, by_part, whole_spec((8, width))],
        [shape((tokens, width), F32), shape((tokens, width), BF), shape((8, width), F32)],
        micros=1.0,
        limit=36,
        far=(0,),
        far_in=(0, 1, 5),
    )(*dpres, fc_a, fc_b, middle, dy, table)

    red_a.finish(branch)
    red_b = feed_add(kept_b, got_b)
    branch = pin(branch, red_a, red_b)
    red_a.start()
    red_b.start()
    d_attended, keep_out, give_out = call(
        branch_kernel,
        "branch",
        (1,),
        [full, full, whole_spec((width, width))],
        [full, whole_spec(half_out), whole_spec(half_out)],
        [shape((tokens, width), BF), shape(half_out, BF), shape(half_out, BF)],
        prefetch=1,
        micros=1.0,
        limit=24,
    )(info, branch, attended, w_out)
    got_out = net.chip(give_out)

    def attention_back(part, d_attended):
        shifted = lambda rows_, cols: pl.BlockSpec((rows_, cols), lambda s, *_: (part * part_seqs + s, 0))
        return call(
            lambda *refs: attention_back_kernel(*refs, first_seq=part * part_seqs, pairs=pairs),
            "attention_back",
            (part_seqs,),
            [shifted(blocks, 3 * width), shifted(WINDOW, 2 * width), shifted(blocks, width), shifted(blocks, width), shifted(blocks, 2 * width), shifted(WINDOW, width), shifted(WINDOW, LANES), shifted(blocks, LANES), pl.BlockSpec((1, 8, LANES), lambda s, *_: (part * part_seqs + s, 0, 0))],
            [by_seq(blocks, 3 * width), by_seq(WINDOW, 3 * width), by_seq(blocks, LANES), pl.BlockSpec((1, 1, LANES), lambda s, *_: (s, 0, 0))],
            [shape((part_tokens, 3 * width), BF), shape((part_tail, 3 * width), BF), shape((part_tokens, LANES), F32), shape((part_seqs, 1, LANES), F32)],
            scratch=[pltpu.VMEM((LANES, LANES), F32)],
            prefetch=2,
            micros=0.1,
            far_in=(0, 1, 4, 5, 6),
        )(info, bounds, qkv, qkv_tail, attended, d_attended, probs, gates, inverse, importance, before)

    def qkv_grad(backs):
        side = lambda i, info: (0, jnp.where(i == 0, 1 - info[1], info[1]))
        result = (shards, rows, half_qkv)
        still = lambda rows_: pl.BlockSpec((rows_, width), lambda *_: (0, 0), pipeline_mode=pl.Buffered(1))
        held = lambda dims: pl.BlockSpec(dims, lambda *_: (0,) * len(dims), pipeline_mode=pl.Buffered(1))
        return call(
            lambda *refs: qkv_grad_kernel(*refs, groups=groups),
            "qkv_grad",
            (2,),
            [still(tokens), still(tail)] + [pl.BlockSpec((part_tokens, half_qkv), side)] * groups + [pl.BlockSpec((part_tail, half_qkv), side)] * groups,
            [held(result), held(result), held((8, half_qkv)), held((8, half_qkv))],
            [shape(result, BF), shape(result, BF), shape((8, half_qkv), F32), shape((8, half_qkv), F32)],
            prefetch=1,
            micros=2,
            limit=26,
            far=(0, 1),
        )(info, normed, normed_tail, *[back[0] for back in backs], *[back[1] for back in backs])

    half_shards = shards // 2

    def halved(total):
        return Reduction(net, total[:half_shards], total[half_shards:])

    red_o = halved(add(keep_out, got_out))
    d_attended = pin(d_attended, red_o)
    red_o.start()
    backs = [list(attention_back(0, d_attended))]
    red_a.finish(backs[0][0])
    d_attended, _ = tie(d_attended, backs[0][0])
    d_attended = pin(d_attended, red_a)
    red_a.start()
    backs.append(list(attention_back(1, d_attended)))
    red_a.finish()
    red_b.finish()
    red_o.finish()
    red_b.keep = jnp.concatenate([red_b.keep, red_o.keep], axis=2)
    red_b.give = jnp.concatenate([red_b.give, red_o.give], axis=2)
    backs[1][0] = pin(backs[1][0], red_a, red_b)
    red_a.start()
    red_b.start()
    total_all = jnp.concatenate([back[3] for back in backs], axis=0)
    total_after = jnp.zeros_like(total_all)

    def suffix_step(total_after, total_all, bit, after=None):
        got = net.along(total_all, bit)
        if after is not None:
            got, _ = tie(got, after)
        earlier = (net.seq >> bit) % 2 == 0
        return jnp.where(earlier, total_after + got, total_after), total_all + got

    give_qkv, keep_qkv, sums_given, sums_kept = qkv_grad(backs)

    total_after, total_all = suffix_step(total_after, total_all, 0, keep_qkv)
    red_a.finish(keep_qkv)
    red_b.finish(keep_qkv)
    give_qkv, total_all, total_after = tie(give_qkv, total_all, total_after)
    give_qkv = pin(give_qkv, red_a, red_b)
    got_qkv = net.chip(give_qkv)
    d_halos = [back[1] for back in backs]
    d_halos[0], _ = tie(d_halos[0], give_qkv)
    d_tail, sums_tail = call(
        tail_back_kernel,
        "tail_back",
        (1,),
        [whole_spec((part_tail, 3 * width))] * groups + [whole_spec((width, 3 * width)), whole_spec((tail, width)), table_spec],
        [whole_spec((tail, width)), whole_spec((8, width))],
        [shape((tail, width), BF), shape((8, width), F32)],
        micros=1,
        limit=32,
    )(*d_halos, w_qkv, x_tail, table)
    for bit in range(1, net.seq_bits - 1):
        total_after, total_all = suffix_step(total_after, total_all, bit, d_tail)
    got_qkv, _ = tie(got_qkv, d_tail)
    red_c = halved(add(keep_qkv, got_qkv))
    d_tail, total_all, total_after = tie(d_tail, total_all, total_after)
    d_tail = pin(d_tail, red_c)
    red_c.start()
    back = net.shifted(d_tail, -1).reshape(seqs, WINDOW, width)
    red_a.start()
    red_b.start()
    middle, d_tail = tie(middle, d_tail)
    block_output = call(
        output_kernel,
        "output",
        (tokens // tile,),
        [pl.BlockSpec((tile, wide), lambda i, *_: (i, 0))] * CHUNKS + [whole_spec((wide, width))] * CHUNKS + [by_tile, table_spec],
        by_tile,
        shape((tokens, width), BF),
        micros=1.0,
        limit=32,
        far_in=(0, 1, 2, 3, 4),
    )(*hids, down_a, down_b, middle, table)
    total_after, _ = suffix_step(total_after, total_all, net.seq_bits - 1, block_output)
    back, _ = tie(back, block_output)
    for red in (red_a, red_b, red_c):
        red.finish(block_output)
    total_after = pin(total_after, red_a, red_b, red_c)
    for red in (red_a, red_b, red_c):
        red.start()

    per_tile = tile // blocks
    per_group = tokens // tile // groups
    grouped_tile = lambda cols: [pl.BlockSpec((tile, cols), lambda i, *_, k=k: (jnp.clip(i - k * per_group, 0, per_group - 1), 0)) for k in range(groups)]
    by_lane = pl.BlockSpec((tile, LANES), lambda i, *_: (i, 0))
    input_grad, sums_first, d_score = call(
        lambda *refs: input_grad_kernel(*refs, groups=groups),
        "input_grad",
        (tokens // tile,),
        grouped_tile(3 * width)
        + grouped_tile(LANES)
        + [
            whole_spec((width, 3 * width)),
            whole_spec((LANES, width)),
            by_tile,
            by_tile,
            table_spec,
            by_tile,
            pl.BlockSpec((per_tile, WINDOW, width), lambda i, *_: (i, 0, 0)),
            by_lane,
            pl.BlockSpec((per_tile, 8, LANES), lambda i, *_: (i, 0, 0)),
            pl.BlockSpec((per_tile, 1, LANES), lambda i, *_: (i, 0, 0)),
        ],
        [by_tile, whole_spec((8, width)), whole_spec((LANES, width))],
        [shape((tokens, width), F32), shape((8, width), F32), shape((LANES, width), F32)],
        prefetch=2,
        micros=1.0,
        limit=28,
        far_in=tuple(2 * groups + k for k in (3, 5)),
    )(info, bounds, *[back_[0] for back_ in backs], *[back_[2] for back_ in backs], w_qkv, score, normed, x_flat, table, d_middle, back, importance, before, total_after)

    for red in (red_a, red_b, red_c):
        if red.pending:
            red.finish(sums_first)
            sums_first = pin(sums_first, red)
    packed = call(
        small_pack_kernel,
        "small_pack",
        (1,),
        [whole_spec((8, width))] * 3 + [whole_spec((8, half_qkv))] * 2 + [whole_spec((8, wide))] * CHUNKS + [whole_spec((LANES, width))],
        whole_spec((shards, small_rows, rows)),
        shape((shards, small_rows, rows), F32),
        scratch=[pltpu.VMEM((32, width), F32)],
        prefetch=1,
        micros=1,
    )(info, sums_first, sums_tail, sums_second, sums_kept, sums_given, *d_fc_bias, d_score)

    def finish(red):
        other = net.chip(red.keep)
        return jnp.where(core == 0, red.keep, other), jnp.where(core == 0, other, red.keep)

    def early_grads():
        fc_grads, down_grads = zip(finish(red_a), finish(red_b))
        out_grads = [fc_grads[1][:, wide:], down_grads[1][:, wide:]]
        fc_grads, down_grads = [part[:, :wide] for part in fc_grads], [part[:, :wide] for part in down_grads]
        d_out = jnp.concatenate(out_grads, axis=1).astype(F32)
        d_fc = jnp.concatenate([part[:, d * deep : (d + 1) * deep] for d in range(shards) for part in fc_grads], axis=1).astype(F32)
        d_down = jnp.concatenate([part[:, k * width : (k + 1) * width] for part in down_grads for k in range(deep // rows)], axis=0).astype(F32)
        return [d_out, d_fc, d_down]

    reds = [red_a, red_b, red_c]
    early = None
    packed = packed + net.chip(packed)

    def small_across(value, step):
        half = value.shape[0] // 2
        return value[:half] + net.send(value[half:], lambda s, d: (s, d ^ (1 << net.orders[0][step])))

    small_steps = [lambda value, k=k: small_across(value, k) for k in range(net.bits)]
    small_steps += [lambda value, k=k: value + net.along(value, k) for k in range(1, net.seq_bits)]
    while small_steps or any(red.todo for red in reds):
        active = [red for red in reds if red.pending]
        for red in active:
            red.finish()
        packed = pin(packed, *active)
        for red in reds:
            if red.todo:
                red.start()
        if early is None and not red_a.todo and not red_b.todo:
            early = early_grads()
        if small_steps:
            packed = small_steps.pop(0)(packed)
    packed, d_out, d_fc, d_down = tie(packed, *early)
    packed = packed[0]

    d_qkv = jnp.concatenate(finish(red_c), axis=1).astype(F32)

    small_outs = [shape(part.shape, F32) for part in vectors] + [shape((heads, rows), F32)]
    dg_first, ds_first, dg_second, ds_second, db_out, db_down, db_qv, db_fc, d_score = call(
        end_kernel,
        "end",
        (1,),
        [whole_spec((small_rows, rows))],
        [pl.BlockSpec(part.shape, lambda *_, n=len(part.shape): (0,) * n) for part in small_outs],
        small_outs,
        micros=1,
    )(packed)
    return (
        block_output.reshape(seqs, blocks, width),
        input_grad.reshape(seqs, blocks, width),
        dg_first,
        ds_first,
        d_qkv,
        db_qv,
        d_score.T,
        d_out,
        db_out,
        dg_second,
        ds_second,
        d_fc,
        db_fc,
        d_down,
        db_down,
    )


def solution(mesh):
    split = P("dp", "seq", None)
    rows = P("dp", None)
    flat = P("dp")
    in_specs = (split, rows, flat, flat, rows, flat, rows, rows, flat, flat, flat, rows, flat, rows, flat, split)
    out_specs = (split, split, flat, flat, rows, flat, rows, rows, flat, flat, flat, rows, flat, rows, flat)
    return jax.shard_map(body, mesh=mesh, in_specs=in_specs, out_specs=out_specs, check_vma=False)
```

```python
import math

import jax
import jax.numpy as jnp
from jax import lax
from jax.experimental import pallas as pl
from jax.experimental.pallas import tpu as pltpu
from jax.sharding import PartitionSpec as P

KTOP = 64
WINDOW = 64
HEAD = 64
LANES = 128
EPSILON = 1e-05
NEGATIVE = -1e30
SCALE = 1.0 / math.sqrt(HEAD)
GELU_A = math.sqrt(2.0 / math.pi)
GELU_B = 0.044715
BF = jnp.bfloat16
F32 = jnp.float32
NN = ((1,), (0,))
NT = ((1,), (1,))
TN = ((0,), (0,))
CHUNKS = 2
BLOCKS = 2
MIB = 2**20
FORWARD_STAGE = 3
BACKWARD_STAGE = 6
GAIN1, SHIFT1, GAIN2, SHIFT2, BIAS_OUT, BIAS_DOWN, BIAS_QKV, BIAS_FC = 0, 1, 2, 3, 4, 5, 6, 9
VECTORS = 6
QV_ROWS = 2
FC_ROWS = 4


def mm(left, right, dims=NN):
    return lax.dot_general(left, right, (dims, ((), ())), preferred_element_type=F32)


def mm_split(mask, value, dims=NN):
    high = value.astype(BF)
    low = (value - high.astype(F32)).astype(BF)
    return mm(mask, high, dims) + mm(mask, low, dims)


def whole_spec(shape):
    return pl.BlockSpec(shape, lambda *_: (0,) * len(shape))


ANY = pl.BlockSpec(memory_space=pl.ANY)


def call(kernel, name, grid, in_specs, out_specs, out_shape, scratch=(), prefetch=0, micros=1.0, limit=16, alias=None, far=(), far_in=(), near=(), near_in=()):
    many = isinstance(out_shape, (list, tuple))
    if grid == (1,):
        once = lambda spec: spec if spec.block_shape is None else pl.BlockSpec(spec.block_shape, spec.index_map, pipeline_mode=pl.Buffered(1))
        in_specs = [once(spec) for spec in in_specs]
        out_specs = [once(spec) for spec in out_specs] if many else once(out_specs)
    outs = [pltpu.HBM(one.shape, one.dtype) if k in far else pltpu.VMEM(one.shape, one.dtype) if k in near else one for k, one in enumerate(out_shape if many else [out_shape])]
    inner = pl.pallas_call(
        kernel,
        grid_spec=pltpu.PrefetchScalarGridSpec(
            num_scalar_prefetch=prefetch,
            grid=grid,
            in_specs=in_specs,
            out_specs=out_specs,
            scratch_shapes=list(scratch),
        ),
        out_shape=outs if many else outs[0],
        input_output_aliases=alias or {},
        compiler_params=pltpu.CompilerParams(vmem_limit_bytes=limit * MIB),
        cost_estimate=pl.CostEstimate(flops=int(micros * 1.1e9), bytes_accessed=1024, transcendentals=0),
        name=name,
    )

    def run(*operands):
        held = []
        for k, one in enumerate(operands):
            if k - prefetch in far_in:
                one = pltpu.with_memory_space_constraint(one, pltpu.HBM)
            elif k - prefetch in near_in:
                one = pltpu.with_memory_space_constraint(one, pltpu.VMEM)
            held.append(one)
        return inner(*held)

    return run


def shape(dims, kind):
    return jax.ShapeDtypeStruct(dims, kind)


def iota(dims, axis):
    return lax.broadcasted_iota(jnp.int32, dims, axis)


def segment(places, first, second):
    return (places >= first).astype(jnp.int32) + (places >= second).astype(jnp.int32)


def normalise(values):
    average = jnp.mean(values, axis=-1, keepdims=True)
    centred = values - average
    variance = jnp.mean(centred * centred, axis=-1, keepdims=True)
    scale = lax.rsqrt(variance + EPSILON)
    return centred * scale, scale


def norm_back(d_norm, unit, scale, gain):
    weighted = d_norm * gain
    return scale * (
        weighted
        - jnp.mean(weighted, axis=-1, keepdims=True)
        - unit * jnp.mean(weighted * unit, axis=-1, keepdims=True)
    )


def bit_orders(count):
    bits = count.bit_length() - 1
    straight = list(range(bits))
    half = bits // 2
    return straight, straight[half:] + straight[:half]


def crossed(count, core, index, first_high):
    order = bit_orders(count)[core]
    mask = 0
    for step, bit in enumerate(order):
        place = len(order) - 1 - step if first_high else step
        mask |= ((index >> place) & 1) << bit
    return mask


def rank(count, core, far, first_high):
    order = bit_orders(count)[core]
    index = 0
    for step, bit in enumerate(order):
        place = len(order) - 1 - step if first_high else step
        index |= ((far >> bit) & 1) << place
    return index


def by_core(core, even, odd):
    return jnp.where(core == 0, even, odd)


def copy_all(copies, sems):
    started = [pltpu.make_async_copy(source, target, sems.at[k]) for k, (source, target) in enumerate(copies)]
    for copy in started:
        copy.start()
    for copy in started:
        copy.wait()


def start_kernel(*refs):
    vectors, (score_ref, small_ref) = refs[:-2], refs[-2:]
    rows = small_ref.shape[1]
    row = 0
    for ref in vectors:
        for k in range(ref.shape[0] // rows):
            small_ref[row : row + 1] = ref[k * rows : (k + 1) * rows].reshape(1, rows)
            row += 1
    small_ref[row:] = score_ref[...]


def first_pack_kernel(info, own_ref, x_ref, own_out, tail_ref):
    own_out[...] = own_ref[...]
    for s in range(x_ref.shape[0]):
        tail_ref[s * WINDOW : (s + 1) * WINDOW] = x_ref[s]


def feed_pack_kernel(info, fc_ref, down_ref, weight_ref, *outs):
    fc_refs, own_refs = outs[:CHUNKS], outs[CHUNKS:]
    rows, hidden = fc_ref.shape
    width = down_ref.shape[1]
    wide = fc_refs[0].shape[1]
    deep = down_ref.shape[0] // CHUNKS
    shards = hidden // (deep * CHUNKS)
    for chunk in range(CHUNKS):
        for shard in range(shards):
            begin = (shard * CHUNKS + chunk) * deep
            fc_refs[chunk][:, shard * deep : (shard + 1) * deep] = fc_ref[:, begin : begin + deep]

        @pl.when(info[1] == 0)
        def _():
            own_refs[chunk][:, :wide] = fc_refs[chunk][...]
            if chunk == 0:
                own_refs[chunk][:, wide:] = weight_ref[:, : width // 2]

        @pl.when(info[1] != 0)
        def _():
            for part in range(deep // rows):
                begin = chunk * deep + part * rows
                own_refs[chunk][:, part * width : (part + 1) * width] = down_ref[begin : begin + rows]
            if chunk == 0:
                own_refs[chunk][:, wide:] = weight_ref[:, width // 2 :]


def end_kernel(packed_ref, *outs):
    row = 0
    rows = packed_ref.shape[1]
    for ref in outs[:-1]:
        for k in range(ref.shape[0] // rows):
            ref[k * rows : (k + 1) * rows] = packed_ref[row : row + 1].reshape(rows)
            row += 1
    outs[-1][...] = packed_ref[row:]


def params_kernel(info, *refs):
    pieces, (table_ref, score_ref, held) = refs[:-3], refs[-3:]
    shards = len(pieces)
    core, me = info[1], info[2]
    for k, piece in enumerate(pieces):
        held[k] = piece[...].astype(F32)

    def at(shard):
        far = shard ^ me
        index = jnp.int32(0)
        for k in range(shards):
            mask = by_core(core, crossed(shards, 0, k, False), crossed(shards, 1, k, False))
            index = jnp.where(mask == far, k, index)
        return held[index]

    parts = [at(shard) for shard in range(shards)]

    def line(shard_range, rows):
        return jnp.concatenate([parts[s][r : r + 1] for s in shard_range for r in rows], axis=1)

    table_ref[...] = jnp.zeros_like(table_ref)
    for r in range(VECTORS):
        table_ref[r : r + 1] = line(range(shards), [r])
    qv = list(range(VECTORS, VECTORS + QV_ROWS))
    table_ref[BIAS_QKV : BIAS_QKV + 1] = line(range(shards // 2), qv)
    table_ref[BIAS_QKV + 2 : BIAS_QKV + 3] = line(range(shards // 2, shards), qv)
    base = VECTORS + QV_ROWS
    per_block = shards // BLOCKS
    per_chunk = FC_ROWS // CHUNKS
    for chunk in range(CHUNKS):
        for block in range(BLOCKS):
            rows = [base + chunk * per_chunk + k for k in range(per_chunk)]
            row = BIAS_FC + chunk * BLOCKS + block
            table_ref[row : row + 1] = line(range(block * per_block, (block + 1) * per_block), rows)
    base += FC_ROWS
    heads = parts[0].shape[0] - base
    score_ref[...] = jnp.zeros_like(score_ref)
    for head in range(heads):
        score_ref[head : head + 1] = line(range(shards), [base + head]).astype(BF)


def prep_kernel(info, bounds, x_ref, table_ref, score_ref, normed_ref, imp_ref, mass_ref, stat_ref):
    seqs = stat_ref.shape[0]
    blocks = x_ref.shape[0] // seqs
    gain = table_ref[GAIN1 : GAIN1 + 1]
    shift = table_ref[SHIFT1 : SHIFT1 + 1]
    start = info[0]
    rows = iota((blocks, blocks), 0)
    cols = iota((blocks, blocks), 1)
    for k in range(seqs):
        rs = slice(k * blocks, (k + 1) * blocks)
        normed = (normalise(x_ref[rs].astype(F32))[0] * gain + shift).astype(BF)
        normed_ref[rs] = normed
        importance = mm(normed, score_ref[...], NT)
        imp_ref[rs] = importance
        s = pl.program_id(0) * seqs + k
        first, second = bounds[0, s], bounds[1, s]
        lower = (cols <= rows) & (segment(start + rows, first, second) == segment(start + cols, first, second))
        peak = jnp.max(importance, axis=0, keepdims=True)
        mass = mm_split(lower.astype(BF), jnp.exp(importance - peak))
        mass_ref[rs] = mass
        stat_ref[k, 0:1, :] = peak
        stat_ref[k, 1:2, :] = mass[blocks - 1 :, :]
        stat_ref[k, 2:3, :] = jnp.full_like(peak, NEGATIVE)
        stat_ref[k, 3:4, :] = jnp.zeros_like(peak)
        stat_ref[k, 4:5, :] = peak


def prep_tail_kernel(x_ref, table_ref, out_ref):
    gain = table_ref[GAIN1 : GAIN1 + 1]
    shift = table_ref[SHIFT1 : SHIFT1 + 1]
    out_ref[...] = (normalise(x_ref[...].astype(F32))[0] * gain + shift).astype(BF)


def scan_kernel(info, mine_ref, *refs, masks):
    got_refs, out_ref = refs[:-1], refs[-1]

    def joined(peak, total, got):
        top = jnp.maximum(peak, got[:, 0:1])
        return top, total * jnp.exp(peak - top) + got[:, 1:2] * jnp.exp(got[:, 0:1] - top)

    out_ref[...] = mine_ref[...]
    for mask, got in zip(masks, got_refs):
        peak, total = joined(out_ref[:, 0:1], out_ref[:, 1:2], got)
        out_ref[:, 0:1] = peak
        out_ref[:, 1:2] = total

        @pl.when((info[3] ^ mask) < info[3])
        def _():
            peak, total = joined(out_ref[:, 2:3], out_ref[:, 3:4], got)
            out_ref[:, 2:3] = peak
            out_ref[:, 3:4] = total


def qkv_build_kernel(info, *refs):
    own, pieces, out, sems = refs[0], refs[1:-2], refs[-2], refs[-1]
    shards = len(pieces) // 2 + 1
    rows, width = own.shape
    half = width // 2
    me = info[2]

    def build(core):
        copies = [(own, out.at[pl.ds(pl.multiple_of(me * rows, 16), rows)])]
        for k in range(1, shards):
            for side, group in ((core, 0), (1 - core, shards - 1)):
                at = pl.multiple_of((me ^ crossed(shards, side, k, False)) * rows, 16)
                target = out.at[pl.ds(at, rows), side * half : (side + 1) * half]
                copies.append((pieces[group + k - 1], target))
        copy_all(copies, sems)

    @pl.when(info[1] == 0)
    def _():
        build(0)

    @pl.when(info[1] != 0)
    def _():
        build(1)


def feed_build_kernel(info, *refs, with_out, by_pair):
    if with_out:
        own_fc, own_down, own_out = refs[:3]
        pieces, (fc_ref, down_ref, out_ref, sems) = refs[3:-4], refs[-4:]
    else:
        own_fc, own_down = refs[:2]
        pieces, (fc_ref, down_ref, sems) = refs[2:-3], refs[-3:]
    shards = len(pieces) // 2 + 1
    rows, wide = own_fc.shape
    deep, width = own_down.shape
    split = width // 2
    me = info[2]

    kinds = [info[1] ^ ((info[3] >> 1) & 1), None] if by_pair else [info[1], None]
    kinds[1] = 1 - kinds[0]

    def away(k, partner):
        return jnp.where(kinds[partner] == 0, crossed(shards, 0, k, False), crossed(shards, 1, k, False))

    def build(core):
        at_rows = lambda shard: pl.multiple_of(shard * rows, 16)
        copies = [
            (own_fc, fc_ref.at[pl.ds(at_rows(me), rows)]),
            (own_down, down_ref.at[pl.ds(pl.multiple_of(me * deep, 16), deep)]),
        ]
        if with_out:
            copies.append((own_out, out_ref.at[pl.ds(at_rows(me), rows)]))
        for k in range(1, shards):
            for partner, side in enumerate((core, 1 - core)):
                piece = pieces[partner * (shards - 1) + k - 1]
                shard = me ^ away(k, partner)
                if side == 0:
                    copies.append((piece.at[:, :wide], fc_ref.at[pl.ds(at_rows(shard), rows)]))
                else:
                    for part in range(deep // rows):
                        at = pl.multiple_of(shard * deep + part * rows, 16)
                        copies.append((piece.at[:, part * width : (part + 1) * width], down_ref.at[pl.ds(at, rows)]))
                if with_out:
                    copies.append((piece.at[:, wide:], out_ref.at[pl.ds(at_rows(shard), rows), side * split : (side + 1) * split]))
        copy_all(copies, sems)

    @pl.when(info[1] == 0)
    def _():
        build(0)

    @pl.when(info[1] != 0)
    def _():
        build(1)


def qkv_kernel(normed_ref, tail_ref, weight_ref, table_ref, out_ref, tail_out_ref):
    j = pl.program_id(0)
    weight = weight_ref[...]
    bias = table_ref[pl.ds(BIAS_QKV + j, 1)]
    factor = jnp.where(j == 0, SCALE, 1.0)
    out_ref[...] = ((mm(normed_ref[...], weight) + bias).astype(BF).astype(F32) * factor).astype(BF)

    @pl.when(j > 0)
    def _():
        tail_out_ref[...] = (mm(tail_ref[...], weight) + bias).astype(BF)


def lane_masks():
    first = iota((1, LANES), 1) < HEAD
    return first.astype(BF), (~first).astype(BF)


def grouped(part, keep_first, keep_second):
    return jnp.concatenate([part * keep_first, part * keep_second], axis=0)


def tile_masks(start, half, first, second):
    dims = (WINDOW, LANES)
    row = iota(dims, 0)
    col = iota(dims, 1) & (HEAD - 1)
    base = start + WINDOW * half
    mine = segment(base + row, first, second)
    far = segment(base - WINDOW + col, first, second) == mine
    near = (col <= row) & (segment(base + col, first, second) == mine)
    if half == 0:
        far = far & (col > row) & (base - WINDOW + col >= 0)
    return far, near, col <= row


def spread(columns, pair, rows):
    left = columns[:, 2 * pair : 2 * pair + 1]
    right = columns[:, 2 * pair + 1 : 2 * pair + 2]
    return jnp.where(iota((rows, LANES), 1) < HEAD, left, right)


def key_groups(qkv_ref, halo_ref, width, pair, keep_first, keep_second, one_group):
    at = slice(pair * LANES, (pair + 1) * LANES)
    ks = slice(width + pair * LANES, width + (pair + 1) * LANES)
    vs = slice(2 * width + pair * LANES, 2 * width + (pair + 1) * LANES)
    keys = [grouped(part, keep_first, keep_second) for part in (halo_ref[:, at], qkv_ref[:WINDOW, ks], qkv_ref[WINDOW:, ks])]
    values = [
        jnp.concatenate([grouped(part, keep_first, keep_second), one_group], axis=1)
        for part in (halo_ref[:, ks], qkv_ref[:WINDOW, vs], qkv_ref[WINDOW:, vs])
    ]
    return keys, values


def attention_kernel(info, bounds, qkv_ref, halo_ref, imp_ref, mass_ref, before_ref, att_ref, probs_ref, sig_ref, inv_ref):
    s = pl.program_id(0)
    blocks, width = att_ref.shape
    start = info[0]
    first, second = bounds[0, s], bounds[1, s]
    pairs = width // LANES
    peak = before_ref[0, 4:5, :]
    carry_peak = before_ref[0, 2:3, :]
    carry_total = before_ref[0, 3:4, :]
    top = before_ref[0, 0:1, :]
    joined = jnp.maximum(peak, carry_peak)
    place = start + iota((blocks, LANES), 0)
    continues = segment(place, first, second) == segment(jnp.full((1, LANES), start - 1, jnp.int32), first, second)
    mass = mass_ref[...] * jnp.exp(peak - joined) + jnp.where(
        continues, carry_total * jnp.exp(carry_peak - joined), 0.0
    )
    threshold = joined + jnp.log(mass) - math.log(KTOP)
    late = threshold[WINDOW:]
    inv_ref[...] = 1.0 / (mass[WINDOW:] * jnp.exp(joined - top))
    imp_rows = imp_ref[...].T
    keep_first, keep_second = lane_masks()
    one_group = grouped(jnp.ones((WINDOW, LANES), BF), keep_first, keep_second)
    masks = [tile_masks(start, half, first, second) for half in (0, 1)]
    lane = iota((WINDOW, LANES), 1) < HEAD
    for p0 in range(0, pairs, FORWARD_STAGE):
        ps = range(p0, min(pairs, p0 + FORWARD_STAGE))
        groups = {p: key_groups(qkv_ref, halo_ref, width, p, keep_first, keep_second, one_group) for p in ps}
        logits = {}
        for p in ps:
            ls = slice(p * LANES, (p + 1) * LANES)
            for half in (0, 1):
                rs = slice(half * WINDOW, (half + 1) * WINDOW)
                logits[p, half] = mm(qkv_ref[rs, ls], jnp.concatenate(groups[p][0][half : half + 2], axis=0), NT)
        soft_in = {}
        for p in ps:
            ls = slice(p * LANES, (p + 1) * LANES)
            for half in (0, 1):
                far_ok, near_ok, gated = masks[half]
                far, near = logits[p, half][:, :LANES], logits[p, half][:, LANES:]
                if half == 1:
                    row = jnp.concatenate([imp_rows[2 * p : 2 * p + 1, :WINDOW], imp_rows[2 * p + 1 : 2 * p + 2, :WINDOW]], axis=1)
                    gap = spread(late, p, WINDOW) - row
                    small = jnp.exp(-jnp.abs(gap))
                    soft = jnp.maximum(gap, 0.0) + jnp.log(1.0 + small)
                    sig_ref[:, ls] = (jnp.where(gap >= 0, 1.0, small) / (1.0 + small)).astype(BF)
                    far = jnp.where(gated, far - soft, far)
                far = jnp.where(far_ok, far, NEGATIVE)
                near = jnp.where(near_ok, near, NEGATIVE)
                best = jnp.maximum(far, near)
                best_first = jnp.max(jnp.where(lane, best, NEGATIVE), axis=1, keepdims=True)
                best_second = jnp.max(jnp.where(lane, NEGATIVE, best), axis=1, keepdims=True)
                best = jnp.where(lane, best_first, best_second)
                soft_in[p, half] = (jnp.exp(far - best), jnp.exp(near - best))
        for p in ps:
            ls = slice(p * LANES, (p + 1) * LANES)
            for half in (0, 1):
                rs = slice(half * WINDOW, (half + 1) * WINDOW)
                far, near = soft_in[p, half]
                weights = jnp.concatenate([far.astype(BF), near.astype(BF)], axis=1)
                mixed = mm(weights, jnp.concatenate(groups[p][1][half : half + 2], axis=0))
                inverse = 1.0 / mixed[:, LANES:]
                att_ref[rs, ls] = (mixed[:, :LANES] * inverse).astype(BF)
                probs_ref[rs, 2 * p * LANES : (2 * p + 1) * LANES] = (far * inverse).astype(BF)
                probs_ref[rs, (2 * p + 1) * LANES : (2 * p + 2) * LANES] = (near * inverse).astype(BF)


def project_kernel(att_ref, x_ref, weight_ref, table_ref, middle_ref, second_ref):
    middle = x_ref[...].astype(F32) + mm(att_ref[...], weight_ref[...]) + table_ref[BIAS_OUT : BIAS_OUT + 1]
    middle_ref[...] = middle
    second_ref[...] = (normalise(middle)[0] * table_ref[GAIN2 : GAIN2 + 1] + table_ref[SHIFT2 : SHIFT2 + 1]).astype(BF)


def feed_kernel(info, sec_ref, dy_ref, fc_ref, down_ref, table_ref, hid_ref, dpre_ref, db_ref, keep_ref, give_ref, *, chunk):
    fc = fc_ref[...]
    down = down_ref[...]
    row = BIAS_FC + chunk * BLOCKS + pl.program_id(0)
    pre = mm(sec_ref[...], fc) + table_ref[pl.ds(row, 1)]
    d_hidden = mm(dy_ref[...], down, NT)
    square = pre * pre
    tanh = jnp.tanh(pre * (GELU_A + GELU_A * GELU_B * square))
    half = 0.5 + 0.5 * tanh
    hidden = (pre * half).astype(BF)
    slope = half + pre * (0.5 * GELU_A + 1.5 * GELU_A * GELU_B * square) * (1.0 - tanh * tanh)
    d_pre = d_hidden * slope
    d_low = d_pre.astype(BF)
    hid_ref[...] = hidden
    dpre_ref[...] = d_low
    db_ref[...] = jnp.broadcast_to(jnp.sum(d_pre, axis=0, keepdims=True), db_ref.shape)
    d_down = mm(hidden, dy_ref[...], TN).astype(BF)
    d_fc = mm(sec_ref[...], d_low, TN).astype(BF)

    @pl.when(info[1] == 0)
    def _():
        keep_ref[...] = d_fc
        give_ref[...] = d_down

    @pl.when(info[1] != 0)
    def _():
        keep_ref[...] = d_down
        give_ref[...] = d_fc


def feed_add_kernel(info, kept_ref, got_ref, keep_ref, give_ref, held):
    shards, rows, wide = held.shape
    width = kept_ref.shape[1]
    me = info[2]
    per_block = shards // BLOCKS
    deep = width // per_block

    def put(core):
        for block in range(BLOCKS):
            at = slice(block * width, (block + 1) * width)
            total = add(kept_ref[at], got_ref[at])
            if core == 0:
                for shard in range(shards):
                    held[ranked(shards, 0, me ^ shard), :, at] = total[shard * rows : (shard + 1) * rows]
            else:
                for k in range(per_block):
                    place = ranked(shards, 1, me ^ (block * per_block + k))
                    for part in range(deep // rows):
                        begin = k * deep + part * rows
                        held[place, :, part * width : (part + 1) * width] = total[begin : begin + rows]

    @pl.when(info[1] == 0)
    def _():
        put(0)

    @pl.when(info[1] != 0)
    def _():
        put(1)

    half = shards // 2
    keep_ref[...] = held[:half]
    give_ref[...] = held[half:]


def ranked(shards, core, far):
    order = bit_orders(shards)[core]
    index = jnp.int32(0)
    for step, bit in enumerate(order):
        index = index | (((far >> bit) & 1) << (len(order) - 1 - step))
    return index


def middle_kernel(*refs):
    dpre_refs = refs[:CHUNKS]
    fc_refs = refs[CHUNKS : 2 * CHUNKS]
    middle_ref, dy_ref, table_ref, dmid_ref, branch_ref, sums_ref = refs[2 * CHUNKS :]
    part_rows = middle_ref.shape[0] // 2
    totals = [0.0] * 4
    for part in range(2):
        rs = slice(part * part_rows, (part + 1) * part_rows)
        d_norm = None
        for dpre_ref, fc_ref in zip(dpre_refs, fc_refs):
            piece = mm(dpre_ref[rs], fc_ref[...], NT)
            d_norm = piece if d_norm is None else d_norm + piece
        unit, scale = normalise(middle_ref[rs])
        dy = dy_ref[rs].astype(F32)
        d_middle = dy + norm_back(d_norm, unit, scale, table_ref[GAIN2 : GAIN2 + 1])
        dmid_ref[rs] = d_middle
        branch = d_middle.astype(BF)
        branch_ref[rs] = branch
        for k, value in enumerate((d_norm * unit, d_norm, branch.astype(F32), dy)):
            totals[k] = totals[k] + jnp.sum(value, axis=0, keepdims=True)

    @pl.when(pl.program_id(0) == 0)
    def _():
        for k in range(4):
            sums_ref[k : k + 1] = totals[k]

    @pl.when(pl.program_id(0) > 0)
    def _():
        for k in range(4):
            sums_ref[k : k + 1] += totals[k]


def branch_kernel(info, branch_ref, att_ref, weight_ref, datt_ref, keep_ref, give_ref):
    shards, rows, split = keep_ref.shape
    store_halves(info, mm(att_ref[...], branch_ref[...], TN), keep_ref, give_ref, shards, rows, split)
    datt_ref[...] = mm(branch_ref[...], weight_ref[...], NT).astype(BF)


def store_halves(info, total, keep_ref, give_ref, shards, rows, split):
    me = info[2]

    def store(side, to):
        for shard in range(shards):
            value = total[shard * rows : (shard + 1) * rows, side * split : (side + 1) * split]
            to[ranked(shards, side, me ^ shard)] = value.astype(BF)

    @pl.when(info[1] == 0)
    def _():
        store(0, keep_ref)
        store(1, give_ref)

    @pl.when(info[1] != 0)
    def _():
        store(1, keep_ref)
        store(0, give_ref)


def attention_back_kernel(info, bounds, qkv_ref, halo_ref, att_ref, datt_ref, probs_ref, sig_ref, inv_ref, imp_ref, before_ref, dqkv_ref, dhalo_ref, dimp_ref, total_ref, rows_scratch, *, first_seq, pairs):
    s = first_seq + pl.program_id(0)
    blocks, width = att_ref.shape
    start = info[0]
    first, second = bounds[0, s], bounds[1, s]
    keep_first, keep_second = lane_masks()
    one_group = grouped(jnp.ones((WINDOW, LANES), BF), keep_first, keep_second)
    lane = iota((WINDOW, LANES), 1) < HEAD
    gated = (iota((WINDOW, LANES), 1) & (HEAD - 1)) <= iota((WINDOW, LANES), 0)
    head_lane = iota((LANES, LANES), 1)
    head_row = iota((LANES, LANES), 0)
    d_threshold = jnp.zeros((WINDOW, LANES), F32)
    rows_scratch[...] = jnp.zeros_like(rows_scratch)
    wide = pairs * LANES
    for k0 in range(0, pairs, BACKWARD_STAGE):
        ks_ = range(k0, min(pairs, k0 + BACKWARD_STAGE))
        groups = {k: key_groups(qkv_ref, halo_ref, width, k, keep_first, keep_second, one_group) for k in ks_}
        centred, low = {}, {}
        for k in ks_:
            ls = slice(k * LANES, (k + 1) * LANES)
            for half in (0, 1):
                rs = slice(half * WINDOW, (half + 1) * WINDOW)
                d_out = datt_ref[rs, ls]
                product = (-(d_out.astype(F32) * att_ref[rs, ls].astype(F32))).astype(BF)
                left = jnp.concatenate([d_out, product], axis=1)
                centred[k, half] = mm(left, jnp.concatenate(groups[k][1][half : half + 2], axis=0), NT)
        for k in ks_:
            ls = slice(k * LANES, (k + 1) * LANES)
            for half in (0, 1):
                rs = slice(half * WINDOW, (half + 1) * WINDOW)
                d_logits = probs_ref[rs, 2 * k * LANES : (2 * k + 2) * LANES].astype(F32) * centred[k, half]
                low[k, half] = d_logits.astype(BF)
                if half == 1:
                    gate = jnp.where(gated, d_logits[:, :LANES] * sig_ref[:, ls].astype(F32), 0.0)
                    rows_scratch[k : k + 1, :] = jnp.sum(gate, axis=0, keepdims=True)
                    chosen = (head_lane == 2 * k + (head_row >= HEAD).astype(jnp.int32)).astype(BF)
                    d_threshold = d_threshold - mm(gate.astype(BF), chosen)
        for k in ks_:
            ls = slice(k * LANES, (k + 1) * LANES)
            far_keys, near_keys, far_values, near_values = [], [], [], []
            for half in (0, 1):
                rs = slice(half * WINDOW, (half + 1) * WINDOW)
                dqkv_ref[rs, ls] = (mm(low[k, half], jnp.concatenate(groups[k][0][half : half + 2], axis=0)) * SCALE).astype(BF)
                d_keys = mm(low[k, half], qkv_ref[rs, ls], TN)
                d_values = mm(probs_ref[rs, 2 * k * LANES : (2 * k + 2) * LANES], datt_ref[rs, ls], TN)
                far_keys.append(jnp.where(lane, d_keys[:WINDOW], d_keys[WINDOW : 2 * WINDOW]))
                near_keys.append(jnp.where(lane, d_keys[2 * WINDOW : 3 * WINDOW], d_keys[3 * WINDOW :]))
                far_values.append(jnp.where(lane, d_values[:WINDOW], d_values[WINDOW : 2 * WINDOW]))
                near_values.append(jnp.where(lane, d_values[2 * WINDOW : 3 * WINDOW], d_values[3 * WINDOW :]))
            ks = slice(wide + k * LANES, wide + (k + 1) * LANES)
            vs = slice(2 * wide + k * LANES, 2 * wide + (k + 1) * LANES)
            dhalo_ref[:, ks] = far_keys[0].astype(BF)
            dhalo_ref[:, vs] = far_values[0].astype(BF)
            dqkv_ref[:WINDOW, ks] = (near_keys[0] + far_keys[1]).astype(BF)
            dqkv_ref[WINDOW:, ks] = near_keys[1].astype(BF)
            dqkv_ref[:WINDOW, vs] = (near_values[0] + far_values[1]).astype(BF)
            dqkv_ref[WINDOW:, vs] = near_values[1].astype(BF)
    dhalo_ref[:, :wide] = jnp.zeros((WINDOW, wide), BF)
    weighted = d_threshold * inv_ref[...]
    row = iota((blocks, WINDOW), 0)
    col = iota((blocks, WINDOW), 1) + WINDOW
    after = (col >= row) & (segment(start + row, first, second) == segment(start + col, first, second))
    later = mm_split(after.astype(BF), weighted)
    total_ref[0, 0:1, :] = later[0:1]
    turned = rows_scratch[...].T
    pick_first = (head_lane == 2 * head_row).astype(BF)
    pick_second = (head_lane == 2 * head_row + 1).astype(BF)

    def pick(values, chosen):
        high = values.astype(BF)
        return mm(high, chosen) + mm((values - high.astype(F32)).astype(BF), chosen)

    direct = pick(turned[:HEAD], pick_first) + pick(turned[HEAD:], pick_second)
    local = jnp.exp(imp_ref[...] - before_ref[0, 0:1, :]) * later
    dimp_ref[:WINDOW] = local[:WINDOW] + direct
    dimp_ref[WINDOW:] = local[WINDOW:]


def tail_back_kernel(*refs):
    dhalo_refs = refs[:-5]
    weight_ref, x_ref, table_ref, out_ref, sums_ref = refs[-5:]
    width = x_ref.shape[1]
    begin = 0
    totals = [0.0, 0.0]
    for dhalo_ref in dhalo_refs:
        rs = slice(begin, begin + dhalo_ref.shape[0])
        begin += dhalo_ref.shape[0]
        d_norm = mm(dhalo_ref[:, width:], weight_ref[:, width:], NT)
        unit, scale = normalise(x_ref[rs].astype(F32))
        out_ref[rs] = norm_back(d_norm, unit, scale, table_ref[GAIN1 : GAIN1 + 1]).astype(BF)
        for k, value in enumerate((d_norm * unit, d_norm)):
            totals[k] = totals[k] + jnp.sum(value, axis=0, keepdims=True)
    for k in range(2):
        sums_ref[k : k + 1] = totals[k]


def qkv_grad_kernel(info, normed_ref, tail_ref, *refs, groups):
    dqkv_refs, dhalo_refs = refs[:groups], refs[groups : 2 * groups]
    give_ref, keep_ref, given_sums, kept_sums = refs[2 * groups :]
    shards, rows, split = keep_ref.shape
    me = info[2]
    step = pl.program_id(0)
    owner = jnp.where(step == 0, 1 - info[1], info[1])
    total, sums = 0.0, 0.0
    for left_ref, right_refs in ((normed_ref, dqkv_refs), (tail_ref, dhalo_refs)):
        begin = 0
        for right_ref in right_refs:
            rs = slice(begin, begin + right_ref.shape[0])
            begin += right_ref.shape[0]
            total = total + mm(left_ref[rs], right_ref[...], TN)
            sums = sums + jnp.sum(right_ref[...].astype(F32), axis=0, keepdims=True)

    def store(to, sums_to):
        sums_to[0:1] = sums
        for shard in range(shards):
            far = me ^ shard
            place = jnp.where(owner == 0, ranked(shards, 0, far), ranked(shards, 1, far))
            to[place] = total[shard * rows : (shard + 1) * rows].astype(BF)

    @pl.when(step == 0)
    def _():
        store(give_ref, given_sums)

    @pl.when(step != 0)
    def _():
        store(keep_ref, kept_sums)


def input_grad_kernel(info, bounds, *refs, groups):
    dqkv_refs, dimp_refs = refs[:groups], refs[groups : 2 * groups]
    weight_ref, score_ref, normed_ref, x_ref, table_ref, dmid_ref, back_ref, imp_ref, before_ref, after_ref, out_ref, sums_ref, score_out_ref = refs[2 * groups :]
    i = pl.program_id(0)
    per_group = pl.num_programs(0) // groups
    seqs = back_ref.shape[0]
    blocks = x_ref.shape[0] // seqs
    start = info[0]

    def chosen(refs):
        value = refs[0][...]
        for k in range(1, groups):
            value = jnp.where(i >= k * per_group, refs[k][...], value)
        return value

    dqkv, d_local = chosen(dqkv_refs), chosen(dimp_refs)
    d_imps = []
    for s in range(seqs):
        rs = slice(s * blocks, (s + 1) * blocks)
        first, second = bounds[0, i * seqs + s], bounds[1, i * seqs + s]
        place = start + iota((blocks, LANES), 0)
        onward = segment(place, first, second) == segment(jnp.full((1, LANES), start + blocks, jnp.int32), first, second)
        extra = jnp.exp(imp_ref[rs] - before_ref[s, 0:1, :]) * after_ref[s, 0:1, :]
        d_imps.append(d_local[rs] + jnp.where(onward, extra, 0.0))
    d_imp = jnp.concatenate(d_imps, axis=0).astype(BF)
    d_norm = mm(dqkv, weight_ref[...], NT) + mm(d_imp, score_ref[...])
    unit, scale = normalise(x_ref[...].astype(F32))
    d_value = norm_back(d_norm, unit, scale, table_ref[GAIN1 : GAIN1 + 1]) + dmid_ref[...]
    for s in range(seqs):
        rs = slice(s * blocks, s * blocks + WINDOW)
        out_ref[rs] = d_value[rs]
        rs = slice(s * blocks + WINDOW, (s + 1) * blocks)
        out_ref[rs] = d_value[rs] + back_ref[s].astype(F32)
    sums = [jnp.sum(value, axis=0, keepdims=True) for value in (d_norm * unit, d_norm)]
    score = mm(d_imp, normed_ref[...], TN)

    @pl.when(i == 0)
    def _():
        score_out_ref[...] = score
        for k in range(2):
            sums_ref[k : k + 1] = sums[k]

    @pl.when(i > 0)
    def _():
        score_out_ref[...] += score
        for k in range(2):
            sums_ref[k : k + 1] += sums[k]


def output_kernel(*refs):
    hid_refs, down_refs, (middle_ref, table_ref) = refs[:CHUNKS], refs[CHUNKS : 2 * CHUNKS], refs[2 * CHUNKS : 2 * CHUNKS + 2]
    out_ref, total = refs[-2:]
    part = 0.0
    for hid_ref, down_ref in zip(hid_refs, down_refs):
        part = part + mm(hid_ref[...], down_ref[...])

    @pl.when(pl.program_id(0) == 0)
    def _():
        total[...] = middle_ref[...] + table_ref[BIAS_DOWN : BIAS_DOWN + 1] + part

    @pl.when(pl.program_id(0) == pl.num_programs(0) - 1)
    def _():
        out_ref[...] = (total[...] + part).astype(BF)


def small_pack_kernel(info, first_ref, tail_ref, second_ref, kept_ref, given_ref, *refs):
    bias_refs = refs[:CHUNKS]
    score_ref, out_ref, whole = refs[CHUNKS:]
    shards, count, rows = out_ref.shape
    me = info[2]
    whole[0:2] = first_ref[0:2] + tail_ref[0:2]
    whole[2:VECTORS] = second_ref[0 : VECTORS - 2]
    width = whole.shape[1]
    even = info[1] == 0
    whole[VECTORS : VECTORS + 1] = jnp.where(even, kept_ref[0:1, :width], given_ref[0:1, :width])
    whole[VECTORS + 1 : VECTORS + 2] = jnp.where(even, given_ref[0:1, width // 2 :], kept_ref[0:1, width // 2 :])
    base = VECTORS + 2
    for k in range(CHUNKS * BLOCKS):
        whole[base + k : base + k + 1] = bias_refs[k // BLOCKS][0:1, (k % BLOCKS) * width : (k % BLOCKS + 1) * width]
    heads = count - VECTORS - QV_ROWS - FC_ROWS
    whole[base + CHUNKS * BLOCKS : base + CHUNKS * BLOCKS + heads] = score_ref[0:heads]
    per_block = shards // BLOCKS
    per_chunk = FC_ROWS // CHUNKS
    for shard in range(shards):
        at = slice(shard * rows, (shard + 1) * rows)
        lines = [whole[0:VECTORS, at]]
        row = VECTORS + shard // (shards // 2)
        for k in range(QV_ROWS):
            begin = (shard % (shards // 2)) * QV_ROWS * rows + k * rows
            lines.append(whole[row : row + 1, begin : begin + rows])
        for chunk in range(CHUNKS):
            row = base + chunk * BLOCKS + shard // per_block
            for k in range(per_chunk):
                begin = (shard % per_block) * per_chunk * rows + k * rows
                lines.append(whole[row : row + 1, begin : begin + rows])
        lines.append(whole[base + CHUNKS * BLOCKS : base + CHUNKS * BLOCKS + heads, at])
        out_ref[ranked(shards, 0, me ^ shard)] = jnp.concatenate(lines, axis=0)


def add(left, right):
    return (left.astype(F32) + right.astype(F32)).astype(BF)


def combine(peak_a, total_a, peak_b, total_b):
    joined = jnp.maximum(peak_a, peak_b)
    return joined, total_a * jnp.exp(peak_a - joined) + total_b * jnp.exp(peak_b - joined)


def tie(*values):
    return lax.optimization_barrier(values)


class Net:
    def __init__(self):
        self.n_seq = lax.axis_size("seq")
        self.n_dp = lax.axis_size("dp")
        self.seq = lax.axis_index("seq")
        self.dp = lax.axis_index("dp")
        self.core = self.seq % 2
        self.orders = bit_orders(self.n_dp)
        self.bits = len(self.orders[0])
        self.seq_bits = self.n_seq.bit_length() - 1
        self.by_pair = self.bits == 2 and self.seq_bits >= 2

    def send(self, value, target):
        pairs = []
        for s in range(self.n_seq):
            for d in range(self.n_dp):
                goal = target(s, d)
                if 0 <= goal[0] < self.n_seq:
                    pairs.append((s * self.n_dp + d, goal[0] * self.n_dp + goal[1]))
        return lax.ppermute(value, ("seq", "dp"), pairs)

    def across(self, value, step):
        return self.send(value, lambda s, d: (s, d ^ (1 << self.orders[s % 2][step])))

    def chip(self, value):
        return self.send(value, lambda s, d: (s ^ 1, d))

    def along(self, value, bit):
        return self.send(value, lambda s, d: (s ^ (1 << bit), d))

    def masked(self, value, mask):
        return self.send(value, lambda s, d: (s ^ mask, d))

    def shifted(self, value, by):
        return self.send(value, lambda s, d: (s + by, d))

    def across_pair(self, value, step):
        return self.send(value, lambda s, d: (s, d ^ (1 << self.orders[(s ^ (s >> 1)) % 2][step])))

    def gather_step(self, pieces, step):
        return pieces + [self.across(piece, step) for piece in pieces]

    def sum_all(self, value):
        value = value + self.chip(value)
        for step in range(self.bits):
            value = value + self.across(value, step)
        for bit in range(1, self.seq_bits):
            value = value + self.along(value, bit)
        return value


class Reduction:
    def __init__(self, net, keep, give):
        self.net = net
        self.keep, self.give = keep, give
        z_bits = list(range(1, net.seq_bits))
        self.z_orders = (z_bits, z_bits[1:2] + z_bits[:1] + z_bits[2:])
        self.todo = ["across"] * net.bits + ["split"] + ["swap"] * (len(z_bits) - 1) + ["join"]
        self.done = 0
        self.got = None
        self.pending = False

    def along(self, value, place):
        return self.net.send(value, lambda s, d: (s ^ (1 << self.z_orders[s % 2][place]), d))

    def start(self):
        if not self.todo:
            return
        kind = self.todo[0]
        self.pending = True
        if kind == "across":
            self.got = self.net.across(self.give, self.done)
        elif kind == "split":
            half = self.keep.shape[0] // 2
            z_bit = jnp.where(self.net.core == 0, self.z_orders[0][0], self.z_orders[1][0])
            self.upper = (self.net.seq >> z_bit) % 2 == 1
            low, high = self.keep[:half], self.keep[half:]
            self.got = self.along(jnp.where(self.upper, low, high), 0)
            self.keep = jnp.where(self.upper, high, low)
        elif kind == "swap":
            self.got = self.along(self.keep, self.done - self.net.bits)
        else:
            self.got = self.along(self.keep, 0)

    def finish(self, after=None):
        if not self.pending:
            return
        if after is not None:
            self.got, _ = tie(self.got, after)
        kind = self.todo.pop(0)
        self.done += 1
        self.pending = False
        if kind == "join":
            low, high = jnp.where(self.upper, self.got, self.keep), jnp.where(self.upper, self.keep, self.got)
            self.keep = jnp.concatenate([low, high], axis=0)
            return
        half = self.keep.shape[0] // 2
        if kind == "across" and half:
            self.keep, self.give = add(self.keep[:half], self.got[:half]), add(self.keep[half:], self.got[half:])
        elif kind == "across":
            self.keep = add(self.keep[0], self.got[0])
        else:
            self.keep = add(self.keep, self.got)


def pin(value, *reds):
    held = [value]
    for red in reds:
        held += [red.keep] + ([red.give] if red.todo and red.todo[0] == "across" else [])
    held = list(tie(*held))
    value = held.pop(0)
    for red in reds:
        red.keep = held.pop(0)
        if red.todo and red.todo[0] == "across":
            red.give = held.pop(0)
    return value


def body(block_input, doc_bounds, first_gain, first_shift, qkv_weight, qv_bias, score_weight, out_weight, out_bias, second_gain, second_shift, fc_weight, fc_bias, down_weight, down_bias, cotangent):
    net = Net()
    seqs, blocks, width = block_input.shape
    tokens = seqs * blocks
    heads = score_weight.shape[1]
    shards = net.n_dp
    rows = width // shards
    hidden = fc_weight.shape[1]
    tail = seqs * WINDOW
    core = net.core
    place = jnp.arange(4, dtype=jnp.int32)
    info = jnp.where(place == 0, net.seq * blocks, jnp.where(place == 1, core, jnp.where(place == 2, net.dp, net.seq))).astype(jnp.int32)
    bounds = doc_bounds.T
    x_flat = block_input.reshape(tokens, width)
    dy = cotangent.reshape(tokens, width)
    wide = hidden // CHUNKS
    deep = hidden // shards // CHUNKS
    half_qkv = 3 * width // 2
    sems = lambda count: pltpu.SemaphoreType.DMA((count,))
    by_seq = lambda rows_, cols: pl.BlockSpec((rows_, cols), lambda s, *_: (s, 0))
    stat = pl.BlockSpec((1, 8, LANES), lambda s, *_: (s, 0, 0))
    table_spec = whole_spec((16, width))
    full = whole_spec((tokens, width))
    tile = 2 * blocks
    by_tile = pl.BlockSpec((tile, width), lambda i, *_: (i, 0))
    pairs = width // LANES
    parts = [(0, pairs)]

    vectors = [first_gain, first_shift, second_gain, second_shift, out_bias, down_bias, qv_bias, fc_bias]
    small_rows = sum(part.shape[0] for part in vectors) // rows + heads
    small = call(
        start_kernel,
        "start",
        (1,),
        [pl.BlockSpec(part.shape, lambda *_: (0,)) for part in vectors] + [whole_spec((heads, rows))],
        whole_spec((small_rows, rows)),
        shape((small_rows, rows), BF),
        micros=1,
        far_in=tuple(range(len(vectors) + 1)),
    )(*vectors, score_weight.T)

    def begin_gather(own):
        return [own, net.across(own, 0)], [net.across(own, 1)] if net.bits > 1 else []

    def end_gather(pieces, ahead):
        if net.bits > 1:
            pieces = pieces + ahead + [net.across(pieces[1], 1)]
        for step in range(2, net.bits):
            pieces = net.gather_step(pieces, step)
        return pieces

    small_state = begin_gather(small)
    first_weight, _ = tie(qkv_weight, small)
    own, x_tail = call(
        first_pack_kernel,
        "first_pack",
        (1,),
        [pl.BlockSpec((rows, half_qkv), lambda _, info: (0, info[1])), pl.BlockSpec((seqs, WINDOW, width), lambda *_: (0, blocks // WINDOW - 1, 0))],
        [whole_spec((rows, half_qkv)), whole_spec((tail, width))],
        [shape((rows, half_qkv), BF), shape((tail, width), BF)],
        prefetch=1,
        micros=2,
        far_in=(0, 1),
    )(info, first_weight, block_input)
    own, x_tail, *held = tie(own, x_tail, *small_state[0], *small_state[1])
    small_pieces = end_gather(held[:2], held[2:])
    qkv_state = begin_gather(own)
    x_tail = net.shifted(x_tail, 1)
    qkv_pieces = end_gather(*qkv_state)

    fc_weight, _ = tie(fc_weight, own)
    packs = call(
        feed_pack_kernel,
        "feed_pack",
        (1,),
        [whole_spec((rows, hidden)), whole_spec(down_weight.shape), whole_spec((rows, width))],
        [whole_spec((rows, wide))] * CHUNKS + [whole_spec((rows, wide + width // 2)), whole_spec((rows, wide))],
        [shape((rows, wide), BF)] * CHUNKS + [shape((rows, wide + width // 2), BF), shape((rows, wide), BF)],
        prefetch=1,
        micros=2,
        limit=24,
        far_in=(0, 1, 2),
    )(info, fc_weight, down_weight, out_weight)
    fc_own, feed_own = packs[:CHUNKS], packs[CHUNKS:]
    small_pieces[-1], *feed_own = tie(small_pieces[-1], *feed_own)
    first_own, _ = tie(feed_own[0], qkv_pieces[1])

    def begin_feed(own):
        if not net.by_pair:
            return begin_gather(own)
        return [own, net.across_pair(own, 0)], []

    def end_feed(pieces, ahead):
        if not net.by_pair:
            return end_gather(pieces, ahead)
        return pieces + [net.masked(pieces[1], 2), net.across_pair(pieces[1], 1)]

    a_state = begin_feed(first_own)

    table, score = call(
        params_kernel,
        "params",
        (1,),
        [whole_spec((small_rows, rows))] * shards,
        [table_spec, whole_spec((LANES, width))],
        [shape((16, width), F32), shape((LANES, width), BF)],
        scratch=[pltpu.VMEM((shards, small_rows, rows), F32)],
        prefetch=1,
        micros=1,
    )(info, *small_pieces)

    group = seqs // 2
    normed, importance, mass, stats = call(
        prep_kernel,
        "prep",
        (seqs // group,),
        [by_seq(group * blocks, width), table_spec, whole_spec((LANES, width))],
        [by_seq(group * blocks, width), by_seq(group * blocks, LANES), by_seq(group * blocks, LANES), pl.BlockSpec((group, 8, LANES), lambda s, *_: (s, 0, 0))],
        [shape((tokens, width), BF), shape((tokens, LANES), F32), shape((tokens, LANES), F32), shape((seqs, 8, LANES), F32)],
        prefetch=2,
        micros=3,
    )(info, bounds, x_flat, table, score)

    def scan_step(state, masks, got):
        spec = whole_spec((seqs, 8, LANES))
        return call(
            lambda *refs: scan_kernel(*refs, masks=masks),
            "scan",
            (1,),
            [spec] * (1 + len(masks)),
            spec,
            shape((seqs, 8, LANES), F32),
            prefetch=1,
            micros=0.5,
        )(info, state, *got)

    for bit in range(net.seq_bits - 1):
        stats = scan_step(stats, [1 << bit], [net.along(stats, bit)])
        if bit == 0:
            stats, *qkv_pieces = tie(stats, *qkv_pieces)
    qkv_others = [net.chip(piece) for piece in qkv_pieces[1:]]
    w_qkv = call(
        qkv_build_kernel,
        "qkv_build",
        (1,),
        [whole_spec((rows, 3 * width))] + [whole_spec((rows, half_qkv))] * (2 * shards - 2),
        ANY,
        shape((width, 3 * width), BF),
        scratch=[sems(2 * shards)],
        prefetch=1,
        micros=2,
    )(info, qkv_weight, *qkv_pieces[1:], *qkv_others)

    def build_feed(chunk, pieces, others):
        with_out = chunk == 0
        owns = [fc_own[chunk], down_weight] + ([out_weight] if with_out else [])
        specs = [whole_spec((rows, wide)), pl.BlockSpec((deep, width), lambda *_: (chunk, 0))] + ([whole_spec((rows, width))] if with_out else [])
        outs = [shape((width, wide), BF), shape((wide, width), BF)] + ([shape((width, width), BF)] if with_out else [])
        count = 3 + (shards - 1) * (1 + deep // rows + 2)
        return call(
            lambda *refs: feed_build_kernel(*refs, with_out=with_out, by_pair=net.by_pair),
            "feed_build",
            (1,),
            specs + [whole_spec(pieces[0].shape)] * (2 * shards - 2),
            [ANY] * len(outs),
            outs,
            scratch=[sems(count)],
            prefetch=1,
            micros=2,
        )(info, *owns, *pieces[1:], *others)

    normed_tail = call(
        prep_tail_kernel,
        "prep_tail",
        (1,),
        [whole_spec((tail, width)), table_spec],
        whole_spec((tail, width)),
        shape((tail, width), BF),
        micros=1,
    )(x_tail, table)
    w_qkv, *held = tie(w_qkv, *a_state[0], *a_state[1])
    a_pieces = end_feed(held[:2], held[2:])
    second_own, _ = tie(feed_own[1], held[1])
    b_state = begin_feed(second_own)
    col = lambda rows_: pl.BlockSpec((rows_, width), lambda j: (0, j))
    qkv, qkv_tail = call(
        qkv_kernel,
        "qkv",
        (3,),
        [full, whole_spec((tail, width)), col(width), table_spec],
        [col(tokens), pl.BlockSpec((tail, width), lambda j: (0, jnp.maximum(j - 1, 0)))],
        [shape((tokens, 3 * width), BF), shape((tail, 2 * width), BF)],
        micros=6.5,
        limit=24,
    )(normed, normed_tail, w_qkv, table)
    qkv, got = tie(qkv, net.along(stats, net.seq_bits - 1))
    before = scan_step(stats, [1 << (net.seq_bits - 1)], [got])

    attended, probs, gates, inverse = call(
        attention_kernel,
        "attention",
        (seqs,),
        [by_seq(blocks, 3 * width), by_seq(WINDOW, 2 * width), by_seq(blocks, LANES), by_seq(blocks, LANES), stat],
        [by_seq(blocks, width), by_seq(blocks, 2 * width), by_seq(WINDOW, width), by_seq(WINDOW, LANES)],
        [shape((tokens, width), BF), shape((tokens, 2 * width), BF), shape((tail, width), BF), shape((tail, LANES), F32)],
        prefetch=2,
        micros=10.5,
        far=(1, 2, 3),
    )(info, bounds, qkv, qkv_tail, importance, mass, before)

    attended, *held = tie(attended, *a_pieces, *b_state[0], *b_state[1])
    a_pieces, held = held[: len(a_pieces)], held[len(a_pieces) :]
    b_pieces = end_feed(held[:2], held[2:])
    fc_a, down_a, w_out = build_feed(0, a_pieces, [net.chip(piece) for piece in a_pieces[1:]])

    middle, normed_second = call(
        project_kernel,
        "project",
        (tokens // tile,),
        [by_tile, by_tile, whole_spec((width, width)), table_spec],
        [by_tile, by_tile],
        [shape((tokens, width), F32), shape((tokens, width), BF)],
        micros=3,
    )(attended, x_flat, w_out, table)

    hids, dpres, d_fc_bias = [], [], []

    def feed(chunk, fc, down, normed_second):
        still = pl.BlockSpec((tokens, width), lambda *_: (0, 0), pipeline_mode=pl.Buffered(1))
        column = lambda rows_: pl.BlockSpec((rows_, width), lambda j, *_: (0, j))
        row = pl.BlockSpec((width, width), lambda j, *_: (j, 0))
        hid, dpre, d_bias, keep, give = call(
            lambda *refs: feed_kernel(*refs, chunk=chunk),
            "feed",
            (BLOCKS,),
            [still, still, column(width), row, table_spec],
            [column(tokens), column(tokens), column(8), row, row],
            [shape((tokens, wide), BF), shape((tokens, wide), BF), shape((8, wide), F32), shape((wide, width), BF), shape((wide, width), BF)],
            prefetch=1,
            micros=15,
            limit=30,
            far=(0, 1, 3, 4),
        )(info, normed_second, dy, fc, down, table)
        hids.append(hid)
        dpres.append(dpre)
        d_fc_bias.append(d_bias)
        return keep, give

    def feed_add(kept, got):
        half = (shards // 2, rows, wide)
        keep, give = call(
            feed_add_kernel,
            "feed_add",
            (1,),
            [whole_spec((wide, width))] * 2,
            [whole_spec(half)] * 2,
            [shape(half, BF)] * 2,
            scratch=[pltpu.VMEM((shards, rows, wide), BF)],
            prefetch=1,
            micros=2,
            limit=20,
        )(info, kept, got)
        return Reduction(net, keep, give)

    b_first = net.chip(b_pieces[1])
    normed_second, b_first = tie(normed_second, b_first)
    kept_a, give_a = feed(0, fc_a, down_a, normed_second)
    give_a, *b_pieces = tie(give_a, *b_pieces)
    got_a = net.chip(give_a)
    fc_b, down_b = build_feed(1, b_pieces, [b_first] + [net.chip(piece) for piece in b_pieces[2:]])
    red_a = feed_add(kept_a, got_a)
    fc_b = pin(fc_b, red_a)
    red_a.start()
    kept_b, give_b = feed(1, fc_b, down_b, normed_second)
    got_b = net.chip(give_b)
    red_a.finish(kept_b)
    dpres[1] = pin(dpres[1], red_a)
    red_a.start()

    half_out = (shards, rows, width // 2)
    groups = 2
    part_tokens, part_tail, part_seqs = tokens // groups, tail // groups, seqs // groups
    by_part = pl.BlockSpec((part_tokens, width), lambda i, *_: (i, 0))
    d_middle, branch, sums_second = call(
        middle_kernel,
        "middle",
        (groups,),
        [pl.BlockSpec((part_tokens, wide), lambda i, *_: (i, 0))] * CHUNKS + [whole_spec((width, wide))] * CHUNKS + [by_part, by_part, table_spec],
        [by_part, by_part, whole_spec((8, width))],
        [shape((tokens, width), F32), shape((tokens, width), BF), shape((8, width), F32)],
        micros=1.0,
        limit=30,
        far=(0,),
        far_in=(0, 1, 5),
    )(*dpres, fc_a, fc_b, middle, dy, table)

    red_a.finish(branch)
    red_b = feed_add(kept_b, got_b)
    branch = pin(branch, red_a, red_b)
    red_a.start()
    red_b.start()
    d_attended, keep_out, give_out = call(
        branch_kernel,
        "branch",
        (1,),
        [full, full, whole_spec((width, width))],
        [full, whole_spec(half_out), whole_spec(half_out)],
        [shape((tokens, width), BF), shape(half_out, BF), shape(half_out, BF)],
        prefetch=1,
        micros=1.0,
        limit=24,
        far=(0,),
        far_in=(1,),
    )(info, branch, attended, w_out)
    got_out = net.chip(give_out)

    def attention_back(part, d_attended):
        shifted = lambda rows_, cols: pl.BlockSpec((rows_, cols), lambda s, *_: (part * part_seqs + s, 0))
        return call(
            lambda *refs: attention_back_kernel(*refs, first_seq=part * part_seqs, pairs=pairs),
            "attention_back",
            (part_seqs,),
            [shifted(blocks, 3 * width), shifted(WINDOW, 2 * width), shifted(blocks, width), shifted(blocks, width), shifted(blocks, 2 * width), shifted(WINDOW, width), shifted(WINDOW, LANES), shifted(blocks, LANES), pl.BlockSpec((1, 8, LANES), lambda s, *_: (part * part_seqs + s, 0, 0))],
            [by_seq(blocks, 3 * width), by_seq(WINDOW, 3 * width), by_seq(blocks, LANES), pl.BlockSpec((1, 1, LANES), lambda s, *_: (s, 0, 0))],
            [shape((part_tokens, 3 * width), BF), shape((part_tail, 3 * width), BF), shape((part_tokens, LANES), F32), shape((part_seqs, 1, LANES), F32)],
            scratch=[pltpu.VMEM((LANES, LANES), F32)],
            prefetch=2,
            micros=0.1,
            far=(0, 1),
            far_in=(0, 1, 2, 3, 4, 5, 6),
        )(info, bounds, qkv, qkv_tail, attended, d_attended, probs, gates, inverse, importance, before)

    def qkv_grad(backs):
        side = lambda i, info: (0, jnp.where(i == 0, 1 - info[1], info[1]))
        result = (shards, rows, half_qkv)
        still = lambda rows_: pl.BlockSpec((rows_, width), lambda *_: (0, 0), pipeline_mode=pl.Buffered(1))
        held = lambda dims: pl.BlockSpec(dims, lambda *_: (0,) * len(dims), pipeline_mode=pl.Buffered(1))
        return call(
            lambda *refs: qkv_grad_kernel(*refs, groups=groups),
            "qkv_grad",
            (2,),
            [still(tokens), still(tail)] + [pl.BlockSpec((part_tokens, half_qkv), side)] * groups + [pl.BlockSpec((part_tail, half_qkv), side)] * groups,
            [held(result), held(result), held((8, half_qkv)), held((8, half_qkv))],
            [shape(result, BF), shape(result, BF), shape((8, half_qkv), F32), shape((8, half_qkv), F32)],
            prefetch=1,
            micros=2,
            limit=22,
            far_in=(0, 1, 2, 3, 4, 5),
            far=(0, 1),
        )(info, normed, normed_tail, *[back[0] for back in backs], *[back[1] for back in backs])

    half_shards = shards // 2

    def halved(kept, got):
        return Reduction(net, add(kept[:half_shards], got[:half_shards]), add(kept[half_shards:], got[half_shards:]))

    red_o = halved(keep_out, got_out)
    d_attended = pin(d_attended, red_o)
    red_o.start()
    backs = [list(attention_back(0, d_attended))]
    red_a.finish(backs[0][0])
    d_attended, _ = tie(d_attended, backs[0][0])
    d_attended = pin(d_attended, red_a)
    red_a.start()
    backs.append(list(attention_back(1, d_attended)))
    red_a.finish()
    red_b.finish()
    red_o.finish()
    red_b.keep = jnp.concatenate([red_b.keep, red_o.keep], axis=2)
    red_b.give = jnp.concatenate([red_b.give, red_o.give], axis=2)
    backs[1][0] = pin(backs[1][0], red_a, red_b)
    red_a.start()
    red_b.start()
    total_all = jnp.concatenate([back[3] for back in backs], axis=0)
    total_after = jnp.zeros_like(total_all)

    def suffix_step(total_after, total_all, bit, after=None):
        got = net.along(total_all, bit)
        if after is not None:
            got, _ = tie(got, after)
        earlier = (net.seq >> bit) % 2 == 0
        return jnp.where(earlier, total_after + got, total_after), total_all + got

    total_after, total_all = suffix_step(total_after, total_all, 0)
    backs[1][0], total_all = tie(backs[1][0], total_all)
    give_qkv, keep_qkv, sums_given, sums_kept = qkv_grad(backs)

    for bit in range(1, net.seq_bits - 1):
        total_after, total_all = suffix_step(total_after, total_all, bit, keep_qkv)
    give_qkv, total_all, total_after, red_a.got, red_b.got = tie(give_qkv, total_all, total_after, red_a.got, red_b.got)
    got_qkv = net.chip(give_qkv)
    red_a.finish()
    red_b.finish()
    d_halos = [back[1] for back in backs]
    d_halos[0], _ = tie(d_halos[0], give_qkv)
    d_halos[0] = pin(d_halos[0], red_a, red_b)
    red_a.start()
    red_b.start()
    d_tail, sums_tail = call(
        tail_back_kernel,
        "tail_back",
        (1,),
        [whole_spec((part_tail, 3 * width))] * groups + [whole_spec((width, 3 * width)), whole_spec((tail, width)), table_spec],
        [whole_spec((tail, width)), whole_spec((8, width))],
        [shape((tail, width), BF), shape((8, width), F32)],
        micros=1,
        limit=16,
        far_in=(0, 1),
    )(*d_halos, w_qkv, x_tail, table)
    got_qkv, _ = tie(got_qkv, d_tail)
    d_tail, got_qkv, total_all, total_after = tie(d_tail, got_qkv, total_all, total_after)
    back = net.shifted(d_tail, -1)
    red_c = halved(keep_qkv, got_qkv)
    middle = pin(middle, red_c)
    red_c.start()

    def output(part, before_):
        still = pl.BlockSpec((part_tokens, width), lambda j: (part, 0))
        extra = [] if before_ is None else [before_]
        return call(
            output_kernel,
            "output",
            (BLOCKS,),
            [pl.BlockSpec((part_tokens, width), lambda j: (part, j))] * CHUNKS + [pl.BlockSpec((width, width), lambda j: (j, 0))] * CHUNKS + [still, table_spec] + [ANY] * len(extra),
            still,
            shape((tokens, width), BF),
            scratch=[pltpu.VMEM((part_tokens, width), F32)],
            micros=1.0,
            limit=24,
            alias={2 * CHUNKS + 2: 0} if extra else {},
            far=(0,),
            far_in=(0, 1, 2, 3, 4),
        )(*hids, down_a, down_b, middle, table, *extra)

    got_last = net.along(total_all, net.seq_bits - 1)
    block_output = output(0, None)
    block_output, red_b.got, got_last, back = tie(block_output, red_b.got, got_last, back)
    red_b.finish()
    total_after = jnp.where((net.seq >> (net.seq_bits - 1)) % 2 == 0, total_after + got_last, total_after)
    back = back.reshape(seqs, WINDOW, width)
    total_after = pin(total_after, red_b)
    red_b.start()

    per_tile = tile // blocks
    per_group = tokens // tile // groups
    grouped_tile = lambda cols: [pl.BlockSpec((tile, cols), lambda i, *_, k=k: (jnp.clip(i - k * per_group, 0, per_group - 1), 0)) for k in range(groups)]
    by_lane = pl.BlockSpec((tile, LANES), lambda i, *_: (i, 0))
    input_grad, sums_first, d_score = call(
        lambda *refs: input_grad_kernel(*refs, groups=groups),
        "input_grad",
        (tokens // tile,),
        grouped_tile(3 * width)
        + grouped_tile(LANES)
        + [
            whole_spec((width, 3 * width)),
            whole_spec((LANES, width)),
            by_tile,
            by_tile,
            table_spec,
            by_tile,
            pl.BlockSpec((per_tile, WINDOW, width), lambda i, *_: (i, 0, 0)),
            by_lane,
            pl.BlockSpec((per_tile, 8, LANES), lambda i, *_: (i, 0, 0)),
            pl.BlockSpec((per_tile, 1, LANES), lambda i, *_: (i, 0, 0)),
        ],
        [by_tile, whole_spec((8, width)), whole_spec((LANES, width))],
        [shape((tokens, width), F32), shape((8, width), F32), shape((LANES, width), F32)],
        prefetch=2,
        micros=1.0,
        limit=24,
        far_in=(0, 1) + tuple(2 * groups + k for k in (2, 3, 5)),
    )(info, bounds, *[back_[0] for back_ in backs], *[back_[2] for back_ in backs], w_qkv, score, normed, x_flat, table, d_middle, back, importance, before, total_after)

    for red in (red_b, red_c):
        red.finish()
        sums_first = pin(sums_first, red)
    packed = call(
        small_pack_kernel,
        "small_pack",
        (1,),
        [whole_spec((8, width))] * 3 + [whole_spec((8, half_qkv))] * 2 + [whole_spec((8, wide))] * CHUNKS + [whole_spec((LANES, width))],
        whole_spec((shards, small_rows, rows)),
        shape((shards, small_rows, rows), F32),
        scratch=[pltpu.VMEM((32, width), F32)],
        prefetch=1,
        micros=1,
    )(info, sums_first, sums_tail, sums_second, sums_kept, sums_given, *d_fc_bias, d_score)

    def finish(red):
        other = net.chip(red.keep)
        return jnp.where(core == 0, red.keep, other), jnp.where(core == 0, other, red.keep)

    def early_grads():
        fc_grads, down_grads = zip(finish(red_a), finish(red_b))
        out_grads = [fc_grads[1][:, wide:], down_grads[1][:, wide:]]
        fc_grads, down_grads = [part[:, :wide] for part in fc_grads], [part[:, :wide] for part in down_grads]
        d_out = jnp.concatenate(out_grads, axis=1).astype(F32)
        d_fc = jnp.concatenate([part[:, d * deep : (d + 1) * deep] for d in range(shards) for part in fc_grads], axis=1).astype(F32)
        d_down = jnp.concatenate([part[:, k * width : (k + 1) * width] for part in down_grads for k in range(deep // rows)], axis=0).astype(F32)
        return [d_out, d_fc, d_down]

    reds = [red_a, red_b, red_c]
    early, tied = None, False
    packed = packed + net.chip(packed)

    def small_across(value, step):
        half = value.shape[0] // 2
        return value[:half] + net.send(value[half:], lambda s, d: (s, d ^ (1 << net.orders[0][step])))

    small_steps = [lambda value, k=k: small_across(value, k) for k in range(net.bits)]
    small_steps += [lambda value, k=k: value + net.along(value, k) for k in range(1, net.seq_bits)]
    packed, middle = tie(packed, middle)
    red_b.start()
    red_c.start()
    packed = small_steps.pop(0)(packed)
    block_output = output(1, block_output)
    packed, block_output = tie(packed, block_output)
    while small_steps or any(red.todo for red in reds):
        active = [red for red in reds if red.pending]
        for red in active:
            red.finish()
        packed = pin(packed, *active)
        if early is not None and not tied:
            packed, *early = tie(packed, *early)
            tied = True
        for red in reds:
            if red.todo:
                red.start()
        if early is None and not red_a.todo and not red_b.todo:
            early = early_grads()
        if small_steps:
            packed = small_steps.pop(0)(packed)
    packed, d_out, d_fc, d_down = tie(packed, *early)
    packed = packed[0]

    d_qkv = jnp.concatenate(finish(red_c), axis=1).astype(F32)

    small_outs = [shape(part.shape, F32) for part in vectors] + [shape((heads, rows), F32)]
    dg_first, ds_first, dg_second, ds_second, db_out, db_down, db_qv, db_fc, d_score = call(
        end_kernel,
        "end",
        (1,),
        [whole_spec((small_rows, rows))],
        [pl.BlockSpec(part.shape, lambda *_, n=len(part.shape): (0,) * n) for part in small_outs],
        small_outs,
        micros=1,
    )(packed)
    return (
        block_output.reshape(seqs, blocks, width),
        input_grad.reshape(seqs, blocks, width),
        dg_first,
        ds_first,
        d_qkv,
        db_qv,
        d_score.T,
        d_out,
        db_out,
        dg_second,
        ds_second,
        d_fc,
        db_fc,
        d_down,
        db_down,
    )


def solution(mesh):
    split = P("dp", "seq", None)
    rows = P("dp", None)
    flat = P("dp")
    in_specs = (split, rows, flat, flat, rows, flat, rows, rows, flat, flat, flat, rows, flat, rows, flat, split)
    out_specs = (split, split, flat, flat, rows, flat, rows, rows, flat, flat, flat, rows, flat, rows, flat)
    return jax.shard_map(body, mesh=mesh, in_specs=in_specs, out_specs=out_specs, check_vma=False)
```

```python
import math

import jax
import jax.numpy as jnp
from jax import lax
from jax.experimental import pallas as pl
from jax.experimental.pallas import tpu as pltpu
from jax.sharding import PartitionSpec as P

KTOP = 64
WINDOW = 64
HEAD = 64
LANES = 128
EPSILON = 1e-05
NEGATIVE = -1e30
SCALE = 1.0 / math.sqrt(HEAD)
GELU_A = math.sqrt(2.0 / math.pi)
GELU_B = 0.044715
BF = jnp.bfloat16
F32 = jnp.float32
NN = ((1,), (0,))
NT = ((1,), (1,))
TN = ((0,), (0,))
CHUNKS = 2
BLOCKS = 2
MIB = 2**20
FORWARD_STAGE = 3
BACKWARD_STAGE = 6
GAIN1, SHIFT1, GAIN2, SHIFT2, BIAS_OUT, BIAS_DOWN, BIAS_QKV, BIAS_FC = 0, 1, 2, 3, 4, 5, 6, 9
VECTORS = 6
QV_ROWS = 2
FC_ROWS = 4


def mm(left, right, dims=NN):
    return lax.dot_general(left, right, (dims, ((), ())), preferred_element_type=F32)


def mm_split(mask, value, dims=NN):
    high = value.astype(BF)
    low = (value - high.astype(F32)).astype(BF)
    return mm(mask, high, dims) + mm(mask, low, dims)


def whole_spec(shape):
    return pl.BlockSpec(shape, lambda *_: (0,) * len(shape))


ANY = pl.BlockSpec(memory_space=pl.ANY)


def call(kernel, name, grid, in_specs, out_specs, out_shape, scratch=(), prefetch=0, micros=1.0, limit=16, alias=None, far=(), far_in=(), near=(), near_in=()):
    many = isinstance(out_shape, (list, tuple))
    if grid == (1,):
        once = lambda spec: spec if spec.block_shape is None else pl.BlockSpec(spec.block_shape, spec.index_map, pipeline_mode=pl.Buffered(1))
        in_specs = [once(spec) for spec in in_specs]
        out_specs = [once(spec) for spec in out_specs] if many else once(out_specs)
    outs = [pltpu.HBM(one.shape, one.dtype) if k in far else pltpu.VMEM(one.shape, one.dtype) if k in near else one for k, one in enumerate(out_shape if many else [out_shape])]
    inner = pl.pallas_call(
        kernel,
        grid_spec=pltpu.PrefetchScalarGridSpec(
            num_scalar_prefetch=prefetch,
            grid=grid,
            in_specs=in_specs,
            out_specs=out_specs,
            scratch_shapes=list(scratch),
        ),
        out_shape=outs if many else outs[0],
        input_output_aliases=alias or {},
        compiler_params=pltpu.CompilerParams(vmem_limit_bytes=limit * MIB),
        cost_estimate=pl.CostEstimate(flops=int(micros * 1.1e9), bytes_accessed=1024, transcendentals=0),
        name=name,
    )

    def run(*operands):
        held = []
        for k, one in enumerate(operands):
            if k - prefetch in far_in:
                one = pltpu.with_memory_space_constraint(one, pltpu.HBM)
            elif k - prefetch in near_in:
                one = pltpu.with_memory_space_constraint(one, pltpu.VMEM)
            held.append(one)
        return inner(*held)

    return run


def shape(dims, kind):
    return jax.ShapeDtypeStruct(dims, kind)


def iota(dims, axis):
    return lax.broadcasted_iota(jnp.int32, dims, axis)


def segment(places, first, second):
    return (places >= first).astype(jnp.int32) + (places >= second).astype(jnp.int32)


def normalise(values):
    average = jnp.mean(values, axis=-1, keepdims=True)
    centred = values - average
    variance = jnp.mean(centred * centred, axis=-1, keepdims=True)
    scale = lax.rsqrt(variance + EPSILON)
    return centred * scale, scale


def norm_back(d_norm, unit, scale, gain):
    weighted = d_norm * gain
    return scale * (
        weighted
        - jnp.mean(weighted, axis=-1, keepdims=True)
        - unit * jnp.mean(weighted * unit, axis=-1, keepdims=True)
    )


def bit_orders(count):
    bits = count.bit_length() - 1
    straight = list(range(bits))
    half = bits // 2
    return straight, straight[half:] + straight[:half]


def crossed(count, core, index, first_high):
    order = bit_orders(count)[core]
    mask = 0
    for step, bit in enumerate(order):
        place = len(order) - 1 - step if first_high else step
        mask |= ((index >> place) & 1) << bit
    return mask


def rank(count, core, far, first_high):
    order = bit_orders(count)[core]
    index = 0
    for step, bit in enumerate(order):
        place = len(order) - 1 - step if first_high else step
        index |= ((far >> bit) & 1) << place
    return index


def by_core(core, even, odd):
    return jnp.where(core == 0, even, odd)


def copy_all(copies, sems):
    started = [pltpu.make_async_copy(source, target, sems.at[k]) for k, (source, target) in enumerate(copies)]
    for copy in started:
        copy.start()
    for copy in started:
        copy.wait()


def start_kernel(*refs):
    vectors, (score_ref, small_ref) = refs[:-2], refs[-2:]
    rows = small_ref.shape[1]
    row = 0
    for ref in vectors:
        for k in range(ref.shape[0] // rows):
            small_ref[row : row + 1] = ref[k * rows : (k + 1) * rows].reshape(1, rows)
            row += 1
    small_ref[row:] = score_ref[...]


def first_pack_kernel(info, own_ref, x_ref, own_out, tail_ref):
    own_out[...] = own_ref[...]
    for s in range(x_ref.shape[0]):
        tail_ref[s * WINDOW : (s + 1) * WINDOW] = x_ref[s]


def feed_pack_kernel(info, fc_ref, down_ref, weight_ref, *outs):
    fc_refs, own_refs = outs[:CHUNKS], outs[CHUNKS:]
    rows, hidden = fc_ref.shape
    width = down_ref.shape[1]
    wide = fc_refs[0].shape[1]
    deep = down_ref.shape[0] // CHUNKS
    shards = hidden // (deep * CHUNKS)
    for chunk in range(CHUNKS):
        for shard in range(shards):
            begin = (shard * CHUNKS + chunk) * deep
            fc_refs[chunk][:, shard * deep : (shard + 1) * deep] = fc_ref[:, begin : begin + deep]

        @pl.when(info[1] == 0)
        def _():
            own_refs[chunk][:, :wide] = fc_refs[chunk][...]
            if chunk == 0:
                own_refs[chunk][:, wide:] = weight_ref[:, : width // 2]

        @pl.when(info[1] != 0)
        def _():
            for part in range(deep // rows):
                begin = chunk * deep + part * rows
                own_refs[chunk][:, part * width : (part + 1) * width] = down_ref[begin : begin + rows]
            if chunk == 0:
                own_refs[chunk][:, wide:] = weight_ref[:, width // 2 :]


def end_kernel(packed_ref, *outs):
    row = 0
    rows = packed_ref.shape[1]
    for ref in outs[:-1]:
        for k in range(ref.shape[0] // rows):
            ref[k * rows : (k + 1) * rows] = packed_ref[row : row + 1].reshape(rows)
            row += 1
    outs[-1][...] = packed_ref[row:]


def params_kernel(info, *refs):
    pieces, (table_ref, score_ref, held) = refs[:-3], refs[-3:]
    shards = len(pieces)
    core, me = info[1], info[2]
    for k, piece in enumerate(pieces):
        held[k] = piece[...].astype(F32)

    def at(shard):
        far = shard ^ me
        index = jnp.int32(0)
        for k in range(shards):
            mask = by_core(core, crossed(shards, 0, k, False), crossed(shards, 1, k, False))
            index = jnp.where(mask == far, k, index)
        return held[index]

    parts = [at(shard) for shard in range(shards)]

    def line(shard_range, rows):
        return jnp.concatenate([parts[s][r : r + 1] for s in shard_range for r in rows], axis=1)

    table_ref[...] = jnp.zeros_like(table_ref)
    for r in range(VECTORS):
        table_ref[r : r + 1] = line(range(shards), [r])
    qv = list(range(VECTORS, VECTORS + QV_ROWS))
    table_ref[BIAS_QKV : BIAS_QKV + 1] = line(range(shards // 2), qv)
    table_ref[BIAS_QKV + 2 : BIAS_QKV + 3] = line(range(shards // 2, shards), qv)
    base = VECTORS + QV_ROWS
    per_block = shards // BLOCKS
    per_chunk = FC_ROWS // CHUNKS
    for chunk in range(CHUNKS):
        for block in range(BLOCKS):
            rows = [base + chunk * per_chunk + k for k in range(per_chunk)]
            row = BIAS_FC + chunk * BLOCKS + block
            table_ref[row : row + 1] = line(range(block * per_block, (block + 1) * per_block), rows)
    base += FC_ROWS
    heads = parts[0].shape[0] - base
    score_ref[...] = jnp.zeros_like(score_ref)
    for head in range(heads):
        score_ref[head : head + 1] = line(range(shards), [base + head]).astype(BF)


def prep_kernel(info, bounds, x_ref, table_ref, score_ref, normed_ref, imp_ref, mass_ref, stat_ref):
    seqs = stat_ref.shape[0]
    blocks = x_ref.shape[0] // seqs
    gain = table_ref[GAIN1 : GAIN1 + 1]
    shift = table_ref[SHIFT1 : SHIFT1 + 1]
    start = info[0]
    rows = iota((blocks, blocks), 0)
    cols = iota((blocks, blocks), 1)
    for k in range(seqs):
        rs = slice(k * blocks, (k + 1) * blocks)
        normed = (normalise(x_ref[rs].astype(F32))[0] * gain + shift).astype(BF)
        normed_ref[rs] = normed
        importance = mm(normed, score_ref[...], NT)
        imp_ref[rs] = importance
        s = pl.program_id(0) * seqs + k
        first, second = bounds[0, s], bounds[1, s]
        lower = (cols <= rows) & (segment(start + rows, first, second) == segment(start + cols, first, second))
        peak = jnp.max(importance, axis=0, keepdims=True)
        mass = mm_split(lower.astype(BF), jnp.exp(importance - peak))
        mass_ref[rs] = mass
        stat_ref[k, 0:1, :] = peak
        stat_ref[k, 1:2, :] = mass[blocks - 1 :, :]
        stat_ref[k, 2:3, :] = jnp.full_like(peak, NEGATIVE)
        stat_ref[k, 3:4, :] = jnp.zeros_like(peak)
        stat_ref[k, 4:5, :] = peak


def prep_tail_kernel(x_ref, table_ref, out_ref):
    gain = table_ref[GAIN1 : GAIN1 + 1]
    shift = table_ref[SHIFT1 : SHIFT1 + 1]
    out_ref[...] = (normalise(x_ref[...].astype(F32))[0] * gain + shift).astype(BF)


def scan_kernel(info, mine_ref, *refs, masks):
    got_refs, out_ref = refs[:-1], refs[-1]

    def joined(peak, total, got):
        top = jnp.maximum(peak, got[:, 0:1])
        return top, total * jnp.exp(peak - top) + got[:, 1:2] * jnp.exp(got[:, 0:1] - top)

    out_ref[...] = mine_ref[...]
    for mask, got in zip(masks, got_refs):
        peak, total = joined(out_ref[:, 0:1], out_ref[:, 1:2], got)
        out_ref[:, 0:1] = peak
        out_ref[:, 1:2] = total

        @pl.when((info[3] ^ mask) < info[3])
        def _():
            peak, total = joined(out_ref[:, 2:3], out_ref[:, 3:4], got)
            out_ref[:, 2:3] = peak
            out_ref[:, 3:4] = total


def qkv_build_kernel(info, *refs):
    own, pieces, out, sems = refs[0], refs[1:-2], refs[-2], refs[-1]
    shards = len(pieces) // 2 + 1
    rows, width = own.shape
    half = width // 2
    me = info[2]

    def build(core):
        copies = [(own, out.at[pl.ds(pl.multiple_of(me * rows, 16), rows)])]
        for k in range(1, shards):
            for side, group in ((core, 0), (1 - core, shards - 1)):
                at = pl.multiple_of((me ^ crossed(shards, side, k, False)) * rows, 16)
                target = out.at[pl.ds(at, rows), side * half : (side + 1) * half]
                copies.append((pieces[group + k - 1], target))
        copy_all(copies, sems)

    @pl.when(info[1] == 0)
    def _():
        build(0)

    @pl.when(info[1] != 0)
    def _():
        build(1)


def feed_build_kernel(info, *refs, with_out, by_pair):
    if with_out:
        own_fc, own_down, own_out = refs[:3]
        pieces, (fc_ref, down_ref, out_ref, sems) = refs[3:-4], refs[-4:]
    else:
        own_fc, own_down = refs[:2]
        pieces, (fc_ref, down_ref, sems) = refs[2:-3], refs[-3:]
    shards = len(pieces) // 2 + 1
    rows, wide = own_fc.shape
    deep, width = own_down.shape
    split = width // 2
    me = info[2]

    kinds = [info[1] ^ ((info[3] >> 1) & 1), None] if by_pair else [info[1], None]
    kinds[1] = 1 - kinds[0]

    def away(k, partner):
        return jnp.where(kinds[partner] == 0, crossed(shards, 0, k, False), crossed(shards, 1, k, False))

    def build(core):
        at_rows = lambda shard: pl.multiple_of(shard * rows, 16)
        copies = [
            (own_fc, fc_ref.at[pl.ds(at_rows(me), rows)]),
            (own_down, down_ref.at[pl.ds(pl.multiple_of(me * deep, 16), deep)]),
        ]
        if with_out:
            copies.append((own_out, out_ref.at[pl.ds(at_rows(me), rows)]))
        for k in range(1, shards):
            for partner, side in enumerate((core, 1 - core)):
                piece = pieces[partner * (shards - 1) + k - 1]
                shard = me ^ away(k, partner)
                if side == 0:
                    copies.append((piece.at[:, :wide], fc_ref.at[pl.ds(at_rows(shard), rows)]))
                else:
                    for part in range(deep // rows):
                        at = pl.multiple_of(shard * deep + part * rows, 16)
                        copies.append((piece.at[:, part * width : (part + 1) * width], down_ref.at[pl.ds(at, rows)]))
                if with_out:
                    copies.append((piece.at[:, wide:], out_ref.at[pl.ds(at_rows(shard), rows), side * split : (side + 1) * split]))
        copy_all(copies, sems)

    @pl.when(info[1] == 0)
    def _():
        build(0)

    @pl.when(info[1] != 0)
    def _():
        build(1)


def qkv_kernel(normed_ref, tail_ref, weight_ref, table_ref, out_ref, tail_out_ref):
    j = pl.program_id(0)
    weight = weight_ref[...]
    bias = table_ref[pl.ds(BIAS_QKV + j, 1)]
    factor = jnp.where(j == 0, SCALE, 1.0)
    out_ref[...] = ((mm(normed_ref[...], weight) + bias).astype(BF).astype(F32) * factor).astype(BF)

    @pl.when(j > 0)
    def _():
        tail_out_ref[...] = (mm(tail_ref[...], weight) + bias).astype(BF)


def lane_masks():
    first = iota((1, LANES), 1) < HEAD
    return first.astype(BF), (~first).astype(BF)


def grouped(part, keep_first, keep_second):
    return jnp.concatenate([part * keep_first, part * keep_second], axis=0)


def tile_masks(start, half, first, second):
    dims = (WINDOW, LANES)
    row = iota(dims, 0)
    col = iota(dims, 1) & (HEAD - 1)
    base = start + WINDOW * half
    mine = segment(base + row, first, second)
    far = segment(base - WINDOW + col, first, second) == mine
    near = (col <= row) & (segment(base + col, first, second) == mine)
    if half == 0:
        far = far & (col > row) & (base - WINDOW + col >= 0)
    return far, near, col <= row


def spread(columns, pair, rows):
    left = columns[:, 2 * pair : 2 * pair + 1]
    right = columns[:, 2 * pair + 1 : 2 * pair + 2]
    return jnp.where(iota((rows, LANES), 1) < HEAD, left, right)


def key_groups(qkv_ref, halo_ref, width, pair, keep_first, keep_second, one_group):
    at = slice(pair * LANES, (pair + 1) * LANES)
    ks = slice(width + pair * LANES, width + (pair + 1) * LANES)
    vs = slice(2 * width + pair * LANES, 2 * width + (pair + 1) * LANES)
    keys = [grouped(part, keep_first, keep_second) for part in (halo_ref[:, at], qkv_ref[:WINDOW, ks], qkv_ref[WINDOW:, ks])]
    values = [
        jnp.concatenate([grouped(part, keep_first, keep_second), one_group], axis=1)
        for part in (halo_ref[:, ks], qkv_ref[:WINDOW, vs], qkv_ref[WINDOW:, vs])
    ]
    return keys, values


def attention_kernel(info, bounds, qkv_ref, halo_ref, imp_ref, mass_ref, before_ref, att_ref, probs_ref, sig_ref, inv_ref):
    s = pl.program_id(0)
    blocks, width = att_ref.shape
    start = info[0]
    first, second = bounds[0, s], bounds[1, s]
    pairs = width // LANES
    peak = before_ref[0, 4:5, :]
    carry_peak = before_ref[0, 2:3, :]
    carry_total = before_ref[0, 3:4, :]
    top = before_ref[0, 0:1, :]
    joined = jnp.maximum(peak, carry_peak)
    place = start + iota((blocks, LANES), 0)
    continues = segment(place, first, second) == segment(jnp.full((1, LANES), start - 1, jnp.int32), first, second)
    mass = mass_ref[...] * jnp.exp(peak - joined) + jnp.where(
        continues, carry_total * jnp.exp(carry_peak - joined), 0.0
    )
    threshold = joined + jnp.log(mass) - math.log(KTOP)
    late = threshold[WINDOW:]
    inv_ref[...] = 1.0 / (mass[WINDOW:] * jnp.exp(joined - top))
    imp_rows = imp_ref[...].T
    keep_first, keep_second = lane_masks()
    one_group = grouped(jnp.ones((WINDOW, LANES), BF), keep_first, keep_second)
    masks = [tile_masks(start, half, first, second) for half in (0, 1)]
    lane = iota((WINDOW, LANES), 1) < HEAD
    for p0 in range(0, pairs, FORWARD_STAGE):
        ps = range(p0, min(pairs, p0 + FORWARD_STAGE))
        groups = {p: key_groups(qkv_ref, halo_ref, width, p, keep_first, keep_second, one_group) for p in ps}
        logits = {}
        for p in ps:
            ls = slice(p * LANES, (p + 1) * LANES)
            for half in (0, 1):
                rs = slice(half * WINDOW, (half + 1) * WINDOW)
                logits[p, half] = mm(qkv_ref[rs, ls], jnp.concatenate(groups[p][0][half : half + 2], axis=0), NT)
        soft_in = {}
        for p in ps:
            ls = slice(p * LANES, (p + 1) * LANES)
            for half in (0, 1):
                far_ok, near_ok, gated = masks[half]
                far, near = logits[p, half][:, :LANES], logits[p, half][:, LANES:]
                if half == 1:
                    row = jnp.concatenate([imp_rows[2 * p : 2 * p + 1, :WINDOW], imp_rows[2 * p + 1 : 2 * p + 2, :WINDOW]], axis=1)
                    gap = spread(late, p, WINDOW) - row
                    small = jnp.exp(-jnp.abs(gap))
                    soft = jnp.maximum(gap, 0.0) + jnp.log(1.0 + small)
                    sig_ref[:, ls] = (jnp.where(gap >= 0, 1.0, small) / (1.0 + small)).astype(BF)
                    far = jnp.where(gated, far - soft, far)
                far = jnp.where(far_ok, far, NEGATIVE)
                near = jnp.where(near_ok, near, NEGATIVE)
                best = jnp.maximum(far, near)
                best_first = jnp.max(jnp.where(lane, best, NEGATIVE), axis=1, keepdims=True)
                best_second = jnp.max(jnp.where(lane, NEGATIVE, best), axis=1, keepdims=True)
                best = jnp.where(lane, best_first, best_second)
                soft_in[p, half] = (jnp.exp(far - best), jnp.exp(near - best))
        for p in ps:
            ls = slice(p * LANES, (p + 1) * LANES)
            for half in (0, 1):
                rs = slice(half * WINDOW, (half + 1) * WINDOW)
                far, near = soft_in[p, half]
                weights = jnp.concatenate([far.astype(BF), near.astype(BF)], axis=1)
                mixed = mm(weights, jnp.concatenate(groups[p][1][half : half + 2], axis=0))
                inverse = 1.0 / mixed[:, LANES:]
                att_ref[rs, ls] = (mixed[:, :LANES] * inverse).astype(BF)
                probs_ref[rs, 2 * p * LANES : (2 * p + 1) * LANES] = (far * inverse).astype(BF)
                probs_ref[rs, (2 * p + 1) * LANES : (2 * p + 2) * LANES] = (near * inverse).astype(BF)


def project_kernel(att_ref, x_ref, weight_ref, table_ref, middle_ref, second_ref):
    middle = x_ref[...].astype(F32) + mm(att_ref[...], weight_ref[...]) + table_ref[BIAS_OUT : BIAS_OUT + 1]
    middle_ref[...] = middle
    second_ref[...] = (normalise(middle)[0] * table_ref[GAIN2 : GAIN2 + 1] + table_ref[SHIFT2 : SHIFT2 + 1]).astype(BF)


def feed_kernel(info, sec_ref, dy_ref, fc_ref, down_ref, table_ref, hid_ref, dpre_ref, db_ref, keep_ref, give_ref, *, chunk):
    fc = fc_ref[...]
    down = down_ref[...]
    row = BIAS_FC + chunk * BLOCKS + pl.program_id(0)
    pre = mm(sec_ref[...], fc) + table_ref[pl.ds(row, 1)]
    d_hidden = mm(dy_ref[...], down, NT)
    square = pre * pre
    tanh = jnp.tanh(pre * (GELU_A + GELU_A * GELU_B * square))
    half = 0.5 + 0.5 * tanh
    hidden = (pre * half).astype(BF)
    slope = half + pre * (0.5 * GELU_A + 1.5 * GELU_A * GELU_B * square) * (1.0 - tanh * tanh)
    d_pre = d_hidden * slope
    d_low = d_pre.astype(BF)
    hid_ref[...] = hidden
    dpre_ref[...] = d_low
    db_ref[...] = jnp.broadcast_to(jnp.sum(d_pre, axis=0, keepdims=True), db_ref.shape)
    d_down = mm(hidden, dy_ref[...], TN).astype(BF)
    d_fc = mm(sec_ref[...], d_low, TN).astype(BF)

    @pl.when(info[1] == 0)
    def _():
        keep_ref[...] = d_fc
        give_ref[...] = d_down

    @pl.when(info[1] != 0)
    def _():
        keep_ref[...] = d_down
        give_ref[...] = d_fc


def feed_add_kernel(info, kept_ref, got_ref, keep_ref, give_ref, held):
    shards, rows, wide = held.shape
    width = kept_ref.shape[1]
    me = info[2]
    per_block = shards // BLOCKS
    deep = width // per_block

    def put(core):
        for block in range(BLOCKS):
            at = slice(block * width, (block + 1) * width)
            total = add(kept_ref[at], got_ref[at])
            if core == 0:
                for shard in range(shards):
                    held[ranked(shards, 0, me ^ shard), :, at] = total[shard * rows : (shard + 1) * rows]
            else:
                for k in range(per_block):
                    place = ranked(shards, 1, me ^ (block * per_block + k))
                    for part in range(deep // rows):
                        begin = k * deep + part * rows
                        held[place, :, part * width : (part + 1) * width] = total[begin : begin + rows]

    @pl.when(info[1] == 0)
    def _():
        put(0)

    @pl.when(info[1] != 0)
    def _():
        put(1)

    half = shards // 2
    keep_ref[...] = held[:half]
    give_ref[...] = held[half:]


def ranked(shards, core, far):
    order = bit_orders(shards)[core]
    index = jnp.int32(0)
    for step, bit in enumerate(order):
        index = index | (((far >> bit) & 1) << (len(order) - 1 - step))
    return index


def middle_kernel(*refs):
    dpre_refs = refs[:CHUNKS]
    fc_refs = refs[CHUNKS : 2 * CHUNKS]
    middle_ref, dy_ref, table_ref, dmid_ref, branch_ref, sums_ref = refs[2 * CHUNKS :]
    part_rows = middle_ref.shape[0] // 2
    totals = [0.0] * 4
    for part in range(2):
        rs = slice(part * part_rows, (part + 1) * part_rows)
        d_norm = None
        for dpre_ref, fc_ref in zip(dpre_refs, fc_refs):
            piece = mm(dpre_ref[rs], fc_ref[...], NT)
            d_norm = piece if d_norm is None else d_norm + piece
        unit, scale = normalise(middle_ref[rs])
        dy = dy_ref[rs].astype(F32)
        d_middle = dy + norm_back(d_norm, unit, scale, table_ref[GAIN2 : GAIN2 + 1])
        dmid_ref[rs] = d_middle
        branch = d_middle.astype(BF)
        branch_ref[rs] = branch
        for k, value in enumerate((d_norm * unit, d_norm, branch.astype(F32), dy)):
            totals[k] = totals[k] + jnp.sum(value, axis=0, keepdims=True)

    @pl.when(pl.program_id(0) == 0)
    def _():
        for k in range(4):
            sums_ref[k : k + 1] = totals[k]

    @pl.when(pl.program_id(0) > 0)
    def _():
        for k in range(4):
            sums_ref[k : k + 1] += totals[k]


def branch_kernel(info, branch_ref, att_ref, weight_ref, datt_ref, keep_ref, give_ref):
    shards, rows, split = keep_ref.shape
    store_halves(info, mm(att_ref[...], branch_ref[...], TN), keep_ref, give_ref, shards, rows, split)
    datt_ref[...] = mm(branch_ref[...], weight_ref[...], NT).astype(BF)


def store_halves(info, total, keep_ref, give_ref, shards, rows, split):
    me = info[2]

    def store(side, to):
        for shard in range(shards):
            value = total[shard * rows : (shard + 1) * rows, side * split : (side + 1) * split]
            to[ranked(shards, side, me ^ shard)] = value.astype(BF)

    @pl.when(info[1] == 0)
    def _():
        store(0, keep_ref)
        store(1, give_ref)

    @pl.when(info[1] != 0)
    def _():
        store(1, keep_ref)
        store(0, give_ref)


def attention_back_kernel(info, bounds, qkv_ref, halo_ref, att_ref, datt_ref, probs_ref, sig_ref, inv_ref, imp_ref, before_ref, dqkv_ref, dhalo_ref, dimp_ref, total_ref, rows_scratch, *, first_seq, pairs):
    s = first_seq + pl.program_id(0)
    blocks, width = att_ref.shape
    start = info[0]
    first, second = bounds[0, s], bounds[1, s]
    keep_first, keep_second = lane_masks()
    one_group = grouped(jnp.ones((WINDOW, LANES), BF), keep_first, keep_second)
    lane = iota((WINDOW, LANES), 1) < HEAD
    gated = (iota((WINDOW, LANES), 1) & (HEAD - 1)) <= iota((WINDOW, LANES), 0)
    head_lane = iota((LANES, LANES), 1)
    head_row = iota((LANES, LANES), 0)
    d_threshold = jnp.zeros((WINDOW, LANES), F32)
    rows_scratch[...] = jnp.zeros_like(rows_scratch)
    wide = pairs * LANES
    for k0 in range(0, pairs, BACKWARD_STAGE):
        ks_ = range(k0, min(pairs, k0 + BACKWARD_STAGE))
        groups = {k: key_groups(qkv_ref, halo_ref, width, k, keep_first, keep_second, one_group) for k in ks_}
        centred, low = {}, {}
        for k in ks_:
            ls = slice(k * LANES, (k + 1) * LANES)
            for half in (0, 1):
                rs = slice(half * WINDOW, (half + 1) * WINDOW)
                d_out = datt_ref[rs, ls]
                product = (-(d_out.astype(F32) * att_ref[rs, ls].astype(F32))).astype(BF)
                left = jnp.concatenate([d_out, product], axis=1)
                centred[k, half] = mm(left, jnp.concatenate(groups[k][1][half : half + 2], axis=0), NT)
        for k in ks_:
            ls = slice(k * LANES, (k + 1) * LANES)
            for half in (0, 1):
                rs = slice(half * WINDOW, (half + 1) * WINDOW)
                d_logits = probs_ref[rs, 2 * k * LANES : (2 * k + 2) * LANES].astype(F32) * centred[k, half]
                low[k, half] = d_logits.astype(BF)
                if half == 1:
                    gate = jnp.where(gated, d_logits[:, :LANES] * sig_ref[:, ls].astype(F32), 0.0)
                    rows_scratch[k : k + 1, :] = jnp.sum(gate, axis=0, keepdims=True)
                    chosen = (head_lane == 2 * k + (head_row >= HEAD).astype(jnp.int32)).astype(BF)
                    d_threshold = d_threshold - mm(gate.astype(BF), chosen)
        for k in ks_:
            ls = slice(k * LANES, (k + 1) * LANES)
            far_keys, near_keys, far_values, near_values = [], [], [], []
            for half in (0, 1):
                rs = slice(half * WINDOW, (half + 1) * WINDOW)
                dqkv_ref[rs, ls] = (mm(low[k, half], jnp.concatenate(groups[k][0][half : half + 2], axis=0)) * SCALE).astype(BF)
                d_keys = mm(low[k, half], qkv_ref[rs, ls], TN)
                d_values = mm(probs_ref[rs, 2 * k * LANES : (2 * k + 2) * LANES], datt_ref[rs, ls], TN)
                far_keys.append(jnp.where(lane, d_keys[:WINDOW], d_keys[WINDOW : 2 * WINDOW]))
                near_keys.append(jnp.where(lane, d_keys[2 * WINDOW : 3 * WINDOW], d_keys[3 * WINDOW :]))
                far_values.append(jnp.where(lane, d_values[:WINDOW], d_values[WINDOW : 2 * WINDOW]))
                near_values.append(jnp.where(lane, d_values[2 * WINDOW : 3 * WINDOW], d_values[3 * WINDOW :]))
            ks = slice(wide + k * LANES, wide + (k + 1) * LANES)
            vs = slice(2 * wide + k * LANES, 2 * wide + (k + 1) * LANES)
            dhalo_ref[:, ks] = far_keys[0].astype(BF)
            dhalo_ref[:, vs] = far_values[0].astype(BF)
            dqkv_ref[:WINDOW, ks] = (near_keys[0] + far_keys[1]).astype(BF)
            dqkv_ref[WINDOW:, ks] = near_keys[1].astype(BF)
            dqkv_ref[:WINDOW, vs] = (near_values[0] + far_values[1]).astype(BF)
            dqkv_ref[WINDOW:, vs] = near_values[1].astype(BF)
    dhalo_ref[:, :wide] = jnp.zeros((WINDOW, wide), BF)
    weighted = d_threshold * inv_ref[...]
    row = iota((blocks, WINDOW), 0)
    col = iota((blocks, WINDOW), 1) + WINDOW
    after = (col >= row) & (segment(start + row, first, second) == segment(start + col, first, second))
    later = mm_split(after.astype(BF), weighted)
    total_ref[0, 0:1, :] = later[0:1]
    turned = rows_scratch[...].T
    pick_first = (head_lane == 2 * head_row).astype(BF)
    pick_second = (head_lane == 2 * head_row + 1).astype(BF)

    def pick(values, chosen):
        high = values.astype(BF)
        return mm(high, chosen) + mm((values - high.astype(F32)).astype(BF), chosen)

    direct = pick(turned[:HEAD], pick_first) + pick(turned[HEAD:], pick_second)
    local = jnp.exp(imp_ref[...] - before_ref[0, 0:1, :]) * later
    dimp_ref[:WINDOW] = local[:WINDOW] + direct
    dimp_ref[WINDOW:] = local[WINDOW:]


def tail_back_kernel(*refs):
    dhalo_refs = refs[:-5]
    weight_ref, x_ref, table_ref, out_ref, sums_ref = refs[-5:]
    width = x_ref.shape[1]
    begin = 0
    totals = [0.0, 0.0]
    for dhalo_ref in dhalo_refs:
        rs = slice(begin, begin + dhalo_ref.shape[0])
        begin += dhalo_ref.shape[0]
        d_norm = mm(dhalo_ref[:, width:], weight_ref[:, width:], NT)
        unit, scale = normalise(x_ref[rs].astype(F32))
        out_ref[rs] = norm_back(d_norm, unit, scale, table_ref[GAIN1 : GAIN1 + 1]).astype(BF)
        for k, value in enumerate((d_norm * unit, d_norm)):
            totals[k] = totals[k] + jnp.sum(value, axis=0, keepdims=True)
    for k in range(2):
        sums_ref[k : k + 1] = totals[k]


def qkv_grad_kernel(info, normed_ref, tail_ref, *refs, groups):
    dqkv_refs, dhalo_refs = refs[:groups], refs[groups : 2 * groups]
    give_ref, keep_ref, given_sums, kept_sums = refs[2 * groups :]
    shards, rows, split = keep_ref.shape
    me = info[2]
    step = pl.program_id(0)
    owner = jnp.where(step == 0, 1 - info[1], info[1])
    total, sums = 0.0, 0.0
    for left_ref, right_refs in ((normed_ref, dqkv_refs), (tail_ref, dhalo_refs)):
        begin = 0
        for right_ref in right_refs:
            rs = slice(begin, begin + right_ref.shape[0])
            begin += right_ref.shape[0]
            total = total + mm(left_ref[rs], right_ref[...], TN)
            sums = sums + jnp.sum(right_ref[...].astype(F32), axis=0, keepdims=True)

    def store(to, sums_to):
        sums_to[0:1] = sums
        for shard in range(shards):
            far = me ^ shard
            place = jnp.where(owner == 0, ranked(shards, 0, far), ranked(shards, 1, far))
            to[place] = total[shard * rows : (shard + 1) * rows].astype(BF)

    @pl.when(step == 0)
    def _():
        store(give_ref, given_sums)

    @pl.when(step != 0)
    def _():
        store(keep_ref, kept_sums)


def input_grad_kernel(info, bounds, *refs, groups):
    dqkv_refs, dimp_refs = refs[:groups], refs[groups : 2 * groups]
    weight_ref, score_ref, normed_ref, x_ref, table_ref, dmid_ref, back_ref, imp_ref, before_ref, after_ref, out_ref, sums_ref, score_out_ref = refs[2 * groups :]
    i = pl.program_id(0)
    per_group = pl.num_programs(0) // groups
    seqs = back_ref.shape[0]
    blocks = x_ref.shape[0] // seqs
    start = info[0]

    def chosen(refs):
        value = refs[0][...]
        for k in range(1, groups):
            value = jnp.where(i >= k * per_group, refs[k][...], value)
        return value

    dqkv, d_local = chosen(dqkv_refs), chosen(dimp_refs)
    d_imps = []
    for s in range(seqs):
        rs = slice(s * blocks, (s + 1) * blocks)
        first, second = bounds[0, i * seqs + s], bounds[1, i * seqs + s]
        place = start + iota((blocks, LANES), 0)
        onward = segment(place, first, second) == segment(jnp.full((1, LANES), start + blocks, jnp.int32), first, second)
        extra = jnp.exp(imp_ref[rs] - before_ref[s, 0:1, :]) * after_ref[s, 0:1, :]
        d_imps.append(d_local[rs] + jnp.where(onward, extra, 0.0))
    d_imp = jnp.concatenate(d_imps, axis=0).astype(BF)
    d_norm = mm(dqkv, weight_ref[...], NT) + mm(d_imp, score_ref[...])
    unit, scale = normalise(x_ref[...].astype(F32))
    d_value = norm_back(d_norm, unit, scale, table_ref[GAIN1 : GAIN1 + 1]) + dmid_ref[...]
    for s in range(seqs):
        rs = slice(s * blocks, s * blocks + WINDOW)
        out_ref[rs] = d_value[rs]
        rs = slice(s * blocks + WINDOW, (s + 1) * blocks)
        out_ref[rs] = d_value[rs] + back_ref[s].astype(F32)
    sums = [jnp.sum(value, axis=0, keepdims=True) for value in (d_norm * unit, d_norm)]
    score = mm(d_imp, normed_ref[...], TN)

    @pl.when(i == 0)
    def _():
        score_out_ref[...] = score
        for k in range(2):
            sums_ref[k : k + 1] = sums[k]

    @pl.when(i > 0)
    def _():
        score_out_ref[...] += score
        for k in range(2):
            sums_ref[k : k + 1] += sums[k]


def output_kernel(*refs):
    hid_refs, down_refs, (middle_ref, table_ref) = refs[:CHUNKS], refs[CHUNKS : 2 * CHUNKS], refs[2 * CHUNKS : 2 * CHUNKS + 2]
    out_ref, total = refs[-2:]
    part = 0.0
    for hid_ref, down_ref in zip(hid_refs, down_refs):
        part = part + mm(hid_ref[...], down_ref[...])

    @pl.when(pl.program_id(0) == 0)
    def _():
        total[...] = middle_ref[...] + table_ref[BIAS_DOWN : BIAS_DOWN + 1] + part

    @pl.when(pl.program_id(0) == pl.num_programs(0) - 1)
    def _():
        out_ref[...] = (total[...] + part).astype(BF)


def small_pack_kernel(info, first_ref, tail_ref, second_ref, kept_ref, given_ref, *refs):
    bias_refs = refs[:CHUNKS]
    score_ref, out_ref, whole = refs[CHUNKS:]
    shards, count, rows = out_ref.shape
    me = info[2]
    whole[0:2] = first_ref[0:2] + tail_ref[0:2]
    whole[2:VECTORS] = second_ref[0 : VECTORS - 2]
    width = whole.shape[1]
    even = info[1] == 0
    whole[VECTORS : VECTORS + 1] = jnp.where(even, kept_ref[0:1, :width], given_ref[0:1, :width])
    whole[VECTORS + 1 : VECTORS + 2] = jnp.where(even, given_ref[0:1, width // 2 :], kept_ref[0:1, width // 2 :])
    base = VECTORS + 2
    for k in range(CHUNKS * BLOCKS):
        whole[base + k : base + k + 1] = bias_refs[k // BLOCKS][0:1, (k % BLOCKS) * width : (k % BLOCKS + 1) * width]
    heads = count - VECTORS - QV_ROWS - FC_ROWS
    whole[base + CHUNKS * BLOCKS : base + CHUNKS * BLOCKS + heads] = score_ref[0:heads]
    per_block = shards // BLOCKS
    per_chunk = FC_ROWS // CHUNKS
    for shard in range(shards):
        at = slice(shard * rows, (shard + 1) * rows)
        lines = [whole[0:VECTORS, at]]
        row = VECTORS + shard // (shards // 2)
        for k in range(QV_ROWS):
            begin = (shard % (shards // 2)) * QV_ROWS * rows + k * rows
            lines.append(whole[row : row + 1, begin : begin + rows])
        for chunk in range(CHUNKS):
            row = base + chunk * BLOCKS + shard // per_block
            for k in range(per_chunk):
                begin = (shard % per_block) * per_chunk * rows + k * rows
                lines.append(whole[row : row + 1, begin : begin + rows])
        lines.append(whole[base + CHUNKS * BLOCKS : base + CHUNKS * BLOCKS + heads, at])
        out_ref[ranked(shards, 0, me ^ shard)] = jnp.concatenate(lines, axis=0)


def add(left, right):
    return (left.astype(F32) + right.astype(F32)).astype(BF)


def combine(peak_a, total_a, peak_b, total_b):
    joined = jnp.maximum(peak_a, peak_b)
    return joined, total_a * jnp.exp(peak_a - joined) + total_b * jnp.exp(peak_b - joined)


def tie(*values):
    return lax.optimization_barrier(values)


class Net:
    def __init__(self):
        self.n_seq = lax.axis_size("seq")
        self.n_dp = lax.axis_size("dp")
        self.seq = lax.axis_index("seq")
        self.dp = lax.axis_index("dp")
        self.core = self.seq % 2
        self.orders = bit_orders(self.n_dp)
        self.bits = len(self.orders[0])
        self.seq_bits = self.n_seq.bit_length() - 1
        self.by_pair = self.bits == 2 and self.seq_bits >= 2

    def send(self, value, target):
        pairs = []
        for s in range(self.n_seq):
            for d in range(self.n_dp):
                goal = target(s, d)
                if 0 <= goal[0] < self.n_seq:
                    pairs.append((s * self.n_dp + d, goal[0] * self.n_dp + goal[1]))
        return lax.ppermute(value, ("seq", "dp"), pairs)

    def across(self, value, step):
        return self.send(value, lambda s, d: (s, d ^ (1 << self.orders[s % 2][step])))

    def chip(self, value):
        return self.send(value, lambda s, d: (s ^ 1, d))

    def along(self, value, bit):
        return self.send(value, lambda s, d: (s ^ (1 << bit), d))

    def masked(self, value, mask):
        return self.send(value, lambda s, d: (s ^ mask, d))

    def shifted(self, value, by):
        return self.send(value, lambda s, d: (s + by, d))

    def across_pair(self, value, step):
        return self.send(value, lambda s, d: (s, d ^ (1 << self.orders[(s ^ (s >> 1)) % 2][step])))

    def gather_step(self, pieces, step):
        return pieces + [self.across(piece, step) for piece in pieces]

    def sum_all(self, value):
        value = value + self.chip(value)
        for step in range(self.bits):
            value = value + self.across(value, step)
        for bit in range(1, self.seq_bits):
            value = value + self.along(value, bit)
        return value


class Reduction:
    def __init__(self, net, keep, give):
        self.net = net
        self.keep, self.give = keep, give
        z_bits = list(range(1, net.seq_bits))
        self.z_orders = (z_bits, z_bits[1:2] + z_bits[:1] + z_bits[2:])
        self.todo = ["across"] * net.bits + ["split"] + ["swap"] * (len(z_bits) - 1) + ["join"]
        self.done = 0
        self.got = None
        self.pending = False

    def along(self, value, place):
        return self.net.send(value, lambda s, d: (s ^ (1 << self.z_orders[s % 2][place]), d))

    def start(self):
        if not self.todo:
            return
        kind = self.todo[0]
        self.pending = True
        if kind == "across":
            self.got = self.net.across(self.give, self.done)
        elif kind == "split":
            half = self.keep.shape[0] // 2
            z_bit = jnp.where(self.net.core == 0, self.z_orders[0][0], self.z_orders[1][0])
            self.upper = (self.net.seq >> z_bit) % 2 == 1
            low, high = self.keep[:half], self.keep[half:]
            self.got = self.along(jnp.where(self.upper, low, high), 0)
            self.keep = jnp.where(self.upper, high, low)
        elif kind == "swap":
            self.got = self.along(self.keep, self.done - self.net.bits)
        else:
            self.got = self.along(self.keep, 0)

    def finish(self, after=None):
        if not self.pending:
            return
        if after is not None:
            self.got, _ = tie(self.got, after)
        kind = self.todo.pop(0)
        self.done += 1
        self.pending = False
        if kind == "join":
            low, high = jnp.where(self.upper, self.got, self.keep), jnp.where(self.upper, self.keep, self.got)
            self.keep = jnp.concatenate([low, high], axis=0)
            return
        half = self.keep.shape[0] // 2
        if kind == "across" and half:
            self.keep, self.give = add(self.keep[:half], self.got[:half]), add(self.keep[half:], self.got[half:])
        elif kind == "across":
            self.keep = add(self.keep[0], self.got[0])
        else:
            self.keep = add(self.keep, self.got)


def pin(value, *reds):
    held = [value]
    for red in reds:
        held += [red.keep] + ([red.give] if red.todo and red.todo[0] == "across" else [])
    held = list(tie(*held))
    value = held.pop(0)
    for red in reds:
        red.keep = held.pop(0)
        if red.todo and red.todo[0] == "across":
            red.give = held.pop(0)
    return value


def body(block_input, doc_bounds, first_gain, first_shift, qkv_weight, qv_bias, score_weight, out_weight, out_bias, second_gain, second_shift, fc_weight, fc_bias, down_weight, down_bias, cotangent):
    net = Net()
    seqs, blocks, width = block_input.shape
    tokens = seqs * blocks
    heads = score_weight.shape[1]
    shards = net.n_dp
    rows = width // shards
    hidden = fc_weight.shape[1]
    tail = seqs * WINDOW
    core = net.core
    place = jnp.arange(4, dtype=jnp.int32)
    info = jnp.where(place == 0, net.seq * blocks, jnp.where(place == 1, core, jnp.where(place == 2, net.dp, net.seq))).astype(jnp.int32)
    bounds = doc_bounds.T
    x_flat = block_input.reshape(tokens, width)
    dy = cotangent.reshape(tokens, width)
    wide = hidden // CHUNKS
    deep = hidden // shards // CHUNKS
    half_qkv = 3 * width // 2
    sems = lambda count: pltpu.SemaphoreType.DMA((count,))
    by_seq = lambda rows_, cols: pl.BlockSpec((rows_, cols), lambda s, *_: (s, 0))
    stat = pl.BlockSpec((1, 8, LANES), lambda s, *_: (s, 0, 0))
    table_spec = whole_spec((16, width))
    full = whole_spec((tokens, width))
    tile = 2 * blocks
    by_tile = pl.BlockSpec((tile, width), lambda i, *_: (i, 0))
    pairs = width // LANES
    parts = [(0, pairs)]

    vectors = [first_gain, first_shift, second_gain, second_shift, out_bias, down_bias, qv_bias, fc_bias]
    small_rows = sum(part.shape[0] for part in vectors) // rows + heads
    small = call(
        start_kernel,
        "start",
        (1,),
        [pl.BlockSpec(part.shape, lambda *_: (0,)) for part in vectors] + [whole_spec((heads, rows))],
        whole_spec((small_rows, rows)),
        shape((small_rows, rows), BF),
        micros=1,
        far_in=tuple(range(len(vectors) + 1)),
    )(*vectors, score_weight.T)

    def begin_gather(own):
        return [own, net.across(own, 0)], [net.across(own, 1)] if net.bits > 1 else []

    def end_gather(pieces, ahead):
        if net.bits > 1:
            pieces = pieces + ahead + [net.across(pieces[1], 1)]
        for step in range(2, net.bits):
            pieces = net.gather_step(pieces, step)
        return pieces

    small_state = begin_gather(small)
    first_weight, _ = tie(qkv_weight, small)
    own, x_tail = call(
        first_pack_kernel,
        "first_pack",
        (1,),
        [pl.BlockSpec((rows, half_qkv), lambda _, info: (0, info[1])), pl.BlockSpec((seqs, WINDOW, width), lambda *_: (0, blocks // WINDOW - 1, 0))],
        [whole_spec((rows, half_qkv)), whole_spec((tail, width))],
        [shape((rows, half_qkv), BF), shape((tail, width), BF)],
        prefetch=1,
        micros=2,
        far_in=(0, 1),
    )(info, first_weight, block_input)
    own, x_tail, *held = tie(own, x_tail, *small_state[0], *small_state[1])
    small_pieces = end_gather(held[:2], held[2:])
    qkv_state = begin_gather(own)
    x_tail = net.shifted(x_tail, 1)
    qkv_pieces = end_gather(*qkv_state)

    fc_weight, _ = tie(fc_weight, own)
    packs = call(
        feed_pack_kernel,
        "feed_pack",
        (1,),
        [whole_spec((rows, hidden)), whole_spec(down_weight.shape), whole_spec((rows, width))],
        [whole_spec((rows, wide))] * CHUNKS + [whole_spec((rows, wide + width // 2)), whole_spec((rows, wide))],
        [shape((rows, wide), BF)] * CHUNKS + [shape((rows, wide + width // 2), BF), shape((rows, wide), BF)],
        prefetch=1,
        micros=2,
        limit=24,
        far_in=(0, 1, 2),
    )(info, fc_weight, down_weight, out_weight)
    fc_own, feed_own = packs[:CHUNKS], packs[CHUNKS:]
    small_pieces[-1], *feed_own = tie(small_pieces[-1], *feed_own)
    first_own, _ = tie(feed_own[0], qkv_pieces[1])

    def begin_feed(own):
        if not net.by_pair:
            return begin_gather(own)
        return [own, net.across_pair(own, 0)], []

    def end_feed(pieces, ahead):
        if not net.by_pair:
            return end_gather(pieces, ahead)
        return pieces + [net.masked(pieces[1], 2), net.across_pair(pieces[1], 1)]

    a_state = begin_feed(first_own)

    table, score = call(
        params_kernel,
        "params",
        (1,),
        [whole_spec((small_rows, rows))] * shards,
        [table_spec, whole_spec((LANES, width))],
        [shape((16, width), F32), shape((LANES, width), BF)],
        scratch=[pltpu.VMEM((shards, small_rows, rows), F32)],
        prefetch=1,
        micros=1,
    )(info, *small_pieces)

    group = seqs // 2
    normed, importance, mass, stats = call(
        prep_kernel,
        "prep",
        (seqs // group,),
        [by_seq(group * blocks, width), table_spec, whole_spec((LANES, width))],
        [by_seq(group * blocks, width), by_seq(group * blocks, LANES), by_seq(group * blocks, LANES), pl.BlockSpec((group, 8, LANES), lambda s, *_: (s, 0, 0))],
        [shape((tokens, width), BF), shape((tokens, LANES), F32), shape((tokens, LANES), F32), shape((seqs, 8, LANES), F32)],
        prefetch=2,
        micros=3,
    )(info, bounds, x_flat, table, score)

    def scan_step(state, masks, got):
        spec = whole_spec((seqs, 8, LANES))
        return call(
            lambda *refs: scan_kernel(*refs, masks=masks),
            "scan",
            (1,),
            [spec] * (1 + len(masks)),
            spec,
            shape((seqs, 8, LANES), F32),
            prefetch=1,
            micros=0.5,
        )(info, state, *got)

    for bit in range(net.seq_bits - 1):
        stats = scan_step(stats, [1 << bit], [net.along(stats, bit)])
        if bit == 0:
            stats, *qkv_pieces = tie(stats, *qkv_pieces)
    qkv_others = [net.chip(piece) for piece in qkv_pieces[1:]]
    w_qkv = call(
        qkv_build_kernel,
        "qkv_build",
        (1,),
        [whole_spec((rows, 3 * width))] + [whole_spec((rows, half_qkv))] * (2 * shards - 2),
        ANY,
        shape((width, 3 * width), BF),
        scratch=[sems(2 * shards)],
        prefetch=1,
        micros=2,
    )(info, qkv_weight, *qkv_pieces[1:], *qkv_others)

    def build_feed(chunk, pieces, others):
        with_out = chunk == 0
        owns = [fc_own[chunk], down_weight] + ([out_weight] if with_out else [])
        specs = [whole_spec((rows, wide)), pl.BlockSpec((deep, width), lambda *_: (chunk, 0))] + ([whole_spec((rows, width))] if with_out else [])
        outs = [shape((width, wide), BF), shape((wide, width), BF)] + ([shape((width, width), BF)] if with_out else [])
        count = 3 + (shards - 1) * (1 + deep // rows + 2)
        return call(
            lambda *refs: feed_build_kernel(*refs, with_out=with_out, by_pair=net.by_pair),
            "feed_build",
            (1,),
            specs + [whole_spec(pieces[0].shape)] * (2 * shards - 2),
            [ANY] * len(outs),
            outs,
            scratch=[sems(count)],
            prefetch=1,
            micros=2,
        )(info, *owns, *pieces[1:], *others)

    normed_tail = call(
        prep_tail_kernel,
        "prep_tail",
        (1,),
        [whole_spec((tail, width)), table_spec],
        whole_spec((tail, width)),
        shape((tail, width), BF),
        micros=1,
    )(x_tail, table)
    w_qkv, *held = tie(w_qkv, *a_state[0], *a_state[1])
    a_pieces = end_feed(held[:2], held[2:])
    second_own, _ = tie(feed_own[1], held[1])
    b_state = begin_feed(second_own)
    col = lambda rows_: pl.BlockSpec((rows_, width), lambda j: (0, j))
    qkv, qkv_tail = call(
        qkv_kernel,
        "qkv",
        (3,),
        [full, whole_spec((tail, width)), col(width), table_spec],
        [col(tokens), pl.BlockSpec((tail, width), lambda j: (0, jnp.maximum(j - 1, 0)))],
        [shape((tokens, 3 * width), BF), shape((tail, 2 * width), BF)],
        micros=6.5,
        limit=24,
    )(normed, normed_tail, w_qkv, table)
    qkv, got = tie(qkv, net.along(stats, net.seq_bits - 1))
    before = scan_step(stats, [1 << (net.seq_bits - 1)], [got])

    attended, probs, gates, inverse = call(
        attention_kernel,
        "attention",
        (seqs,),
        [by_seq(blocks, 3 * width), by_seq(WINDOW, 2 * width), by_seq(blocks, LANES), by_seq(blocks, LANES), stat],
        [by_seq(blocks, width), by_seq(blocks, 2 * width), by_seq(WINDOW, width), by_seq(WINDOW, LANES)],
        [shape((tokens, width), BF), shape((tokens, 2 * width), BF), shape((tail, width), BF), shape((tail, LANES), F32)],
        prefetch=2,
        micros=10.5,
        far=(1, 2, 3),
    )(info, bounds, qkv, qkv_tail, importance, mass, before)

    attended, *held = tie(attended, *a_pieces, *b_state[0], *b_state[1])
    a_pieces, held = held[: len(a_pieces)], held[len(a_pieces) :]
    b_pieces = end_feed(held[:2], held[2:])
    fc_a, down_a, w_out = build_feed(0, a_pieces, [net.chip(piece) for piece in a_pieces[1:]])

    middle, normed_second = call(
        project_kernel,
        "project",
        (tokens // tile,),
        [by_tile, by_tile, whole_spec((width, width)), table_spec],
        [by_tile, by_tile],
        [shape((tokens, width), F32), shape((tokens, width), BF)],
        micros=3,
    )(attended, x_flat, w_out, table)

    hids, dpres, d_fc_bias = [], [], []

    def feed(chunk, fc, down, normed_second):
        still = pl.BlockSpec((tokens, width), lambda *_: (0, 0), pipeline_mode=pl.Buffered(1))
        column = lambda rows_: pl.BlockSpec((rows_, width), lambda j, *_: (0, j))
        row = pl.BlockSpec((width, width), lambda j, *_: (j, 0))
        hid, dpre, d_bias, keep, give = call(
            lambda *refs: feed_kernel(*refs, chunk=chunk),
            "feed",
            (BLOCKS,),
            [still, still, column(width), row, table_spec],
            [column(tokens), column(tokens), column(8), row, row],
            [shape((tokens, wide), BF), shape((tokens, wide), BF), shape((8, wide), F32), shape((wide, width), BF), shape((wide, width), BF)],
            prefetch=1,
            micros=15,
            limit=30,
            far=(0, 1, 3, 4),
        )(info, normed_second, dy, fc, down, table)
        hids.append(hid)
        dpres.append(dpre)
        d_fc_bias.append(d_bias)
        return keep, give

    def feed_add(kept, got):
        half = (shards // 2, rows, wide)
        keep, give = call(
            feed_add_kernel,
            "feed_add",
            (1,),
            [whole_spec((wide, width))] * 2,
            [whole_spec(half)] * 2,
            [shape(half, BF)] * 2,
            scratch=[pltpu.VMEM((shards, rows, wide), BF)],
            prefetch=1,
            micros=2,
            limit=20,
        )(info, kept, got)
        return Reduction(net, keep, give)

    b_first = net.chip(b_pieces[1])
    normed_second, b_first = tie(normed_second, b_first)
    kept_a, give_a = feed(0, fc_a, down_a, normed_second)
    give_a, *b_pieces = tie(give_a, *b_pieces)
    got_a = net.chip(give_a)
    fc_b, down_b = build_feed(1, b_pieces, [b_first] + [net.chip(piece) for piece in b_pieces[2:]])
    red_a = feed_add(kept_a, got_a)
    fc_b = pin(fc_b, red_a)
    red_a.start()
    kept_b, give_b = feed(1, fc_b, down_b, normed_second)
    got_b = net.chip(give_b)
    red_a.finish(kept_b)
    dpres[1] = pin(dpres[1], red_a)
    red_a.start()

    half_out = (shards, rows, width // 2)
    groups = 2
    part_tokens, part_tail, part_seqs = tokens // groups, tail // groups, seqs // groups
    by_part = pl.BlockSpec((part_tokens, width), lambda i, *_: (i, 0))
    d_middle, branch, sums_second = call(
        middle_kernel,
        "middle",
        (groups,),
        [pl.BlockSpec((part_tokens, wide), lambda i, *_: (i, 0))] * CHUNKS + [whole_spec((width, wide))] * CHUNKS + [by_part, by_part, table_spec],
        [by_part, by_part, whole_spec((8, width))],
        [shape((tokens, width), F32), shape((tokens, width), BF), shape((8, width), F32)],
        micros=1.0,
        limit=30,
        far=(0,),
        far_in=(0, 1, 5),
    )(*dpres, fc_a, fc_b, middle, dy, table)

    red_a.finish(branch)
    red_b = feed_add(kept_b, got_b)
    branch = pin(branch, red_a, red_b)
    red_a.start()
    red_b.start()
    d_attended, keep_out, give_out = call(
        branch_kernel,
        "branch",
        (1,),
        [full, full, whole_spec((width, width))],
        [full, whole_spec(half_out), whole_spec(half_out)],
        [shape((tokens, width), BF), shape(half_out, BF), shape(half_out, BF)],
        prefetch=1,
        micros=1.0,
        limit=24,
        far=(0,),
        far_in=(1,),
    )(info, branch, attended, w_out)
    got_out = net.chip(give_out)

    def attention_back(part, d_attended):
        shifted = lambda rows_, cols: pl.BlockSpec((rows_, cols), lambda s, *_: (part * part_seqs + s, 0))
        return call(
            lambda *refs: attention_back_kernel(*refs, first_seq=part * part_seqs, pairs=pairs),
            "attention_back",
            (part_seqs,),
            [shifted(blocks, 3 * width), shifted(WINDOW, 2 * width), shifted(blocks, width), shifted(blocks, width), shifted(blocks, 2 * width), shifted(WINDOW, width), shifted(WINDOW, LANES), shifted(blocks, LANES), pl.BlockSpec((1, 8, LANES), lambda s, *_: (part * part_seqs + s, 0, 0))],
            [by_seq(blocks, 3 * width), by_seq(WINDOW, 3 * width), by_seq(blocks, LANES), pl.BlockSpec((1, 1, LANES), lambda s, *_: (s, 0, 0))],
            [shape((part_tokens, 3 * width), BF), shape((part_tail, 3 * width), BF), shape((part_tokens, LANES), F32), shape((part_seqs, 1, LANES), F32)],
            scratch=[pltpu.VMEM((LANES, LANES), F32)],
            prefetch=2,
            micros=0.1,
            far=(0, 1),
            far_in=(0, 1, 2, 3, 4, 5, 6),
        )(info, bounds, qkv, qkv_tail, attended, d_attended, probs, gates, inverse, importance, before)

    def qkv_grad(backs):
        side = lambda i, info: (0, jnp.where(i == 0, 1 - info[1], info[1]))
        result = (shards, rows, half_qkv)
        still = lambda rows_: pl.BlockSpec((rows_, width), lambda *_: (0, 0), pipeline_mode=pl.Buffered(1))
        held = lambda dims: pl.BlockSpec(dims, lambda *_: (0,) * len(dims), pipeline_mode=pl.Buffered(1))
        return call(
            lambda *refs: qkv_grad_kernel(*refs, groups=groups),
            "qkv_grad",
            (2,),
            [still(tokens), still(tail)] + [pl.BlockSpec((part_tokens, half_qkv), side)] * groups + [pl.BlockSpec((part_tail, half_qkv), side)] * groups,
            [held(result), held(result), held((8, half_qkv)), held((8, half_qkv))],
            [shape(result, BF), shape(result, BF), shape((8, half_qkv), F32), shape((8, half_qkv), F32)],
            prefetch=1,
            micros=2,
            limit=22,
            far_in=(0, 1, 2, 3, 4, 5),
            far=(0, 1),
        )(info, normed, normed_tail, *[back[0] for back in backs], *[back[1] for back in backs])

    half_shards = shards // 2

    def halved(kept, got):
        return Reduction(net, add(kept[:half_shards], got[:half_shards]), add(kept[half_shards:], got[half_shards:]))

    red_o = halved(keep_out, got_out)
    d_attended = pin(d_attended, red_o)
    red_o.start()
    backs = [list(attention_back(0, d_attended))]
    red_a.finish(backs[0][0])
    d_attended, _ = tie(d_attended, backs[0][0])
    d_attended = pin(d_attended, red_a)
    red_a.start()
    backs.append(list(attention_back(1, d_attended)))
    red_a.finish()
    red_b.finish()
    red_o.finish()
    red_b.keep = jnp.concatenate([red_b.keep, red_o.keep], axis=2)
    red_b.give = jnp.concatenate([red_b.give, red_o.give], axis=2)
    backs[1][0] = pin(backs[1][0], red_a, red_b)
    red_a.start()
    red_b.start()
    total_all = jnp.concatenate([back[3] for back in backs], axis=0)
    total_after = jnp.zeros_like(total_all)

    def suffix_step(total_after, total_all, bit, after=None):
        got = net.along(total_all, bit)
        if after is not None:
            got, _ = tie(got, after)
        earlier = (net.seq >> bit) % 2 == 0
        return jnp.where(earlier, total_after + got, total_after), total_all + got

    total_after, total_all = suffix_step(total_after, total_all, 0)
    backs[1][0], total_all = tie(backs[1][0], total_all)
    give_qkv, keep_qkv, sums_given, sums_kept = qkv_grad(backs)

    for bit in range(1, net.seq_bits - 1):
        total_after, total_all = suffix_step(total_after, total_all, bit, keep_qkv)
    give_qkv, total_all, total_after, red_a.got, red_b.got = tie(give_qkv, total_all, total_after, red_a.got, red_b.got)
    got_qkv = net.chip(give_qkv)
    red_a.finish()
    red_b.finish()
    d_halos = [back[1] for back in backs]
    d_halos[0] = pin(d_halos[0], red_a, red_b)
    red_a.start()
    red_b.start()
    red_c = halved(keep_qkv, got_qkv)
    d_halos[0] = pin(d_halos[0], red_c)
    red_c.start()
    d_tail, sums_tail = call(
        tail_back_kernel,
        "tail_back",
        (1,),
        [whole_spec((part_tail, 3 * width))] * groups + [whole_spec((width, 3 * width)), whole_spec((tail, width)), table_spec],
        [whole_spec((tail, width)), whole_spec((8, width))],
        [shape((tail, width), BF), shape((8, width), F32)],
        micros=1,
        limit=16,
        far_in=(0, 1),
    )(*d_halos, w_qkv, x_tail, table)
    got_qkv, _ = tie(got_qkv, d_tail)
    d_tail, total_all, total_after, middle, red_b.got = tie(d_tail, total_all, total_after, middle, red_b.got)
    red_b.finish()
    middle = pin(middle, red_b)
    back = net.shifted(d_tail, -1)

    def output(part, before_):
        still = pl.BlockSpec((part_tokens, width), lambda j: (part, 0))
        extra = [] if before_ is None else [before_]
        return call(
            output_kernel,
            "output",
            (BLOCKS,),
            [pl.BlockSpec((part_tokens, width), lambda j: (part, j))] * CHUNKS + [pl.BlockSpec((width, width), lambda j: (j, 0))] * CHUNKS + [still, table_spec] + [ANY] * len(extra),
            still,
            shape((tokens, width), BF),
            scratch=[pltpu.VMEM((part_tokens, width), F32)],
            micros=1.0,
            limit=24,
            alias={2 * CHUNKS + 2: 0} if extra else {},
            far=(0,),
            far_in=(0, 1, 2, 3, 4),
        )(*hids, down_a, down_b, middle, table, *extra)

    got_last = net.along(total_all, net.seq_bits - 1)
    block_output = output(0, None)
    block_output, red_c.got, got_last, back = tie(block_output, red_c.got, got_last, back)
    red_c.finish()
    total_after = jnp.where((net.seq >> (net.seq_bits - 1)) % 2 == 0, total_after + got_last, total_after)
    back = back.reshape(seqs, WINDOW, width)
    total_after = pin(total_after, red_b, red_c)
    red_b.start()
    red_c.start()

    per_tile = tile // blocks
    per_group = tokens // tile // groups
    grouped_tile = lambda cols: [pl.BlockSpec((tile, cols), lambda i, *_, k=k: (jnp.clip(i - k * per_group, 0, per_group - 1), 0)) for k in range(groups)]
    by_lane = pl.BlockSpec((tile, LANES), lambda i, *_: (i, 0))
    input_grad, sums_first, d_score = call(
        lambda *refs: input_grad_kernel(*refs, groups=groups),
        "input_grad",
        (tokens // tile,),
        grouped_tile(3 * width)
        + grouped_tile(LANES)
        + [
            whole_spec((width, 3 * width)),
            whole_spec((LANES, width)),
            by_tile,
            by_tile,
            table_spec,
            by_tile,
            pl.BlockSpec((per_tile, WINDOW, width), lambda i, *_: (i, 0, 0)),
            by_lane,
            pl.BlockSpec((per_tile, 8, LANES), lambda i, *_: (i, 0, 0)),
            pl.BlockSpec((per_tile, 1, LANES), lambda i, *_: (i, 0, 0)),
        ],
        [by_tile, whole_spec((8, width)), whole_spec((LANES, width))],
        [shape((tokens, width), F32), shape((8, width), F32), shape((LANES, width), F32)],
        prefetch=2,
        micros=1.0,
        limit=24,
        far_in=(0, 1) + tuple(2 * groups + k for k in (2, 3, 5)),
    )(info, bounds, *[back_[0] for back_ in backs], *[back_[2] for back_ in backs], w_qkv, score, normed, x_flat, table, d_middle, back, importance, before, total_after)

    sums_first, red_b.got, red_c.got = tie(sums_first, red_b.got, red_c.got)
    red_b.finish()
    red_c.finish()
    sums_first = pin(sums_first, red_b, red_c)
    packed = call(
        small_pack_kernel,
        "small_pack",
        (1,),
        [whole_spec((8, width))] * 3 + [whole_spec((8, half_qkv))] * 2 + [whole_spec((8, wide))] * CHUNKS + [whole_spec((LANES, width))],
        whole_spec((shards, small_rows, rows)),
        shape((shards, small_rows, rows), F32),
        scratch=[pltpu.VMEM((32, width), F32)],
        prefetch=1,
        micros=1,
    )(info, sums_first, sums_tail, sums_second, sums_kept, sums_given, *d_fc_bias, d_score)

    def finish(red):
        other = net.chip(red.keep)
        return jnp.where(core == 0, red.keep, other), jnp.where(core == 0, other, red.keep)

    def early_grads():
        fc_grads, down_grads = zip(finish(red_a), finish(red_b))
        out_grads = [fc_grads[1][:, wide:], down_grads[1][:, wide:]]
        fc_grads, down_grads = [part[:, :wide] for part in fc_grads], [part[:, :wide] for part in down_grads]
        d_out = jnp.concatenate(out_grads, axis=1).astype(F32)
        d_fc = jnp.concatenate([part[:, d * deep : (d + 1) * deep] for d in range(shards) for part in fc_grads], axis=1).astype(F32)
        d_down = jnp.concatenate([part[:, k * width : (k + 1) * width] for part in down_grads for k in range(deep // rows)], axis=0).astype(F32)
        return [d_out, d_fc, d_down]

    reds = [red_a, red_b, red_c]
    early, tied = None, False
    packed = packed + net.chip(packed)

    def small_step(value, step):
        if step < net.bits:
            half = value.shape[0] // 2
            return value[:half], net.send(value[half:], lambda s, d: (s, d ^ (1 << net.orders[0][step])))
        return value, net.along(value, step - net.bits + 1)

    def small_direct(value):
        masks = [crossed(shards, 0, k, True) for k in range(1, shards)]
        return value[:1], [net.send(value[k : k + 1], lambda s, d, mask=mask: (s, d ^ mask)) for k, mask in enumerate(masks, 1)]

    small_count, small_done = net.bits + net.seq_bits - 1, 0
    packed, middle = tie(packed, middle)
    red_b.start()
    red_c.start()
    if net.bits == 2:
        packed, small_gots = small_direct(packed)
        small_done = net.bits
    else:
        packed, small_got = small_step(packed, 0)
        small_gots = [small_got]
        small_done = 1
    block_output = output(1, block_output)
    block_output, red_b.got, red_c.got, *small_gots = tie(block_output, red_b.got, red_c.got, *small_gots)
    small_got = sum(small_gots[1:], small_gots[0])
    while small_got is not None or any(red.todo for red in reds):
        active = [red for red in reds if red.pending]
        for red in active:
            red.finish()
        if small_got is not None:
            packed, small_got = packed + small_got, None
        packed = pin(packed, *active)
        for red in reds:
            if red.todo:
                red.start()
        if small_done < small_count:
            packed, small_got = small_step(packed, small_done)
            small_done += 1
        if early is None and not red_a.todo and not red_b.todo:
            early = early_grads()
        if red_c.todo == ["join"] and red_c.pending and early is not None:
            red_c.got, *early = tie(red_c.got, *early)
    d_out, d_fc, d_down = early
    packed = packed[0]

    d_qkv = jnp.concatenate(finish(red_c), axis=1).astype(F32)

    small_outs = [shape(part.shape, F32) for part in vectors] + [shape((heads, rows), F32)]
    dg_first, ds_first, dg_second, ds_second, db_out, db_down, db_qv, db_fc, d_score = call(
        end_kernel,
        "end",
        (1,),
        [whole_spec((small_rows, rows))],
        [pl.BlockSpec(part.shape, lambda *_, n=len(part.shape): (0,) * n) for part in small_outs],
        small_outs,
        micros=1,
    )(packed)
    return (
        block_output.reshape(seqs, blocks, width),
        input_grad.reshape(seqs, blocks, width),
        dg_first,
        ds_first,
        d_qkv,
        db_qv,
        d_score.T,
        d_out,
        db_out,
        dg_second,
        ds_second,
        d_fc,
        db_fc,
        d_down,
        db_down,
    )


def solution(mesh):
    split = P("dp", "seq", None)
    rows = P("dp", None)
    flat = P("dp")
    in_specs = (split, rows, flat, flat, rows, flat, rows, rows, flat, flat, flat, rows, flat, rows, flat, split)
    out_specs = (split, split, flat, flat, rows, flat, rows, rows, flat, flat, flat, rows, flat, rows, flat)
    return jax.shard_map(body, mesh=mesh, in_specs=in_specs, out_specs=out_specs, check_vma=False)
```

```python
import math

import jax
import jax.numpy as jnp
from jax import lax
from jax.experimental import pallas as pl
from jax.experimental.pallas import tpu as pltpu
from jax.sharding import PartitionSpec as P

KTOP = 64
WINDOW = 64
HEAD = 64
LANES = 128
EPSILON = 1e-05
NEGATIVE = -1e30
SCALE = 1.0 / math.sqrt(HEAD)
GELU_A = math.sqrt(2.0 / math.pi)
GELU_B = 0.044715
BF = jnp.bfloat16
F32 = jnp.float32
NN = ((1,), (0,))
NT = ((1,), (1,))
TN = ((0,), (0,))
CHUNKS = 2
BLOCKS = 2
MIB = 2**20
FORWARD_STAGE = 3
BACKWARD_STAGE = 6
GAIN1, SHIFT1, GAIN2, SHIFT2, BIAS_OUT, BIAS_DOWN, BIAS_QKV, BIAS_FC = 0, 1, 2, 3, 4, 5, 6, 9
VECTORS = 6
QV_ROWS = 2
FC_ROWS = 4


def mm(left, right, dims=NN):
    return lax.dot_general(left, right, (dims, ((), ())), preferred_element_type=F32)


def mm_split(mask, value, dims=NN):
    high = value.astype(BF)
    low = (value - high.astype(F32)).astype(BF)
    return mm(mask, high, dims) + mm(mask, low, dims)


def whole_spec(shape):
    return pl.BlockSpec(shape, lambda *_: (0,) * len(shape))


ANY = pl.BlockSpec(memory_space=pl.ANY)


def call(kernel, name, grid, in_specs, out_specs, out_shape, scratch=(), prefetch=0, micros=1.0, limit=16, alias=None, far=(), far_in=(), near=(), near_in=()):
    many = isinstance(out_shape, (list, tuple))
    if grid == (1,):
        once = lambda spec: spec if spec.block_shape is None else pl.BlockSpec(spec.block_shape, spec.index_map, pipeline_mode=pl.Buffered(1))
        in_specs = [once(spec) for spec in in_specs]
        out_specs = [once(spec) for spec in out_specs] if many else once(out_specs)
    outs = [pltpu.HBM(one.shape, one.dtype) if k in far else pltpu.VMEM(one.shape, one.dtype) if k in near else one for k, one in enumerate(out_shape if many else [out_shape])]
    inner = pl.pallas_call(
        kernel,
        grid_spec=pltpu.PrefetchScalarGridSpec(
            num_scalar_prefetch=prefetch,
            grid=grid,
            in_specs=in_specs,
            out_specs=out_specs,
            scratch_shapes=list(scratch),
        ),
        out_shape=outs if many else outs[0],
        input_output_aliases=alias or {},
        compiler_params=pltpu.CompilerParams(vmem_limit_bytes=limit * MIB),
        cost_estimate=pl.CostEstimate(flops=int(micros * 1.1e9), bytes_accessed=1024, transcendentals=0),
        name=name,
    )

    def run(*operands):
        held = []
        for k, one in enumerate(operands):
            if k - prefetch in far_in:
                one = pltpu.with_memory_space_constraint(one, pltpu.HBM)
            elif k - prefetch in near_in:
                one = pltpu.with_memory_space_constraint(one, pltpu.VMEM)
            held.append(one)
        return inner(*held)

    return run


def shape(dims, kind):
    return jax.ShapeDtypeStruct(dims, kind)


def iota(dims, axis):
    return lax.broadcasted_iota(jnp.int32, dims, axis)


def segment(places, first, second):
    return (places >= first).astype(jnp.int32) + (places >= second).astype(jnp.int32)


def normalise(values):
    average = jnp.mean(values, axis=-1, keepdims=True)
    centred = values - average
    variance = jnp.mean(centred * centred, axis=-1, keepdims=True)
    scale = lax.rsqrt(variance + EPSILON)
    return centred * scale, scale


def norm_back(d_norm, unit, scale, gain):
    weighted = d_norm * gain
    return scale * (
        weighted
        - jnp.mean(weighted, axis=-1, keepdims=True)
        - unit * jnp.mean(weighted * unit, axis=-1, keepdims=True)
    )


def bit_orders(count):
    bits = count.bit_length() - 1
    straight = list(range(bits))
    half = bits // 2
    return straight, straight[half:] + straight[:half]


def crossed(count, core, index, first_high):
    order = bit_orders(count)[core]
    mask = 0
    for step, bit in enumerate(order):
        place = len(order) - 1 - step if first_high else step
        mask |= ((index >> place) & 1) << bit
    return mask


def rank(count, core, far, first_high):
    order = bit_orders(count)[core]
    index = 0
    for step, bit in enumerate(order):
        place = len(order) - 1 - step if first_high else step
        index |= ((far >> bit) & 1) << place
    return index


def by_core(core, even, odd):
    return jnp.where(core == 0, even, odd)


def copy_all(copies, sems):
    started = [pltpu.make_async_copy(source, target, sems.at[k]) for k, (source, target) in enumerate(copies)]
    for copy in started:
        copy.start()
    for copy in started:
        copy.wait()


def start_kernel(*refs):
    vectors, (score_ref, small_ref) = refs[:-2], refs[-2:]
    rows = small_ref.shape[1]
    row = 0
    for ref in vectors:
        for k in range(ref.shape[0] // rows):
            small_ref[row : row + 1] = ref[k * rows : (k + 1) * rows].reshape(1, rows)
            row += 1
    small_ref[row:] = score_ref[...]


def first_pack_kernel(info, own_ref, x_ref, own_out, tail_ref):
    own_out[...] = own_ref[...]
    for s in range(x_ref.shape[0]):
        tail_ref[s * WINDOW : (s + 1) * WINDOW] = x_ref[s]


def feed_pack_kernel(info, fc_ref, down_ref, weight_ref, *outs):
    fc_refs, own_refs = outs[:CHUNKS], outs[CHUNKS:]
    rows, hidden = fc_ref.shape
    width = down_ref.shape[1]
    wide = fc_refs[0].shape[1]
    deep = down_ref.shape[0] // CHUNKS
    shards = hidden // (deep * CHUNKS)
    for chunk in range(CHUNKS):
        for shard in range(shards):
            begin = (shard * CHUNKS + chunk) * deep
            fc_refs[chunk][:, shard * deep : (shard + 1) * deep] = fc_ref[:, begin : begin + deep]

        @pl.when(info[1] == 0)
        def _():
            own_refs[chunk][:, :wide] = fc_refs[chunk][...]
            if chunk == 0:
                own_refs[chunk][:, wide:] = weight_ref[:, : width // 2]

        @pl.when(info[1] != 0)
        def _():
            for part in range(deep // rows):
                begin = chunk * deep + part * rows
                own_refs[chunk][:, part * width : (part + 1) * width] = down_ref[begin : begin + rows]
            if chunk == 0:
                own_refs[chunk][:, wide:] = weight_ref[:, width // 2 :]


def end_kernel(packed_ref, *outs):
    row = 0
    rows = packed_ref.shape[1]
    for ref in outs[:-1]:
        for k in range(ref.shape[0] // rows):
            ref[k * rows : (k + 1) * rows] = packed_ref[row : row + 1].reshape(rows)
            row += 1
    outs[-1][...] = packed_ref[row:]


def params_kernel(info, *refs):
    pieces, (table_ref, score_ref, held) = refs[:-3], refs[-3:]
    shards = len(pieces)
    core, me = info[1], info[2]
    for k, piece in enumerate(pieces):
        held[k] = piece[...].astype(F32)

    def at(shard):
        far = shard ^ me
        index = jnp.int32(0)
        for k in range(shards):
            mask = by_core(core, crossed(shards, 0, k, False), crossed(shards, 1, k, False))
            index = jnp.where(mask == far, k, index)
        return held[index]

    parts = [at(shard) for shard in range(shards)]

    def line(shard_range, rows):
        return jnp.concatenate([parts[s][r : r + 1] for s in shard_range for r in rows], axis=1)

    table_ref[...] = jnp.zeros_like(table_ref)
    for r in range(VECTORS):
        table_ref[r : r + 1] = line(range(shards), [r])
    qv = list(range(VECTORS, VECTORS + QV_ROWS))
    table_ref[BIAS_QKV : BIAS_QKV + 1] = line(range(shards // 2), qv)
    table_ref[BIAS_QKV + 2 : BIAS_QKV + 3] = line(range(shards // 2, shards), qv)
    base = VECTORS + QV_ROWS
    per_block = shards // BLOCKS
    per_chunk = FC_ROWS // CHUNKS
    for chunk in range(CHUNKS):
        for block in range(BLOCKS):
            rows = [base + chunk * per_chunk + k for k in range(per_chunk)]
            row = BIAS_FC + chunk * BLOCKS + block
            table_ref[row : row + 1] = line(range(block * per_block, (block + 1) * per_block), rows)
    base += FC_ROWS
    heads = parts[0].shape[0] - base
    score_ref[...] = jnp.zeros_like(score_ref)
    for head in range(heads):
        score_ref[head : head + 1] = line(range(shards), [base + head]).astype(BF)


def prep_kernel(info, bounds, x_ref, table_ref, score_ref, normed_ref, imp_ref, mass_ref, stat_ref):
    seqs = stat_ref.shape[0]
    blocks = x_ref.shape[0] // seqs
    gain = table_ref[GAIN1 : GAIN1 + 1]
    shift = table_ref[SHIFT1 : SHIFT1 + 1]
    start = info[0]
    rows = iota((blocks, blocks), 0)
    cols = iota((blocks, blocks), 1)
    for k in range(seqs):
        rs = slice(k * blocks, (k + 1) * blocks)
        normed = (normalise(x_ref[rs].astype(F32))[0] * gain + shift).astype(BF)
        normed_ref[rs] = normed
        importance = mm(normed, score_ref[...], NT)
        imp_ref[rs] = importance
        s = pl.program_id(0) * seqs + k
        first, second = bounds[0, s], bounds[1, s]
        lower = (cols <= rows) & (segment(start + rows, first, second) == segment(start + cols, first, second))
        peak = jnp.max(importance, axis=0, keepdims=True)
        mass = mm_split(lower.astype(BF), jnp.exp(importance - peak))
        mass_ref[rs] = mass
        stat_ref[k, 0:1, :] = peak
        stat_ref[k, 1:2, :] = mass[blocks - 1 :, :]
        stat_ref[k, 2:3, :] = jnp.full_like(peak, NEGATIVE)
        stat_ref[k, 3:4, :] = jnp.zeros_like(peak)
        stat_ref[k, 4:5, :] = peak


def prep_tail_kernel(x_ref, table_ref, out_ref):
    gain = table_ref[GAIN1 : GAIN1 + 1]
    shift = table_ref[SHIFT1 : SHIFT1 + 1]
    out_ref[...] = (normalise(x_ref[...].astype(F32))[0] * gain + shift).astype(BF)


def scan_kernel(info, mine_ref, *refs, masks):
    got_refs, out_ref = refs[:-1], refs[-1]

    def joined(peak, total, got):
        top = jnp.maximum(peak, got[:, 0:1])
        return top, total * jnp.exp(peak - top) + got[:, 1:2] * jnp.exp(got[:, 0:1] - top)

    out_ref[...] = mine_ref[...]
    for mask, got in zip(masks, got_refs):
        peak, total = joined(out_ref[:, 0:1], out_ref[:, 1:2], got)
        out_ref[:, 0:1] = peak
        out_ref[:, 1:2] = total

        @pl.when((info[3] ^ mask) < info[3])
        def _():
            peak, total = joined(out_ref[:, 2:3], out_ref[:, 3:4], got)
            out_ref[:, 2:3] = peak
            out_ref[:, 3:4] = total


def qkv_build_kernel(info, *refs):
    own, pieces, out, sems = refs[0], refs[1:-2], refs[-2], refs[-1]
    shards = len(pieces) // 2 + 1
    rows, width = own.shape
    half = width // 2
    me = info[2]

    def build(core):
        copies = [(own, out.at[pl.ds(pl.multiple_of(me * rows, 16), rows)])]
        for k in range(1, shards):
            for side, group in ((core, 0), (1 - core, shards - 1)):
                at = pl.multiple_of((me ^ crossed(shards, side, k, False)) * rows, 16)
                target = out.at[pl.ds(at, rows), side * half : (side + 1) * half]
                copies.append((pieces[group + k - 1], target))
        copy_all(copies, sems)

    @pl.when(info[1] == 0)
    def _():
        build(0)

    @pl.when(info[1] != 0)
    def _():
        build(1)


def feed_build_kernel(info, *refs, with_out, by_pair):
    if with_out:
        own_fc, own_down, own_out = refs[:3]
        pieces, (fc_ref, down_ref, out_ref, sems) = refs[3:-4], refs[-4:]
    else:
        own_fc, own_down = refs[:2]
        pieces, (fc_ref, down_ref, sems) = refs[2:-3], refs[-3:]
    shards = len(pieces) // 2 + 1
    rows, wide = own_fc.shape
    deep, width = own_down.shape
    split = width // 2
    me = info[2]

    kinds = [info[1] ^ ((info[3] >> 1) & 1), None] if by_pair else [info[1], None]
    kinds[1] = 1 - kinds[0]

    def away(k, partner):
        return jnp.where(kinds[partner] == 0, crossed(shards, 0, k, False), crossed(shards, 1, k, False))

    def build(core):
        at_rows = lambda shard: pl.multiple_of(shard * rows, 16)
        copies = [
            (own_fc, fc_ref.at[pl.ds(at_rows(me), rows)]),
            (own_down, down_ref.at[pl.ds(pl.multiple_of(me * deep, 16), deep)]),
        ]
        if with_out:
            copies.append((own_out, out_ref.at[pl.ds(at_rows(me), rows)]))
        for k in range(1, shards):
            for partner, side in enumerate((core, 1 - core)):
                piece = pieces[partner * (shards - 1) + k - 1]
                shard = me ^ away(k, partner)
                if side == 0:
                    copies.append((piece.at[:, :wide], fc_ref.at[pl.ds(at_rows(shard), rows)]))
                else:
                    for part in range(deep // rows):
                        at = pl.multiple_of(shard * deep + part * rows, 16)
                        copies.append((piece.at[:, part * width : (part + 1) * width], down_ref.at[pl.ds(at, rows)]))
                if with_out:
                    copies.append((piece.at[:, wide:], out_ref.at[pl.ds(at_rows(shard), rows), side * split : (side + 1) * split]))
        copy_all(copies, sems)

    @pl.when(info[1] == 0)
    def _():
        build(0)

    @pl.when(info[1] != 0)
    def _():
        build(1)


def qkv_kernel(normed_ref, tail_ref, weight_ref, table_ref, out_ref, tail_out_ref):
    j = pl.program_id(0)
    weight = weight_ref[...]
    bias = table_ref[pl.ds(BIAS_QKV + j, 1)]
    factor = jnp.where(j == 0, SCALE, 1.0)
    out_ref[...] = ((mm(normed_ref[...], weight) + bias).astype(BF).astype(F32) * factor).astype(BF)

    @pl.when(j > 0)
    def _():
        tail_out_ref[...] = (mm(tail_ref[...], weight) + bias).astype(BF)


def lane_masks():
    first = iota((1, LANES), 1) < HEAD
    return first.astype(BF), (~first).astype(BF)


def grouped(part, keep_first, keep_second):
    return jnp.concatenate([part * keep_first, part * keep_second], axis=0)


def tile_masks(start, half, first, second):
    dims = (WINDOW, LANES)
    row = iota(dims, 0)
    col = iota(dims, 1) & (HEAD - 1)
    base = start + WINDOW * half
    mine = segment(base + row, first, second)
    far = segment(base - WINDOW + col, first, second) == mine
    near = (col <= row) & (segment(base + col, first, second) == mine)
    if half == 0:
        far = far & (col > row) & (base - WINDOW + col >= 0)
    return far, near, col <= row


def spread(columns, pair, rows):
    left = columns[:, 2 * pair : 2 * pair + 1]
    right = columns[:, 2 * pair + 1 : 2 * pair + 2]
    return jnp.where(iota((rows, LANES), 1) < HEAD, left, right)


def key_groups(qkv_ref, halo_ref, width, pair, keep_first, keep_second, one_group):
    at = slice(pair * LANES, (pair + 1) * LANES)
    ks = slice(width + pair * LANES, width + (pair + 1) * LANES)
    vs = slice(2 * width + pair * LANES, 2 * width + (pair + 1) * LANES)
    keys = [grouped(part, keep_first, keep_second) for part in (halo_ref[:, at], qkv_ref[:WINDOW, ks], qkv_ref[WINDOW:, ks])]
    values = [
        jnp.concatenate([grouped(part, keep_first, keep_second), one_group], axis=1)
        for part in (halo_ref[:, ks], qkv_ref[:WINDOW, vs], qkv_ref[WINDOW:, vs])
    ]
    return keys, values


def attention_kernel(info, bounds, qkv_ref, halo_ref, imp_ref, mass_ref, before_ref, att_ref, probs_ref, sig_ref, inv_ref):
    s = pl.program_id(0)
    blocks, width = att_ref.shape
    start = info[0]
    first, second = bounds[0, s], bounds[1, s]
    pairs = width // LANES
    peak = before_ref[0, 4:5, :]
    carry_peak = before_ref[0, 2:3, :]
    carry_total = before_ref[0, 3:4, :]
    top = before_ref[0, 0:1, :]
    joined = jnp.maximum(peak, carry_peak)
    place = start + iota((blocks, LANES), 0)
    continues = segment(place, first, second) == segment(jnp.full((1, LANES), start - 1, jnp.int32), first, second)
    mass = mass_ref[...] * jnp.exp(peak - joined) + jnp.where(
        continues, carry_total * jnp.exp(carry_peak - joined), 0.0
    )
    threshold = joined + jnp.log(mass) - math.log(KTOP)
    late = threshold[WINDOW:]
    inv_ref[...] = 1.0 / (mass[WINDOW:] * jnp.exp(joined - top))
    imp_rows = imp_ref[...].T
    keep_first, keep_second = lane_masks()
    one_group = grouped(jnp.ones((WINDOW, LANES), BF), keep_first, keep_second)
    masks = [tile_masks(start, half, first, second) for half in (0, 1)]
    lane = iota((WINDOW, LANES), 1) < HEAD
    for p0 in range(0, pairs, FORWARD_STAGE):
        ps = range(p0, min(pairs, p0 + FORWARD_STAGE))
        groups = {p: key_groups(qkv_ref, halo_ref, width, p, keep_first, keep_second, one_group) for p in ps}
        logits = {}
        for p in ps:
            ls = slice(p * LANES, (p + 1) * LANES)
            for half in (0, 1):
                rs = slice(half * WINDOW, (half + 1) * WINDOW)
                logits[p, half] = mm(qkv_ref[rs, ls], jnp.concatenate(groups[p][0][half : half + 2], axis=0), NT)
        soft_in = {}
        for p in ps:
            ls = slice(p * LANES, (p + 1) * LANES)
            for half in (0, 1):
                far_ok, near_ok, gated = masks[half]
                far, near = logits[p, half][:, :LANES], logits[p, half][:, LANES:]
                if half == 1:
                    row = jnp.concatenate([imp_rows[2 * p : 2 * p + 1, :WINDOW], imp_rows[2 * p + 1 : 2 * p + 2, :WINDOW]], axis=1)
                    gap = spread(late, p, WINDOW) - row
                    small = jnp.exp(-jnp.abs(gap))
                    soft = jnp.maximum(gap, 0.0) + jnp.log(1.0 + small)
                    sig_ref[:, ls] = (jnp.where(gap >= 0, 1.0, small) / (1.0 + small)).astype(BF)
                    far = jnp.where(gated, far - soft, far)
                far = jnp.where(far_ok, far, NEGATIVE)
                near = jnp.where(near_ok, near, NEGATIVE)
                best = jnp.maximum(far, near)
                best_first = jnp.max(jnp.where(lane, best, NEGATIVE), axis=1, keepdims=True)
                best_second = jnp.max(jnp.where(lane, NEGATIVE, best), axis=1, keepdims=True)
                best = jnp.where(lane, best_first, best_second)
                soft_in[p, half] = (jnp.exp(far - best), jnp.exp(near - best))
        for p in ps:
            ls = slice(p * LANES, (p + 1) * LANES)
            for half in (0, 1):
                rs = slice(half * WINDOW, (half + 1) * WINDOW)
                far, near = soft_in[p, half]
                weights = jnp.concatenate([far.astype(BF), near.astype(BF)], axis=1)
                mixed = mm(weights, jnp.concatenate(groups[p][1][half : half + 2], axis=0))
                inverse = 1.0 / mixed[:, LANES:]
                att_ref[rs, ls] = (mixed[:, :LANES] * inverse).astype(BF)
                probs_ref[rs, 2 * p * LANES : (2 * p + 1) * LANES] = (far * inverse).astype(BF)
                probs_ref[rs, (2 * p + 1) * LANES : (2 * p + 2) * LANES] = (near * inverse).astype(BF)


def project_kernel(att_ref, x_ref, weight_ref, table_ref, middle_ref, second_ref):
    middle = x_ref[...].astype(F32) + mm(att_ref[...], weight_ref[...]) + table_ref[BIAS_OUT : BIAS_OUT + 1]
    middle_ref[...] = middle
    second_ref[...] = (normalise(middle)[0] * table_ref[GAIN2 : GAIN2 + 1] + table_ref[SHIFT2 : SHIFT2 + 1]).astype(BF)


def feed_kernel(info, sec_ref, dy_ref, fc_ref, down_ref, table_ref, hid_ref, dpre_ref, db_ref, keep_ref, give_ref, *, chunk):
    fc = fc_ref[...]
    down = down_ref[...]
    row = BIAS_FC + chunk * BLOCKS + pl.program_id(0)
    pre = mm(sec_ref[...], fc) + table_ref[pl.ds(row, 1)]
    d_hidden = mm(dy_ref[...], down, NT)
    value = pre.astype(BF)
    square = value * value
    tanh = jnp.tanh(value * (BF(GELU_A) + BF(GELU_A * GELU_B) * square))
    half = BF(0.5) + BF(0.5) * tanh
    hidden = value * half
    slope = half + value * (BF(0.5 * GELU_A) + BF(1.5 * GELU_A * GELU_B) * square) * (BF(1.0) - tanh * tanh)
    d_low = d_hidden.astype(BF) * slope
    hid_ref[...] = hidden
    dpre_ref[...] = d_low
    db_ref[...] = mm(jnp.ones((db_ref.shape[0], d_low.shape[0]), BF), d_low)
    d_down = mm(hidden, dy_ref[...], TN).astype(BF)
    d_fc = mm(sec_ref[...], d_low, TN).astype(BF)

    @pl.when(info[1] == 0)
    def _():
        keep_ref[...] = d_fc
        give_ref[...] = d_down

    @pl.when(info[1] != 0)
    def _():
        keep_ref[...] = d_down
        give_ref[...] = d_fc


def feed_add_kernel(info, kept_ref, got_ref, keep_ref, give_ref, held):
    shards, rows, wide = held.shape
    width = kept_ref.shape[1]
    me = info[2]
    per_block = shards // BLOCKS
    deep = width // per_block

    def put(core):
        for block in range(BLOCKS):
            at = slice(block * width, (block + 1) * width)
            total = add(kept_ref[at], got_ref[at])
            if core == 0:
                for shard in range(shards):
                    held[ranked(shards, 0, me ^ shard), :, at] = total[shard * rows : (shard + 1) * rows]
            else:
                for k in range(per_block):
                    place = ranked(shards, 1, me ^ (block * per_block + k))
                    for part in range(deep // rows):
                        begin = k * deep + part * rows
                        held[place, :, part * width : (part + 1) * width] = total[begin : begin + rows]

    @pl.when(info[1] == 0)
    def _():
        put(0)

    @pl.when(info[1] != 0)
    def _():
        put(1)

    half = shards // 2
    keep_ref[...] = held[:half]
    give_ref[...] = held[half:]


def ranked(shards, core, far):
    order = bit_orders(shards)[core]
    index = jnp.int32(0)
    for step, bit in enumerate(order):
        index = index | (((far >> bit) & 1) << (len(order) - 1 - step))
    return index


def middle_kernel(*refs):
    dpre_refs = refs[:CHUNKS]
    fc_refs = refs[CHUNKS : 2 * CHUNKS]
    middle_ref, dy_ref, table_ref, dmid_ref, branch_ref, sums_ref = refs[2 * CHUNKS :]
    part_rows = middle_ref.shape[0] // 2
    totals = [0.0] * 4
    for part in range(2):
        rs = slice(part * part_rows, (part + 1) * part_rows)
        d_norm = None
        for dpre_ref, fc_ref in zip(dpre_refs, fc_refs):
            piece = mm(dpre_ref[rs], fc_ref[...], NT)
            d_norm = piece if d_norm is None else d_norm + piece
        unit, scale = normalise(middle_ref[rs])
        dy = dy_ref[rs].astype(F32)
        d_middle = dy + norm_back(d_norm, unit, scale, table_ref[GAIN2 : GAIN2 + 1])
        dmid_ref[rs] = d_middle
        branch = d_middle.astype(BF)
        branch_ref[rs] = branch
        for k, value in enumerate((d_norm * unit, d_norm, branch.astype(F32), dy)):
            totals[k] = totals[k] + jnp.sum(value, axis=0, keepdims=True)

    @pl.when(pl.program_id(0) == 0)
    def _():
        for k in range(4):
            sums_ref[k : k + 1] = totals[k]

    @pl.when(pl.program_id(0) > 0)
    def _():
        for k in range(4):
            sums_ref[k : k + 1] += totals[k]


def branch_kernel(info, branch_ref, att_ref, weight_ref, datt_ref, keep_ref, give_ref):
    shards, rows, split = keep_ref.shape
    store_halves(info, mm(att_ref[...], branch_ref[...], TN), keep_ref, give_ref, shards, rows, split)
    datt_ref[...] = mm(branch_ref[...], weight_ref[...], NT).astype(BF)


def store_halves(info, total, keep_ref, give_ref, shards, rows, split):
    me = info[2]

    def store(side, to):
        for shard in range(shards):
            value = total[shard * rows : (shard + 1) * rows, side * split : (side + 1) * split]
            to[ranked(shards, side, me ^ shard)] = value.astype(BF)

    @pl.when(info[1] == 0)
    def _():
        store(0, keep_ref)
        store(1, give_ref)

    @pl.when(info[1] != 0)
    def _():
        store(1, keep_ref)
        store(0, give_ref)


def attention_back_kernel(info, bounds, qkv_ref, halo_ref, att_ref, datt_ref, probs_ref, sig_ref, inv_ref, imp_ref, before_ref, dqkv_ref, dhalo_ref, dimp_ref, total_ref, rows_scratch, *, first_seq, pairs):
    s = first_seq + pl.program_id(0)
    blocks, width = att_ref.shape
    start = info[0]
    first, second = bounds[0, s], bounds[1, s]
    keep_first, keep_second = lane_masks()
    one_group = grouped(jnp.ones((WINDOW, LANES), BF), keep_first, keep_second)
    lane = iota((WINDOW, LANES), 1) < HEAD
    gated = (iota((WINDOW, LANES), 1) & (HEAD - 1)) <= iota((WINDOW, LANES), 0)
    head_lane = iota((LANES, LANES), 1)
    head_row = iota((LANES, LANES), 0)
    d_threshold = jnp.zeros((WINDOW, LANES), F32)
    rows_scratch[...] = jnp.zeros_like(rows_scratch)
    wide = pairs * LANES
    for k0 in range(0, pairs, BACKWARD_STAGE):
        ks_ = range(k0, min(pairs, k0 + BACKWARD_STAGE))
        groups = {k: key_groups(qkv_ref, halo_ref, width, k, keep_first, keep_second, one_group) for k in ks_}
        centred, low = {}, {}
        for k in ks_:
            ls = slice(k * LANES, (k + 1) * LANES)
            for half in (0, 1):
                rs = slice(half * WINDOW, (half + 1) * WINDOW)
                d_out = datt_ref[rs, ls]
                product = (-(d_out.astype(F32) * att_ref[rs, ls].astype(F32))).astype(BF)
                left = jnp.concatenate([d_out, product], axis=1)
                centred[k, half] = mm(left, jnp.concatenate(groups[k][1][half : half + 2], axis=0), NT)
        for k in ks_:
            ls = slice(k * LANES, (k + 1) * LANES)
            for half in (0, 1):
                rs = slice(half * WINDOW, (half + 1) * WINDOW)
                d_logits = probs_ref[rs, 2 * k * LANES : (2 * k + 2) * LANES].astype(F32) * centred[k, half]
                low[k, half] = d_logits.astype(BF)
                if half == 1:
                    gate = jnp.where(gated, d_logits[:, :LANES] * sig_ref[:, ls].astype(F32), 0.0)
                    rows_scratch[k : k + 1, :] = jnp.sum(gate, axis=0, keepdims=True)
                    chosen = (head_lane == 2 * k + (head_row >= HEAD).astype(jnp.int32)).astype(BF)
                    d_threshold = d_threshold - mm(gate.astype(BF), chosen)
        for k in ks_:
            ls = slice(k * LANES, (k + 1) * LANES)
            far_keys, near_keys, far_values, near_values = [], [], [], []
            for half in (0, 1):
                rs = slice(half * WINDOW, (half + 1) * WINDOW)
                dqkv_ref[rs, ls] = (mm(low[k, half], jnp.concatenate(groups[k][0][half : half + 2], axis=0)) * SCALE).astype(BF)
                d_keys = mm(low[k, half], qkv_ref[rs, ls], TN)
                d_values = mm(probs_ref[rs, 2 * k * LANES : (2 * k + 2) * LANES], datt_ref[rs, ls], TN)
                far_keys.append(jnp.where(lane, d_keys[:WINDOW], d_keys[WINDOW : 2 * WINDOW]))
                near_keys.append(jnp.where(lane, d_keys[2 * WINDOW : 3 * WINDOW], d_keys[3 * WINDOW :]))
                far_values.append(jnp.where(lane, d_values[:WINDOW], d_values[WINDOW : 2 * WINDOW]))
                near_values.append(jnp.where(lane, d_values[2 * WINDOW : 3 * WINDOW], d_values[3 * WINDOW :]))
            ks = slice(wide + k * LANES, wide + (k + 1) * LANES)
            vs = slice(2 * wide + k * LANES, 2 * wide + (k + 1) * LANES)
            dhalo_ref[:, ks] = far_keys[0].astype(BF)
            dhalo_ref[:, vs] = far_values[0].astype(BF)
            dqkv_ref[:WINDOW, ks] = (near_keys[0] + far_keys[1]).astype(BF)
            dqkv_ref[WINDOW:, ks] = near_keys[1].astype(BF)
            dqkv_ref[:WINDOW, vs] = (near_values[0] + far_values[1]).astype(BF)
            dqkv_ref[WINDOW:, vs] = near_values[1].astype(BF)
    dhalo_ref[:, :wide] = jnp.zeros((WINDOW, wide), BF)
    weighted = d_threshold * inv_ref[...]
    row = iota((blocks, WINDOW), 0)
    col = iota((blocks, WINDOW), 1) + WINDOW
    after = (col >= row) & (segment(start + row, first, second) == segment(start + col, first, second))
    later = mm_split(after.astype(BF), weighted)
    total_ref[0, 0:1, :] = later[0:1]
    turned = rows_scratch[...].T
    pick_first = (head_lane == 2 * head_row).astype(BF)
    pick_second = (head_lane == 2 * head_row + 1).astype(BF)

    def pick(values, chosen):
        high = values.astype(BF)
        return mm(high, chosen) + mm((values - high.astype(F32)).astype(BF), chosen)

    direct = pick(turned[:HEAD], pick_first) + pick(turned[HEAD:], pick_second)
    local = jnp.exp(imp_ref[...] - before_ref[0, 0:1, :]) * later
    dimp_ref[:WINDOW] = local[:WINDOW] + direct
    dimp_ref[WINDOW:] = local[WINDOW:]


def tail_back_kernel(*refs):
    dhalo_refs = refs[:-5]
    weight_ref, x_ref, table_ref, out_ref, sums_ref = refs[-5:]
    width = x_ref.shape[1]
    begin = 0
    totals = [0.0, 0.0]
    for dhalo_ref in dhalo_refs:
        rs = slice(begin, begin + dhalo_ref.shape[0])
        begin += dhalo_ref.shape[0]
        d_norm = mm(dhalo_ref[:, width:], weight_ref[:, width:], NT)
        unit, scale = normalise(x_ref[rs].astype(F32))
        out_ref[rs] = norm_back(d_norm, unit, scale, table_ref[GAIN1 : GAIN1 + 1]).astype(BF)
        for k, value in enumerate((d_norm * unit, d_norm)):
            totals[k] = totals[k] + jnp.sum(value, axis=0, keepdims=True)
    for k in range(2):
        sums_ref[k : k + 1] = totals[k]


def qkv_grad_kernel(info, normed_ref, tail_ref, *refs, groups):
    dqkv_refs, dhalo_refs = refs[:groups], refs[groups : 2 * groups]
    give_ref, keep_ref, given_sums, kept_sums = refs[2 * groups :]
    shards, rows, split = keep_ref.shape
    me = info[2]
    step = pl.program_id(0)
    owner = jnp.where(step == 0, 1 - info[1], info[1])
    total, sums = 0.0, 0.0
    for left_ref, right_refs in ((normed_ref, dqkv_refs), (tail_ref, dhalo_refs)):
        begin = 0
        for right_ref in right_refs:
            rs = slice(begin, begin + right_ref.shape[0])
            begin += right_ref.shape[0]
            total = total + mm(left_ref[rs], right_ref[...], TN)
            sums = sums + jnp.sum(right_ref[...].astype(F32), axis=0, keepdims=True)

    def store(to, sums_to):
        sums_to[0:1] = sums
        for shard in range(shards):
            far = me ^ shard
            place = jnp.where(owner == 0, ranked(shards, 0, far), ranked(shards, 1, far))
            to[place] = total[shard * rows : (shard + 1) * rows].astype(BF)

    @pl.when(step == 0)
    def _():
        store(give_ref, given_sums)

    @pl.when(step != 0)
    def _():
        store(keep_ref, kept_sums)


def input_grad_kernel(info, bounds, *refs, groups):
    dqkv_refs, dimp_refs = refs[:groups], refs[groups : 2 * groups]
    weight_ref, score_ref, normed_ref, x_ref, table_ref, dmid_ref, back_ref, imp_ref, before_ref, after_ref, out_ref, sums_ref, score_out_ref = refs[2 * groups :]
    i = pl.program_id(0)
    per_group = pl.num_programs(0) // groups
    seqs = back_ref.shape[0]
    blocks = x_ref.shape[0] // seqs
    start = info[0]

    def chosen(refs):
        value = refs[0][...]
        for k in range(1, groups):
            value = jnp.where(i >= k * per_group, refs[k][...], value)
        return value

    dqkv, d_local = chosen(dqkv_refs), chosen(dimp_refs)
    d_imps = []
    for s in range(seqs):
        rs = slice(s * blocks, (s + 1) * blocks)
        first, second = bounds[0, i * seqs + s], bounds[1, i * seqs + s]
        place = start + iota((blocks, LANES), 0)
        onward = segment(place, first, second) == segment(jnp.full((1, LANES), start + blocks, jnp.int32), first, second)
        extra = jnp.exp(imp_ref[rs] - before_ref[s, 0:1, :]) * after_ref[s, 0:1, :]
        d_imps.append(d_local[rs] + jnp.where(onward, extra, 0.0))
    d_imp = jnp.concatenate(d_imps, axis=0).astype(BF)
    d_norm = mm(dqkv, weight_ref[...], NT) + mm(d_imp, score_ref[...])
    unit, scale = normalise(x_ref[...].astype(F32))
    d_value = norm_back(d_norm, unit, scale, table_ref[GAIN1 : GAIN1 + 1]) + dmid_ref[...]
    for s in range(seqs):
        rs = slice(s * blocks, s * blocks + WINDOW)
        out_ref[rs] = d_value[rs]
        rs = slice(s * blocks + WINDOW, (s + 1) * blocks)
        out_ref[rs] = d_value[rs] + back_ref[s].astype(F32)
    sums = [jnp.sum(value, axis=0, keepdims=True) for value in (d_norm * unit, d_norm)]
    score = mm(d_imp, normed_ref[...], TN)

    @pl.when(i == 0)
    def _():
        score_out_ref[...] = score
        for k in range(2):
            sums_ref[k : k + 1] = sums[k]

    @pl.when(i > 0)
    def _():
        score_out_ref[...] += score
        for k in range(2):
            sums_ref[k : k + 1] += sums[k]


def output_kernel(*refs):
    hid_refs, down_refs, (middle_ref, table_ref) = refs[:CHUNKS], refs[CHUNKS : 2 * CHUNKS], refs[2 * CHUNKS : 2 * CHUNKS + 2]
    out_ref, total = refs[-2:]
    part = 0.0
    for hid_ref, down_ref in zip(hid_refs, down_refs):
        part = part + mm(hid_ref[...], down_ref[...])

    @pl.when(pl.program_id(0) == 0)
    def _():
        total[...] = middle_ref[...] + table_ref[BIAS_DOWN : BIAS_DOWN + 1] + part

    @pl.when(pl.program_id(0) == pl.num_programs(0) - 1)
    def _():
        out_ref[...] = (total[...] + part).astype(BF)


def small_pack_kernel(info, first_ref, tail_ref, second_ref, kept_ref, given_ref, *refs):
    bias_refs = refs[:CHUNKS]
    score_ref, out_ref, whole = refs[CHUNKS:]
    shards, count, rows = out_ref.shape
    me = info[2]
    whole[0:2] = first_ref[0:2] + tail_ref[0:2]
    whole[2:VECTORS] = second_ref[0 : VECTORS - 2]
    width = whole.shape[1]
    even = info[1] == 0
    whole[VECTORS : VECTORS + 1] = jnp.where(even, kept_ref[0:1, :width], given_ref[0:1, :width])
    whole[VECTORS + 1 : VECTORS + 2] = jnp.where(even, given_ref[0:1, width // 2 :], kept_ref[0:1, width // 2 :])
    base = VECTORS + 2
    for k in range(CHUNKS * BLOCKS):
        whole[base + k : base + k + 1] = bias_refs[k // BLOCKS][0:1, (k % BLOCKS) * width : (k % BLOCKS + 1) * width]
    heads = count - VECTORS - QV_ROWS - FC_ROWS
    whole[base + CHUNKS * BLOCKS : base + CHUNKS * BLOCKS + heads] = score_ref[0:heads]
    per_block = shards // BLOCKS
    per_chunk = FC_ROWS // CHUNKS
    for shard in range(shards):
        at = slice(shard * rows, (shard + 1) * rows)
        lines = [whole[0:VECTORS, at]]
        row = VECTORS + shard // (shards // 2)
        for k in range(QV_ROWS):
            begin = (shard % (shards // 2)) * QV_ROWS * rows + k * rows
            lines.append(whole[row : row + 1, begin : begin + rows])
        for chunk in range(CHUNKS):
            row = base + chunk * BLOCKS + shard // per_block
            for k in range(per_chunk):
                begin = (shard % per_block) * per_chunk * rows + k * rows
                lines.append(whole[row : row + 1, begin : begin + rows])
        lines.append(whole[base + CHUNKS * BLOCKS : base + CHUNKS * BLOCKS + heads, at])
        out_ref[ranked(shards, 0, me ^ shard)] = jnp.concatenate(lines, axis=0)


def add(left, right):
    return (left.astype(F32) + right.astype(F32)).astype(BF)


def combine(peak_a, total_a, peak_b, total_b):
    joined = jnp.maximum(peak_a, peak_b)
    return joined, total_a * jnp.exp(peak_a - joined) + total_b * jnp.exp(peak_b - joined)


def tie(*values):
    return lax.optimization_barrier(values)


class Net:
    def __init__(self):
        self.n_seq = lax.axis_size("seq")
        self.n_dp = lax.axis_size("dp")
        self.seq = lax.axis_index("seq")
        self.dp = lax.axis_index("dp")
        self.core = self.seq % 2
        self.orders = bit_orders(self.n_dp)
        self.bits = len(self.orders[0])
        self.seq_bits = self.n_seq.bit_length() - 1
        self.by_pair = self.bits == 2 and self.seq_bits >= 2

    def send(self, value, target):
        pairs = []
        for s in range(self.n_seq):
            for d in range(self.n_dp):
                goal = target(s, d)
                if 0 <= goal[0] < self.n_seq:
                    pairs.append((s * self.n_dp + d, goal[0] * self.n_dp + goal[1]))
        return lax.ppermute(value, ("seq", "dp"), pairs)

    def across(self, value, step):
        return self.send(value, lambda s, d: (s, d ^ (1 << self.orders[s % 2][step])))

    def chip(self, value):
        return self.send(value, lambda s, d: (s ^ 1, d))

    def along(self, value, bit):
        return self.send(value, lambda s, d: (s ^ (1 << bit), d))

    def masked(self, value, mask):
        return self.send(value, lambda s, d: (s ^ mask, d))

    def shifted(self, value, by):
        return self.send(value, lambda s, d: (s + by, d))

    def across_pair(self, value, step):
        return self.send(value, lambda s, d: (s, d ^ (1 << self.orders[(s ^ (s >> 1)) % 2][step])))

    def gather_step(self, pieces, step):
        return pieces + [self.across(piece, step) for piece in pieces]

    def sum_all(self, value):
        value = value + self.chip(value)
        for step in range(self.bits):
            value = value + self.across(value, step)
        for bit in range(1, self.seq_bits):
            value = value + self.along(value, bit)
        return value


class Reduction:
    def __init__(self, net, keep, give):
        self.net = net
        self.keep, self.give = keep, give
        z_bits = list(range(1, net.seq_bits))
        self.z_orders = (z_bits, z_bits[1:2] + z_bits[:1] + z_bits[2:])
        self.todo = ["across"] * net.bits + ["split"] + ["swap"] * (len(z_bits) - 1) + ["join"]
        self.done = 0
        self.got = None
        self.pending = False

    def along(self, value, place):
        return self.net.send(value, lambda s, d: (s ^ (1 << self.z_orders[s % 2][place]), d))

    def start(self):
        if not self.todo:
            return
        kind = self.todo[0]
        self.pending = True
        if kind == "across":
            self.got = self.net.across(self.give, self.done)
        elif kind == "split":
            half = self.keep.shape[0] // 2
            z_bit = jnp.where(self.net.core == 0, self.z_orders[0][0], self.z_orders[1][0])
            self.upper = (self.net.seq >> z_bit) % 2 == 1
            low, high = self.keep[:half], self.keep[half:]
            self.got = self.along(jnp.where(self.upper, low, high), 0)
            self.keep = jnp.where(self.upper, high, low)
        elif kind == "swap":
            self.got = self.along(self.keep, self.done - self.net.bits)
        else:
            self.got = self.along(self.keep, 0)

    def finish(self, after=None):
        if not self.pending:
            return
        if after is not None:
            self.got, _ = tie(self.got, after)
        kind = self.todo.pop(0)
        self.done += 1
        self.pending = False
        if kind == "join":
            low, high = jnp.where(self.upper, self.got, self.keep), jnp.where(self.upper, self.keep, self.got)
            self.keep = jnp.concatenate([low, high], axis=0)
            return
        half = self.keep.shape[0] // 2
        if kind == "across" and half:
            self.keep, self.give = add(self.keep[:half], self.got[:half]), add(self.keep[half:], self.got[half:])
        elif kind == "across":
            self.keep = add(self.keep[0], self.got[0])
        else:
            self.keep = add(self.keep, self.got)


def pin(value, *reds):
    held = [value]
    for red in reds:
        held += [red.keep] + ([red.give] if red.todo and red.todo[0] == "across" else [])
    held = list(tie(*held))
    value = held.pop(0)
    for red in reds:
        red.keep = held.pop(0)
        if red.todo and red.todo[0] == "across":
            red.give = held.pop(0)
    return value


def body(block_input, doc_bounds, first_gain, first_shift, qkv_weight, qv_bias, score_weight, out_weight, out_bias, second_gain, second_shift, fc_weight, fc_bias, down_weight, down_bias, cotangent):
    net = Net()
    seqs, blocks, width = block_input.shape
    tokens = seqs * blocks
    heads = score_weight.shape[1]
    shards = net.n_dp
    rows = width // shards
    hidden = fc_weight.shape[1]
    tail = seqs * WINDOW
    core = net.core
    place = jnp.arange(4, dtype=jnp.int32)
    info = jnp.where(place == 0, net.seq * blocks, jnp.where(place == 1, core, jnp.where(place == 2, net.dp, net.seq))).astype(jnp.int32)
    bounds = doc_bounds.T
    x_flat = block_input.reshape(tokens, width)
    dy = cotangent.reshape(tokens, width)
    wide = hidden // CHUNKS
    deep = hidden // shards // CHUNKS
    half_qkv = 3 * width // 2
    sems = lambda count: pltpu.SemaphoreType.DMA((count,))
    by_seq = lambda rows_, cols: pl.BlockSpec((rows_, cols), lambda s, *_: (s, 0))
    stat = pl.BlockSpec((1, 8, LANES), lambda s, *_: (s, 0, 0))
    table_spec = whole_spec((16, width))
    full = whole_spec((tokens, width))
    tile = 2 * blocks
    by_tile = pl.BlockSpec((tile, width), lambda i, *_: (i, 0))
    pairs = width // LANES
    parts = [(0, pairs)]

    vectors = [first_gain, first_shift, second_gain, second_shift, out_bias, down_bias, qv_bias, fc_bias]
    small_rows = sum(part.shape[0] for part in vectors) // rows + heads
    small = call(
        start_kernel,
        "start",
        (1,),
        [pl.BlockSpec(part.shape, lambda *_: (0,)) for part in vectors] + [whole_spec((heads, rows))],
        whole_spec((small_rows, rows)),
        shape((small_rows, rows), BF),
        micros=1,
        far_in=tuple(range(len(vectors) + 1)),
    )(*vectors, score_weight.T)

    def begin_gather(own):
        return [own, net.across(own, 0)], [net.across(own, 1)] if net.bits > 1 else []

    def end_gather(pieces, ahead):
        if net.bits > 1:
            pieces = pieces + ahead + [net.across(pieces[1], 1)]
        for step in range(2, net.bits):
            pieces = net.gather_step(pieces, step)
        return pieces

    small_state = begin_gather(small)
    first_weight, _ = tie(qkv_weight, small)
    own, x_tail = call(
        first_pack_kernel,
        "first_pack",
        (1,),
        [pl.BlockSpec((rows, half_qkv), lambda _, info: (0, info[1])), pl.BlockSpec((seqs, WINDOW, width), lambda *_: (0, blocks // WINDOW - 1, 0))],
        [whole_spec((rows, half_qkv)), whole_spec((tail, width))],
        [shape((rows, half_qkv), BF), shape((tail, width), BF)],
        prefetch=1,
        micros=2,
        far_in=(0, 1),
    )(info, first_weight, block_input)
    own, x_tail, *held = tie(own, x_tail, *small_state[0], *small_state[1])
    small_pieces = end_gather(held[:2], held[2:])
    qkv_state = begin_gather(own)
    x_tail = net.shifted(x_tail, 1)
    qkv_pieces = end_gather(*qkv_state)

    fc_weight, _ = tie(fc_weight, own)
    packs = call(
        feed_pack_kernel,
        "feed_pack",
        (1,),
        [whole_spec((rows, hidden)), whole_spec(down_weight.shape), whole_spec((rows, width))],
        [whole_spec((rows, wide))] * CHUNKS + [whole_spec((rows, wide + width // 2)), whole_spec((rows, wide))],
        [shape((rows, wide), BF)] * CHUNKS + [shape((rows, wide + width // 2), BF), shape((rows, wide), BF)],
        prefetch=1,
        micros=2,
        limit=24,
        far_in=(0, 1, 2),
    )(info, fc_weight, down_weight, out_weight)
    fc_own, feed_own = packs[:CHUNKS], packs[CHUNKS:]
    small_pieces[-1], *feed_own = tie(small_pieces[-1], *feed_own)
    first_own, _ = tie(feed_own[0], qkv_pieces[1])

    def begin_feed(own):
        if not net.by_pair:
            return begin_gather(own)
        return [own, net.across_pair(own, 0)], []

    def end_feed(pieces, ahead):
        if not net.by_pair:
            return end_gather(pieces, ahead)
        return pieces + [net.masked(pieces[1], 2), net.across_pair(pieces[1], 1)]

    a_state = begin_feed(first_own)

    table, score = call(
        params_kernel,
        "params",
        (1,),
        [whole_spec((small_rows, rows))] * shards,
        [table_spec, whole_spec((LANES, width))],
        [shape((16, width), F32), shape((LANES, width), BF)],
        scratch=[pltpu.VMEM((shards, small_rows, rows), F32)],
        prefetch=1,
        micros=1,
    )(info, *small_pieces)

    group = seqs // 2
    normed, importance, mass, stats = call(
        prep_kernel,
        "prep",
        (seqs // group,),
        [by_seq(group * blocks, width), table_spec, whole_spec((LANES, width))],
        [by_seq(group * blocks, width), by_seq(group * blocks, LANES), by_seq(group * blocks, LANES), pl.BlockSpec((group, 8, LANES), lambda s, *_: (s, 0, 0))],
        [shape((tokens, width), BF), shape((tokens, LANES), F32), shape((tokens, LANES), F32), shape((seqs, 8, LANES), F32)],
        prefetch=2,
        micros=3,
    )(info, bounds, x_flat, table, score)

    def scan_step(state, masks, got):
        spec = whole_spec((seqs, 8, LANES))
        return call(
            lambda *refs: scan_kernel(*refs, masks=masks),
            "scan",
            (1,),
            [spec] * (1 + len(masks)),
            spec,
            shape((seqs, 8, LANES), F32),
            prefetch=1,
            micros=0.5,
        )(info, state, *got)

    for bit in range(net.seq_bits - 1):
        stats = scan_step(stats, [1 << bit], [net.along(stats, bit)])
        if bit == 0:
            stats, *qkv_pieces = tie(stats, *qkv_pieces)
    qkv_others = [net.chip(piece) for piece in qkv_pieces[1:]]
    w_qkv = call(
        qkv_build_kernel,
        "qkv_build",
        (1,),
        [whole_spec((rows, 3 * width))] + [whole_spec((rows, half_qkv))] * (2 * shards - 2),
        ANY,
        shape((width, 3 * width), BF),
        scratch=[sems(2 * shards)],
        prefetch=1,
        micros=2,
    )(info, qkv_weight, *qkv_pieces[1:], *qkv_others)

    def build_feed(chunk, pieces, others):
        with_out = chunk == 0
        owns = [fc_own[chunk], down_weight] + ([out_weight] if with_out else [])
        specs = [whole_spec((rows, wide)), pl.BlockSpec((deep, width), lambda *_: (chunk, 0))] + ([whole_spec((rows, width))] if with_out else [])
        outs = [shape((width, wide), BF), shape((wide, width), BF)] + ([shape((width, width), BF)] if with_out else [])
        count = 3 + (shards - 1) * (1 + deep // rows + 2)
        return call(
            lambda *refs: feed_build_kernel(*refs, with_out=with_out, by_pair=net.by_pair),
            "feed_build",
            (1,),
            specs + [whole_spec(pieces[0].shape)] * (2 * shards - 2),
            [ANY] * len(outs),
            outs,
            scratch=[sems(count)],
            prefetch=1,
            micros=2,
        )(info, *owns, *pieces[1:], *others)

    normed_tail = call(
        prep_tail_kernel,
        "prep_tail",
        (1,),
        [whole_spec((tail, width)), table_spec],
        whole_spec((tail, width)),
        shape((tail, width), BF),
        micros=1,
    )(x_tail, table)
    w_qkv, *held = tie(w_qkv, *a_state[0], *a_state[1])
    a_pieces = end_feed(held[:2], held[2:])
    second_own, _ = tie(feed_own[1], held[1])
    b_state = begin_feed(second_own)
    col = lambda rows_: pl.BlockSpec((rows_, width), lambda j: (0, j))
    qkv, qkv_tail = call(
        qkv_kernel,
        "qkv",
        (3,),
        [full, whole_spec((tail, width)), col(width), table_spec],
        [col(tokens), pl.BlockSpec((tail, width), lambda j: (0, jnp.maximum(j - 1, 0)))],
        [shape((tokens, 3 * width), BF), shape((tail, 2 * width), BF)],
        micros=6.5,
        limit=24,
    )(normed, normed_tail, w_qkv, table)
    qkv, got = tie(qkv, net.along(stats, net.seq_bits - 1))
    before = scan_step(stats, [1 << (net.seq_bits - 1)], [got])

    attended, probs, gates, inverse = call(
        attention_kernel,
        "attention",
        (seqs,),
        [by_seq(blocks, 3 * width), by_seq(WINDOW, 2 * width), by_seq(blocks, LANES), by_seq(blocks, LANES), stat],
        [by_seq(blocks, width), by_seq(blocks, 2 * width), by_seq(WINDOW, width), by_seq(WINDOW, LANES)],
        [shape((tokens, width), BF), shape((tokens, 2 * width), BF), shape((tail, width), BF), shape((tail, LANES), F32)],
        prefetch=2,
        micros=10.5,
        far=(1, 2, 3),
    )(info, bounds, qkv, qkv_tail, importance, mass, before)

    attended, *held = tie(attended, *a_pieces, *b_state[0], *b_state[1])
    a_pieces, held = held[: len(a_pieces)], held[len(a_pieces) :]
    b_pieces = end_feed(held[:2], held[2:])
    fc_a, down_a, w_out = build_feed(0, a_pieces, [net.chip(piece) for piece in a_pieces[1:]])

    middle, normed_second = call(
        project_kernel,
        "project",
        (tokens // tile,),
        [by_tile, by_tile, whole_spec((width, width)), table_spec],
        [by_tile, by_tile],
        [shape((tokens, width), F32), shape((tokens, width), BF)],
        micros=3,
    )(attended, x_flat, w_out, table)

    hids, dpres, d_fc_bias = [], [], []

    def feed(chunk, fc, down, normed_second):
        still = pl.BlockSpec((tokens, width), lambda *_: (0, 0), pipeline_mode=pl.Buffered(1))
        column = lambda rows_: pl.BlockSpec((rows_, width), lambda j, *_: (0, j))
        row = pl.BlockSpec((width, width), lambda j, *_: (j, 0))
        hid, dpre, d_bias, keep, give = call(
            lambda *refs: feed_kernel(*refs, chunk=chunk),
            "feed",
            (BLOCKS,),
            [still, still, column(width), row, table_spec],
            [column(tokens), column(tokens), column(8), row, row],
            [shape((tokens, wide), BF), shape((tokens, wide), BF), shape((8, wide), F32), shape((wide, width), BF), shape((wide, width), BF)],
            prefetch=1,
            micros=15,
            limit=30,
            far=(0, 1, 3, 4),
        )(info, normed_second, dy, fc, down, table)
        hids.append(hid)
        dpres.append(dpre)
        d_fc_bias.append(d_bias)
        return keep, give

    def feed_add(kept, got):
        half = (shards // 2, rows, wide)
        keep, give = call(
            feed_add_kernel,
            "feed_add",
            (1,),
            [whole_spec((wide, width))] * 2,
            [whole_spec(half)] * 2,
            [shape(half, BF)] * 2,
            scratch=[pltpu.VMEM((shards, rows, wide), BF)],
            prefetch=1,
            micros=2,
            limit=20,
        )(info, kept, got)
        return Reduction(net, keep, give)

    b_first = net.chip(b_pieces[1])
    normed_second, b_first = tie(normed_second, b_first)
    kept_a, give_a = feed(0, fc_a, down_a, normed_second)
    give_a, *b_pieces = tie(give_a, *b_pieces)
    got_a = net.chip(give_a)
    fc_b, down_b = build_feed(1, b_pieces, [b_first] + [net.chip(piece) for piece in b_pieces[2:]])
    red_a = feed_add(kept_a, got_a)
    fc_b = pin(fc_b, red_a)
    red_a.start()
    kept_b, give_b = feed(1, fc_b, down_b, normed_second)
    got_b = net.chip(give_b)
    red_a.finish(kept_b)
    dpres[1] = pin(dpres[1], red_a)
    red_a.start()

    half_out = (shards, rows, width // 2)
    groups = 2
    part_tokens, part_tail, part_seqs = tokens // groups, tail // groups, seqs // groups
    by_part = pl.BlockSpec((part_tokens, width), lambda i, *_: (i, 0))
    d_middle, branch, sums_second = call(
        middle_kernel,
        "middle",
        (groups,),
        [pl.BlockSpec((part_tokens, wide), lambda i, *_: (i, 0))] * CHUNKS + [whole_spec((width, wide))] * CHUNKS + [by_part, by_part, table_spec],
        [by_part, by_part, whole_spec((8, width))],
        [shape((tokens, width), F32), shape((tokens, width), BF), shape((8, width), F32)],
        micros=1.0,
        limit=30,
        far=(0,),
        far_in=(0, 1, 5),
    )(*dpres, fc_a, fc_b, middle, dy, table)

    red_a.finish(branch)
    red_b = feed_add(kept_b, got_b)
    branch = pin(branch, red_a, red_b)
    red_a.start()
    red_b.start()
    d_attended, keep_out, give_out = call(
        branch_kernel,
        "branch",
        (1,),
        [full, full, whole_spec((width, width))],
        [full, whole_spec(half_out), whole_spec(half_out)],
        [shape((tokens, width), BF), shape(half_out, BF), shape(half_out, BF)],
        prefetch=1,
        micros=1.0,
        limit=24,
        far=(0,),
        far_in=(1,),
    )(info, branch, attended, w_out)
    got_out = net.chip(give_out)

    def attention_back(part, d_attended):
        shifted = lambda rows_, cols: pl.BlockSpec((rows_, cols), lambda s, *_: (part * part_seqs + s, 0))
        return call(
            lambda *refs: attention_back_kernel(*refs, first_seq=part * part_seqs, pairs=pairs),
            "attention_back",
            (part_seqs,),
            [shifted(blocks, 3 * width), shifted(WINDOW, 2 * width), shifted(blocks, width), shifted(blocks, width), shifted(blocks, 2 * width), shifted(WINDOW, width), shifted(WINDOW, LANES), shifted(blocks, LANES), pl.BlockSpec((1, 8, LANES), lambda s, *_: (part * part_seqs + s, 0, 0))],
            [by_seq(blocks, 3 * width), by_seq(WINDOW, 3 * width), by_seq(blocks, LANES), pl.BlockSpec((1, 1, LANES), lambda s, *_: (s, 0, 0))],
            [shape((part_tokens, 3 * width), BF), shape((part_tail, 3 * width), BF), shape((part_tokens, LANES), F32), shape((part_seqs, 1, LANES), F32)],
            scratch=[pltpu.VMEM((LANES, LANES), F32)],
            prefetch=2,
            micros=0.1,
            far=(0, 1),
            far_in=(0, 1, 2, 3, 4, 5, 6),
        )(info, bounds, qkv, qkv_tail, attended, d_attended, probs, gates, inverse, importance, before)

    def qkv_grad(backs):
        side = lambda i, info: (0, jnp.where(i == 0, 1 - info[1], info[1]))
        result = (shards, rows, half_qkv)
        still = lambda rows_: pl.BlockSpec((rows_, width), lambda *_: (0, 0), pipeline_mode=pl.Buffered(1))
        held = lambda dims: pl.BlockSpec(dims, lambda *_: (0,) * len(dims), pipeline_mode=pl.Buffered(1))
        return call(
            lambda *refs: qkv_grad_kernel(*refs, groups=groups),
            "qkv_grad",
            (2,),
            [still(tokens), still(tail)] + [pl.BlockSpec((part_tokens, half_qkv), side)] * groups + [pl.BlockSpec((part_tail, half_qkv), side)] * groups,
            [held(result), held(result), held((8, half_qkv)), held((8, half_qkv))],
            [shape(result, BF), shape(result, BF), shape((8, half_qkv), F32), shape((8, half_qkv), F32)],
            prefetch=1,
            micros=2,
            limit=22,
            far_in=(0, 1, 2, 3, 4, 5),
            far=(0, 1),
        )(info, normed, normed_tail, *[back[0] for back in backs], *[back[1] for back in backs])

    half_shards = shards // 2

    def halved(kept, got):
        return Reduction(net, add(kept[:half_shards], got[:half_shards]), add(kept[half_shards:], got[half_shards:]))

    red_o = halved(keep_out, got_out)
    d_attended = pin(d_attended, red_o)
    red_o.start()
    backs = [list(attention_back(0, d_attended))]
    red_a.finish(backs[0][0])
    d_attended, _ = tie(d_attended, backs[0][0])
    d_attended = pin(d_attended, red_a)
    red_a.start()
    backs.append(list(attention_back(1, d_attended)))
    red_a.finish()
    red_b.finish()
    red_o.finish()
    red_b.keep = jnp.concatenate([red_b.keep, red_o.keep], axis=2)
    red_b.give = jnp.concatenate([red_b.give, red_o.give], axis=2)
    backs[1][0] = pin(backs[1][0], red_a, red_b)
    red_a.start()
    red_b.start()
    total_all = jnp.concatenate([back[3] for back in backs], axis=0)
    total_after = jnp.zeros_like(total_all)

    def suffix_step(total_after, total_all, bit, after=None):
        got = net.along(total_all, bit)
        if after is not None:
            got, _ = tie(got, after)
        earlier = (net.seq >> bit) % 2 == 0
        return jnp.where(earlier, total_after + got, total_after), total_all + got

    total_after, total_all = suffix_step(total_after, total_all, 0)
    backs[1][0], total_all = tie(backs[1][0], total_all)
    give_qkv, keep_qkv, sums_given, sums_kept = qkv_grad(backs)

    for bit in range(1, net.seq_bits - 1):
        total_after, total_all = suffix_step(total_after, total_all, bit, keep_qkv)
    give_qkv, total_all, total_after, red_a.got, red_b.got = tie(give_qkv, total_all, total_after, red_a.got, red_b.got)
    got_qkv = net.chip(give_qkv)
    red_a.finish()
    red_b.finish()
    d_halos = [back[1] for back in backs]
    d_halos[0], _ = tie(d_halos[0], give_qkv)
    d_halos[0] = pin(d_halos[0], red_a, red_b)
    red_a.start()
    red_b.start()
    d_tail, sums_tail = call(
        tail_back_kernel,
        "tail_back",
        (1,),
        [whole_spec((part_tail, 3 * width))] * groups + [whole_spec((width, 3 * width)), whole_spec((tail, width)), table_spec],
        [whole_spec((tail, width)), whole_spec((8, width))],
        [shape((tail, width), BF), shape((8, width), F32)],
        micros=1,
        limit=16,
        far_in=(0, 1),
    )(*d_halos, w_qkv, x_tail, table)
    got_qkv, _ = tie(got_qkv, d_tail)
    d_tail, got_qkv, total_all, total_after = tie(d_tail, got_qkv, total_all, total_after)
    back = net.shifted(d_tail, -1)
    red_c = halved(keep_qkv, got_qkv)
    middle = pin(middle, red_c)
    red_c.start()

    def output(part, before_):
        still = pl.BlockSpec((part_tokens, width), lambda j: (part, 0))
        extra = [] if before_ is None else [before_]
        return call(
            output_kernel,
            "output",
            (BLOCKS,),
            [pl.BlockSpec((part_tokens, width), lambda j: (part, j))] * CHUNKS + [pl.BlockSpec((width, width), lambda j: (j, 0))] * CHUNKS + [still, table_spec] + [ANY] * len(extra),
            still,
            shape((tokens, width), BF),
            scratch=[pltpu.VMEM((part_tokens, width), F32)],
            micros=1.0,
            limit=24,
            alias={2 * CHUNKS + 2: 0} if extra else {},
            far=(0,),
            far_in=(0, 1, 2, 3, 4),
        )(*hids, down_a, down_b, middle, table, *extra)

    got_last = net.along(total_all, net.seq_bits - 1)
    block_output = output(0, None)
    block_output, red_b.got, got_last, back = tie(block_output, red_b.got, got_last, back)
    red_b.finish()
    total_after = jnp.where((net.seq >> (net.seq_bits - 1)) % 2 == 0, total_after + got_last, total_after)
    back = back.reshape(seqs, WINDOW, width)
    total_after = pin(total_after, red_b)
    red_b.start()

    per_tile = tile // blocks
    per_group = tokens // tile // groups
    grouped_tile = lambda cols: [pl.BlockSpec((tile, cols), lambda i, *_, k=k: (jnp.clip(i - k * per_group, 0, per_group - 1), 0)) for k in range(groups)]
    by_lane = pl.BlockSpec((tile, LANES), lambda i, *_: (i, 0))
    input_grad, sums_first, d_score = call(
        lambda *refs: input_grad_kernel(*refs, groups=groups),
        "input_grad",
        (tokens // tile,),
        grouped_tile(3 * width)
        + grouped_tile(LANES)
        + [
            whole_spec((width, 3 * width)),
            whole_spec((LANES, width)),
            by_tile,
            by_tile,
            table_spec,
            by_tile,
            pl.BlockSpec((per_tile, WINDOW, width), lambda i, *_: (i, 0, 0)),
            by_lane,
            pl.BlockSpec((per_tile, 8, LANES), lambda i, *_: (i, 0, 0)),
            pl.BlockSpec((per_tile, 1, LANES), lambda i, *_: (i, 0, 0)),
        ],
        [by_tile, whole_spec((8, width)), whole_spec((LANES, width))],
        [shape((tokens, width), F32), shape((8, width), F32), shape((LANES, width), F32)],
        prefetch=2,
        micros=1.0,
        limit=24,
        far_in=(0, 1) + tuple(2 * groups + k for k in (2, 3, 5)),
    )(info, bounds, *[back_[0] for back_ in backs], *[back_[2] for back_ in backs], w_qkv, score, normed, x_flat, table, d_middle, back, importance, before, total_after)

    for red in (red_b, red_c):
        red.finish()
        sums_first = pin(sums_first, red)
    packed = call(
        small_pack_kernel,
        "small_pack",
        (1,),
        [whole_spec((8, width))] * 3 + [whole_spec((8, half_qkv))] * 2 + [whole_spec((8, wide))] * CHUNKS + [whole_spec((LANES, width))],
        whole_spec((shards, small_rows, rows)),
        shape((shards, small_rows, rows), F32),
        scratch=[pltpu.VMEM((32, width), F32)],
        prefetch=1,
        micros=1,
    )(info, sums_first, sums_tail, sums_second, sums_kept, sums_given, *d_fc_bias, d_score)

    def finish(red):
        other = net.chip(red.keep)
        return jnp.where(core == 0, red.keep, other), jnp.where(core == 0, other, red.keep)

    def early_grads():
        fc_grads, down_grads = zip(finish(red_a), finish(red_b))
        out_grads = [fc_grads[1][:, wide:], down_grads[1][:, wide:]]
        fc_grads, down_grads = [part[:, :wide] for part in fc_grads], [part[:, :wide] for part in down_grads]
        d_out = jnp.concatenate(out_grads, axis=1).astype(F32)
        d_fc = jnp.concatenate([part[:, d * deep : (d + 1) * deep] for d in range(shards) for part in fc_grads], axis=1).astype(F32)
        d_down = jnp.concatenate([part[:, k * width : (k + 1) * width] for part in down_grads for k in range(deep // rows)], axis=0).astype(F32)
        return [d_out, d_fc, d_down]

    reds = [red_a, red_b, red_c]
    early, tied = None, False
    packed = packed + net.chip(packed)

    def small_across(value, step):
        half = value.shape[0] // 2
        return value[:half] + net.send(value[half:], lambda s, d: (s, d ^ (1 << net.orders[0][step])))

    small_steps = [lambda value, k=k: small_across(value, k) for k in range(net.bits)]
    small_steps += [lambda value, k=k: value + net.along(value, k) for k in range(1, net.seq_bits)]
    packed, middle = tie(packed, middle)
    red_b.start()
    red_c.start()
    packed = small_steps.pop(0)(packed)
    block_output = output(1, block_output)
    packed, block_output = tie(packed, block_output)
    while small_steps or any(red.todo for red in reds):
        active = [red for red in reds if red.pending]
        for red in active:
            red.finish()
        packed = pin(packed, *active)
        if early is not None and not tied:
            packed, *early = tie(packed, *early)
            tied = True
        for red in reds:
            if red.todo:
                red.start()
        if early is None and not red_a.todo and not red_b.todo:
            early = early_grads()
        if small_steps:
            packed = small_steps.pop(0)(packed)
    packed, d_out, d_fc, d_down = tie(packed, *early)
    packed = packed[0]

    d_qkv = jnp.concatenate(finish(red_c), axis=1).astype(F32)

    small_outs = [shape(part.shape, F32) for part in vectors] + [shape((heads, rows), F32)]
    dg_first, ds_first, dg_second, ds_second, db_out, db_down, db_qv, db_fc, d_score = call(
        end_kernel,
        "end",
        (1,),
        [whole_spec((small_rows, rows))],
        [pl.BlockSpec(part.shape, lambda *_, n=len(part.shape): (0,) * n) for part in small_outs],
        small_outs,
        micros=1,
    )(packed)
    return (
        block_output.reshape(seqs, blocks, width),
        input_grad.reshape(seqs, blocks, width),
        dg_first,
        ds_first,
        d_qkv,
        db_qv,
        d_score.T,
        d_out,
        db_out,
        dg_second,
        ds_second,
        d_fc,
        db_fc,
        d_down,
        db_down,
    )


def solution(mesh):
    split = P("dp", "seq", None)
    rows = P("dp", None)
    flat = P("dp")
    in_specs = (split, rows, flat, flat, rows, flat, rows, rows, flat, flat, flat, rows, flat, rows, flat, split)
    out_specs = (split, split, flat, flat, rows, flat, rows, rows, flat, flat, flat, rows, flat, rows, flat)
    return jax.shard_map(body, mesh=mesh, in_specs=in_specs, out_specs=out_specs, check_vma=False)
```
